32 devices in a mesh: wide: 16 (over z, x, core), narrow: 2 (over y).
Axes of the slice: x: 2, y: 2, z: 4, core: 2. Of those that a mesh axis runs over, the one named last changes fastest.
Arguments:
- features: bfloat16 [128, 16, 8, 192], P('wide', 'narrow'), may hold values from -6 to 6
- weight: bfloat16 [5184, 192], replicated, may hold values from -0.078125 to 0.078125
- voxel_mask: int32 [128, 16, 8], P('wide', 'narrow'), may hold values 0 or 1
- cotangent: bfloat16 [128, 16, 8, 192], P('wide', 'narrow'), may hold values from -6 to 6
Outputs:
- activation: bfloat16 [128, 16, 8, 192], P('wide', 'narrow')
- grad_input: bfloat16 [128, 16, 8, 192], P('wide', 'narrow')
- grad_weight: float32 [192, 5184], P('wide')
The draws below stay inside these ranges and needn't reach their ends.
All inputs are finite; a program needn't handle non-finite values. No bound on the sum of `voxel_mask` on one device may be relied on, other than what follows from the above.
Results may differ from the reference program's by a relative error of at most 0.0049.
Values may be sent and summed in bfloat16 or wider, within the bound.
No kernel may reach another device: no remote copies, remote signals or barrier semaphores. Data moves between devices by JAX's collectives and lax.ppermute only.
A program may use at most 64 MiB of HBM per device.

```python
import jax
import jax.numpy as jnp

C = 192
BZ = 8
NX = 128
NY = 16
VOXELS = 16384


def plant(entries, own_key, low, largest):
    place = [jax.random.randint(jax.random.fold_in(own_key, axis), (), 0, length) for axis, length in enumerate(entries.shape)]
    main_axis = entries.shape.index(max(entries.shape))
    neighbour = place[:main_axis] + [(place[main_axis] + 1) % entries.shape[main_axis]] + place[main_axis + 1:]
    return entries.at[tuple(place)].set(low).at[tuple(neighbour)].set(largest)


def spiked(drawn, stream_key, source, target, blocks, factor):
    def block_of(axis_at):
        return (jnp.arange(drawn.shape[axis_at]) // (drawn.shape[axis_at] // blocks)).reshape((-1,) + (1,) * (drawn.ndim - 1 - axis_at))

    first = jax.random.permutation(stream_key, blocks)[block_of(target)]
    far = (block_of(target) + blocks // 2) % blocks
    return jnp.where((block_of(source) == first) | (block_of(source) == far), factor * drawn, drawn)


def block_levels(own_key, dims, pieces, least, high):
    loudness, own = 1.0, jax.random.fold_in(own_key, 6)
    for axis_at, shards_of in pieces:
        steps = jnp.exp(jax.random.uniform(jax.random.fold_in(own, axis_at), (shards_of,), jnp.float32, least / len(pieces), high / len(pieces)))
        loudness = loudness * jnp.repeat(steps, dims[axis_at] // shards_of).reshape([-1 if axis == axis_at else 1 for axis in range(len(dims))])
    return loudness


def bell_draw(stream_key, extent, width, reach, cuts=(), held_as=jnp.bfloat16):
    gain = block_levels(stream_key, extent, cuts, -0.22, 0.18) if cuts else 1.0
    result = jax.random.normal(stream_key, extent, jnp.float32) * width * gain
    return jnp.minimum(jnp.maximum(result, -reach), reach).astype(held_as)


def heavy_noise(own_key, shape, width, reach, shards, heavy, kind=jnp.bfloat16):
    array = width * jax.random.normal(own_key, shape, jnp.float32)
    if shards:
        array = array * block_levels(own_key, shape, shards, -0.22, 0.18)
    return jnp.clip(spiked(array, jax.random.fold_in(own_key, 3), *heavy), -reach, reach).astype(kind)


def setup_inputs(seed: int = 0) -> dict:
    arg_keys = jax.random.split(jax.random.key(seed), 5)
    return {
        "features": bell_draw(arg_keys[0], (NX, NY, BZ, C), 1.0, 6.0, ((0, 16), (1, 2))),
        "weight": bell_draw(arg_keys[1], (27 * C, C), (27 * C) ** -0.5, 0.078125),
        "voxel_mask": plant((jax.random.randint(arg_keys[2], (NX, NY, BZ), 0, 2) < 1).astype(jnp.int32), jax.random.fold_in(arg_keys[2], 1), 0, 1),
        "cotangent": heavy_noise(arg_keys[3], (NX, NY, BZ, C), 1.0, 6.0, ((0, 16), (1, 2)), (0, 3, 16, 2.0)),
    }


def shifted(field, off_a, off_b, off_c):
    padded = jnp.pad(field, ((1, 1), (1, 1), (1, 1), (0, 0)))
    size_x, size_y, size_z = (field.shape[0], field.shape[1], field.shape[2])
    return padded[1 + off_a:1 + off_a + size_x, 1 + off_b:1 + off_b + size_y, 1 + off_c:1 + off_c + size_z, :]

def reference(features, weight, voxel_mask, cotangent):
    channels = features.shape[3]
    live = voxel_mask.astype(jnp.float32).reshape(-1, 1)
    masked = features * voxel_mask.astype(features.dtype)[..., None]
    pre = jnp.zeros((masked.shape[0] * masked.shape[1] * masked.shape[2], channels), jnp.float32)
    tap_index = 0
    for off_a in (-1, 0, 1):
        for off_b in (-1, 0, 1):
            for off_c in (-1, 0, 1):
                block = weight[tap_index * channels:(tap_index + 1) * channels]
                source = shifted(masked, off_a, off_b, off_c).reshape(-1, channels)
                pre = pre + jnp.dot(source, block, preferred_element_type=jnp.float32)
                tap_index += 1
    sig = jax.nn.sigmoid(pre)
    activation = (pre * sig * live).astype(features.dtype).reshape(features.shape)
    slope = sig * (1.0 + pre * (1.0 - sig))
    grad_pre = (cotangent.reshape(-1, channels).astype(jnp.float32) * live * slope).astype(features.dtype)
    grad_grid = grad_pre.reshape(features.shape)
    masked_flat = masked.reshape(-1, channels)
    grad_field = jnp.zeros_like(pre)
    blocks = []
    tap_index = 0
    for off_a in (-1, 0, 1):
        for off_b in (-1, 0, 1):
            for off_c in (-1, 0, 1):
                block = weight[tap_index * channels:(tap_index + 1) * channels]
                back = shifted(grad_grid, -off_a, -off_b, -off_c).reshape(-1, channels)
                grad_field = grad_field + jnp.dot(back, block.T, preferred_element_type=jnp.float32)
                source = shifted(masked, off_a, off_b, off_c).reshape(-1, channels)
                blocks.append(jnp.dot(grad_pre.T, source, preferred_element_type=jnp.float32))
                tap_index += 1
    grad_input = (grad_field * live).astype(features.dtype).reshape(features.shape)
    grad_weight = jnp.concatenate(blocks, axis=1) / jnp.sqrt(jnp.float32(VOXELS))
    return (activation, grad_input, grad_weight)
```

```python
import functools

import jax
import jax.numpy as jnp
from jax import lax
from jax.experimental import pallas as pl
from jax.experimental.pallas import tpu as pltpu
from jax.sharding import Mesh
from jax.sharding import PartitionSpec as P

WIDE = ("depth", "quad")
QUAD = 4
VMEM_BYTES = 56 * 1024 * 1024
OFFSETS = (-1, 0, 1)


def shift_z(field, step):
    if step == 0:
        return field
    depth = field.shape[1]
    moved = pltpu.roll(field, (-step) % depth, 1)
    z = lax.broadcasted_iota(jnp.int32, field.shape, 1) + step
    return jnp.where((z >= 0) & (z < depth), moved, 0.0)


def forward_kernel(
    flags, masked, cot, left, right, low, high, live, weight, pick,
    act_ref, gp_ref, slices_ref, ext, cols,
):
    width, rows, channels = masked.shape
    depth = 8
    f32 = jnp.float32
    use_low = flags[0].astype(f32)
    use_high = flags[1].astype(f32)
    tall = rows + 4 * depth
    mid = rows + 2 * depth
    span = width + 4
    strip = span * 2 * depth
    ext[0:2, 16 : 16 + rows, :] = left[0:2].astype(f32)
    ext[2 : 2 + width, 16 : 16 + rows, :] = masked[...].astype(f32)
    ext[2 + width :, 16 : 16 + rows, :] = right[0:2].astype(f32)
    ext[:, 0:16, :] = low[0:strip].astype(f32).reshape(span, 16, channels) * use_low
    ext[:, 16 + rows :, :] = high[0:strip].astype(f32).reshape(span, 16, channels) * use_high
    field = ext[...].reshape(span * tall // depth, depth, channels)
    for c in OFFSETS:
        moved = shift_z(field, c).reshape(span, tall, channels)
        for b in OFFSETS:
            at = ((b + 1) * 3 + c + 1) * channels
            start = depth * (b + 1)
            cols[:, :, at : at + channels] = moved[:, start : start + mid].astype(jnp.bfloat16)
    nine = 9 * channels
    pre = jnp.zeros(((width + 2) * mid, channels), f32)
    for a in range(3):
        pre += jnp.dot(
            cols[a : a + width + 2].reshape((width + 2) * mid, nine),
            weight[a * nine : (a + 1) * nine, :],
            preferred_element_type=f32,
        )
    sig = jax.nn.sigmoid(pre)
    act = (pre * sig).reshape(width + 2, mid, channels)[1 : 1 + width, depth : depth + rows]
    act_ref[...] = (act * live[...]).astype(jnp.bfloat16)
    slope = (sig * (1.0 + pre * (1.0 - sig))).reshape(width + 2, mid, channels)
    low_cot = low[strip:].astype(f32).reshape(width + 2, depth, channels) * use_low
    high_cot = high[strip:].astype(f32).reshape(width + 2, depth, channels) * use_high
    centre = jnp.concatenate([left[2:3], cot[...], right[2:3]], axis=0).astype(f32)
    full = jnp.concatenate([low_cot, centre, high_cot], axis=1)
    grad = (full * slope).astype(jnp.bfloat16)
    gp_ref[...] = grad
    inner = (full * slope)[:, depth : depth + rows].astype(jnp.bfloat16)
    turned = lax.dot_general(
        pick[...],
        inner.reshape((width + 2) * rows, channels),
        (((1,), (1,)), ((), ())),
        preferred_element_type=f32,
    )
    slices_ref[...] = turned.reshape(slices_ref.shape).astype(jnp.bfloat16)


def input_kernel(gp, live, weight, out_ref, cols):
    width, rows, channels = out_ref.shape
    depth = 8
    f32 = jnp.float32
    tall = rows + 2 * depth
    field = gp[...].astype(f32).reshape((width + 2) * tall // depth, depth, channels)
    for c in OFFSETS:
        moved = shift_z(field, -c).reshape(width + 2, tall, channels)
        for b in OFFSETS:
            at = ((b + 1) * 3 + c + 1) * channels
            start = depth * (1 - b)
            cols[:, :, at : at + channels] = moved[:, start : start + rows].astype(jnp.bfloat16)
    nine = 9 * channels
    total = jnp.zeros((width * rows, channels), f32)
    for a in range(3):
        total += jnp.dot(
            cols[2 - a : 2 - a + width].reshape(width * rows, nine),
            weight[a * nine : (a + 1) * nine, :],
            preferred_element_type=f32,
        )
    out_ref[...] = (total.reshape(width, rows, channels) * live[...]).astype(jnp.bfloat16)


def kernel_grad_kernel(place, slices, masked, own_ref, one_ref, two_ref, three_ref, cols, part):
    f32 = jnp.float32
    members, group, lanes = slices.shape
    slabs, lane, channels = masked.shape
    per = slabs // QUAD
    depth = 8
    at = lax.broadcasted_iota(jnp.int32, (group, lane), 1)
    y, z = at // depth, at % depth
    half = lane // 2
    tall = lane // depth
    base = [None] * (slabs + 2)
    for quad in range(QUAD):
        first = slices[2 * quad].astype(f32)
        second = slices[2 * quad + 1].astype(f32)
        for m in range((per + 2) // 2):
            one = first[:, m * lane : (m + 1) * lane]
            two = second[:, m * lane : (m + 1) * lane]
            pair = (
                jnp.where(at < half, one, pltpu.roll(two, half, 1)),
                jnp.where(at < half, pltpu.roll(one, half, 1), two),
            )
            for odd in range(2):
                k = 2 * m + odd
                slab = quad * per + k
                inside = 1 <= k <= per
                edge = (quad == 0 and k == 0) or (quad == QUAD - 1 and k == per + 1)
                if inside or edge:
                    base[slab] = pair[odd]
    for slab in range(slabs + 2):
        pieces = []
        for b in OFFSETS:
            for c in OFFSETS:
                step = (depth * b + c) % lane
                moved = base[slab] if step == 0 else pltpu.roll(base[slab], step, 1)
                keep = (y - b >= 0) & (y - b < tall) & (z - c >= 0) & (z - c < depth)
                pieces.append(jnp.where(keep, moved, 0.0))
        cols[:, slab * lane : (slab + 1) * lane] = jnp.concatenate(pieces, axis=0).astype(
            jnp.bfloat16
        )
    field = masked[...].reshape(slabs * lane, channels)
    planes, rows, _ = part.shape
    for a in range(3):
        start = (2 - a) * lane
        got = jnp.dot(
            cols[:, start : start + slabs * lane], field, preferred_element_type=f32
        ).reshape(9, planes, rows, channels)
        for plane in range(planes):
            part[plane, :, a * 9 * channels : (a + 1) * 9 * channels] = jnp.concatenate(
                [got[tap, plane] for tap in range(9)], axis=1
            )
    me = place[0]
    own_ref[...] = part[me]
    for step, ref in ((1, one_ref), (2, two_ref), (3, three_ref)):
        ref[...] = part[lax.rem(me + step, planes)].astype(jnp.bfloat16)


def sum_kernel(scale, own, one, two, three, out_ref):
    f32 = jnp.float32
    total = own[...] + one[...].astype(f32) + two[...].astype(f32) + three[...].astype(f32)
    out_ref[...] = total * scale


def vmem(count):
    return [pl.BlockSpec(memory_space=pltpu.VMEM)] * count


SMEM = pl.BlockSpec(memory_space=pltpu.SMEM)


def params():
    return pltpu.CompilerParams(vmem_limit_bytes=VMEM_BYTES)


def cost(flops, moved):
    return pl.CostEstimate(flops=flops, bytes_accessed=moved, transcendentals=0)


def planes_local(features, weight, voxel_mask, cotangent):
    bf16 = jnp.bfloat16
    f32 = jnp.float32
    width, wide_y, depth, channels = features.shape
    rows = wide_y * depth
    planes = lax.axis_size("depth")
    quads = lax.axis_size("quad")
    count = planes * quads
    plane = lax.axis_index("depth")
    side = lax.axis_index("narrow")
    sides = lax.axis_size("narrow")

    live = voxel_mask.reshape(width, rows, 1)
    masked = features.reshape(width, rows, channels) * live.astype(bf16)
    cot = cotangent.reshape(width, rows, channels) * live.astype(bf16)
    live = live.astype(f32)

    up = [(i, i + 1) for i in range(count - 1)]
    down = [(i + 1, i) for i in range(count - 1)]
    left = lax.ppermute(jnp.concatenate([masked[-2:], cot[-1:]], axis=0), WIDE, up)
    right = lax.ppermute(jnp.concatenate([masked[:2], cot[:1]], axis=0), WIDE, down)

    halo = 2 * depth
    wide_masked = jnp.concatenate([left[:2], masked, right[:2]], axis=0)
    wide_cot = jnp.concatenate([left[2:], cot, right[2:]], axis=0)

    def strip(first):
        if first:
            parts = wide_masked[:, :halo], wide_cot[:, :depth]
        else:
            parts = wide_masked[:, rows - halo :], wide_cot[:, rows - depth :]
        return jnp.concatenate([part.reshape(-1, channels) for part in parts], axis=0)

    swapped = lax.ppermute(
        jnp.where(side == 0, strip(False), strip(True)), "narrow", [(0, 1), (1, 0)]
    )
    flags = jnp.stack([side, 1 - side]).astype(jnp.int32)

    group = 4 * 8
    members = quads * sides
    per = channels // count
    share = per // sides
    index = jnp.arange(members * group)
    q, s = index // (sides * group), index // group % sides
    p, r = index // 8 % planes, index % 8
    source = jnp.where(r < share, per * (quads * p + q) + share * s + r, -1)
    pick = (source[:, None] == jnp.arange(channels)[None, :]).astype(bf16)

    bricks = lax.all_gather(masked, "narrow", axis=1, tiled=True)
    bricks = lax.all_gather(bricks, "quad", axis=0, tiled=True)

    span = (width + 2) * rows
    act, gp, slices = pl.pallas_call(
        forward_kernel,
        out_shape=(
            jax.ShapeDtypeStruct((width, rows, channels), bf16),
            jax.ShapeDtypeStruct((width + 2, rows + 2 * depth, channels), bf16),
            jax.ShapeDtypeStruct((members, group, span), bf16),
        ),
        in_specs=[SMEM] + vmem(9),
        out_specs=tuple(vmem(3)),
        scratch_shapes=[
            pltpu.VMEM((width + 4, rows + 4 * depth, channels), f32),
            pltpu.VMEM((width + 4, rows + 2 * depth, 9 * channels), bf16),
        ],
        compiler_params=params(),
        cost_estimate=cost(2 * 800 * 5184 * 256, 4 << 20),
        name="forward",
    )(flags, masked, cot, left, right, swapped, swapped, live, weight, pick)

    slices = lax.all_to_all(slices, ("quad", "narrow"), 0, 0, tiled=True)

    taps = weight.reshape(27, channels, channels)
    turned = jnp.transpose(taps, (0, 2, 1)).reshape(27 * channels, channels)
    grad_input = pl.pallas_call(
        input_kernel,
        out_shape=jax.ShapeDtypeStruct((width, rows, channels), bf16),
        in_specs=vmem(3),
        out_specs=vmem(1)[0],
        scratch_shapes=[pltpu.VMEM((width + 2, rows, 9 * channels), bf16)],
        compiler_params=params(),
        cost_estimate=cost(2 * 512 * 5184 * 256, 4 << 20),
        name="input_gradient",
    )(gp, live, turned)

    total = 27 * channels
    place = plane.reshape(1).astype(jnp.int32)
    small = jax.ShapeDtypeStruct((8, total), bf16)
    own, *sends = pl.pallas_call(
        kernel_grad_kernel,
        out_shape=(jax.ShapeDtypeStruct((8, total), f32), small, small, small),
        in_specs=[SMEM] + vmem(2),
        out_specs=tuple(vmem(4)),
        scratch_shapes=[
            pltpu.VMEM((9 * group, (quads * width + 2) * sides * rows), bf16),
            pltpu.VMEM((planes, 8, total), f32),
        ],
        compiler_params=params(),
        cost_estimate=cost(2 * 288 * 3 * 4096 * 256, 4 << 20),
        name="kernel_gradient",
    )(place, slices, bricks)

    got = [
        lax.ppermute(sent, "depth", [(i, (i + step) % planes) for i in range(planes)])
        for step, sent in zip((1, 2, 3), sends)
    ]
    voxels = count * sides * width * rows
    mine = pl.pallas_call(
        functools.partial(sum_kernel, float(1.0 / voxels**0.5)),
        out_shape=jax.ShapeDtypeStruct((8, total), f32),
        in_specs=vmem(4),
        out_specs=vmem(1)[0],
        compiler_params=params(),
        cost_estimate=cost(8 * total * 4, 8 * total * 14),
        name="plane_sum",
    )(own, *got)
    grad_weight = lax.all_gather(mine[:share], "narrow", axis=0, tiled=True)
    shape = features.shape
    return act.reshape(shape), grad_input.reshape(shape), grad_weight


def padded_2(cells, sides, width):
    for axis, dim in sides:
        count = lax.axis_size(axis)
        ends = count - 1
        head = lax.slice_in_dim(cells, 0, width, axis=dim)
        tail = lax.slice_in_dim(cells, cells.shape[dim] - width, cells.shape[dim], axis=dim)
        cells = jnp.concatenate(
            [
                lax.ppermute(tail, axis, [(i, (i + 1) % count) for i in range(ends)]),
                cells,
                lax.ppermute(head, axis, [((i + 1) % count, i) for i in range(ends)]),
            ],
            axis=dim,
        )
    return cells


def gather_taps(padded, width_x, width_y, depth_z, channels, flip):
    pieces = []
    for shift_x in range(3):
        for shift_y in range(3):
            for shift_z in range(3):
                start_x = 2 - shift_x if flip else shift_x
                start_y = 2 - shift_y if flip else shift_y
                start_z = 2 - shift_z if flip else shift_z
                piece = padded[
                    start_x : start_x + width_x,
                    start_y : start_y + width_y,
                    start_z : start_z + depth_z,
                    :,
                ]
                pieces.append(piece.reshape(-1, channels))
    return jnp.concatenate(pieces, axis=1)


def summed_local(features, weight, voxel_mask, cotangent):
    width_x, width_y, depth_z, channels = features.shape
    masked = features * voxel_mask.astype(jnp.bfloat16)[..., None]
    padded = padded_2(masked, (("wide", 0), ("narrow", 1)), 1)
    padded = jnp.pad(padded, ((0, 0), (0, 0), (1, 1), (0, 0)))
    columns = gather_taps(padded, width_x, width_y, depth_z, channels, False)
    pre = jnp.dot(columns, weight, preferred_element_type=jnp.float32)
    live = voxel_mask.reshape(-1, 1).astype(jnp.float32)
    sig = jax.nn.sigmoid(pre)
    activation = (
        (pre * sig * live).astype(jnp.bfloat16).reshape(width_x, width_y, depth_z, channels)
    )
    slope = sig * (1.0 + pre * (1.0 - sig))
    grad_pre = (cotangent.reshape(-1, channels).astype(jnp.float32) * live * slope).astype(
        jnp.bfloat16
    )
    taps = weight.reshape(27, channels, channels)
    grid = grad_pre.reshape(width_x, width_y, depth_z, channels)
    grad_pad = padded_2(grid, (("wide", 0), ("narrow", 1)), 1)
    grad_pad = jnp.pad(grad_pad, ((0, 0), (0, 0), (1, 1), (0, 0)))
    grad_columns = gather_taps(grad_pad, width_x, width_y, depth_z, channels, True)
    flipped = jnp.transpose(taps, (0, 2, 1)).reshape(27 * channels, channels)
    grad_field = jnp.dot(grad_columns, flipped, preferred_element_type=jnp.float32)
    grad_input = (
        (grad_field * live).astype(jnp.bfloat16).reshape(width_x, width_y, depth_z, channels)
    )
    scale = 1.0 / jnp.sqrt(
        jnp.float32(width_x * width_y * depth_z * lax.axis_size("wide") * lax.axis_size("narrow"))
    )
    whole = lax.dot_general(
        grad_pre, columns, (((0,), (0,)), ((), ())), preferred_element_type=jnp.float32
    )
    piece_flat = lax.psum_scatter(
        whole.reshape(-1), ("wide", "narrow"), scatter_dimension=0, tiled=True
    )
    gathered = lax.all_gather(piece_flat, "narrow", axis=0, tiled=True)
    summed = gathered.reshape(channels // lax.axis_size("wide"), 27 * channels)
    grad_weight = summed * scale
    return (activation, grad_input, grad_weight)


def sharded(body, mesh, wide):
    return jax.shard_map(
        body,
        mesh=mesh,
        in_specs=(
            P(wide, "narrow", None, None),
            P(),
            P(wide, "narrow", None),
            P(wide, "narrow", None, None),
        ),
        out_specs=(
            P(wide, "narrow", None, None),
            P(wide, "narrow", None, None),
            P(wide, None),
        ),
        check_vma=False,
    )


def solution(mesh):
    wide, narrow = mesh.shape["wide"], mesh.shape["narrow"]
    if wide != 4 * QUAD or narrow != 2:
        return sharded(summed_local, mesh, "wide")
    planes = Mesh(
        mesh.devices.reshape(wide // QUAD, QUAD, narrow), ("depth", "quad", "narrow")
    )
    return sharded(planes_local, planes, WIDE)
```

```python
import functools

import jax
import jax.numpy as jnp
from jax import lax
from jax.experimental import pallas as pl
from jax.experimental.pallas import tpu as pltpu
from jax.sharding import Mesh
from jax.sharding import PartitionSpec as P

WIDE = ("depth", "quad")
QUAD = 4
VMEM_BYTES = 56 * 1024 * 1024
OFFSETS = (-1, 0, 1)


def shift_z(field, step):
    if step == 0:
        return field
    depth = field.shape[1]
    moved = pltpu.roll(field, (-step) % depth, 1)
    z = lax.broadcasted_iota(jnp.int32, field.shape, 1) + step
    return jnp.where((z >= 0) & (z < depth), moved, 0.0)


def prepare_kernel(place, features, cot, mask, masked_ref, cot_ref, live_ref, near_ref, far_ref):
    width, rows, channels = features.shape
    depth = mask.shape[2]
    f32 = jnp.float32
    flat = mask[...].astype(f32).reshape(width * rows // depth, depth)
    live = jnp.broadcast_to(flat[:, :, None], flat.shape + (channels,)).reshape(features.shape)
    live_ref[...] = live[:, :, :128]
    masked_ref[...] = (features[...].astype(f32) * live).astype(jnp.bfloat16)
    cot_ref[...] = (cot[...].astype(f32) * live).astype(jnp.bfloat16)
    odd = place[0]
    for ref, upper in ((near_ref, 1 - odd), (far_ref, odd)):
        ref[0:2] = masked_ref[pl.ds(upper * (width - 2), 2)]
        ref[2:3] = cot_ref[pl.ds(upper * (width - 1), 1)]


def forward_kernel(
    flags, masked, cot, near, far, low, high, live, weight, pick,
    act_ref, gp_ref, slices_ref, ext, edge, cols,
):
    width, rows, channels = masked.shape
    depth = 8
    f32 = jnp.float32
    use_low = flags[0].astype(f32)
    use_high = flags[1].astype(f32)
    tall = rows + 4 * depth
    mid = rows + 2 * depth
    span = width + 4
    strip = span * 2 * depth
    odd = flags[2]
    edge[odd] = far[...]
    edge[1 - odd] = near[...]
    ext[0:2, 16 : 16 + rows, :] = edge[0, 0:2].astype(f32)
    ext[2 : 2 + width, 16 : 16 + rows, :] = masked[...].astype(f32)
    ext[2 + width :, 16 : 16 + rows, :] = edge[1, 0:2].astype(f32)
    ext[:, 0:16, :] = low[0:strip].astype(f32).reshape(span, 16, channels) * use_low
    ext[:, 16 + rows :, :] = high[0:strip].astype(f32).reshape(span, 16, channels) * use_high
    field = ext[...].reshape(span * tall // depth, depth, channels)
    for c in OFFSETS:
        moved = shift_z(field, c).reshape(span, tall, channels)
        for b in OFFSETS:
            at = ((b + 1) * 3 + c + 1) * channels
            start = depth * (b + 1)
            cols[:, :, at : at + channels] = moved[:, start : start + mid].astype(jnp.bfloat16)
    nine = 9 * channels
    pre = jnp.zeros(((width + 2) * mid, channels), f32)
    for a in range(3):
        pre += jnp.dot(
            cols[a : a + width + 2].reshape((width + 2) * mid, nine),
            weight[a * nine : (a + 1) * nine, :],
            preferred_element_type=f32,
        )
    sig = jax.nn.sigmoid(pre)
    act = (pre * sig).reshape(width + 2, mid, channels)[1 : 1 + width, depth : depth + rows]
    act_ref[...] = (act * live[:, :, 0:1]).astype(jnp.bfloat16)
    slope = (sig * (1.0 + pre * (1.0 - sig))).reshape(width + 2, mid, channels)
    low_cot = low[strip:].astype(f32).reshape(width + 2, depth, channels) * use_low
    high_cot = high[strip:].astype(f32).reshape(width + 2, depth, channels) * use_high
    centre = jnp.concatenate([edge[0, 2:3], cot[...], edge[1, 2:3]], axis=0).astype(f32)
    full = jnp.concatenate([low_cot, centre, high_cot], axis=1)
    grad = (full * slope).astype(jnp.bfloat16)
    gp_ref[...] = grad
    inner = (full * slope)[:, depth : depth + rows].astype(jnp.bfloat16)
    turned = lax.dot_general(
        pick[...],
        inner.reshape((width + 2) * rows, channels),
        (((1,), (1,)), ((), ())),
        preferred_element_type=f32,
    )
    slices_ref[...] = turned.reshape(slices_ref.shape).astype(jnp.bfloat16)


def input_kernel(gp, live, turned, out_ref, cols, weight):
    width, rows, channels = out_ref.shape
    depth = 8
    f32 = jnp.float32
    tall = rows + 2 * depth
    for tap in range(27):
        weight[tap * channels : (tap + 1) * channels, :] = turned[
            :, tap * channels : (tap + 1) * channels
        ]
    field = gp[...].astype(f32).reshape((width + 2) * tall // depth, depth, channels)
    for c in OFFSETS:
        moved = shift_z(field, -c).reshape(width + 2, tall, channels)
        for b in OFFSETS:
            at = ((b + 1) * 3 + c + 1) * channels
            start = depth * (1 - b)
            cols[:, :, at : at + channels] = moved[:, start : start + rows].astype(jnp.bfloat16)
    nine = 9 * channels
    total = jnp.zeros((width * rows, channels), f32)
    for a in range(3):
        total += jnp.dot(
            cols[2 - a : 2 - a + width].reshape(width * rows, nine),
            weight[a * nine : (a + 1) * nine, :],
            preferred_element_type=f32,
        )
    out_ref[...] = (total.reshape(width, rows, channels) * live[:, :, 0:1]).astype(jnp.bfloat16)


def kernel_grad_kernel(place, slices, bricks, own_ref, one_ref, two_ref, three_ref, cols, part, masked, sems):
    f32 = jnp.float32
    members, group, lanes = slices.shape
    slabs, lane, channels = masked.shape
    per = slabs // QUAD
    half = lane // 2
    copies = [
        pltpu.make_async_copy(
            bricks.at[pl.ds(member * per, per)],
            masked.at[pl.ds(member // 2 * per, per), pl.ds(member % 2 * half, half)],
            sems.at[member],
        )
        for member in range(members)
    ]
    for copy in copies:
        copy.start()
    depth = 8
    at = lax.broadcasted_iota(jnp.int32, (group, lane), 1)
    y, z = at // depth, at % depth
    tall = lane // depth
    base = [None] * (slabs + 2)
    for quad in range(QUAD):
        first = slices[2 * quad].astype(f32)
        second = slices[2 * quad + 1].astype(f32)
        for m in range((per + 2) // 2):
            one = first[:, m * lane : (m + 1) * lane]
            two = second[:, m * lane : (m + 1) * lane]
            pair = (
                jnp.where(at < half, one, pltpu.roll(two, half, 1)),
                jnp.where(at < half, pltpu.roll(one, half, 1), two),
            )
            for odd in range(2):
                k = 2 * m + odd
                slab = quad * per + k
                inside = 1 <= k <= per
                edge = (quad == 0 and k == 0) or (quad == QUAD - 1 and k == per + 1)
                if inside or edge:
                    base[slab] = pair[odd]
    for slab in range(slabs + 2):
        pieces = []
        for b in OFFSETS:
            for c in OFFSETS:
                step = (depth * b + c) % lane
                moved = base[slab] if step == 0 else pltpu.roll(base[slab], step, 1)
                keep = (y - b >= 0) & (y - b < tall) & (z - c >= 0) & (z - c < depth)
                pieces.append(jnp.where(keep, moved, 0.0))
        cols[:, slab * lane : (slab + 1) * lane] = jnp.concatenate(pieces, axis=0).astype(
            jnp.bfloat16
        )
    for copy in copies:
        copy.wait()
    field = masked[...].reshape(slabs * lane, channels)
    planes, rows, _ = part.shape
    for a in range(3):
        start = (2 - a) * lane
        got = jnp.dot(
            cols[:, start : start + slabs * lane], field, preferred_element_type=f32
        ).reshape(9, planes, rows, channels)
        for plane in range(planes):
            part[plane, :, a * 9 * channels : (a + 1) * 9 * channels] = jnp.concatenate(
                [got[tap, plane] for tap in range(9)], axis=1
            )
    me = place[0]
    own_ref[...] = part[me]
    for step, ref in ((1, one_ref), (2, two_ref), (3, three_ref)):
        ref[...] = part[lax.rem(me + step, planes)].astype(jnp.bfloat16)


def sum_kernel(scale, own, one, two, three, out_ref):
    f32 = jnp.float32
    total = own[...] + one[...].astype(f32) + two[...].astype(f32) + three[...].astype(f32)
    out_ref[...] = total * scale


def join_kernel(place, mine, other, out_ref):
    share = out_ref.shape[0] // 2
    first = jnp.where(place[0] == 0, mine[...], other[...])
    second = jnp.where(place[0] == 0, other[...], mine[...])
    out_ref[0:share] = first[:share]
    out_ref[share:] = second[:share]


def vmem(count):
    return [pl.BlockSpec(memory_space=pltpu.VMEM)] * count


SMEM = pl.BlockSpec(memory_space=pltpu.SMEM)


def params():
    return pltpu.CompilerParams(vmem_limit_bytes=VMEM_BYTES)


def cost(flops, moved):
    return pl.CostEstimate(flops=flops, bytes_accessed=moved, transcendentals=0)


def planes_local(features, weight, voxel_mask, cotangent):
    bf16 = jnp.bfloat16
    f32 = jnp.float32
    width, wide_y, depth, channels = features.shape
    rows = wide_y * depth
    planes = lax.axis_size("depth")
    quads = lax.axis_size("quad")
    count = planes * quads
    plane = lax.axis_index("depth")
    side = lax.axis_index("narrow")
    sides = lax.axis_size("narrow")

    odd = lax.axis_index("quad") % 2
    brick = jax.ShapeDtypeStruct((width, rows, channels), bf16)
    slab = jax.ShapeDtypeStruct((3, rows, channels), bf16)
    masked, cot, live, near, far = pl.pallas_call(
        prepare_kernel,
        out_shape=(brick, brick, jax.ShapeDtypeStruct((width, rows, 128), f32), slab, slab),
        in_specs=[SMEM] + vmem(3),
        out_specs=tuple(vmem(5)),
        compiler_params=params(),
        cost_estimate=cost(1 << 20, 1 << 20),
        name="prepare",
    )(
        odd.reshape(1).astype(jnp.int32),
        features.reshape(width, rows, channels),
        cotangent.reshape(width, rows, channels),
        voxel_mask,
    )

    near = lax.ppermute(near, WIDE, [(i, i ^ 1) for i in range(count)])
    far = lax.ppermute(
        far, WIDE, [(i, j) for i in range(count) if 0 <= (j := ((i + 1) ^ 1) - 1) < count]
    )
    bricks = lax.all_gather(masked, ("quad", "narrow"), axis=0, tiled=True)
    left = jnp.where(odd == 1, near, far)
    right = jnp.where(odd == 1, far, near)

    halo = 2 * depth
    wide_masked = jnp.concatenate([left[:2], masked, right[:2]], axis=0)
    wide_cot = jnp.concatenate([left[2:], cot, right[2:]], axis=0)

    def strip(first):
        if first:
            parts = wide_masked[:, :halo], wide_cot[:, :depth]
        else:
            parts = wide_masked[:, rows - halo :], wide_cot[:, rows - depth :]
        return jnp.concatenate([part.reshape(-1, channels) for part in parts], axis=0)

    swapped = lax.ppermute(
        jnp.where(side == 0, strip(False), strip(True)), "narrow", [(0, 1), (1, 0)]
    )
    flags = jnp.stack([side, 1 - side, odd]).astype(jnp.int32)

    group = 4 * 8
    members = quads * sides
    per = channels // count
    share = per // sides
    index = jnp.arange(members * group)
    q, s = index // (sides * group), index // group % sides
    p, r = index // 8 % planes, index % 8
    source = jnp.where(r < share, per * (quads * p + q) + share * s + r, -1)
    pick = (source[:, None] == jnp.arange(channels)[None, :]).astype(bf16)

    span = (width + 2) * rows
    act, gp, slices = pl.pallas_call(
        forward_kernel,
        out_shape=(
            jax.ShapeDtypeStruct((width, rows, channels), bf16),
            jax.ShapeDtypeStruct((width + 2, rows + 2 * depth, channels), bf16),
            jax.ShapeDtypeStruct((members, group, span), bf16),
        ),
        in_specs=[SMEM] + vmem(9),
        out_specs=tuple(vmem(3)),
        scratch_shapes=[
            pltpu.VMEM((width + 4, rows + 4 * depth, channels), f32),
            pltpu.VMEM((2, 3, rows, channels), bf16),
            pltpu.VMEM((width + 4, rows + 2 * depth, 9 * channels), bf16),
        ],
        compiler_params=params(),
        cost_estimate=cost(2 * 800 * 5184 * 256, 4 << 20),
        name="forward",
    )(flags, masked, cot, near, far, swapped, swapped, live, weight, pick)

    slices = lax.all_to_all(slices, ("quad", "narrow"), 0, 0, tiled=True)

    grad_input = pl.pallas_call(
        input_kernel,
        out_shape=jax.ShapeDtypeStruct((width, rows, channels), bf16),
        in_specs=vmem(3),
        out_specs=vmem(1)[0],
        scratch_shapes=[
            pltpu.VMEM((width + 2, rows, 9 * channels), bf16),
            pltpu.VMEM((27 * channels, channels), bf16),
        ],
        compiler_params=params(),
        cost_estimate=cost(2 * 512 * 5184 * 256, 4 << 20),
        name="input_gradient",
    )(gp, live, weight.T)

    total = 27 * channels
    place = plane.reshape(1).astype(jnp.int32)
    small = jax.ShapeDtypeStruct((8, total), bf16)
    own, *sends = pl.pallas_call(
        kernel_grad_kernel,
        out_shape=(jax.ShapeDtypeStruct((8, total), f32), small, small, small),
        in_specs=[SMEM] + vmem(1) + [pl.BlockSpec(memory_space=pl.ANY)],
        out_specs=tuple(vmem(4)),
        scratch_shapes=[
            pltpu.VMEM((9 * group, (quads * width + 2) * sides * rows), bf16),
            pltpu.VMEM((planes, 8, total), f32),
            pltpu.VMEM((quads * width, sides * rows, channels), bf16),
            pltpu.SemaphoreType.DMA((members,)),
        ],
        compiler_params=params(),
        cost_estimate=cost(2 * 288 * 3 * 4096 * 256, 4 << 20),
        name="kernel_gradient",
    )(place, slices, bricks)

    got = [
        lax.ppermute(sent, "depth", [(i, (i + step) % planes) for i in range(planes)])
        for step, sent in zip((1, 2, 3), sends)
    ]
    voxels = count * sides * width * rows
    mine = pl.pallas_call(
        functools.partial(sum_kernel, float(1.0 / voxels**0.5)),
        out_shape=jax.ShapeDtypeStruct((8, total), f32),
        in_specs=vmem(4),
        out_specs=vmem(1)[0],
        compiler_params=params(),
        cost_estimate=cost(8 * total * 4, 8 * total * 14),
        name="plane_sum",
    )(own, *got)
    other = lax.ppermute(mine, "narrow", [(0, 1), (1, 0)])
    grad_weight = pl.pallas_call(
        join_kernel,
        out_shape=jax.ShapeDtypeStruct((per, total), f32),
        in_specs=[SMEM] + vmem(2),
        out_specs=vmem(1)[0],
        compiler_params=params(),
        cost_estimate=cost(8 * total, 8 * total * 14),
        name="join",
    )(side.reshape(1).astype(jnp.int32), mine, other)
    shape = features.shape
    return act.reshape(shape), grad_input.reshape(shape), grad_weight


def padded_2(cells, sides, width):
    for axis, dim in sides:
        count = lax.axis_size(axis)
        ends = count - 1
        head = lax.slice_in_dim(cells, 0, width, axis=dim)
        tail = lax.slice_in_dim(cells, cells.shape[dim] - width, cells.shape[dim], axis=dim)
        cells = jnp.concatenate(
            [
                lax.ppermute(tail, axis, [(i, (i + 1) % count) for i in range(ends)]),
                cells,
                lax.ppermute(head, axis, [((i + 1) % count, i) for i in range(ends)]),
            ],
            axis=dim,
        )
    return cells


def gather_taps(padded, width_x, width_y, depth_z, channels, flip):
    pieces = []
    for shift_x in range(3):
        for shift_y in range(3):
            for shift_z in range(3):
                start_x = 2 - shift_x if flip else shift_x
                start_y = 2 - shift_y if flip else shift_y
                start_z = 2 - shift_z if flip else shift_z
                piece = padded[
                    start_x : start_x + width_x,
                    start_y : start_y + width_y,
                    start_z : start_z + depth_z,
                    :,
                ]
                pieces.append(piece.reshape(-1, channels))
    return jnp.concatenate(pieces, axis=1)


def summed_local(features, weight, voxel_mask, cotangent):
    width_x, width_y, depth_z, channels = features.shape
    masked = features * voxel_mask.astype(jnp.bfloat16)[..., None]
    padded = padded_2(masked, (("wide", 0), ("narrow", 1)), 1)
    padded = jnp.pad(padded, ((0, 0), (0, 0), (1, 1), (0, 0)))
    columns = gather_taps(padded, width_x, width_y, depth_z, channels, False)
    pre = jnp.dot(columns, weight, preferred_element_type=jnp.float32)
    live = voxel_mask.reshape(-1, 1).astype(jnp.float32)
    sig = jax.nn.sigmoid(pre)
    activation = (
        (pre * sig * live).astype(jnp.bfloat16).reshape(width_x, width_y, depth_z, channels)
    )
    slope = sig * (1.0 + pre * (1.0 - sig))
    grad_pre = (cotangent.reshape(-1, channels).astype(jnp.float32) * live * slope).astype(
        jnp.bfloat16
    )
    taps = weight.reshape(27, channels, channels)
    grid = grad_pre.reshape(width_x, width_y, depth_z, channels)
    grad_pad = padded_2(grid, (("wide", 0), ("narrow", 1)), 1)
    grad_pad = jnp.pad(grad_pad, ((0, 0), (0, 0), (1, 1), (0, 0)))
    grad_columns = gather_taps(grad_pad, width_x, width_y, depth_z, channels, True)
    flipped = jnp.transpose(taps, (0, 2, 1)).reshape(27 * channels, channels)
    grad_field = jnp.dot(grad_columns, flipped, preferred_element_type=jnp.float32)
    grad_input = (
        (grad_field * live).astype(jnp.bfloat16).reshape(width_x, width_y, depth_z, channels)
    )
    scale = 1.0 / jnp.sqrt(
        jnp.float32(width_x * width_y * depth_z * lax.axis_size("wide") * lax.axis_size("narrow"))
    )
    whole = lax.dot_general(
        grad_pre, columns, (((0,), (0,)), ((), ())), preferred_element_type=jnp.float32
    )
    piece_flat = lax.psum_scatter(
        whole.reshape(-1), ("wide", "narrow"), scatter_dimension=0, tiled=True
    )
    gathered = lax.all_gather(piece_flat, "narrow", axis=0, tiled=True)
    summed = gathered.reshape(channels // lax.axis_size("wide"), 27 * channels)
    grad_weight = summed * scale
    return (activation, grad_input, grad_weight)


def sharded(body, mesh, wide):
    return jax.shard_map(
        body,
        mesh=mesh,
        in_specs=(
            P(wide, "narrow", None, None),
            P(),
            P(wide, "narrow", None),
            P(wide, "narrow", None, None),
        ),
        out_specs=(
            P(wide, "narrow", None, None),
            P(wide, "narrow", None, None),
            P(wide, None),
        ),
        check_vma=False,
    )


def solution(mesh):
    wide, narrow = mesh.shape["wide"], mesh.shape["narrow"]
    if wide != 4 * QUAD or narrow != 2:
        return sharded(summed_local, mesh, "wide")
    planes = Mesh(
        mesh.devices.reshape(wide // QUAD, QUAD, narrow), ("depth", "quad", "narrow")
    )
    return sharded(planes_local, planes, WIDE)
```

```python
import functools

import jax
import jax.numpy as jnp
from jax import lax
from jax.experimental import pallas as pl
from jax.experimental.pallas import tpu as pltpu
from jax.sharding import Mesh
from jax.sharding import PartitionSpec as P

WIDE = ("depth", "quad")
QUAD = 4
OFFSETS = (-1, 0, 1)


def shift_z(field, step):
    if step == 0:
        return field
    depth = field.shape[1]
    moved = pltpu.roll(field, (-step) % depth, 1)
    z = lax.broadcasted_iota(jnp.int32, field.shape, 1) + step
    return jnp.where((z >= 0) & (z < depth), moved, 0.0)


def prepare_kernel(place, features, cot, mask, masked_ref, cot_ref, live_ref, near_ref, far_ref):
    width, rows, channels = features.shape
    depth = mask.shape[2]
    f32 = jnp.float32
    flat = mask[...].astype(f32).reshape(width * rows // depth, depth)
    live = jnp.broadcast_to(flat[:, :, None], flat.shape + (channels,)).reshape(features.shape)
    live_ref[...] = live[:, :, :128]
    masked_ref[...] = (features[...].astype(f32) * live).astype(jnp.bfloat16)
    cot_ref[...] = (cot[...].astype(f32) * live).astype(jnp.bfloat16)
    odd = place[0]
    for ref, upper in ((near_ref, 1 - odd), (far_ref, odd)):
        ref[0:2] = masked_ref[pl.ds(upper * (width - 2), 2)]
        ref[2:3] = cot_ref[pl.ds(upper * (width - 1), 1)]


def pack_kernel(masked, packed_ref):
    width = masked.shape[0]
    half = width // 2
    packed_ref[:width] = masked[:, :, :128]
    packed_ref[width:] = jnp.concatenate([masked[:half, :, 128:], masked[half:, :, 128:]], axis=2)


def forward_kernel(
    flags, masked, cot, near, far, low, high, live, weight, pick,
    act_ref, gp_ref, slices_ref, ext, edge, cols,
):
    width, rows, channels = masked.shape
    depth = 8
    f32 = jnp.float32
    use_low = flags[0].astype(f32)
    use_high = flags[1].astype(f32)
    tall = rows + 4 * depth
    mid = rows + 2 * depth
    span = width + 4
    strip = span * 2 * depth
    odd = flags[2]
    edge[odd] = far[...]
    edge[1 - odd] = near[...]
    ext[0:2, 16 : 16 + rows, :] = edge[0, 0:2].astype(f32)
    ext[2 : 2 + width, 16 : 16 + rows, :] = masked[...].astype(f32)
    ext[2 + width :, 16 : 16 + rows, :] = edge[1, 0:2].astype(f32)
    ext[:, 0:16, :] = low[0:strip].astype(f32).reshape(span, 16, channels) * use_low
    ext[:, 16 + rows :, :] = high[0:strip].astype(f32).reshape(span, 16, channels) * use_high
    field = ext[...].reshape(span * tall // depth, depth, channels)
    for c in OFFSETS:
        moved = shift_z(field, c).reshape(span, tall, channels)
        for b in OFFSETS:
            at = ((b + 1) * 3 + c + 1) * channels
            start = depth * (b + 1)
            cols[:, :, at : at + channels] = moved[:, start : start + mid].astype(jnp.bfloat16)
    nine = 9 * channels
    pre = jnp.zeros(((width + 2) * mid, channels), f32)
    for a in range(3):
        pre += jnp.dot(
            cols[a : a + width + 2].reshape((width + 2) * mid, nine),
            weight[a * nine : (a + 1) * nine, :],
            preferred_element_type=f32,
        )
    sig = jax.nn.sigmoid(pre)
    act = (pre * sig).reshape(width + 2, mid, channels)[1 : 1 + width, depth : depth + rows]
    act_ref[...] = (act * live[:, :, 0:1]).astype(jnp.bfloat16)
    slope = (sig * (1.0 + pre * (1.0 - sig))).reshape(width + 2, mid, channels)
    low_cot = low[strip:].astype(f32).reshape(width + 2, depth, channels) * use_low
    high_cot = high[strip:].astype(f32).reshape(width + 2, depth, channels) * use_high
    centre = jnp.concatenate([edge[0, 2:3], cot[...], edge[1, 2:3]], axis=0).astype(f32)
    full = jnp.concatenate([low_cot, centre, high_cot], axis=1)
    grad = (full * slope).astype(jnp.bfloat16)
    gp_ref[...] = grad
    inner = (full * slope)[:, depth : depth + rows].astype(jnp.bfloat16)
    turned = lax.dot_general(
        pick[...],
        inner.reshape((width + 2) * rows, channels),
        (((1,), (1,)), ((), ())),
        preferred_element_type=f32,
    )
    slices_ref[...] = turned.reshape(slices_ref.shape).astype(jnp.bfloat16)


def input_kernel(gp, live, turned, out_ref, cols, weight):
    width, rows, channels = out_ref.shape
    depth = 8
    f32 = jnp.float32
    tall = rows + 2 * depth
    for tap in range(27):
        weight[tap * channels : (tap + 1) * channels, :] = turned[
            :, tap * channels : (tap + 1) * channels
        ]
    field = gp[...].astype(f32).reshape((width + 2) * tall // depth, depth, channels)
    for c in OFFSETS:
        moved = shift_z(field, -c).reshape(width + 2, tall, channels)
        for b in OFFSETS:
            at = ((b + 1) * 3 + c + 1) * channels
            start = depth * (1 - b)
            cols[:, :, at : at + channels] = moved[:, start : start + rows].astype(jnp.bfloat16)
    nine = 9 * channels
    total = jnp.zeros((width * rows, channels), f32)
    for a in range(3):
        total += jnp.dot(
            cols[2 - a : 2 - a + width].reshape(width * rows, nine),
            weight[a * nine : (a + 1) * nine, :],
            preferred_element_type=f32,
        )
    out_ref[...] = (total.reshape(width, rows, channels) * live[:, :, 0:1]).astype(jnp.bfloat16)


def kernel_grad_kernel(place, slices, *refs):
    bricks = refs[:8]
    own_ref, send_ref, cols, part, stage, masked, sems = refs[8:]
    f32 = jnp.float32
    members, group, lanes = slices.shape
    slabs, lane, channels = masked.shape
    per = slabs // QUAD
    half = lane // 2
    copies = []
    for member in range(members):
        quad, side = place[1] ^ (member // 2), place[2] ^ (member % 2)
        copies.append(
            pltpu.make_async_copy(bricks[member], stage.at[quad, side], sems.at[member])
        )
    for copy in copies:
        copy.start()
    depth = 8
    at = lax.broadcasted_iota(jnp.int32, (group, lane), 1)
    y, z = at // depth, at % depth
    tall = lane // depth
    base = [None] * (slabs + 2)
    for quad in range(QUAD):
        first = slices[2 * quad].astype(f32)
        second = slices[2 * quad + 1].astype(f32)
        for m in range((per + 2) // 2):
            one = first[:, m * lane : (m + 1) * lane]
            two = second[:, m * lane : (m + 1) * lane]
            pair = (
                jnp.where(at < half, one, pltpu.roll(two, half, 1)),
                jnp.where(at < half, pltpu.roll(one, half, 1), two),
            )
            for odd in range(2):
                k = 2 * m + odd
                slab = quad * per + k
                inside = 1 <= k <= per
                edge = (quad == 0 and k == 0) or (quad == QUAD - 1 and k == per + 1)
                if inside or edge:
                    base[slab] = pair[odd]
    for slab in range(slabs + 2):
        pieces = []
        for b in OFFSETS:
            for c in OFFSETS:
                step = (depth * b + c) % lane
                moved = base[slab] if step == 0 else pltpu.roll(base[slab], step, 1)
                keep = (y - b >= 0) & (y - b < tall) & (z - c >= 0) & (z - c < depth)
                pieces.append(jnp.where(keep, moved, 0.0))
        cols[:, slab * lane : (slab + 1) * lane] = jnp.concatenate(pieces, axis=0).astype(
            jnp.bfloat16
        )
    for copy in copies:
        copy.wait()
    for quad in range(QUAD):
        for side in range(2):
            at_rows = pl.ds(side * half, half)
            for x in range(per):
                shift = 64 * (x // (per // 2))
                rest = stage[quad, side, per + x % (per // 2)]
                masked[quad * per + x, at_rows, :128] = stage[quad, side, x]
                masked[quad * per + x, at_rows, 128:] = rest[:, shift : shift + 64]
    field = masked[...].reshape(slabs * lane, channels)
    planes, rows, _ = part.shape
    for a in range(3):
        start = (2 - a) * lane
        got = jnp.dot(
            cols[:, start : start + slabs * lane], field, preferred_element_type=f32
        ).reshape(9, planes, rows, channels)
        for plane in range(planes):
            part[plane, :, a * 9 * channels : (a + 1) * 9 * channels] = jnp.concatenate(
                [got[tap, plane] for tap in range(9)], axis=1
            )
    me = place[0]
    own_ref[...] = part[me]
    send_ref[...] = part[...].astype(jnp.bfloat16)


def sum_kernel(scale, place, own, parts, out_ref):
    total = own[...]
    for plane in range(parts.shape[0]):
        total += jnp.where(plane == place[0], 0.0, parts[plane].astype(jnp.float32))
    out_ref[...] = total * scale


def join_kernel(place, mine, other, out_ref):
    share = out_ref.shape[0] // 2
    first = jnp.where(place[0] == 0, mine[...], other[...])
    second = jnp.where(place[0] == 0, other[...], mine[...])
    out_ref[0:share] = first[:share]
    out_ref[share:] = second[:share]


def vmem(count):
    return [pl.BlockSpec(memory_space=pltpu.VMEM)] * count


SMEM = pl.BlockSpec(memory_space=pltpu.SMEM)


def params(mebibytes):
    return pltpu.CompilerParams(vmem_limit_bytes=mebibytes * 1024 * 1024)


def cost(flops, moved):
    return pl.CostEstimate(flops=flops, bytes_accessed=moved, transcendentals=0)


def planes_local(features, weight, voxel_mask, cotangent):
    bf16 = jnp.bfloat16
    f32 = jnp.float32
    width, wide_y, depth, channels = features.shape
    rows = wide_y * depth
    planes = lax.axis_size("depth")
    quads = lax.axis_size("quad")
    count = planes * quads
    plane = lax.axis_index("depth")
    side = lax.axis_index("narrow")
    sides = lax.axis_size("narrow")

    odd = lax.axis_index("quad") % 2
    brick = jax.ShapeDtypeStruct((width, rows, channels), bf16)
    slab = jax.ShapeDtypeStruct((3, rows, channels), bf16)
    column = jax.ShapeDtypeStruct((width, rows, 128), f32)
    masked, cot, live, near, far = pl.pallas_call(
        prepare_kernel,
        out_shape=(brick, brick, column, slab, slab),
        in_specs=[SMEM] + vmem(3),
        out_specs=tuple(vmem(5)),
        compiler_params=params(8),
        cost_estimate=cost(1 << 20, 1 << 20),
        name="prepare",
    )(
        odd.reshape(1).astype(jnp.int32),
        features.reshape(width, rows, channels),
        cotangent.reshape(width, rows, channels),
        voxel_mask,
    )

    near = lax.ppermute(near, WIDE, [(i, i ^ 1) for i in range(count)])
    far = lax.ppermute(
        far, WIDE, [(i, j) for i in range(count) if 0 <= (j := ((i + 1) ^ 1) - 1) < count]
    )
    packed = pl.pallas_call(
        pack_kernel,
        out_shape=jax.ShapeDtypeStruct((width * channels // 128, rows, 128), bf16),
        in_specs=vmem(1),
        out_specs=vmem(1)[0],
        compiler_params=params(4),
        cost_estimate=cost(1 << 16, 1 << 19),
        name="pack",
    )(masked)

    def across(piece):
        return lax.ppermute(piece, "narrow", [(0, 1), (1, 0)])

    def beside(piece, distance):
        return lax.ppermute(piece, "quad", [(i, i ^ distance) for i in range(quads)])

    bricks = [packed, across(packed), beside(packed, 1), None, beside(packed, 2)] + [None] * 3
    left = jnp.where(odd == 1, near, far)
    right = jnp.where(odd == 1, far, near)

    halo = 2 * depth
    wide_masked = jnp.concatenate([left[:2], masked, right[:2]], axis=0)
    wide_cot = jnp.concatenate([left[2:], cot, right[2:]], axis=0)

    def strip(first):
        if first:
            parts = wide_masked[:, :halo], wide_cot[:, :depth]
        else:
            parts = wide_masked[:, rows - halo :], wide_cot[:, rows - depth :]
        return jnp.concatenate([part.reshape(-1, channels) for part in parts], axis=0)

    edge, bricks[1], bricks[4] = lax.optimization_barrier(
        (jnp.where(side == 0, strip(False), strip(True)), bricks[1], bricks[4])
    )
    swapped = across(edge)
    bricks[3] = beside(bricks[1], 1)
    bricks[5] = beside(bricks[1], 2)
    bricks[6] = beside(bricks[4], 1)
    flags = jnp.stack([side, 1 - side, odd]).astype(jnp.int32)

    group = 4 * 8
    members = quads * sides
    per = channels // count
    share = per // sides
    index = jnp.arange(members * group)
    q, s = index // (sides * group), index // group % sides
    p, r = index // 8 % planes, index % 8
    source = jnp.where(r < share, per * (quads * p + q) + share * s + r, -1)
    pick = (source[:, None] == jnp.arange(channels)[None, :]).astype(bf16)

    span = (width + 2) * rows
    act, gp, slices = pl.pallas_call(
        forward_kernel,
        out_shape=(
            jax.ShapeDtypeStruct((width, rows, channels), bf16),
            jax.ShapeDtypeStruct((width + 2, rows + 2 * depth, channels), bf16),
            jax.ShapeDtypeStruct((members, group, span), bf16),
        ),
        in_specs=[SMEM] + vmem(9),
        out_specs=tuple(vmem(3)),
        scratch_shapes=[
            pltpu.VMEM((width + 4, rows + 4 * depth, channels), f32),
            pltpu.VMEM((2, 3, rows, channels), bf16),
            pltpu.VMEM((width + 4, rows + 2 * depth, 9 * channels), bf16),
        ],
        compiler_params=params(28),
        cost_estimate=cost(2 * 800 * 5184 * 256, 4 << 20),
        name="forward",
    )(flags, masked, cot, near, far, swapped, swapped, live, weight, pick)

    slices, bricks[5] = lax.optimization_barrier((slices, bricks[5]))
    bricks[7] = beside(bricks[5], 1)
    slices = lax.all_to_all(slices, ("quad", "narrow"), 0, 0, tiled=True)

    grad_input = pl.pallas_call(
        input_kernel,
        out_shape=jax.ShapeDtypeStruct((width, rows, channels), bf16),
        in_specs=vmem(3),
        out_specs=vmem(1)[0],
        scratch_shapes=[
            pltpu.VMEM((width + 2, rows, 9 * channels), bf16),
            pltpu.VMEM((27 * channels, channels), bf16),
        ],
        compiler_params=params(20),
        cost_estimate=cost(2 * 512 * 5184 * 256, 4 << 20),
        name="input_gradient",
    )(gp, live, weight.T)

    total = 27 * channels
    place = jnp.stack([plane, lax.axis_index("quad"), side]).astype(jnp.int32)
    own, sends = pl.pallas_call(
        kernel_grad_kernel,
        out_shape=(
            jax.ShapeDtypeStruct((8, total), f32),
            jax.ShapeDtypeStruct((planes, 8, total), bf16),
        ),
        in_specs=[SMEM] + vmem(1) + [pl.BlockSpec(memory_space=pl.ANY)] * 8,
        out_specs=tuple(vmem(2)),
        scratch_shapes=[
            pltpu.VMEM((9 * group, (quads * width + 2) * sides * rows), bf16),
            pltpu.VMEM((planes, 8, total), f32),
            pltpu.VMEM((quads, sides, width * channels // 128, rows, 128), bf16),
            pltpu.VMEM((quads * width, sides * rows, channels), bf16),
            pltpu.SemaphoreType.DMA((members,)),
        ],
        compiler_params=params(24),
        cost_estimate=cost(2 * 288 * 3 * 4096 * 256, 4 << 20),
        name="kernel_gradient",
    )(place, slices, *bricks)

    parts = lax.all_to_all(sends, "depth", 0, 0, tiled=True)
    voxels = count * sides * width * rows
    mine = pl.pallas_call(
        functools.partial(sum_kernel, float(1.0 / voxels**0.5)),
        out_shape=jax.ShapeDtypeStruct((8, total), f32),
        in_specs=[SMEM] + vmem(2),
        out_specs=vmem(1)[0],
        compiler_params=params(4),
        cost_estimate=cost(8 * total * 4, 8 * total * 14),
        name="plane_sum",
    )(place, own, parts)
    other = lax.ppermute(mine, "narrow", [(0, 1), (1, 0)])
    grad_weight = pl.pallas_call(
        join_kernel,
        out_shape=jax.ShapeDtypeStruct((per, total), f32),
        in_specs=[SMEM] + vmem(2),
        out_specs=vmem(1)[0],
        compiler_params=params(4),
        cost_estimate=cost(8 * total, 8 * total * 14),
        name="join",
    )(side.reshape(1).astype(jnp.int32), mine, other)
    shape = features.shape
    return act.reshape(shape), grad_input.reshape(shape), grad_weight


def padded_2(cells, sides, width):
    for axis, dim in sides:
        count = lax.axis_size(axis)
        ends = count - 1
        head = lax.slice_in_dim(cells, 0, width, axis=dim)
        tail = lax.slice_in_dim(cells, cells.shape[dim] - width, cells.shape[dim], axis=dim)
        cells = jnp.concatenate(
            [
                lax.ppermute(tail, axis, [(i, (i + 1) % count) for i in range(ends)]),
                cells,
                lax.ppermute(head, axis, [((i + 1) % count, i) for i in range(ends)]),
            ],
            axis=dim,
        )
    return cells


def gather_taps(padded, width_x, width_y, depth_z, channels, flip):
    pieces = []
    for shift_x in range(3):
        for shift_y in range(3):
            for shift_z in range(3):
                start_x = 2 - shift_x if flip else shift_x
                start_y = 2 - shift_y if flip else shift_y
                start_z = 2 - shift_z if flip else shift_z
                piece = padded[
                    start_x : start_x + width_x,
                    start_y : start_y + width_y,
                    start_z : start_z + depth_z,
                    :,
                ]
                pieces.append(piece.reshape(-1, channels))
    return jnp.concatenate(pieces, axis=1)


def summed_local(features, weight, voxel_mask, cotangent):
    width_x, width_y, depth_z, channels = features.shape
    masked = features * voxel_mask.astype(jnp.bfloat16)[..., None]
    padded = padded_2(masked, (("wide", 0), ("narrow", 1)), 1)
    padded = jnp.pad(padded, ((0, 0), (0, 0), (1, 1), (0, 0)))
    columns = gather_taps(padded, width_x, width_y, depth_z, channels, False)
    pre = jnp.dot(columns, weight, preferred_element_type=jnp.float32)
    live = voxel_mask.reshape(-1, 1).astype(jnp.float32)
    sig = jax.nn.sigmoid(pre)
    activation = (
        (pre * sig * live).astype(jnp.bfloat16).reshape(width_x, width_y, depth_z, channels)
    )
    slope = sig * (1.0 + pre * (1.0 - sig))
    grad_pre = (cotangent.reshape(-1, channels).astype(jnp.float32) * live * slope).astype(
        jnp.bfloat16
    )
    taps = weight.reshape(27, channels, channels)
    grid = grad_pre.reshape(width_x, width_y, depth_z, channels)
    grad_pad = padded_2(grid, (("wide", 0), ("narrow", 1)), 1)
    grad_pad = jnp.pad(grad_pad, ((0, 0), (0, 0), (1, 1), (0, 0)))
    grad_columns = gather_taps(grad_pad, width_x, width_y, depth_z, channels, True)
    flipped = jnp.transpose(taps, (0, 2, 1)).reshape(27 * channels, channels)
    grad_field = jnp.dot(grad_columns, flipped, preferred_element_type=jnp.float32)
    grad_input = (
        (grad_field * live).astype(jnp.bfloat16).reshape(width_x, width_y, depth_z, channels)
    )
    scale = 1.0 / jnp.sqrt(
        jnp.float32(width_x * width_y * depth_z * lax.axis_size("wide") * lax.axis_size("narrow"))
    )
    whole = lax.dot_general(
        grad_pre, columns, (((0,), (0,)), ((), ())), preferred_element_type=jnp.float32
    )
    piece_flat = lax.psum_scatter(
        whole.reshape(-1), ("wide", "narrow"), scatter_dimension=0, tiled=True
    )
    gathered = lax.all_gather(piece_flat, "narrow", axis=0, tiled=True)
    summed = gathered.reshape(channels // lax.axis_size("wide"), 27 * channels)
    grad_weight = summed * scale
    return (activation, grad_input, grad_weight)


def sharded(body, mesh, wide):
    return jax.shard_map(
        body,
        mesh=mesh,
        in_specs=(
            P(wide, "narrow", None, None),
            P(),
            P(wide, "narrow", None),
            P(wide, "narrow", None, None),
        ),
        out_specs=(
            P(wide, "narrow", None, None),
            P(wide, "narrow", None, None),
            P(wide, None),
        ),
        check_vma=False,
    )


def solution(mesh):
    wide, narrow = mesh.shape["wide"], mesh.shape["narrow"]
    if wide != 4 * QUAD or narrow != 2:
        return sharded(summed_local, mesh, "wide")
    planes = Mesh(
        mesh.devices.reshape(wide // QUAD, QUAD, narrow), ("depth", "quad", "narrow")
    )
    return sharded(planes_local, planes, WIDE)
```

```python
import functools

import jax
import jax.numpy as jnp
import numpy as np
from jax import lax
from jax.experimental import pallas as pl
from jax.experimental.pallas import tpu as pltpu
from jax.sharding import Mesh
from jax.sharding import PartitionSpec as P

WIDE = ("depth", "quad")
QUAD = 4
SIDES = 2
MEMBERS = QUAD * SIDES
OFFSETS = (-1, 0, 1)
DEPTH = 8


def position():
    quad, side = lax.axis_index("quad"), lax.axis_index("narrow")
    return lax.axis_index("depth"), quad * SIDES + side, quad, side


def shift_z(field, step):
    if step == 0:
        return field
    depth = field.shape[1]
    moved = pltpu.roll(field, (-step) % depth, 1)
    z = lax.broadcasted_iota(jnp.int32, field.shape, 1) + step
    return jnp.where((z >= 0) & (z < depth), moved, 0.0)


def prepare_kernel(
    features_in, cot_in, mask_in, masked_ref, cot_ref, live_ref, near_ref, far_ref,
    features, cot, mask, sems,
):
    copies = [
        pltpu.make_async_copy(source, held, sems.at[i])
        for i, (source, held) in enumerate(
            ((mask_in, mask), (features_in, features), (cot_in, cot))
        )
    ]
    for copy in copies:
        copy.start()
    width, rows, channels = features.shape
    f32 = jnp.float32
    copies[0].wait()
    flat = mask[...].astype(f32).reshape(width * rows // DEPTH, DEPTH)
    live = jnp.broadcast_to(flat[:, :, None], flat.shape + (channels,)).reshape(features.shape)
    live_ref[...] = live[:, :, :128]
    copies[1].wait()
    masked_ref[...] = (features[...].astype(f32) * live).astype(jnp.bfloat16)
    copies[2].wait()
    cot_ref[...] = (cot[...].astype(f32) * live).astype(jnp.bfloat16)
    odd = lax.rem(position()[2], 2)
    for ref, upper in ((near_ref, 1 - odd), (far_ref, odd)):
        ref[0:2] = masked_ref[pl.ds(upper * (width - 2), 2)]
        ref[2:3] = cot_ref[pl.ds(upper * (width - 1), 1)]


def pack_kernel(masked, packed_ref):
    width = masked.shape[0]
    half = width // 2
    packed_ref[:width] = masked[:, :, :128]
    packed_ref[width:] = jnp.concatenate([masked[:half, :, 128:], masked[half:, :, 128:]], axis=2)


def turn_kernel(weight, out_ref):
    step = 2 * weight.shape[0]
    total = weight.shape[1]
    for start in range(0, total, step):
        stop = min(start + step, total)
        out_ref[start:stop, :] = weight[:, start:stop].T


def strip_kernel(near, far, masked, cot, out_ref, edge):
    width, rows, channels = masked.shape
    f32 = jnp.float32
    _, _, quad, side = position()
    odd = lax.rem(quad, 2)
    edge[odd] = far[...]
    edge[1 - odd] = near[...]
    ahead = side == 0

    def rows_of(block, count):
        block = block.astype(f32)
        return jnp.where(ahead, block[:, rows - count :], block[:, :count])

    halo = 2 * DEPTH
    strips = [rows_of(edge[0, 0:2], halo), rows_of(masked[...], halo), rows_of(edge[1, 0:2], halo)]
    cots = [rows_of(edge[0, 2:3], DEPTH), rows_of(cot[...], DEPTH), rows_of(edge[1, 2:3], DEPTH)]
    first = (width + 4) * halo
    out_ref[:first] = jnp.concatenate(strips).reshape(first, channels).astype(jnp.bfloat16)
    last = (width + 2) * DEPTH
    out_ref[first:] = jnp.concatenate(cots).reshape(last, channels).astype(jnp.bfloat16)


def forward_kernel(masked, cot, near, far, across, live, weight, pick, *refs):
    act_ref, gp_ref = refs[:2]
    slice_refs = refs[2 : 2 + MEMBERS]
    ext, edge, cols, slices = refs[2 + MEMBERS :]
    width, rows, channels = masked.shape
    f32 = jnp.float32
    _, me, quad, side = position()
    use_low = side.astype(f32)
    use_high = (1 - side).astype(f32)
    halo = 2 * DEPTH
    tall = rows + 2 * halo
    mid = rows + 2 * DEPTH
    span = width + 4
    strip = span * halo
    odd = lax.rem(quad, 2)
    edge[odd] = far[...]
    edge[1 - odd] = near[...]
    ext[0:2, halo : halo + rows, :] = edge[0, 0:2].astype(f32)
    ext[2 : 2 + width, halo : halo + rows, :] = masked[...].astype(f32)
    ext[2 + width :, halo : halo + rows, :] = edge[1, 0:2].astype(f32)
    beyond = across[0:strip].astype(f32).reshape(span, halo, channels)
    ext[:, 0:halo, :] = beyond * use_low
    ext[:, halo + rows :, :] = beyond * use_high
    field = ext[...].reshape(span * tall // DEPTH, DEPTH, channels)
    for c in OFFSETS:
        moved = shift_z(field, c).reshape(span, tall, channels)
        for b in OFFSETS:
            at = ((b + 1) * 3 + c + 1) * channels
            start = DEPTH * (b + 1)
            cols[:, :, at : at + channels] = moved[:, start : start + mid].astype(jnp.bfloat16)
    nine = 9 * channels
    pre = jnp.zeros(((width + 2) * mid, channels), f32)
    for a in range(3):
        pre += jnp.dot(
            cols[a : a + width + 2].reshape((width + 2) * mid, nine),
            weight[a * nine : (a + 1) * nine, :],
            preferred_element_type=f32,
        )
    sig = jax.nn.sigmoid(pre)
    act = (pre * sig).reshape(width + 2, mid, channels)[1 : 1 + width, DEPTH : DEPTH + rows]
    act_ref[...] = (act * live[:, :, 0:1]).astype(jnp.bfloat16)
    slope = (sig * (1.0 + pre * (1.0 - sig))).reshape(width + 2, mid, channels)
    beyond = across[strip:].astype(f32).reshape(width + 2, DEPTH, channels)
    centre = jnp.concatenate([edge[0, 2:3], cot[...], edge[1, 2:3]], axis=0).astype(f32)
    full = jnp.concatenate([beyond * use_low, centre, beyond * use_high], axis=1)
    grad = full * slope
    gp_ref[...] = grad.astype(jnp.bfloat16)
    inner = grad[:, DEPTH : DEPTH + rows].astype(jnp.bfloat16)
    turned = lax.dot_general(
        pick[...],
        inner.reshape((width + 2) * rows, channels),
        (((1,), (1,)), ((), ())),
        preferred_element_type=f32,
    )
    slices[...] = turned.reshape(slices.shape).astype(jnp.bfloat16)
    for distance, ref in enumerate(slice_refs):
        ref[...] = slices[me ^ distance]


def input_kernel(gp, live, turned, out_ref, cols, weight):
    width, rows, channels = out_ref.shape
    f32 = jnp.float32
    tall = rows + 2 * DEPTH
    for tap in range(27):
        weight[tap * channels : (tap + 1) * channels, :] = turned[
            :, tap * channels : (tap + 1) * channels
        ]
    field = gp[...].astype(f32).reshape((width + 2) * tall // DEPTH, DEPTH, channels)
    for c in OFFSETS:
        moved = shift_z(field, -c).reshape(width + 2, tall, channels)
        for b in OFFSETS:
            at = ((b + 1) * 3 + c + 1) * channels
            start = DEPTH * (1 - b)
            cols[:, :, at : at + channels] = moved[:, start : start + rows].astype(jnp.bfloat16)
    nine = 9 * channels
    total = jnp.zeros((width * rows, channels), f32)
    for a in range(3):
        total += jnp.dot(
            cols[2 - a : 2 - a + width].reshape(width * rows, nine),
            weight[a * nine : (a + 1) * nine, :],
            preferred_element_type=f32,
        )
    out_ref[...] = (total.reshape(width, rows, channels) * live[:, :, 0:1]).astype(jnp.bfloat16)


def kernel_grad_kernel(*refs):
    received, bricks = refs[:MEMBERS], refs[MEMBERS : 2 * MEMBERS]
    own_ref, *send_refs = refs[2 * MEMBERS : 2 * MEMBERS + 4]
    slices, cols, part, stage, masked, sems = refs[2 * MEMBERS + 4 :]
    f32 = jnp.float32
    group, lanes = received[0].shape
    slabs, lane, channels = masked.shape
    per = slabs // QUAD
    half = lane // 2
    plane, me, quad, side = position()
    copies = []
    for member in range(MEMBERS):
        to_quad, to_side = quad ^ (member // SIDES), side ^ (member % SIDES)
        copies.append(
            pltpu.make_async_copy(bricks[member], stage.at[to_quad, to_side], sems.at[member])
        )
    for copy in copies:
        copy.start()
    for distance in range(MEMBERS):
        slices[me ^ distance] = received[distance][...]
    at = lax.broadcasted_iota(jnp.int32, (group, lane), 1)
    y, z = at // DEPTH, at % DEPTH
    tall = lane // DEPTH
    base = [None] * (slabs + 2)
    for quad in range(QUAD):
        first = slices[2 * quad].astype(f32)
        second = slices[2 * quad + 1].astype(f32)
        for m in range((per + 2) // 2):
            one = first[:, m * lane : (m + 1) * lane]
            two = second[:, m * lane : (m + 1) * lane]
            pair = (
                jnp.where(at < half, one, pltpu.roll(two, half, 1)),
                jnp.where(at < half, pltpu.roll(one, half, 1), two),
            )
            for odd in range(2):
                k = 2 * m + odd
                slab = quad * per + k
                inside = 1 <= k <= per
                edge = (quad == 0 and k == 0) or (quad == QUAD - 1 and k == per + 1)
                if inside or edge:
                    base[slab] = pair[odd]
    for slab in range(slabs + 2):
        pieces = []
        for b in OFFSETS:
            for c in OFFSETS:
                step = (DEPTH * b + c) % lane
                moved = base[slab] if step == 0 else pltpu.roll(base[slab], step, 1)
                keep = (y - b >= 0) & (y - b < tall) & (z - c >= 0) & (z - c < DEPTH)
                pieces.append(jnp.where(keep, moved, 0.0))
        cols[:, slab * lane : (slab + 1) * lane] = jnp.concatenate(pieces, axis=0).astype(
            jnp.bfloat16
        )
    for copy in copies:
        copy.wait()
    for quad in range(QUAD):
        for side in range(SIDES):
            at_rows = pl.ds(side * half, half)
            for x in range(per):
                shift = 64 * (x // (per // 2))
                rest = stage[quad, side, per + x % (per // 2)]
                masked[quad * per + x, at_rows, :128] = stage[quad, side, x]
                masked[quad * per + x, at_rows, 128:] = rest[:, shift : shift + 64]
    field = masked[...].reshape(slabs * lane, channels)
    planes = part.shape[0]
    for a in range(3):
        start = (2 - a) * lane
        got = jnp.dot(
            cols[:, start : start + slabs * lane], field, preferred_element_type=f32
        ).reshape(9, planes, 8, channels)
        for to in range(planes):
            part[to, :, a * 9 * channels : (a + 1) * 9 * channels] = jnp.concatenate(
                [got[tap, to] for tap in range(9)], axis=1
            )
    own_ref[...] = part[plane]
    for distance, ref in enumerate(send_refs, 1):
        ref[...] = part[plane ^ distance].astype(jnp.bfloat16)


def sum_kernel(scale, own, one, two, three, out_ref):
    f32 = jnp.float32
    total = own[...] + one[...].astype(f32) + two[...].astype(f32) + three[...].astype(f32)
    out_ref[...] = total * scale


def join_kernel(mine, other, out_ref):
    share = out_ref.shape[0] // SIDES
    ahead = position()[3] == 0
    first = jnp.where(ahead, mine[...], other[...])
    second = jnp.where(ahead, other[...], mine[...])
    out_ref[0:share] = first[:share]
    out_ref[share:] = second[:share]


def call(body, name, mebibytes, flops, moved, out_shape, scratch=(), in_specs=None):
    spec = pl.BlockSpec(memory_space=pltpu.VMEM)

    def run(*operands):
        return pl.pallas_call(
            body,
            out_shape=out_shape,
            in_specs=in_specs or [spec] * len(operands),
            out_specs=jax.tree.map(lambda _: spec, out_shape),
            scratch_shapes=scratch,
            compiler_params=pltpu.CompilerParams(vmem_limit_bytes=mebibytes << 20),
            cost_estimate=pl.CostEstimate(flops=flops, bytes_accessed=moved, transcendentals=0),
            name=name,
        )(*operands)

    return run


def channel_order(channels, planes):
    per = channels // (planes * QUAD)
    share = per // SIDES
    index = np.arange(MEMBERS * planes * 8)
    quad, side = index // (SIDES * planes * 8), index // (planes * 8) % SIDES
    plane, row = index // 8 % planes, index % 8
    channel = per * (QUAD * plane + quad) + share * side + row
    return (np.where(row < share, channel, -1)[:, None] == np.arange(channels)[None, :])


def planes_local(features, weight, voxel_mask, cotangent):
    bf16 = jnp.bfloat16
    f32 = jnp.float32
    array = jax.ShapeDtypeStruct
    width, wide_y, depth, channels = features.shape
    rows = wide_y * depth
    planes = lax.axis_size("depth")
    count = planes * QUAD
    total = 27 * channels
    halo = 2 * DEPTH
    span = (width + 2) * rows
    group = planes * 8

    def swap(piece, axes, distance, size):
        return lax.ppermute(piece, axes, [(i, i ^ distance) for i in range(size)])

    def in_plane(piece, distance):
        return swap(piece, ("quad", "narrow"), distance, MEMBERS)

    brick = array((width, rows, channels), bf16)
    slab = array((3, rows, channels), bf16)
    masked, cot, live, near, far = call(
        prepare_kernel, "prepare", 16, 1 << 20, 1 << 20,
        (brick, brick, array((width, rows, 128), f32), slab, slab),
        (
            pltpu.VMEM(brick.shape, bf16),
            pltpu.VMEM(brick.shape, bf16),
            pltpu.VMEM((width, wide_y, depth), jnp.int32),
            pltpu.SemaphoreType.DMA((3,)),
        ),
        [pl.BlockSpec(memory_space=pltpu.HBM)] * 3,
    )(
        features.reshape(width, rows, channels),
        cotangent.reshape(width, rows, channels),
        voxel_mask,
    )
    near = swap(near, WIDE, 1, count)
    far = lax.ppermute(
        far, WIDE, [(i, j) for i in range(count) if 0 <= (j := ((i + 1) ^ 1) - 1) < count]
    )
    weight_rows = call(
        turn_kernel, "turn", 8, 1 << 20, 4 << 20, array((total, channels), bf16)
    )(weight.T)
    edge = call(
        strip_kernel, "strip", 4, 1 << 16, 1 << 18,
        array(((width + 4) * halo + (width + 2) * DEPTH, channels), bf16),
        (pltpu.VMEM((2,) + slab.shape, bf16),),
    )(near, far, masked, cot)
    packed = call(
        pack_kernel, "pack", 4, 1 << 16, 1 << 19,
        array((width * channels // 128, rows, 128), bf16),
    )(masked)
    packed, edge = lax.optimization_barrier((packed, edge))
    across = in_plane(edge, 1)
    bricks = [packed] + [None] * (MEMBERS - 1)
    for distance in (5, 4, 1, 2):
        bricks[distance] = in_plane(packed, distance)

    mid = rows + 2 * DEPTH
    pick = jnp.asarray(channel_order(channels, planes), bf16)
    act, gp, *slices = call(
        forward_kernel, "forward", 28, 800 * 5184 * 256, 1 << 20,
        (brick, array((width + 2, mid, channels), bf16)) + (array((group, span), bf16),) * MEMBERS,
        (
            pltpu.VMEM((width + 4, rows + 2 * halo, channels), f32),
            pltpu.VMEM((2,) + slab.shape, bf16),
            pltpu.VMEM((width + 4, mid, 9 * channels), bf16),
            pltpu.VMEM((MEMBERS, group, span), bf16),
        ),
    )(masked, cot, near, far, across, live, weight_rows, pick)
    for distance in (5, 7, 4, 6, 1, 3, 2):
        slices[distance] = in_plane(slices[distance], distance)
    for distance in (5, 4, 1):
        bricks[distance ^ 2] = in_plane(bricks[distance], 2)

    grad_input = call(
        input_kernel, "input_gradient", 20, 2 * 512 * 5184 * 256, 4 << 20, brick,
        (
            pltpu.VMEM((width + 2, rows, 9 * channels), bf16),
            pltpu.VMEM((total, channels), bf16),
        ),
    )(gp, live, weight.T)

    plane_rows = QUAD * width, SIDES * rows
    send = array((8, total), bf16)
    own, *sends = call(
        kernel_grad_kernel, "kernel_gradient", 24, 2 * 288 * 3 * 4096 * 256, 4 << 20,
        (array((8, total), f32),) + (send,) * (planes - 1),
        (
            pltpu.VMEM((MEMBERS, group, span), bf16),
            pltpu.VMEM((9 * group, (plane_rows[0] + 2) * plane_rows[1]), bf16),
            pltpu.VMEM((planes, 8, total), f32),
            pltpu.VMEM((QUAD, SIDES) + packed.shape, bf16),
            pltpu.VMEM(plane_rows + (channels,), bf16),
            pltpu.SemaphoreType.DMA((MEMBERS,)),
        ),
        [pl.BlockSpec(memory_space=pltpu.VMEM)] * MEMBERS
        + [pl.BlockSpec(memory_space=pl.ANY)] * MEMBERS,
    )(*slices, *bricks)
    got = [swap(sent, "depth", d, planes) for d, sent in enumerate(sends, 1)]
    voxels = count * SIDES * width * rows
    mine = call(
        functools.partial(sum_kernel, float(1.0 / voxels**0.5)),
        "plane_sum", 4, 8 * total * 4, 8 * total * 14, array((8, total), f32),
    )(own, *got)
    other = in_plane(mine, 1)
    grad_weight = call(
        join_kernel, "join", 4, 8 * total, 8 * total * 14, array((channels // count, total), f32)
    )(mine, other)
    shape = features.shape
    return act.reshape(shape), grad_input.reshape(shape), grad_weight


def padded_2(cells, sides, width):
    for axis, dim in sides:
        count = lax.axis_size(axis)
        ends = count - 1
        head = lax.slice_in_dim(cells, 0, width, axis=dim)
        tail = lax.slice_in_dim(cells, cells.shape[dim] - width, cells.shape[dim], axis=dim)
        cells = jnp.concatenate(
            [
                lax.ppermute(tail, axis, [(i, (i + 1) % count) for i in range(ends)]),
                cells,
                lax.ppermute(head, axis, [((i + 1) % count, i) for i in range(ends)]),
            ],
            axis=dim,
        )
    return cells


def gather_taps(padded, width_x, width_y, depth_z, channels, flip):
    pieces = []
    for shift_x in range(3):
        for shift_y in range(3):
            for shift_z in range(3):
                start_x = 2 - shift_x if flip else shift_x
                start_y = 2 - shift_y if flip else shift_y
                start_z = 2 - shift_z if flip else shift_z
                piece = padded[
                    start_x : start_x + width_x,
                    start_y : start_y + width_y,
                    start_z : start_z + depth_z,
                    :,
                ]
                pieces.append(piece.reshape(-1, channels))
    return jnp.concatenate(pieces, axis=1)


def summed_local(features, weight, voxel_mask, cotangent):
    width_x, width_y, depth_z, channels = features.shape
    masked = features * voxel_mask.astype(jnp.bfloat16)[..., None]
    padded = padded_2(masked, (("wide", 0), ("narrow", 1)), 1)
    padded = jnp.pad(padded, ((0, 0), (0, 0), (1, 1), (0, 0)))
    columns = gather_taps(padded, width_x, width_y, depth_z, channels, False)
    pre = jnp.dot(columns, weight, preferred_element_type=jnp.float32)
    live = voxel_mask.reshape(-1, 1).astype(jnp.float32)
    sig = jax.nn.sigmoid(pre)
    activation = (
        (pre * sig * live).astype(jnp.bfloat16).reshape(width_x, width_y, depth_z, channels)
    )
    slope = sig * (1.0 + pre * (1.0 - sig))
    grad_pre = (cotangent.reshape(-1, channels).astype(jnp.float32) * live * slope).astype(
        jnp.bfloat16
    )
    taps = weight.reshape(27, channels, channels)
    grid = grad_pre.reshape(width_x, width_y, depth_z, channels)
    grad_pad = padded_2(grid, (("wide", 0), ("narrow", 1)), 1)
    grad_pad = jnp.pad(grad_pad, ((0, 0), (0, 0), (1, 1), (0, 0)))
    grad_columns = gather_taps(grad_pad, width_x, width_y, depth_z, channels, True)
    flipped = jnp.transpose(taps, (0, 2, 1)).reshape(27 * channels, channels)
    grad_field = jnp.dot(grad_columns, flipped, preferred_element_type=jnp.float32)
    grad_input = (
        (grad_field * live).astype(jnp.bfloat16).reshape(width_x, width_y, depth_z, channels)
    )
    scale = 1.0 / jnp.sqrt(
        jnp.float32(width_x * width_y * depth_z * lax.axis_size("wide") * lax.axis_size("narrow"))
    )
    whole = lax.dot_general(
        grad_pre, columns, (((0,), (0,)), ((), ())), preferred_element_type=jnp.float32
    )
    piece_flat = lax.psum_scatter(
        whole.reshape(-1), ("wide", "narrow"), scatter_dimension=0, tiled=True
    )
    gathered = lax.all_gather(piece_flat, "narrow", axis=0, tiled=True)
    summed = gathered.reshape(channels // lax.axis_size("wide"), 27 * channels)
    grad_weight = summed * scale
    return (activation, grad_input, grad_weight)


def sharded(body, mesh, wide):
    return jax.shard_map(
        body,
        mesh=mesh,
        in_specs=(
            P(wide, "narrow", None, None),
            P(),
            P(wide, "narrow", None),
            P(wide, "narrow", None, None),
        ),
        out_specs=(
            P(wide, "narrow", None, None),
            P(wide, "narrow", None, None),
            P(wide, None),
        ),
        check_vma=False,
    )


def solution(mesh):
    wide, narrow = mesh.shape["wide"], mesh.shape["narrow"]
    if wide != 4 * QUAD or narrow != SIDES:
        return sharded(summed_local, mesh, "wide")
    planes = Mesh(
        mesh.devices.reshape(wide // QUAD, QUAD, narrow), ("depth", "quad", "narrow")
    )
    return sharded(planes_local, planes, WIDE)
```

```python
import functools

import jax
import jax.numpy as jnp
from jax import lax
from jax.experimental import pallas as pl
from jax.experimental.pallas import tpu as pltpu
from jax.sharding import Mesh
from jax.sharding import PartitionSpec as P

WIDE = ("depth", "quad")
QUAD = 4
SIDES = 2
MEMBERS = QUAD * SIDES
CHIPS = (0, 1, 4, 5)
OFFSETS = (-1, 0, 1)
DEPTH = 8


def position():
    quad, side = lax.axis_index("quad"), lax.axis_index("narrow")
    return lax.axis_index("depth"), quad * SIDES + side, quad, side


def shift_z(field, step):
    if step == 0:
        return field
    depth = field.shape[1]
    moved = pltpu.roll(field, (-step) % depth, 1)
    z = lax.broadcasted_iota(jnp.int32, field.shape, 1) + step
    return jnp.where((z >= 0) & (z < depth), moved, 0.0)


def pick_kernel(planes, out_ref):
    index = lax.broadcasted_iota(jnp.int32, out_ref.shape, 0)
    column = lax.broadcasted_iota(jnp.int32, out_ref.shape, 1)
    per = out_ref.shape[1] // (planes * QUAD)
    share = per // SIDES
    quad, side = index // (SIDES * planes * 8), index // (planes * 8) % SIDES
    plane, row = index // 8 % planes, index % 8
    channel = per * (QUAD * plane + quad) + share * side + row
    out_ref[...] = jnp.where((row < share) & (channel == column), 1.0, 0.0).astype(jnp.bfloat16)


def prepare_kernel(
    features, cot, mask, first, masked_ref, cot_ref, live_ref,
    near_ref, far_ref, across_ref, near_across_ref, far_across_ref,
):
    width, rows, channels = features.shape
    f32 = jnp.float32
    bf16 = jnp.bfloat16
    flat = mask[...].astype(f32).reshape(width * rows // DEPTH, DEPTH)
    live = jnp.broadcast_to(flat[:, :, None], flat.shape + (channels,)).reshape(features.shape)
    live_ref[...] = live[:, :, :128]
    masked = features[...].astype(f32) * live
    masked_ref[...] = masked.astype(bf16)
    grown = cot[...].astype(f32) * live
    cot_ref[...] = grown.astype(bf16)
    _, _, quad, side = position()
    odd = lax.rem(quad, 2)
    ahead = side == 0
    halo = 2 * DEPTH
    strip = jnp.where(ahead, masked[:, rows - halo :], masked[:, :halo])
    cots = jnp.where(ahead, grown[:, rows - DEPTH :], grown[:, :DEPTH])
    across_ref[: width * halo] = strip.reshape(-1, channels).astype(bf16)
    across_ref[width * halo :] = cots.reshape(-1, channels).astype(bf16)
    blank = jnp.zeros((DEPTH, channels), f32)
    corners = [
        jnp.concatenate([strip[x : x + 2].reshape(-1, channels), cots[y], blank], axis=0)
        for x, y in ((0, 0), (width - 2, width - 1))
    ]
    for upper, ref, corner_ref in ((1 - odd, near_ref, near_across_ref), (odd, far_ref, far_across_ref)):
        ref[0:2] = masked_ref[pl.ds(upper * (width - 2), 2)]
        ref[2:3] = cot_ref[pl.ds(upper * (width - 1), 1)]
        corner_ref[...] = jnp.where(upper == 1, corners[1], corners[0]).astype(bf16)


def pack_kernel(masked, packed_ref):
    width = masked.shape[0]
    half = width // 2
    packed_ref[:width] = masked[:, :, :128]
    packed_ref[width:] = jnp.concatenate([masked[:half, :, 128:], masked[half:, :, 128:]], axis=2)


def turn_kernel(weight, out_ref):
    step = 2 * weight.shape[0]
    total = weight.shape[1]
    for start in range(0, total, step):
        stop = min(start + step, total)
        out_ref[start:stop, :] = weight[:, start:stop].T


def forward_kernel(
    masked, cot, near, far, across, near_across, far_across, live, weight, pick, *refs
):
    act_ref, gp_ref = refs[:2]
    slice_refs = refs[2 : 2 + len(CHIPS)]
    ext, edge, corner, cols, slices = refs[2 + len(CHIPS) :]
    width, rows, channels = masked.shape
    f32 = jnp.float32
    plane, me, quad, side = position()
    use_low = side.astype(f32)
    use_high = (1 - side).astype(f32)
    place = plane * QUAD + quad
    use_left = (place > 0).astype(f32)
    use_right = (place < QUAD * lax.axis_size("depth") - 1).astype(f32)
    halo = 2 * DEPTH
    tall = rows + 2 * halo
    mid = rows + 2 * DEPTH
    span = width + 4
    odd = lax.rem(quad, 2)
    edge[odd] = far[...]
    edge[1 - odd] = near[...]
    corner[odd] = far_across[...]
    corner[1 - odd] = near_across[...]
    left, right = edge[0].astype(f32) * use_left, edge[1].astype(f32) * use_right
    lower, upper = corner[0].astype(f32) * use_left, corner[1].astype(f32) * use_right
    ext[0:2, halo : halo + rows, :] = left[0:2]
    ext[2 : 2 + width, halo : halo + rows, :] = masked[...].astype(f32)
    ext[2 + width :, halo : halo + rows, :] = right[0:2]
    beside = across[: width * halo].astype(f32).reshape(width, halo, channels)
    for use, start in ((use_low, 0), (use_high, halo + rows)):
        at = slice(start, start + halo)
        ext[0:2, at, :] = lower[: 2 * halo].reshape(2, halo, channels) * use
        ext[2 : 2 + width, at, :] = beside * use
        ext[2 + width :, at, :] = upper[: 2 * halo].reshape(2, halo, channels) * use
    field = ext[...].reshape(span * tall // DEPTH, DEPTH, channels)
    for c in OFFSETS:
        moved = shift_z(field, c).reshape(span, tall, channels)
        for b in OFFSETS:
            at = ((b + 1) * 3 + c + 1) * channels
            start = DEPTH * (b + 1)
            cols[:, :, at : at + channels] = moved[:, start : start + mid].astype(jnp.bfloat16)
    nine = 9 * channels
    pre = jnp.zeros(((width + 2) * mid, channels), f32)
    for a in range(3):
        pre += jnp.dot(
            cols[a : a + width + 2].reshape((width + 2) * mid, nine),
            weight[a * nine : (a + 1) * nine, :],
            preferred_element_type=f32,
        )
    sig = jax.nn.sigmoid(pre)
    act = (pre * sig).reshape(width + 2, mid, channels)[1 : 1 + width, DEPTH : DEPTH + rows]
    act_ref[...] = (act * live[:, :, 0:1]).astype(jnp.bfloat16)
    slope = (sig * (1.0 + pre * (1.0 - sig))).reshape(width + 2, mid, channels)
    beyond = jnp.concatenate(
        [
            lower[None, 2 * halo : 2 * halo + DEPTH],
            across[width * halo :].astype(f32).reshape(width, DEPTH, channels),
            upper[None, 2 * halo : 2 * halo + DEPTH],
        ],
        axis=0,
    )
    centre = jnp.concatenate([left[2:3], cot[...].astype(f32), right[2:3]], axis=0)
    full = jnp.concatenate([beyond * use_low, centre, beyond * use_high], axis=1)
    grad = full * slope
    gp_ref[...] = grad.astype(jnp.bfloat16)
    inner = grad[:, DEPTH : DEPTH + rows].astype(jnp.bfloat16)
    turned = lax.dot_general(
        pick[...],
        inner.reshape((width + 2) * rows, channels),
        (((1,), (1,)), ((), ())),
        preferred_element_type=f32,
    )
    slices[...] = turned.reshape(slices.shape).astype(jnp.bfloat16)
    group = slices.shape[1]
    chip = me - lax.rem(quad, 2) * SIDES
    for distance, ref in zip(CHIPS, slice_refs):
        ref[:group] = slices[chip ^ distance]
        ref[group:] = slices[(chip ^ distance) + SIDES]


def input_kernel(gp, live, turned, out_ref, cols, weight):
    width, rows, channels = out_ref.shape
    f32 = jnp.float32
    tall = rows + 2 * DEPTH
    for tap in range(27):
        weight[tap * channels : (tap + 1) * channels, :] = turned[
            :, tap * channels : (tap + 1) * channels
        ]
    field = gp[...].astype(f32).reshape((width + 2) * tall // DEPTH, DEPTH, channels)
    for c in OFFSETS:
        moved = shift_z(field, -c).reshape(width + 2, tall, channels)
        for b in OFFSETS:
            at = ((b + 1) * 3 + c + 1) * channels
            start = DEPTH * (1 - b)
            cols[:, :, at : at + channels] = moved[:, start : start + rows].astype(jnp.bfloat16)
    nine = 9 * channels
    total = jnp.zeros((width * rows, channels), f32)
    for a in range(3):
        total += jnp.dot(
            cols[2 - a : 2 - a + width].reshape(width * rows, nine),
            weight[a * nine : (a + 1) * nine, :],
            preferred_element_type=f32,
        )
    out_ref[...] = (total.reshape(width, rows, channels) * live[:, :, 0:1]).astype(jnp.bfloat16)


def kernel_grad_kernel(*refs):
    chips = len(CHIPS)
    received, bricks = refs[:chips], refs[chips : 2 * chips]
    keep_ref, send_ref, slices, cols, part, stage, masked, sems = refs[2 * chips :]
    f32 = jnp.float32
    group, lanes = received[0].shape
    blocks, per, lane, channels = masked.shape
    half = lane // 2
    _, _, quad, side = position()
    copies = []
    for i, distance in enumerate(CHIPS):
        to = stage.at[distance // 4, side ^ (distance % 2)]
        copies.append(pltpu.make_async_copy(bricks[i], to, sems.at[i]))
        copies[i].start()
        slices[distance // 4, side ^ (distance % 2)] = received[i][...]
    at = lax.broadcasted_iota(jnp.int32, (group, lane), 1)
    y, z = at // DEPTH, at % DEPTH
    tall = lane // DEPTH
    for block in range(blocks):
        first = slices[block, 0].astype(f32)
        second = slices[block, 1].astype(f32)
        for k in range(per + 2):
            one = first[:, k // 2 * lane : (k // 2 + 1) * lane]
            two = second[:, k // 2 * lane : (k // 2 + 1) * lane]
            if k % 2 == 0:
                base = jnp.where(at < half, one, pltpu.roll(two, half, 1))
            else:
                base = jnp.where(at < half, pltpu.roll(one, half, 1), two)
            pieces = []
            for b in OFFSETS:
                for c in OFFSETS:
                    step = (DEPTH * b + c) % lane
                    moved = base if step == 0 else pltpu.roll(base, step, 1)
                    keep = (y - b >= 0) & (y - b < tall) & (z - c >= 0) & (z - c < DEPTH)
                    pieces.append(jnp.where(keep, moved, 0.0))
            slab = block * (per + 2) + k
            cols[:, slab * lane : (slab + 1) * lane] = jnp.concatenate(pieces, axis=0).astype(
                jnp.bfloat16
            )
    for copy in copies:
        copy.wait()
    for block in range(blocks):
        for sided in range(SIDES):
            at_rows = pl.ds(sided * half, half)
            for x in range(per):
                shift = 64 * (x // (per // 2))
                rest = stage[block, sided, per + x % (per // 2)]
                masked[block, x, at_rows, :128] = stage[block, sided, x]
                masked[block, x, at_rows, 128:] = rest[:, shift : shift + 64]
    _, planes, eight, _ = part.shape
    for a in range(3):
        got = jnp.zeros((cols.shape[0], channels), f32)
        for block in range(blocks):
            start = (block * (per + 2) + 2 - a) * lane
            got += jnp.dot(
                cols[:, start : start + per * lane],
                masked[block].reshape(per * lane, channels),
                preferred_element_type=f32,
            )
        got = got.reshape(9, 2, planes, eight, channels)
        for core in range(2):
            for to in range(planes):
                part[core, to, :, a * 9 * channels : (a + 1) * 9 * channels] = jnp.concatenate(
                    [got[tap, core, to] for tap in range(9)], axis=1
                )
    core = lax.rem(quad, 2)
    keep_ref[...] = part[core]
    send_ref[...] = part[1 - core].astype(jnp.bfloat16)


def fold_kernel(keep, other, own_ref, *send_refs):
    plane = position()[0]
    own_ref[...] = keep[plane] + other[plane].astype(jnp.float32)
    for distance, ref in enumerate(send_refs, 1):
        to = plane ^ distance
        ref[...] = (keep[to] + other[to].astype(jnp.float32)).astype(jnp.bfloat16)


def sum_kernel(scale, own, one, two, three, out_ref):
    f32 = jnp.float32
    total = own[...] + one[...].astype(f32) + two[...].astype(f32) + three[...].astype(f32)
    out_ref[...] = (total * scale).astype(out_ref.dtype)


def join_kernel(mine, other, out_ref):
    share = out_ref.shape[0] // SIDES
    ahead = position()[3] == 0
    here, there = mine[...].astype(jnp.float32), other[...].astype(jnp.float32)
    first = jnp.where(ahead, here, there)
    second = jnp.where(ahead, there, here)
    out_ref[0:share] = first[:share]
    out_ref[share:] = second[:share]


def call(body, name, mebibytes, flops, moved, out_shape, scratch=(), in_specs=None):
    spec = pl.BlockSpec(memory_space=pltpu.VMEM)

    def run(*operands):
        return pl.pallas_call(
            body,
            out_shape=out_shape,
            in_specs=in_specs or [spec] * len(operands),
            out_specs=jax.tree.map(lambda _: spec, out_shape),
            scratch_shapes=scratch,
            compiler_params=pltpu.CompilerParams(vmem_limit_bytes=mebibytes << 20),
            cost_estimate=pl.CostEstimate(flops=flops, bytes_accessed=moved, transcendentals=0),
            name=name,
        )(*operands)

    return run


def planes_local(features, weight, voxel_mask, cotangent):
    bf16 = jnp.bfloat16
    f32 = jnp.float32
    array = jax.ShapeDtypeStruct
    width, wide_y, depth, channels = features.shape
    rows = wide_y * depth
    planes = lax.axis_size("depth")
    count = planes * QUAD
    total = 27 * channels
    halo = 2 * DEPTH
    span = (width + 2) * rows
    group = planes * 8

    def swap(piece, axes, distance, size):
        return lax.ppermute(piece, axes, [(i, i ^ distance) for i in range(size)])

    def in_plane(piece, distance):
        return swap(piece, ("quad", "narrow"), distance, MEMBERS)

    brick = array((width, rows, channels), bf16)
    slab = array((3, rows, channels), bf16)
    side_rows = array((width * (halo + DEPTH), channels), bf16)
    edge_rows = array((2 * halo + 2 * DEPTH, channels), bf16)
    pick = call(
        functools.partial(pick_kernel, planes), "pick", 4, 1 << 16, 1 << 16,
        array((MEMBERS * group, channels), bf16),
    )()
    vmem = pl.BlockSpec(memory_space=pltpu.VMEM)
    masked, cot, live, *halos = call(
        prepare_kernel, "prepare", 16, 1 << 20, 1 << 20,
        (brick, brick, array((width, rows, 128), f32), slab, slab, side_rows, edge_rows, edge_rows),
        (),
        [vmem] * 3 + [pl.BlockSpec(memory_space=pl.ANY)],
    )(
        features.reshape(width, rows, channels),
        cotangent.reshape(width, rows, channels),
        voxel_mask,
        pick,
    )
    pairs = [i ^ 1 for i in range(count)], [min(max(((i + 1) ^ 1) - 1, 0), count - 1) for i in range(count)]
    to_near, to_far = ([(i, j) for i, j in enumerate(pair)] for pair in pairs)
    near_across, far_across = (
        [(SIDES * i + s, SIDES * j + 1 - s) for i, j in pair for s in range(SIDES)]
        for pair in (to_near, to_far)
    )
    halos = [
        lax.ppermute(halos[0], WIDE, to_near),
        lax.ppermute(halos[1], WIDE, to_far),
        in_plane(halos[2], 1),
        lax.ppermute(halos[3], WIDE + ("narrow",), near_across),
        lax.ppermute(halos[4], WIDE + ("narrow",), far_across),
    ]
    weight_rows = call(
        turn_kernel, "turn", 8, 1 << 20, 4 << 20, array((total, channels), bf16)
    )(weight.T)
    packed = call(
        pack_kernel, "pack", 4, 1 << 16, 1 << 19,
        array((width * channels // 128, rows, 128), bf16),
    )(masked)
    packed, weight_rows, *halos = lax.optimization_barrier((packed, weight_rows, *halos))
    bricks = [packed] + [in_plane(packed, distance) for distance in CHIPS[1:]]

    mid = rows + 2 * DEPTH
    act, gp, *slices = call(
        forward_kernel, "forward", 28, 800 * 5184 * 256, 1 << 20,
        (brick, array((width + 2, mid, channels), bf16))
        + (array((2 * group, span), bf16),) * len(CHIPS),
        (
            pltpu.VMEM((width + 4, rows + 2 * halo, channels), f32),
            pltpu.VMEM((2,) + slab.shape, bf16),
            pltpu.VMEM((2,) + edge_rows.shape, bf16),
            pltpu.VMEM((width + 4, mid, 9 * channels), bf16),
            pltpu.VMEM((MEMBERS, group, span), bf16),
        ),
    )(masked, cot, *halos, live, weight_rows, pick)
    bricks[1], bricks[2], *slices = lax.optimization_barrier((bricks[1], bricks[2], *slices))
    slices = [slices[0]] + [in_plane(part, d) for part, d in zip(slices[1:], CHIPS[1:])]

    grad_input = call(
        input_kernel, "input_gradient", 20, 2 * 512 * 5184 * 256, 4 << 20, brick,
        (
            pltpu.VMEM((width + 2, rows, 9 * channels), bf16),
            pltpu.VMEM((total, channels), bf16),
        ),
    )(gp, live, weight.T)
    grad_input, *slices = lax.optimization_barrier((grad_input, *slices))

    blocks = QUAD // 2
    chips = len(CHIPS)
    keep, fold = call(
        kernel_grad_kernel, "kernel_gradient", 28, 2 * 576 * 3 * 2048 * 256, 4 << 20,
        (array((planes, 8, total), f32), array((planes, 8, total), bf16)),
        (
            pltpu.VMEM((blocks, SIDES, 2 * group, span), bf16),
            pltpu.VMEM((9 * 2 * group, blocks * (width + 2) * SIDES * rows), bf16),
            pltpu.VMEM((2, planes, 8, total), f32),
            pltpu.VMEM((blocks, SIDES) + packed.shape, bf16),
            pltpu.VMEM((blocks, width, SIDES * rows, channels), bf16),
            pltpu.SemaphoreType.DMA((chips,)),
        ),
        [vmem] * chips + [pl.BlockSpec(memory_space=pl.ANY)] * chips,
    )(*slices, *bricks)
    own, *sends = call(
        fold_kernel, "fold", 8, 8 * total * 4, 8 * total * 40,
        (array((8, total), f32),) + (array((8, total), bf16),) * (planes - 1),
    )(keep, in_plane(fold, 2))
    got = [swap(sent, "depth", d, planes) for d, sent in enumerate(sends, 1)]
    voxels = count * SIDES * width * rows
    mine = call(
        functools.partial(sum_kernel, float(1.0 / voxels**0.5)),
        "plane_sum", 4, 8 * total * 4, 8 * total * 14, array((8, total), bf16),
    )(own, *got)
    grad_weight = call(
        join_kernel, "join", 4, 8 * total, 8 * total * 14, array((channels // count, total), f32)
    )(mine, in_plane(mine, 1))
    shape = features.shape
    return act.reshape(shape), grad_input.reshape(shape), grad_weight


def padded_2(cells, sides, width):
    for axis, dim in sides:
        count = lax.axis_size(axis)
        ends = count - 1
        head = lax.slice_in_dim(cells, 0, width, axis=dim)
        tail = lax.slice_in_dim(cells, cells.shape[dim] - width, cells.shape[dim], axis=dim)
        cells = jnp.concatenate(
            [
                lax.ppermute(tail, axis, [(i, (i + 1) % count) for i in range(ends)]),
                cells,
                lax.ppermute(head, axis, [((i + 1) % count, i) for i in range(ends)]),
            ],
            axis=dim,
        )
    return cells


def gather_taps(padded, width_x, width_y, depth_z, channels, flip):
    pieces = []
    for shift_x in range(3):
        for shift_y in range(3):
            for shift_z in range(3):
                start_x = 2 - shift_x if flip else shift_x
                start_y = 2 - shift_y if flip else shift_y
                start_z = 2 - shift_z if flip else shift_z
                piece = padded[
                    start_x : start_x + width_x,
                    start_y : start_y + width_y,
                    start_z : start_z + depth_z,
                    :,
                ]
                pieces.append(piece.reshape(-1, channels))
    return jnp.concatenate(pieces, axis=1)


def summed_local(features, weight, voxel_mask, cotangent):
    width_x, width_y, depth_z, channels = features.shape
    masked = features * voxel_mask.astype(jnp.bfloat16)[..., None]
    padded = padded_2(masked, (("wide", 0), ("narrow", 1)), 1)
    padded = jnp.pad(padded, ((0, 0), (0, 0), (1, 1), (0, 0)))
    columns = gather_taps(padded, width_x, width_y, depth_z, channels, False)
    pre = jnp.dot(columns, weight, preferred_element_type=jnp.float32)
    live = voxel_mask.reshape(-1, 1).astype(jnp.float32)
    sig = jax.nn.sigmoid(pre)
    activation = (
        (pre * sig * live).astype(jnp.bfloat16).reshape(width_x, width_y, depth_z, channels)
    )
    slope = sig * (1.0 + pre * (1.0 - sig))
    grad_pre = (cotangent.reshape(-1, channels).astype(jnp.float32) * live * slope).astype(
        jnp.bfloat16
    )
    taps = weight.reshape(27, channels, channels)
    grid = grad_pre.reshape(width_x, width_y, depth_z, channels)
    grad_pad = padded_2(grid, (("wide", 0), ("narrow", 1)), 1)
    grad_pad = jnp.pad(grad_pad, ((0, 0), (0, 0), (1, 1), (0, 0)))
    grad_columns = gather_taps(grad_pad, width_x, width_y, depth_z, channels, True)
    flipped = jnp.transpose(taps, (0, 2, 1)).reshape(27 * channels, channels)
    grad_field = jnp.dot(grad_columns, flipped, preferred_element_type=jnp.float32)
    grad_input = (
        (grad_field * live).astype(jnp.bfloat16).reshape(width_x, width_y, depth_z, channels)
    )
    scale = 1.0 / jnp.sqrt(
        jnp.float32(width_x * width_y * depth_z * lax.axis_size("wide") * lax.axis_size("narrow"))
    )
    whole = lax.dot_general(
        grad_pre, columns, (((0,), (0,)), ((), ())), preferred_element_type=jnp.float32
    )
    piece_flat = lax.psum_scatter(
        whole.reshape(-1), ("wide", "narrow"), scatter_dimension=0, tiled=True
    )
    gathered = lax.all_gather(piece_flat, "narrow", axis=0, tiled=True)
    summed = gathered.reshape(channels // lax.axis_size("wide"), 27 * channels)
    grad_weight = summed * scale
    return (activation, grad_input, grad_weight)


def sharded(body, mesh, wide):
    return jax.shard_map(
        body,
        mesh=mesh,
        in_specs=(
            P(wide, "narrow", None, None),
            P(),
            P(wide, "narrow", None),
            P(wide, "narrow", None, None),
        ),
        out_specs=(
            P(wide, "narrow", None, None),
            P(wide, "narrow", None, None),
            P(wide, None),
        ),
        check_vma=False,
    )


def solution(mesh):
    wide, narrow = mesh.shape["wide"], mesh.shape["narrow"]
    if wide != 4 * QUAD or narrow != SIDES:
        return sharded(summed_local, mesh, "wide")
    planes = Mesh(
        mesh.devices.reshape(wide // QUAD, QUAD, narrow), ("depth", "quad", "narrow")
    )
    return sharded(planes_local, planes, WIDE)
```

```python
import functools

import jax
import jax.numpy as jnp
from jax import lax
from jax.experimental import pallas as pl
from jax.experimental.pallas import tpu as pltpu
from jax.sharding import Mesh
from jax.sharding import PartitionSpec as P

WIDE = ("depth", "quad")
QUAD = 4
SIDES = 2
MEMBERS = QUAD * SIDES
CHIPS = (0, 1, 4, 5)
OFFSETS = (-1, 0, 1)
DEPTH = 8


def position():
    quad, side = lax.axis_index("quad"), lax.axis_index("narrow")
    return lax.axis_index("depth"), quad * SIDES + side, quad, side


def shift_z(field, step):
    if step == 0:
        return field
    depth = field.shape[1]
    moved = pltpu.roll(field, (-step) % depth, 1)
    z = lax.broadcasted_iota(jnp.int32, field.shape, 1) + step
    return jnp.where((z >= 0) & (z < depth), moved, 0.0)


def pick_kernel(planes, out_ref):
    index = lax.broadcasted_iota(jnp.int32, out_ref.shape, 0)
    column = lax.broadcasted_iota(jnp.int32, out_ref.shape, 1)
    per = out_ref.shape[1] // (planes * QUAD)
    share = per // SIDES
    quad, side = index // (SIDES * planes * 8), index // (planes * 8) % SIDES
    plane, row = index // 8 % planes, index % 8
    channel = per * (QUAD * plane + quad) + share * side + row
    out_ref[...] = jnp.where((row < share) & (channel == column), 1.0, 0.0).astype(jnp.bfloat16)


def prepare_kernel(features, cot, mask, first, masked_ref, cot_ref, live_ref, near_ref, far_ref):
    width, rows, channels = features.shape
    f32 = jnp.float32
    flat = mask[...].astype(f32).reshape(width * rows // DEPTH, DEPTH)
    live = jnp.broadcast_to(flat[:, :, None], flat.shape + (channels,)).reshape(features.shape)
    live_ref[...] = live[:, :, :128]
    masked_ref[...] = (features[...].astype(f32) * live).astype(jnp.bfloat16)
    cot_ref[...] = (cot[...].astype(f32) * live).astype(jnp.bfloat16)
    odd = lax.rem(position()[2], 2)
    for ref, upper in ((near_ref, 1 - odd), (far_ref, odd)):
        ref[0:2] = masked_ref[pl.ds(upper * (width - 2), 2)]
        ref[2:3] = cot_ref[pl.ds(upper * (width - 1), 1)]


def pack_kernel(masked, cot, packed_ref, across_ref):
    width, rows, channels = masked.shape
    half = width // 2
    packed_ref[:width] = masked[:, :, :128]
    packed_ref[width:] = jnp.concatenate([masked[:half, :, 128:], masked[half:, :, 128:]], axis=2)
    count = packed_ref.shape[0]
    across_ref[:count] = packed_ref[...]
    ahead = position()[3] == 0
    grown = cot[...].astype(jnp.float32)
    strip = jnp.where(ahead, grown[:, rows - DEPTH :], grown[:, :DEPTH])
    strip = strip.reshape(width * DEPTH, channels)
    rest = jnp.concatenate([strip[:, 128:], jnp.zeros_like(strip[:, 128:])], axis=1)
    across_ref[count] = strip[:, :128].astype(jnp.bfloat16)
    across_ref[count + 1] = rest.astype(jnp.bfloat16)


def corner_kernel(near, far, out_ref, edge):
    _, rows, channels = near.shape
    _, _, quad, side = position()
    odd = lax.rem(quad, 2)
    edge[odd] = far[...]
    edge[1 - odd] = near[...]
    halo = 2 * DEPTH
    ahead = side == 0
    held = edge[...].astype(jnp.float32)
    strip = jnp.where(ahead, held[:, :2, rows - halo :], held[:, :2, :halo])
    cots = jnp.where(ahead, held[:, 2, rows - DEPTH :], held[:, 2, :DEPTH])
    out_ref[: 4 * halo] = strip.reshape(4 * halo, channels).astype(jnp.bfloat16)
    out_ref[4 * halo :] = cots.reshape(2 * DEPTH, channels).astype(jnp.bfloat16)


def turn_kernel(weight, out_ref):
    step = 2 * weight.shape[0]
    total = weight.shape[1]
    for start in range(0, total, step):
        stop = min(start + step, total)
        out_ref[start:stop, :] = weight[:, start:stop].T


def forward_kernel(
    masked, cot, near, far, across, corner, live, weight, pick, *refs
):
    act_ref, gp_ref = refs[:2]
    slice_refs = refs[2 : 2 + len(CHIPS)]
    ext, edge, cols, slices = refs[2 + len(CHIPS) :]
    width, rows, channels = masked.shape
    f32 = jnp.float32
    plane, me, quad, side = position()
    use_low = side.astype(f32)
    use_high = (1 - side).astype(f32)
    place = plane * QUAD + quad
    use_left = (place > 0).astype(f32)
    use_right = (place < QUAD * lax.axis_size("depth") - 1).astype(f32)
    halo = 2 * DEPTH
    tall = rows + 2 * halo
    mid = rows + 2 * DEPTH
    span = width + 4
    odd = lax.rem(quad, 2)
    edge[odd] = far[...]
    edge[1 - odd] = near[...]
    left, right = edge[0].astype(f32) * use_left, edge[1].astype(f32) * use_right
    corners = corner[: 4 * halo].astype(f32).reshape(2, 2, halo, channels)
    lower, upper = corners[0] * use_left, corners[1] * use_right
    ends = corner[4 * halo :].astype(f32).reshape(2, 1, DEPTH, channels)
    ext[0:2, halo : halo + rows, :] = left[0:2]
    ext[2 : 2 + width, halo : halo + rows, :] = masked[...].astype(f32)
    ext[2 + width :, halo : halo + rows, :] = right[0:2]
    half = width // 2
    ahead = side == 0
    held = across[...].astype(f32)
    brick = jnp.where(ahead, held[: width + half, :halo], held[: width + half, rows - halo :])
    rest = jnp.concatenate([brick[width:, :, :64], brick[width:, :, 64:]], axis=0)
    beside = jnp.concatenate([brick[:width], rest], axis=2)
    for use, start in ((use_low, 0), (use_high, halo + rows)):
        at = slice(start, start + halo)
        ext[0:2, at, :] = lower * use
        ext[2 : 2 + width, at, :] = beside * use
        ext[2 + width :, at, :] = upper * use
    field = ext[...].reshape(span * tall // DEPTH, DEPTH, channels)
    for c in OFFSETS:
        moved = shift_z(field, c).reshape(span, tall, channels)
        for b in OFFSETS:
            at = ((b + 1) * 3 + c + 1) * channels
            start = DEPTH * (b + 1)
            cols[:, :, at : at + channels] = moved[:, start : start + mid].astype(jnp.bfloat16)
    nine = 9 * channels
    pre = jnp.zeros(((width + 2) * mid, channels), f32)
    for a in range(3):
        pre += jnp.dot(
            cols[a : a + width + 2].reshape((width + 2) * mid, nine),
            weight[a * nine : (a + 1) * nine, :],
            preferred_element_type=f32,
        )
    sig = jax.nn.sigmoid(pre)
    act = (pre * sig).reshape(width + 2, mid, channels)[1 : 1 + width, DEPTH : DEPTH + rows]
    act_ref[...] = (act * live[:, :, 0:1]).astype(jnp.bfloat16)
    slope = (sig * (1.0 + pre * (1.0 - sig))).reshape(width + 2, mid, channels)
    beyond = jnp.concatenate(
        [
            ends[0] * use_left,
            jnp.concatenate([held[width + half], held[width + half + 1, :, :64]], axis=1).reshape(
                width, DEPTH, channels
            ),
            ends[1] * use_right,
        ],
        axis=0,
    )
    centre = jnp.concatenate([left[2:3], cot[...].astype(f32), right[2:3]], axis=0)
    full = jnp.concatenate([beyond * use_low, centre, beyond * use_high], axis=1)
    grad = full * slope
    gp_ref[...] = grad.astype(jnp.bfloat16)
    inner = grad[:, DEPTH : DEPTH + rows].astype(jnp.bfloat16)
    turned = lax.dot_general(
        pick[...],
        inner.reshape((width + 2) * rows, channels),
        (((1,), (1,)), ((), ())),
        preferred_element_type=f32,
    )
    slices[...] = turned.reshape(slices.shape).astype(jnp.bfloat16)
    group = slices.shape[1]
    chip = me - lax.rem(quad, 2) * SIDES
    for distance, ref in zip(CHIPS, slice_refs):
        ref[:group] = slices[chip ^ distance]
        ref[group:] = slices[(chip ^ distance) + SIDES]


def input_kernel(gp, live, turned, out_ref, cols, weight):
    width, rows, channels = out_ref.shape
    f32 = jnp.float32
    tall = rows + 2 * DEPTH
    for tap in range(27):
        weight[tap * channels : (tap + 1) * channels, :] = turned[
            :, tap * channels : (tap + 1) * channels
        ]
    field = gp[...].astype(f32).reshape((width + 2) * tall // DEPTH, DEPTH, channels)
    for c in OFFSETS:
        moved = shift_z(field, -c).reshape(width + 2, tall, channels)
        for b in OFFSETS:
            at = ((b + 1) * 3 + c + 1) * channels
            start = DEPTH * (1 - b)
            cols[:, :, at : at + channels] = moved[:, start : start + rows].astype(jnp.bfloat16)
    nine = 9 * channels
    total = jnp.zeros((width * rows, channels), f32)
    for a in range(3):
        total += jnp.dot(
            cols[2 - a : 2 - a + width].reshape(width * rows, nine),
            weight[a * nine : (a + 1) * nine, :],
            preferred_element_type=f32,
        )
    out_ref[...] = (total.reshape(width, rows, channels) * live[:, :, 0:1]).astype(jnp.bfloat16)


def kernel_grad_kernel(*refs):
    chips = len(CHIPS)
    received, bricks = refs[:chips], refs[chips : 2 * chips]
    keep_ref, send_ref, slices, cols, part, stage, masked, sems = refs[2 * chips :]
    f32 = jnp.float32
    group, lanes = received[0].shape
    blocks, per, lane, channels = masked.shape
    half = lane // 2
    _, _, quad, side = position()
    copies = []
    for i, distance in enumerate(CHIPS):
        to = stage.at[distance // 4, side ^ (distance % 2)]
        packed = bricks[i].at[pl.ds(0, stage.shape[2])]
        copies.append(pltpu.make_async_copy(packed, to, sems.at[i]))
        copies[i].start()
        slices[distance // 4, side ^ (distance % 2)] = received[i][...]
    at = lax.broadcasted_iota(jnp.int32, (group, lane), 1)
    y, z = at // DEPTH, at % DEPTH
    tall = lane // DEPTH
    for block in range(blocks):
        first = slices[block, 0].astype(f32)
        second = slices[block, 1].astype(f32)
        for k in range(per + 2):
            one = first[:, k // 2 * lane : (k // 2 + 1) * lane]
            two = second[:, k // 2 * lane : (k // 2 + 1) * lane]
            if k % 2 == 0:
                base = jnp.where(at < half, one, pltpu.roll(two, half, 1))
            else:
                base = jnp.where(at < half, pltpu.roll(one, half, 1), two)
            pieces = []
            for b in OFFSETS:
                for c in OFFSETS:
                    step = (DEPTH * b + c) % lane
                    moved = base if step == 0 else pltpu.roll(base, step, 1)
                    keep = (y - b >= 0) & (y - b < tall) & (z - c >= 0) & (z - c < DEPTH)
                    pieces.append(jnp.where(keep, moved, 0.0))
            slab = block * (per + 2) + k
            cols[:, slab * lane : (slab + 1) * lane] = jnp.concatenate(pieces, axis=0).astype(
                jnp.bfloat16
            )
    for copy in copies:
        copy.wait()
    for block in range(blocks):
        for sided in range(SIDES):
            at_rows = pl.ds(sided * half, half)
            for x in range(per):
                shift = 64 * (x // (per // 2))
                rest = stage[block, sided, per + x % (per // 2)]
                masked[block, x, at_rows, :128] = stage[block, sided, x]
                masked[block, x, at_rows, 128:] = rest[:, shift : shift + 64]
    _, planes, eight, _ = part.shape
    for a in range(3):
        got = jnp.zeros((cols.shape[0], channels), f32)
        for block in range(blocks):
            start = (block * (per + 2) + 2 - a) * lane
            got += jnp.dot(
                cols[:, start : start + per * lane],
                masked[block].reshape(per * lane, channels),
                preferred_element_type=f32,
            )
        got = got.reshape(9, 2, planes, eight, channels)
        for core in range(2):
            for to in range(planes):
                part[core, to, :, a * 9 * channels : (a + 1) * 9 * channels] = jnp.concatenate(
                    [got[tap, core, to] for tap in range(9)], axis=1
                )
    core = lax.rem(quad, 2)
    keep_ref[...] = part[core]
    send_ref[...] = part[1 - core].astype(jnp.bfloat16)


def fold_kernel(keep, other, own_ref, *send_refs):
    plane = position()[0]
    own_ref[...] = keep[plane] + other[plane].astype(jnp.float32)
    for distance, ref in enumerate(send_refs, 1):
        to = plane ^ distance
        ref[...] = (keep[to] + other[to].astype(jnp.float32)).astype(jnp.bfloat16)


def sum_kernel(scale, own, one, two, three, out_ref):
    f32 = jnp.float32
    total = own[...] + one[...].astype(f32) + two[...].astype(f32) + three[...].astype(f32)
    out_ref[...] = (total * scale).astype(out_ref.dtype)


def join_kernel(mine, other, out_ref):
    share = out_ref.shape[0] // SIDES
    ahead = position()[3] == 0
    here, there = mine[...].astype(jnp.float32), other[...].astype(jnp.float32)
    first = jnp.where(ahead, here, there)
    second = jnp.where(ahead, there, here)
    out_ref[0:share] = first[:share]
    out_ref[share:] = second[:share]


def call(body, name, mebibytes, flops, moved, out_shape, scratch=(), in_specs=None):
    spec = pl.BlockSpec(memory_space=pltpu.VMEM)

    def run(*operands):
        return pl.pallas_call(
            body,
            out_shape=out_shape,
            in_specs=in_specs or [spec] * len(operands),
            out_specs=jax.tree.map(lambda _: spec, out_shape),
            scratch_shapes=scratch,
            compiler_params=pltpu.CompilerParams(vmem_limit_bytes=mebibytes << 20),
            cost_estimate=pl.CostEstimate(flops=flops, bytes_accessed=moved, transcendentals=0),
            name=name,
        )(*operands)

    return run


def planes_local(features, weight, voxel_mask, cotangent):
    bf16 = jnp.bfloat16
    f32 = jnp.float32
    array = jax.ShapeDtypeStruct
    width, wide_y, depth, channels = features.shape
    rows = wide_y * depth
    planes = lax.axis_size("depth")
    count = planes * QUAD
    total = 27 * channels
    halo = 2 * DEPTH
    span = (width + 2) * rows
    group = planes * 8

    def swap(piece, axes, distance, size):
        return lax.ppermute(piece, axes, [(i, i ^ distance) for i in range(size)])

    def in_plane(piece, distance):
        return swap(piece, ("quad", "narrow"), distance, MEMBERS)

    brick = array((width, rows, channels), bf16)
    slab = array((3, rows, channels), bf16)
    pick = call(
        functools.partial(pick_kernel, planes), "pick", 4, 1 << 16, 1 << 16,
        array((MEMBERS * group, channels), bf16),
    )()
    vmem = pl.BlockSpec(memory_space=pltpu.VMEM)
    masked, cot, live, near, far = call(
        prepare_kernel, "prepare", 16, 1 << 20, 1 << 20,
        (brick, brick, array((width, rows, 128), f32), slab, slab),
        (),
        [vmem] * 3 + [pl.BlockSpec(memory_space=pl.ANY)],
    )(
        features.reshape(width, rows, channels),
        cotangent.reshape(width, rows, channels),
        voxel_mask,
        pick,
    )
    near = swap(near, WIDE, 1, count)
    ends = [min(max(((i + 1) ^ 1) - 1, 0), count - 1) for i in range(count)]
    far = lax.ppermute(far, WIDE, list(enumerate(ends)))
    weight_rows = call(
        turn_kernel, "turn", 8, 1 << 20, 4 << 20, array((total, channels), bf16)
    )(weight.T)
    slabs = width * channels // 128
    packed, across = call(
        pack_kernel, "pack", 4, 1 << 16, 1 << 19,
        (array((slabs, rows, 128), bf16), array((slabs + 2, rows, 128), bf16)),
    )(masked, cot)
    across = in_plane(across, CHIPS[1])
    bricks = [packed, across, in_plane(packed, CHIPS[2]), None]
    packed, near, far = lax.optimization_barrier((packed, near, far))
    corner = call(
        corner_kernel, "corner", 4, 1 << 16, 1 << 18,
        array((4 * halo + 2 * DEPTH, channels), bf16),
        (pltpu.VMEM((2,) + slab.shape, bf16),),
    )(near, far)
    corner = in_plane(corner, 1)
    bricks[3] = in_plane(packed, CHIPS[3])

    mid = rows + 2 * DEPTH
    act, gp, *slices = call(
        forward_kernel, "forward", 28, 800 * 5184 * 256, 1 << 20,
        (brick, array((width + 2, mid, channels), bf16))
        + (array((2 * group, span), bf16),) * len(CHIPS),
        (
            pltpu.VMEM((width + 4, rows + 2 * halo, channels), f32),
            pltpu.VMEM((2,) + slab.shape, bf16),
            pltpu.VMEM((width + 4, mid, 9 * channels), bf16),
            pltpu.VMEM((MEMBERS, group, span), bf16),
        ),
    )(masked, cot, near, far, bricks[1], corner, live, weight_rows, pick)
    slices = [slices[0]] + [in_plane(part, d) for part, d in zip(slices[1:], CHIPS[1:])]

    grad_input = call(
        input_kernel, "input_gradient", 20, 2 * 512 * 5184 * 256, 4 << 20, brick,
        (
            pltpu.VMEM((width + 2, rows, 9 * channels), bf16),
            pltpu.VMEM((total, channels), bf16),
        ),
    )(gp, live, weight.T)
    grad_input, *slices = lax.optimization_barrier((grad_input, *slices))

    blocks = QUAD // 2
    chips = len(CHIPS)
    keep, fold = call(
        kernel_grad_kernel, "kernel_gradient", 28, 2 * 576 * 3 * 2048 * 256, 4 << 20,
        (array((planes, 8, total), f32), array((planes, 8, total), bf16)),
        (
            pltpu.VMEM((blocks, SIDES, 2 * group, span), bf16),
            pltpu.VMEM((9 * 2 * group, blocks * (width + 2) * SIDES * rows), bf16),
            pltpu.VMEM((2, planes, 8, total), f32),
            pltpu.VMEM((blocks, SIDES) + packed.shape, bf16),
            pltpu.VMEM((blocks, width, SIDES * rows, channels), bf16),
            pltpu.SemaphoreType.DMA((chips,)),
        ),
        [vmem] * chips + [pl.BlockSpec(memory_space=pl.ANY)] * chips,
    )(*slices, *bricks)
    own, *sends = call(
        fold_kernel, "fold", 8, 8 * total * 4, 8 * total * 40,
        (array((8, total), f32),) + (array((8, total), bf16),) * (planes - 1),
    )(keep, in_plane(fold, 2))
    got = [swap(sent, "depth", d, planes) for d, sent in enumerate(sends, 1)]
    voxels = count * SIDES * width * rows
    mine = call(
        functools.partial(sum_kernel, float(1.0 / voxels**0.5)),
        "plane_sum", 4, 8 * total * 4, 8 * total * 14, array((8, total), bf16),
    )(own, *got)
    grad_weight = call(
        join_kernel, "join", 4, 8 * total, 8 * total * 14, array((channels // count, total), f32)
    )(mine, in_plane(mine, 1))
    shape = features.shape
    return act.reshape(shape), grad_input.reshape(shape), grad_weight


def padded_2(cells, sides, width):
    for axis, dim in sides:
        count = lax.axis_size(axis)
        ends = count - 1
        head = lax.slice_in_dim(cells, 0, width, axis=dim)
        tail = lax.slice_in_dim(cells, cells.shape[dim] - width, cells.shape[dim], axis=dim)
        cells = jnp.concatenate(
            [
                lax.ppermute(tail, axis, [(i, (i + 1) % count) for i in range(ends)]),
                cells,
                lax.ppermute(head, axis, [((i + 1) % count, i) for i in range(ends)]),
            ],
            axis=dim,
        )
    return cells


def gather_taps(padded, width_x, width_y, depth_z, channels, flip):
    pieces = []
    for shift_x in range(3):
        for shift_y in range(3):
            for shift_z in range(3):
                start_x = 2 - shift_x if flip else shift_x
                start_y = 2 - shift_y if flip else shift_y
                start_z = 2 - shift_z if flip else shift_z
                piece = padded[
                    start_x : start_x + width_x,
                    start_y : start_y + width_y,
                    start_z : start_z + depth_z,
                    :,
                ]
                pieces.append(piece.reshape(-1, channels))
    return jnp.concatenate(pieces, axis=1)


def summed_local(features, weight, voxel_mask, cotangent):
    width_x, width_y, depth_z, channels = features.shape
    masked = features * voxel_mask.astype(jnp.bfloat16)[..., None]
    padded = padded_2(masked, (("wide", 0), ("narrow", 1)), 1)
    padded = jnp.pad(padded, ((0, 0), (0, 0), (1, 1), (0, 0)))
    columns = gather_taps(padded, width_x, width_y, depth_z, channels, False)
    pre = jnp.dot(columns, weight, preferred_element_type=jnp.float32)
    live = voxel_mask.reshape(-1, 1).astype(jnp.float32)
    sig = jax.nn.sigmoid(pre)
    activation = (
        (pre * sig * live).astype(jnp.bfloat16).reshape(width_x, width_y, depth_z, channels)
    )
    slope = sig * (1.0 + pre * (1.0 - sig))
    grad_pre = (cotangent.reshape(-1, channels).astype(jnp.float32) * live * slope).astype(
        jnp.bfloat16
    )
    taps = weight.reshape(27, channels, channels)
    grid = grad_pre.reshape(width_x, width_y, depth_z, channels)
    grad_pad = padded_2(grid, (("wide", 0), ("narrow", 1)), 1)
    grad_pad = jnp.pad(grad_pad, ((0, 0), (0, 0), (1, 1), (0, 0)))
    grad_columns = gather_taps(grad_pad, width_x, width_y, depth_z, channels, True)
    flipped = jnp.transpose(taps, (0, 2, 1)).reshape(27 * channels, channels)
    grad_field = jnp.dot(grad_columns, flipped, preferred_element_type=jnp.float32)
    grad_input = (
        (grad_field * live).astype(jnp.bfloat16).reshape(width_x, width_y, depth_z, channels)
    )
    scale = 1.0 / jnp.sqrt(
        jnp.float32(width_x * width_y * depth_z * lax.axis_size("wide") * lax.axis_size("narrow"))
    )
    whole = lax.dot_general(
        grad_pre, columns, (((0,), (0,)), ((), ())), preferred_element_type=jnp.float32
    )
    piece_flat = lax.psum_scatter(
        whole.reshape(-1), ("wide", "narrow"), scatter_dimension=0, tiled=True
    )
    gathered = lax.all_gather(piece_flat, "narrow", axis=0, tiled=True)
    summed = gathered.reshape(channels // lax.axis_size("wide"), 27 * channels)
    grad_weight = summed * scale
    return (activation, grad_input, grad_weight)


def sharded(body, mesh, wide):
    return jax.shard_map(
        body,
        mesh=mesh,
        in_specs=(
            P(wide, "narrow", None, None),
            P(),
            P(wide, "narrow", None),
            P(wide, "narrow", None, None),
        ),
        out_specs=(
            P(wide, "narrow", None, None),
            P(wide, "narrow", None, None),
            P(wide, None),
        ),
        check_vma=False,
    )


def solution(mesh):
    wide, narrow = mesh.shape["wide"], mesh.shape["narrow"]
    if wide != 4 * QUAD or narrow != SIDES:
        return sharded(summed_local, mesh, "wide")
    planes = Mesh(
        mesh.devices.reshape(wide // QUAD, QUAD, narrow), ("depth", "quad", "narrow")
    )
    return sharded(planes_local, planes, WIDE)
```

```python
import functools

import jax
import jax.numpy as jnp
from jax import lax
from jax.experimental import pallas as pl
from jax.experimental.pallas import tpu as pltpu
from jax.sharding import Mesh
from jax.sharding import PartitionSpec as P

WIDE = ("depth", "quad")
QUAD = 4
SIDES = 2
MEMBERS = QUAD * SIDES
CHIPS = (0, 1, 4, 5)
OFFSETS = (-1, 0, 1)
DEPTH = 8


def position():
    quad, side = lax.axis_index("quad"), lax.axis_index("narrow")
    return lax.axis_index("depth"), quad * SIDES + side, quad, side


def shift_z(field, step):
    if step == 0:
        return field
    depth = field.shape[1]
    moved = pltpu.roll(field, (-step) % depth, 1)
    z = lax.broadcasted_iota(jnp.int32, field.shape, 1) + step
    return jnp.where((z >= 0) & (z < depth), moved, 0.0)


def pick_kernel(planes, out_ref):
    index = lax.broadcasted_iota(jnp.int32, out_ref.shape, 0)
    column = lax.broadcasted_iota(jnp.int32, out_ref.shape, 1)
    per = out_ref.shape[1] // (planes * QUAD)
    share = per // SIDES
    quad, side = index // (SIDES * planes * 8), index // (planes * 8) % SIDES
    plane, row = index // 8 % planes, index % 8
    channel = per * (QUAD * plane + quad) + share * side + row
    out_ref[...] = jnp.where((row < share) & (channel == column), 1.0, 0.0).astype(jnp.bfloat16)


def dense(total):
    tiles = -(-total // 128)
    moved = tiles // 4
    return (tiles - moved) * 128, moved * 128


def fold_rows(block, total):
    kept, moved = dense(total)
    tail = block[:, kept : kept + moved]
    row = lax.broadcasted_iota(jnp.int32, tail.shape, 0)
    pieces = []
    for k in range(3):
        spare = jnp.where(row == 6, pltpu.roll(tail, 6 - k, 0), pltpu.roll(tail, 4 - k, 0))
        pieces.append(jnp.where(row < 6, block[:, k * moved : (k + 1) * moved], spare))
    return jnp.concatenate(pieces + [block[:, 3 * moved : kept]], axis=1)


def unfold_rows(block, total):
    kept, moved = dense(total)
    row = lax.broadcasted_iota(jnp.int32, (8, moved), 0)
    tail = jnp.zeros((8, moved), block.dtype)
    for k in range(3):
        piece = block[:, k * moved : (k + 1) * moved]
        tail = jnp.where(row == k, pltpu.roll(piece, 2 + k, 0), tail)
        tail = jnp.where(row == 3 + k, pltpu.roll(piece, 4 + k, 0), tail)
    return jnp.concatenate([block, tail], axis=1)[:, :total]


def prepare_kernel(features, cot, mask, first, masked_ref, cot_ref, live_ref, near_ref, far_ref):
    width, rows, channels = features.shape
    f32 = jnp.float32
    flat = mask[...].astype(f32).reshape(width * rows // DEPTH, DEPTH)
    live = jnp.broadcast_to(flat[:, :, None], flat.shape + (channels,)).reshape(features.shape)
    live_ref[...] = live[:, :, :128]
    masked_ref[...] = (features[...].astype(f32) * live).astype(jnp.bfloat16)
    cot_ref[...] = (cot[...].astype(f32) * live).astype(jnp.bfloat16)
    odd = lax.rem(position()[2], 2)
    for ref, upper in ((near_ref, 1 - odd), (far_ref, odd)):
        ref[0:2] = masked_ref[pl.ds(upper * (width - 2), 2)]
        ref[2:3] = cot_ref[pl.ds(upper * (width - 1), 1)]


def pack_kernel(masked, cot, packed_ref, across_ref):
    width, rows, channels = masked.shape
    half = width // 2
    packed_ref[:width] = masked[:, :, :128]
    packed_ref[width:] = jnp.concatenate([masked[:half, :, 128:], masked[half:, :, 128:]], axis=2)
    count = packed_ref.shape[0]
    across_ref[:count] = packed_ref[...]
    ahead = position()[3] == 0
    grown = cot[...].astype(jnp.float32)
    strip = jnp.where(ahead, grown[:, rows - DEPTH :], grown[:, :DEPTH])
    strip = strip.reshape(width * DEPTH, channels)
    rest = jnp.concatenate([strip[:, 128:], jnp.zeros_like(strip[:, 128:])], axis=1)
    across_ref[count] = strip[:, :128].astype(jnp.bfloat16)
    across_ref[count + 1] = rest.astype(jnp.bfloat16)


def corner_kernel(near, far, out_ref, edge):
    _, rows, channels = near.shape
    _, _, quad, side = position()
    odd = lax.rem(quad, 2)
    edge[odd] = far[...]
    edge[1 - odd] = near[...]
    halo = 2 * DEPTH
    ahead = side == 0
    held = edge[...].astype(jnp.float32)
    strip = jnp.where(ahead, held[:, :2, rows - halo :], held[:, :2, :halo])
    cots = jnp.where(ahead, held[:, 2, rows - DEPTH :], held[:, 2, :DEPTH])
    out_ref[: 4 * halo] = strip.reshape(4 * halo, channels).astype(jnp.bfloat16)
    out_ref[4 * halo :] = cots.reshape(2 * DEPTH, channels).astype(jnp.bfloat16)


def turn_kernel(weight, out_ref):
    step = 2 * weight.shape[0]
    total = weight.shape[1]
    for start in range(0, total, step):
        stop = min(start + step, total)
        out_ref[start:stop, :] = weight[:, start:stop].T


def forward_kernel(
    masked, cot, near, far, across, corner, live, weight, pick, *refs
):
    act_ref, gp_ref = refs[:2]
    slice_refs = refs[2 : 2 + len(CHIPS)]
    ext, edge, cols, slices = refs[2 + len(CHIPS) :]
    width, rows, channels = masked.shape
    f32 = jnp.float32
    plane, me, quad, side = position()
    use_low = side.astype(f32)
    use_high = (1 - side).astype(f32)
    place = plane * QUAD + quad
    use_left = (place > 0).astype(f32)
    use_right = (place < QUAD * lax.axis_size("depth") - 1).astype(f32)
    halo = 2 * DEPTH
    tall = rows + 2 * halo
    mid = rows + 2 * DEPTH
    span = width + 4
    odd = lax.rem(quad, 2)
    edge[odd] = far[...]
    edge[1 - odd] = near[...]
    left, right = edge[0].astype(f32) * use_left, edge[1].astype(f32) * use_right
    corners = corner[: 4 * halo].astype(f32).reshape(2, 2, halo, channels)
    lower, upper = corners[0] * use_left, corners[1] * use_right
    ends = corner[4 * halo :].astype(f32).reshape(2, 1, DEPTH, channels)
    ext[0:2, halo : halo + rows, :] = left[0:2]
    ext[2 : 2 + width, halo : halo + rows, :] = masked[...].astype(f32)
    ext[2 + width :, halo : halo + rows, :] = right[0:2]
    half = width // 2
    ahead = side == 0
    held = across[...].astype(f32)
    brick = jnp.where(ahead, held[: width + half, :halo], held[: width + half, rows - halo :])
    rest = jnp.concatenate([brick[width:, :, :64], brick[width:, :, 64:]], axis=0)
    beside = jnp.concatenate([brick[:width], rest], axis=2)
    for use, start in ((use_low, 0), (use_high, halo + rows)):
        at = slice(start, start + halo)
        ext[0:2, at, :] = lower * use
        ext[2 : 2 + width, at, :] = beside * use
        ext[2 + width :, at, :] = upper * use
    field = ext[...].reshape(span * tall // DEPTH, DEPTH, channels)
    for c in OFFSETS:
        moved = shift_z(field, c).reshape(span, tall, channels)
        for b in OFFSETS:
            at = ((b + 1) * 3 + c + 1) * channels
            start = DEPTH * (b + 1)
            cols[:, :, at : at + channels] = moved[:, start : start + mid].astype(jnp.bfloat16)
    nine = 9 * channels
    pre = jnp.zeros(((width + 2) * mid, channels), f32)
    for a in range(3):
        pre += jnp.dot(
            cols[a : a + width + 2].reshape((width + 2) * mid, nine),
            weight[a * nine : (a + 1) * nine, :],
            preferred_element_type=f32,
        )
    sig = jax.nn.sigmoid(pre)
    act = (pre * sig).reshape(width + 2, mid, channels)[1 : 1 + width, DEPTH : DEPTH + rows]
    act_ref[...] = (act * live[:, :, 0:1]).astype(jnp.bfloat16)
    slope = (sig * (1.0 + pre * (1.0 - sig))).reshape(width + 2, mid, channels)
    beyond = jnp.concatenate(
        [
            ends[0] * use_left,
            jnp.concatenate([held[width + half], held[width + half + 1, :, :64]], axis=1).reshape(
                width, DEPTH, channels
            ),
            ends[1] * use_right,
        ],
        axis=0,
    )
    centre = jnp.concatenate([left[2:3], cot[...].astype(f32), right[2:3]], axis=0)
    full = jnp.concatenate([beyond * use_low, centre, beyond * use_high], axis=1)
    grad = full * slope
    gp_ref[...] = grad.astype(jnp.bfloat16)
    inner = grad[:, DEPTH : DEPTH + rows].astype(jnp.bfloat16)
    turned = lax.dot_general(
        pick[...],
        inner.reshape((width + 2) * rows, channels),
        (((1,), (1,)), ((), ())),
        preferred_element_type=f32,
    )
    slices[...] = turned.reshape(slices.shape).astype(jnp.bfloat16)
    group = slices.shape[1]
    chip = me - lax.rem(quad, 2) * SIDES
    for distance, ref in zip(CHIPS, slice_refs):
        ref[:group] = slices[chip ^ distance]
        ref[group:] = slices[(chip ^ distance) + SIDES]


def input_kernel(gp, live, turned, out_ref, cols, weight):
    width, rows, channels = out_ref.shape
    f32 = jnp.float32
    tall = rows + 2 * DEPTH
    for tap in range(27):
        weight[tap * channels : (tap + 1) * channels, :] = turned[
            :, tap * channels : (tap + 1) * channels
        ]
    field = gp[...].astype(f32).reshape((width + 2) * tall // DEPTH, DEPTH, channels)
    for c in OFFSETS:
        moved = shift_z(field, -c).reshape(width + 2, tall, channels)
        for b in OFFSETS:
            at = ((b + 1) * 3 + c + 1) * channels
            start = DEPTH * (1 - b)
            cols[:, :, at : at + channels] = moved[:, start : start + rows].astype(jnp.bfloat16)
    nine = 9 * channels
    total = jnp.zeros((width * rows, channels), f32)
    for a in range(3):
        total += jnp.dot(
            cols[2 - a : 2 - a + width].reshape(width * rows, nine),
            weight[a * nine : (a + 1) * nine, :],
            preferred_element_type=f32,
        )
    out_ref[...] = (total.reshape(width, rows, channels) * live[:, :, 0:1]).astype(jnp.bfloat16)


def kernel_grad_kernel(*refs):
    chips = len(CHIPS)
    received, bricks = refs[:chips], refs[chips : 2 * chips]
    keep_ref, send_ref, slices, cols, part, stage, masked, sems = refs[2 * chips :]
    f32 = jnp.float32
    group, lanes = received[0].shape
    blocks, per, lane, channels = masked.shape
    half = lane // 2
    _, _, quad, side = position()
    copies = []
    for i, distance in enumerate(CHIPS):
        to = stage.at[distance // 4, side ^ (distance % 2)]
        packed = bricks[i].at[pl.ds(0, stage.shape[2])]
        copies.append(pltpu.make_async_copy(packed, to, sems.at[i]))
        copies[i].start()
        slices[distance // 4, side ^ (distance % 2)] = received[i][...]
    at = lax.broadcasted_iota(jnp.int32, (group, lane), 1)
    y, z = at // DEPTH, at % DEPTH
    tall = lane // DEPTH
    for block in range(blocks):
        first = slices[block, 0].astype(f32)
        second = slices[block, 1].astype(f32)
        for k in range(per + 2):
            one = first[:, k // 2 * lane : (k // 2 + 1) * lane]
            two = second[:, k // 2 * lane : (k // 2 + 1) * lane]
            if k % 2 == 0:
                base = jnp.where(at < half, one, pltpu.roll(two, half, 1))
            else:
                base = jnp.where(at < half, pltpu.roll(one, half, 1), two)
            pieces = []
            for b in OFFSETS:
                for c in OFFSETS:
                    step = (DEPTH * b + c) % lane
                    moved = base if step == 0 else pltpu.roll(base, step, 1)
                    keep = (y - b >= 0) & (y - b < tall) & (z - c >= 0) & (z - c < DEPTH)
                    pieces.append(jnp.where(keep, moved, 0.0))
            slab = block * (per + 2) + k
            cols[:, slab * lane : (slab + 1) * lane] = jnp.concatenate(pieces, axis=0).astype(
                jnp.bfloat16
            )
    for copy in copies:
        copy.wait()
    for block in range(blocks):
        for sided in range(SIDES):
            at_rows = pl.ds(sided * half, half)
            for x in range(per):
                shift = 64 * (x // (per // 2))
                rest = stage[block, sided, per + x % (per // 2)]
                masked[block, x, at_rows, :128] = stage[block, sided, x]
                masked[block, x, at_rows, 128:] = rest[:, shift : shift + 64]
    _, planes, eight, _ = part.shape
    for a in range(3):
        got = jnp.zeros((cols.shape[0], channels), f32)
        for block in range(blocks):
            start = (block * (per + 2) + 2 - a) * lane
            got += jnp.dot(
                cols[:, start : start + per * lane],
                masked[block].reshape(per * lane, channels),
                preferred_element_type=f32,
            )
        got = got.reshape(9, 2, planes, eight, channels)
        for core in range(2):
            for to in range(planes):
                part[core, to, :, a * 9 * channels : (a + 1) * 9 * channels] = jnp.concatenate(
                    [got[tap, core, to] for tap in range(9)], axis=1
                )
    core = lax.rem(quad, 2)
    total = 27 * channels
    part[:, :, :, total:] = jnp.zeros((2, planes, eight, part.shape[3] - total), f32)
    for to in range(planes):
        keep_ref[to] = fold_rows(part[core, to], total)
        send_ref[to] = fold_rows(part[1 - core, to], total).astype(jnp.bfloat16)


def fold_kernel(keep, other, own_ref, *send_refs):
    plane = position()[0]
    own_ref[...] = keep[plane] + other[plane].astype(jnp.float32)
    for distance, ref in enumerate(send_refs, 1):
        to = plane ^ distance
        ref[...] = (keep[to] + other[to].astype(jnp.float32)).astype(jnp.bfloat16)


def sum_kernel(scale, own, one, two, three, out_ref):
    f32 = jnp.float32
    total = own[...] + one[...].astype(f32) + two[...].astype(f32) + three[...].astype(f32)
    out_ref[...] = (total * scale).astype(out_ref.dtype)


def join_kernel(mine, other, out_ref):
    share = out_ref.shape[0] // SIDES
    ahead = position()[3] == 0
    total = out_ref.shape[1]
    here = unfold_rows(mine[...].astype(jnp.float32), total)
    there = unfold_rows(other[...].astype(jnp.float32), total)
    first = jnp.where(ahead, here, there)
    second = jnp.where(ahead, there, here)
    out_ref[0:share] = first[:share]
    out_ref[share:] = second[:share]


def call(body, name, mebibytes, flops, moved, out_shape, scratch=(), in_specs=None):
    spec = pl.BlockSpec(memory_space=pltpu.VMEM)

    def run(*operands):
        return pl.pallas_call(
            body,
            out_shape=out_shape,
            in_specs=in_specs or [spec] * len(operands),
            out_specs=jax.tree.map(lambda _: spec, out_shape),
            scratch_shapes=scratch,
            compiler_params=pltpu.CompilerParams(vmem_limit_bytes=mebibytes << 20),
            cost_estimate=pl.CostEstimate(flops=flops, bytes_accessed=moved, transcendentals=0),
            name=name,
        )(*operands)

    return run


def planes_local(features, weight, voxel_mask, cotangent):
    bf16 = jnp.bfloat16
    f32 = jnp.float32
    array = jax.ShapeDtypeStruct
    width, wide_y, depth, channels = features.shape
    rows = wide_y * depth
    planes = lax.axis_size("depth")
    count = planes * QUAD
    total = 27 * channels
    halo = 2 * DEPTH
    span = (width + 2) * rows
    group = planes * 8

    def swap(piece, axes, distance, size):
        return lax.ppermute(piece, axes, [(i, i ^ distance) for i in range(size)])

    def in_plane(piece, distance):
        return swap(piece, ("quad", "narrow"), distance, MEMBERS)

    brick = array((width, rows, channels), bf16)
    slab = array((3, rows, channels), bf16)
    pick = call(
        functools.partial(pick_kernel, planes), "pick", 4, 1 << 32, 1 << 16,
        array((MEMBERS * group, channels), bf16),
    )()
    vmem = pl.BlockSpec(memory_space=pltpu.VMEM)
    masked, cot, live, near, far = call(
        prepare_kernel, "prepare", 16, 1 << 20, 1 << 20,
        (brick, brick, array((width, rows, 128), f32), slab, slab),
        (),
        [vmem] * 3 + [pl.BlockSpec(memory_space=pl.ANY)],
    )(
        features.reshape(width, rows, channels),
        cotangent.reshape(width, rows, channels),
        voxel_mask,
        pick,
    )
    near = swap(near, WIDE, 1, count)
    ends = [min(max(((i + 1) ^ 1) - 1, 0), count - 1) for i in range(count)]
    far = lax.ppermute(far, WIDE, list(enumerate(ends)))
    weight_rows = call(
        turn_kernel, "turn", 8, 1 << 20, 4 << 20, array((total, channels), bf16)
    )(weight.T)
    slabs = width * channels // 128
    packed, across = call(
        pack_kernel, "pack", 4, 1 << 16, 1 << 19,
        (array((slabs, rows, 128), bf16), array((slabs + 2, rows, 128), bf16)),
    )(masked, cot)
    across = in_plane(across, CHIPS[1])
    bricks = [packed, across, in_plane(packed, CHIPS[2]), None]
    packed, near, far, weight_rows = lax.optimization_barrier((packed, near, far, weight_rows))
    corner = call(
        corner_kernel, "corner", 4, 1 << 16, 1 << 18,
        array((4 * halo + 2 * DEPTH, channels), bf16),
        (pltpu.VMEM((2,) + slab.shape, bf16),),
    )(near, far)
    corner = in_plane(corner, 1)
    bricks[3] = in_plane(packed, CHIPS[3])

    mid = rows + 2 * DEPTH
    act, gp, *slices = call(
        forward_kernel, "forward", 28, 800 * 5184 * 256, 1 << 20,
        (brick, array((width + 2, mid, channels), bf16))
        + (array((2 * group, span), bf16),) * len(CHIPS),
        (
            pltpu.VMEM((width + 4, rows + 2 * halo, channels), f32),
            pltpu.VMEM((2,) + slab.shape, bf16),
            pltpu.VMEM((width + 4, mid, 9 * channels), bf16),
            pltpu.VMEM((MEMBERS, group, span), bf16),
        ),
    )(masked, cot, near, far, bricks[1], corner, live, weight_rows, pick)
    slices = [slices[0]] + [in_plane(part, d) for part, d in zip(slices[1:], CHIPS[1:])]

    grad_input = call(
        input_kernel, "input_gradient", 20, 2 * 512 * 5184 * 256, 4 << 20, brick,
        (
            pltpu.VMEM((width + 2, rows, 9 * channels), bf16),
            pltpu.VMEM((total, channels), bf16),
        ),
    )(gp, live, weight.T)

    blocks = QUAD // 2
    chips = len(CHIPS)
    lanes = dense(total)[0]
    keep, fold = call(
        kernel_grad_kernel, "kernel_gradient", 28, 2 * 576 * 3 * 2048 * 256, 4 << 20,
        (array((planes, 8, lanes), f32), array((planes, 8, lanes), bf16)),
        (
            pltpu.VMEM((blocks, SIDES, 2 * group, span), bf16),
            pltpu.VMEM((9 * 2 * group, blocks * (width + 2) * SIDES * rows), bf16),
            pltpu.VMEM((2, planes, 8, sum(dense(total))), f32),
            pltpu.VMEM((blocks, SIDES) + packed.shape, bf16),
            pltpu.VMEM((blocks, width, SIDES * rows, channels), bf16),
            pltpu.SemaphoreType.DMA((chips,)),
        ),
        [vmem] * chips + [pl.BlockSpec(memory_space=pl.ANY)] * chips,
    )(*slices, *bricks)
    own, *sends = call(
        fold_kernel, "fold", 8, 8 * total * 4, 8 * total * 40,
        (array((8, lanes), f32),) + (array((8, lanes), bf16),) * (planes - 1),
    )(keep, in_plane(fold, 2))
    got = [swap(sent, "depth", d, planes) for d, sent in enumerate(sends, 1)]
    grad_input, *got = lax.optimization_barrier((grad_input, *got))
    voxels = count * SIDES * width * rows
    mine = call(
        functools.partial(sum_kernel, float(1.0 / voxels**0.5)),
        "plane_sum", 4, 8 * total * 4, 8 * total * 14, array((8, lanes), bf16),
    )(own, *got)
    grad_weight = call(
        join_kernel, "join", 4, 8 * total, 8 * total * 14, array((channels // count, total), f32)
    )(mine, in_plane(mine, 1))
    shape = features.shape
    return act.reshape(shape), grad_input.reshape(shape), grad_weight


def padded_2(cells, sides, width):
    for axis, dim in sides:
        count = lax.axis_size(axis)
        ends = count - 1
        head = lax.slice_in_dim(cells, 0, width, axis=dim)
        tail = lax.slice_in_dim(cells, cells.shape[dim] - width, cells.shape[dim], axis=dim)
        cells = jnp.concatenate(
            [
                lax.ppermute(tail, axis, [(i, (i + 1) % count) for i in range(ends)]),
                cells,
                lax.ppermute(head, axis, [((i + 1) % count, i) for i in range(ends)]),
            ],
            axis=dim,
        )
    return cells


def gather_taps(padded, width_x, width_y, depth_z, channels, flip):
    pieces = []
    for shift_x in range(3):
        for shift_y in range(3):
            for shift_z in range(3):
                start_x = 2 - shift_x if flip else shift_x
                start_y = 2 - shift_y if flip else shift_y
                start_z = 2 - shift_z if flip else shift_z
                piece = padded[
                    start_x : start_x + width_x,
                    start_y : start_y + width_y,
                    start_z : start_z + depth_z,
                    :,
                ]
                pieces.append(piece.reshape(-1, channels))
    return jnp.concatenate(pieces, axis=1)


def summed_local(features, weight, voxel_mask, cotangent):
    width_x, width_y, depth_z, channels = features.shape
    masked = features * voxel_mask.astype(jnp.bfloat16)[..., None]
    padded = padded_2(masked, (("wide", 0), ("narrow", 1)), 1)
    padded = jnp.pad(padded, ((0, 0), (0, 0), (1, 1), (0, 0)))
    columns = gather_taps(padded, width_x, width_y, depth_z, channels, False)
    pre = jnp.dot(columns, weight, preferred_element_type=jnp.float32)
    live = voxel_mask.reshape(-1, 1).astype(jnp.float32)
    sig = jax.nn.sigmoid(pre)
    activation = (
        (pre * sig * live).astype(jnp.bfloat16).reshape(width_x, width_y, depth_z, channels)
    )
    slope = sig * (1.0 + pre * (1.0 - sig))
    grad_pre = (cotangent.reshape(-1, channels).astype(jnp.float32) * live * slope).astype(
        jnp.bfloat16
    )
    taps = weight.reshape(27, channels, channels)
    grid = grad_pre.reshape(width_x, width_y, depth_z, channels)
    grad_pad = padded_2(grid, (("wide", 0), ("narrow", 1)), 1)
    grad_pad = jnp.pad(grad_pad, ((0, 0), (0, 0), (1, 1), (0, 0)))
    grad_columns = gather_taps(grad_pad, width_x, width_y, depth_z, channels, True)
    flipped = jnp.transpose(taps, (0, 2, 1)).reshape(27 * channels, channels)
    grad_field = jnp.dot(grad_columns, flipped, preferred_element_type=jnp.float32)
    grad_input = (
        (grad_field * live).astype(jnp.bfloat16).reshape(width_x, width_y, depth_z, channels)
    )
    scale = 1.0 / jnp.sqrt(
        jnp.float32(width_x * width_y * depth_z * lax.axis_size("wide") * lax.axis_size("narrow"))
    )
    whole = lax.dot_general(
        grad_pre, columns, (((0,), (0,)), ((), ())), preferred_element_type=jnp.float32
    )
    piece_flat = lax.psum_scatter(
        whole.reshape(-1), ("wide", "narrow"), scatter_dimension=0, tiled=True
    )
    gathered = lax.all_gather(piece_flat, "narrow", axis=0, tiled=True)
    summed = gathered.reshape(channels // lax.axis_size("wide"), 27 * channels)
    grad_weight = summed * scale
    return (activation, grad_input, grad_weight)


def sharded(body, mesh, wide):
    return jax.shard_map(
        body,
        mesh=mesh,
        in_specs=(
            P(wide, "narrow", None, None),
            P(),
            P(wide, "narrow", None),
            P(wide, "narrow", None, None),
        ),
        out_specs=(
            P(wide, "narrow", None, None),
            P(wide, "narrow", None, None),
            P(wide, None),
        ),
        check_vma=False,
    )


def solution(mesh):
    wide, narrow = mesh.shape["wide"], mesh.shape["narrow"]
    if wide != 4 * QUAD or narrow != SIDES:
        return sharded(summed_local, mesh, "wide")
    planes = Mesh(
        mesh.devices.reshape(wide // QUAD, QUAD, narrow), ("depth", "quad", "narrow")
    )
    return sharded(planes_local, planes, WIDE)
```

```python
import functools

import jax
import jax.numpy as jnp
from jax import lax
from jax.experimental import pallas as pl
from jax.experimental.pallas import tpu as pltpu
from jax.sharding import Mesh
from jax.sharding import PartitionSpec as P

WIDE = ("depth", "quad")
QUAD = 4
SIDES = 2
MEMBERS = QUAD * SIDES
CHIPS = (0, 1, 4, 5)
OFFSETS = (-1, 0, 1)
DEPTH = 8


def position():
    quad, side = lax.axis_index("quad"), lax.axis_index("narrow")
    return lax.axis_index("depth"), quad * SIDES + side, quad, side


def shift_z(field, step):
    if step == 0:
        return field
    depth = field.shape[1]
    moved = pltpu.roll(field, (-step) % depth, 1)
    z = lax.broadcasted_iota(jnp.int32, field.shape, 1) + step
    return jnp.where((z >= 0) & (z < depth), moved, 0.0)


def pick_kernel(planes, out_ref):
    index = lax.broadcasted_iota(jnp.int32, out_ref.shape, 0)
    column = lax.broadcasted_iota(jnp.int32, out_ref.shape, 1)
    per = out_ref.shape[1] // (planes * QUAD)
    share = per // SIDES
    quad, side = index // (SIDES * planes * 8), index // (planes * 8) % SIDES
    plane, row = index // 8 % planes, index % 8
    channel = per * (QUAD * plane + quad) + share * side + row
    out_ref[...] = jnp.where((row < share) & (channel == column), 1.0, 0.0).astype(jnp.bfloat16)


def dense(total):
    tiles = -(-total // 128)
    moved = tiles // 4
    return (tiles - moved) * 128, moved * 128


def fold_rows(block, total):
    kept, moved = dense(total)
    tail = block[:, kept : kept + moved]
    row = lax.broadcasted_iota(jnp.int32, tail.shape, 0)
    pieces = []
    for k in range(3):
        spare = jnp.where(row == 6, pltpu.roll(tail, 6 - k, 0), pltpu.roll(tail, 4 - k, 0))
        pieces.append(jnp.where(row < 6, block[:, k * moved : (k + 1) * moved], spare))
    return jnp.concatenate(pieces + [block[:, 3 * moved : kept]], axis=1)


def unfold_rows(block, total):
    kept, moved = dense(total)
    row = lax.broadcasted_iota(jnp.int32, (8, moved), 0)
    tail = jnp.zeros((8, moved), block.dtype)
    for k in range(3):
        piece = block[:, k * moved : (k + 1) * moved]
        tail = jnp.where(row == k, pltpu.roll(piece, 2 + k, 0), tail)
        tail = jnp.where(row == 3 + k, pltpu.roll(piece, 4 + k, 0), tail)
    return jnp.concatenate([block, tail], axis=1)[:, :total]


def prepare_kernel(features, cot, mask, first, masked_ref, cot_ref, live_ref, near_ref, far_ref):
    width, rows, channels = features.shape
    f32 = jnp.float32
    flat = mask[...].astype(f32).reshape(width * rows // DEPTH, DEPTH)
    live = jnp.broadcast_to(flat[:, :, None], flat.shape + (channels,)).reshape(features.shape)
    live_ref[...] = live[:, :, :128]
    masked_ref[...] = (features[...].astype(f32) * live).astype(jnp.bfloat16)
    cot_ref[...] = (cot[...].astype(f32) * live).astype(jnp.bfloat16)
    odd = lax.rem(position()[2], 2)
    for ref, upper in ((near_ref, 1 - odd), (far_ref, odd)):
        ref[0:2] = masked_ref[pl.ds(upper * (width - 2), 2)]
        ref[2:3] = cot_ref[pl.ds(upper * (width - 1), 1)]


def pack_kernel(masked, cot, packed_ref, across_ref):
    width, rows, channels = masked.shape
    half = width // 2
    packed_ref[:width] = masked[:, :, :128]
    packed_ref[width:] = jnp.concatenate([masked[:half, :, 128:], masked[half:, :, 128:]], axis=2)
    count = packed_ref.shape[0]
    across_ref[:count] = packed_ref[...]
    ahead = position()[3] == 0
    grown = cot[...].astype(jnp.float32)
    strip = jnp.where(ahead, grown[:, rows - DEPTH :], grown[:, :DEPTH])
    strip = strip.reshape(width * DEPTH, channels)
    rest = jnp.concatenate([strip[:, 128:], jnp.zeros_like(strip[:, 128:])], axis=1)
    across_ref[count] = strip[:, :128].astype(jnp.bfloat16)
    across_ref[count + 1] = rest.astype(jnp.bfloat16)


def corner_kernel(near, far, out_ref, edge):
    _, rows, channels = near.shape
    _, _, quad, side = position()
    odd = lax.rem(quad, 2)
    edge[odd] = far[...]
    edge[1 - odd] = near[...]
    halo = 2 * DEPTH
    ahead = side == 0
    held = edge[...].astype(jnp.float32)
    strip = jnp.where(ahead, held[:, :2, rows - halo :], held[:, :2, :halo])
    cots = jnp.where(ahead, held[:, 2, rows - DEPTH :], held[:, 2, :DEPTH])
    out_ref[: 4 * halo] = strip.reshape(4 * halo, channels).astype(jnp.bfloat16)
    out_ref[4 * halo :] = cots.reshape(2 * DEPTH, channels).astype(jnp.bfloat16)


def turn_kernel(weight, out_ref):
    step = 2 * weight.shape[0]
    total = weight.shape[1]
    for start in range(0, total, step):
        stop = min(start + step, total)
        out_ref[start:stop, :] = weight[:, start:stop].T


def forward_kernel(
    masked, cot, near, far, across, corner, live, weight, pick, *refs
):
    act_ref, gp_ref = refs[:2]
    slice_refs = refs[2 : 2 + len(CHIPS)]
    ext, edge, cols, slices = refs[2 + len(CHIPS) :]
    width, rows, channels = masked.shape
    f32 = jnp.float32
    plane, me, quad, side = position()
    use_low = side.astype(f32)
    use_high = (1 - side).astype(f32)
    place = plane * QUAD + quad
    use_left = (place > 0).astype(f32)
    use_right = (place < QUAD * lax.axis_size("depth") - 1).astype(f32)
    halo = 2 * DEPTH
    tall = rows + 2 * halo
    mid = rows + 2 * DEPTH
    span = width + 4
    odd = lax.rem(quad, 2)
    edge[odd] = far[...]
    edge[1 - odd] = near[...]
    left, right = edge[0].astype(f32) * use_left, edge[1].astype(f32) * use_right
    corners = corner[: 4 * halo].astype(f32).reshape(2, 2, halo, channels)
    lower, upper = corners[0] * use_left, corners[1] * use_right
    ends = corner[4 * halo :].astype(f32).reshape(2, 1, DEPTH, channels)
    ext[0:2, halo : halo + rows, :] = left[0:2]
    ext[2 : 2 + width, halo : halo + rows, :] = masked[...].astype(f32)
    ext[2 + width :, halo : halo + rows, :] = right[0:2]
    half = width // 2
    ahead = side == 0
    held = across[...].astype(f32)
    brick = jnp.where(ahead, held[: width + half, :halo], held[: width + half, rows - halo :])
    rest = jnp.concatenate([brick[width:, :, :64], brick[width:, :, 64:]], axis=0)
    beside = jnp.concatenate([brick[:width], rest], axis=2)
    for use, start in ((use_low, 0), (use_high, halo + rows)):
        at = slice(start, start + halo)
        ext[0:2, at, :] = lower * use
        ext[2 : 2 + width, at, :] = beside * use
        ext[2 + width :, at, :] = upper * use
    field = ext[...].reshape(span * tall // DEPTH, DEPTH, channels)
    for c in OFFSETS:
        moved = shift_z(field, c).reshape(span, tall, channels)
        for b in OFFSETS:
            at = ((b + 1) * 3 + c + 1) * channels
            start = DEPTH * (b + 1)
            cols[:, :, at : at + channels] = moved[:, start : start + mid].astype(jnp.bfloat16)
    nine = 9 * channels
    pre = jnp.zeros(((width + 2) * mid, channels), f32)
    for a in range(3):
        pre += jnp.dot(
            cols[a : a + width + 2].reshape((width + 2) * mid, nine),
            weight[a * nine : (a + 1) * nine, :],
            preferred_element_type=f32,
        )
    sig = jax.nn.sigmoid(pre)
    act = (pre * sig).reshape(width + 2, mid, channels)[1 : 1 + width, DEPTH : DEPTH + rows]
    act_ref[...] = (act * live[:, :, 0:1]).astype(jnp.bfloat16)
    slope = (sig * (1.0 + pre * (1.0 - sig))).reshape(width + 2, mid, channels)
    beyond = jnp.concatenate(
        [
            ends[0] * use_left,
            jnp.concatenate([held[width + half], held[width + half + 1, :, :64]], axis=1).reshape(
                width, DEPTH, channels
            ),
            ends[1] * use_right,
        ],
        axis=0,
    )
    centre = jnp.concatenate([left[2:3], cot[...].astype(f32), right[2:3]], axis=0)
    full = jnp.concatenate([beyond * use_low, centre, beyond * use_high], axis=1)
    grad = full * slope
    gp_ref[...] = grad.astype(jnp.bfloat16)
    inner = grad[:, DEPTH : DEPTH + rows].astype(jnp.bfloat16)
    turned = lax.dot_general(
        pick[...],
        inner.reshape((width + 2) * rows, channels),
        (((1,), (1,)), ((), ())),
        preferred_element_type=f32,
    )
    slices[...] = turned.reshape(slices.shape).astype(jnp.bfloat16)
    group = slices.shape[1]
    chip = me - lax.rem(quad, 2) * SIDES
    for distance, ref in zip(CHIPS, slice_refs):
        ref[:group] = slices[chip ^ distance]
        ref[group:] = slices[(chip ^ distance) + SIDES]


def input_kernel(gp, live, turned, out_ref, cols, weight):
    width, rows, channels = out_ref.shape
    f32 = jnp.float32
    tall = rows + 2 * DEPTH
    for tap in range(27):
        weight[tap * channels : (tap + 1) * channels, :] = turned[
            :, tap * channels : (tap + 1) * channels
        ]
    field = gp[...].astype(f32).reshape((width + 2) * tall // DEPTH, DEPTH, channels)
    for c in OFFSETS:
        moved = shift_z(field, -c).reshape(width + 2, tall, channels)
        for b in OFFSETS:
            at = ((b + 1) * 3 + c + 1) * channels
            start = DEPTH * (1 - b)
            cols[:, :, at : at + channels] = moved[:, start : start + rows].astype(jnp.bfloat16)
    nine = 9 * channels
    total = jnp.zeros((width * rows, channels), f32)
    for a in range(3):
        total += jnp.dot(
            cols[2 - a : 2 - a + width].reshape(width * rows, nine),
            weight[a * nine : (a + 1) * nine, :],
            preferred_element_type=f32,
        )
    out_ref[...] = (total.reshape(width, rows, channels) * live[:, :, 0:1]).astype(jnp.bfloat16)


def kernel_grad_kernel(*refs):
    chips = len(CHIPS)
    received, bricks = refs[:chips], refs[chips : 2 * chips]
    keep_ref, send_ref, slices, cols, part, stage, masked, sems = refs[2 * chips :]
    f32 = jnp.float32
    group, lanes = received[0].shape
    blocks, per, lane, channels = masked.shape
    half = lane // 2
    _, _, quad, side = position()
    copies = []
    for i, distance in enumerate(CHIPS):
        to = stage.at[distance // 4, side ^ (distance % 2)]
        packed = bricks[i].at[pl.ds(0, stage.shape[2])]
        copies.append(pltpu.make_async_copy(packed, to, sems.at[i]))
        copies[i].start()
        slices[distance // 4, side ^ (distance % 2)] = received[i][...]
    at = lax.broadcasted_iota(jnp.int32, (group, lane), 1)
    y, z = at // DEPTH, at % DEPTH
    tall = lane // DEPTH
    for block in range(blocks):
        first = slices[block, 0].astype(f32)
        second = slices[block, 1].astype(f32)
        for k in range(per + 2):
            one = first[:, k // 2 * lane : (k // 2 + 1) * lane]
            two = second[:, k // 2 * lane : (k // 2 + 1) * lane]
            if k % 2 == 0:
                base = jnp.where(at < half, one, pltpu.roll(two, half, 1))
            else:
                base = jnp.where(at < half, pltpu.roll(one, half, 1), two)
            pieces = []
            for b in OFFSETS:
                for c in OFFSETS:
                    step = (DEPTH * b + c) % lane
                    moved = base if step == 0 else pltpu.roll(base, step, 1)
                    keep = (y - b >= 0) & (y - b < tall) & (z - c >= 0) & (z - c < DEPTH)
                    pieces.append(jnp.where(keep, moved, 0.0))
            slab = block * (per + 2) + k
            cols[:, slab * lane : (slab + 1) * lane] = jnp.concatenate(pieces, axis=0).astype(
                jnp.bfloat16
            )
    for copy in copies:
        copy.wait()
    for block in range(blocks):
        for sided in range(SIDES):
            at_rows = pl.ds(sided * half, half)
            for x in range(per):
                shift = 64 * (x // (per // 2))
                rest = stage[block, sided, per + x % (per // 2)]
                masked[block, x, at_rows, :128] = stage[block, sided, x]
                masked[block, x, at_rows, 128:] = rest[:, shift : shift + 64]
    _, planes, eight, _ = part.shape
    for a in range(3):
        got = jnp.zeros((cols.shape[0], channels), f32)
        for block in range(blocks):
            start = (block * (per + 2) + 2 - a) * lane
            got += jnp.dot(
                cols[:, start : start + per * lane],
                masked[block].reshape(per * lane, channels),
                preferred_element_type=f32,
            )
        got = got.reshape(9, 2, planes, eight, channels)
        for core in range(2):
            for to in range(planes):
                part[core, to, :, a * 9 * channels : (a + 1) * 9 * channels] = jnp.concatenate(
                    [got[tap, core, to] for tap in range(9)], axis=1
                )
    core = lax.rem(quad, 2)
    total = 27 * channels
    part[:, :, :, total:] = jnp.zeros((2, planes, eight, part.shape[3] - total), f32)
    for to in range(planes):
        keep_ref[to] = fold_rows(part[core, to], total)
        send_ref[to] = fold_rows(part[1 - core, to], total).astype(jnp.bfloat16)


def fold_kernel(keep, other, own_ref, *send_refs):
    plane = position()[0]
    own_ref[...] = keep[plane] + other[plane].astype(jnp.float32)
    for distance, ref in enumerate(send_refs, 1):
        to = plane ^ distance
        ref[...] = (keep[to] + other[to].astype(jnp.float32)).astype(jnp.bfloat16)


def sum_kernel(scale, own, one, two, three, out_ref):
    f32 = jnp.float32
    total = own[...] + one[...].astype(f32) + two[...].astype(f32) + three[...].astype(f32)
    out_ref[...] = (total * scale).astype(out_ref.dtype)


def join_kernel(mine, other, out_ref):
    share = out_ref.shape[0] // SIDES
    ahead = position()[3] == 0
    total = out_ref.shape[1]
    here = unfold_rows(mine[...].astype(jnp.float32), total)
    there = unfold_rows(other[...].astype(jnp.float32), total)
    first = jnp.where(ahead, here, there)
    second = jnp.where(ahead, there, here)
    out_ref[0:share] = first[:share]
    out_ref[share:] = second[:share]


def call(body, name, mebibytes, flops, moved, out_shape, scratch=(), in_specs=None):
    spec = pl.BlockSpec(memory_space=pltpu.VMEM)

    def run(*operands):
        return pl.pallas_call(
            body,
            out_shape=out_shape,
            in_specs=in_specs or [spec] * len(operands),
            out_specs=jax.tree.map(lambda _: spec, out_shape),
            scratch_shapes=scratch,
            compiler_params=pltpu.CompilerParams(vmem_limit_bytes=mebibytes << 20),
            cost_estimate=pl.CostEstimate(flops=flops, bytes_accessed=moved, transcendentals=0),
            name=name,
        )(*operands)

    return run


def planes_local(features, weight, voxel_mask, cotangent):
    bf16 = jnp.bfloat16
    f32 = jnp.float32
    array = jax.ShapeDtypeStruct
    width, wide_y, depth, channels = features.shape
    rows = wide_y * depth
    planes = lax.axis_size("depth")
    count = planes * QUAD
    total = 27 * channels
    halo = 2 * DEPTH
    span = (width + 2) * rows
    group = planes * 8

    def swap(piece, axes, distance, size):
        return lax.ppermute(piece, axes, [(i, i ^ distance) for i in range(size)])

    def in_plane(piece, distance):
        return swap(piece, ("quad", "narrow"), distance, MEMBERS)

    brick = array((width, rows, channels), bf16)
    slab = array((3, rows, channels), bf16)
    pick = call(
        functools.partial(pick_kernel, planes), "pick", 4, 1 << 32, 1 << 16,
        array((MEMBERS * group, channels), bf16),
    )()
    vmem = pl.BlockSpec(memory_space=pltpu.VMEM)
    masked, cot, live, near, far = call(
        prepare_kernel, "prepare", 16, 1 << 20, 1 << 20,
        (brick, brick, array((width, rows, 128), f32), slab, slab),
        (),
        [vmem] * 3 + [pl.BlockSpec(memory_space=pl.ANY)],
    )(
        features.reshape(width, rows, channels),
        cotangent.reshape(width, rows, channels),
        voxel_mask,
        pick,
    )
    near = swap(near, WIDE, 1, count)
    ends = [min(max(((i + 1) ^ 1) - 1, 0), count - 1) for i in range(count)]
    far = lax.ppermute(far, WIDE, list(enumerate(ends)))
    weight_rows = call(
        turn_kernel, "turn", 8, 1 << 34, 4 << 20, array((total, channels), bf16)
    )(weight.T)
    slabs = width * channels // 128
    packed, across = call(
        pack_kernel, "pack", 4, 1 << 16, 1 << 19,
        (array((slabs, rows, 128), bf16), array((slabs + 2, rows, 128), bf16)),
    )(masked, cot)
    across = in_plane(across, CHIPS[1])
    bricks = [packed, across, in_plane(packed, CHIPS[2]), None]
    packed, near, far, weight_rows = lax.optimization_barrier((packed, near, far, weight_rows))
    corner = call(
        corner_kernel, "corner", 4, 1 << 16, 1 << 18,
        array((4 * halo + 2 * DEPTH, channels), bf16),
        (pltpu.VMEM((2,) + slab.shape, bf16),),
    )(near, far)
    corner, bricks[2] = lax.optimization_barrier((in_plane(corner, 1), bricks[2]))
    bricks[3] = in_plane(packed, CHIPS[3])

    mid = rows + 2 * DEPTH
    act, gp, *slices = call(
        forward_kernel, "forward", 28, 800 * 5184 * 256, 1 << 20,
        (brick, array((width + 2, mid, channels), bf16))
        + (array((2 * group, span), bf16),) * len(CHIPS),
        (
            pltpu.VMEM((width + 4, rows + 2 * halo, channels), f32),
            pltpu.VMEM((2,) + slab.shape, bf16),
            pltpu.VMEM((width + 4, mid, 9 * channels), bf16),
            pltpu.VMEM((MEMBERS, group, span), bf16),
        ),
    )(masked, cot, near, far, bricks[1], corner, live, weight_rows, pick)
    slices = [slices[0]] + [in_plane(part, d) for part, d in zip(slices[1:], CHIPS[1:])]

    grad_input = call(
        input_kernel, "input_gradient", 20, 2 * 512 * 5184 * 256, 4 << 20, brick,
        (
            pltpu.VMEM((width + 2, rows, 9 * channels), bf16),
            pltpu.VMEM((total, channels), bf16),
        ),
    )(gp, live, weight.T)

    blocks = QUAD // 2
    chips = len(CHIPS)
    lanes = dense(total)[0]
    keep, fold = call(
        kernel_grad_kernel, "kernel_gradient", 28, 2 * 576 * 3 * 2048 * 256, 4 << 20,
        (array((planes, 8, lanes), f32), array((planes, 8, lanes), bf16)),
        (
            pltpu.VMEM((blocks, SIDES, 2 * group, span), bf16),
            pltpu.VMEM((9 * 2 * group, blocks * (width + 2) * SIDES * rows), bf16),
            pltpu.VMEM((2, planes, 8, sum(dense(total))), f32),
            pltpu.VMEM((blocks, SIDES) + packed.shape, bf16),
            pltpu.VMEM((blocks, width, SIDES * rows, channels), bf16),
            pltpu.SemaphoreType.DMA((chips,)),
        ),
        [vmem] * chips + [pl.BlockSpec(memory_space=pl.ANY)] * chips,
    )(*slices, *bricks)
    own, *sends = call(
        fold_kernel, "fold", 8, 8 * total * 4, 8 * total * 40,
        (array((8, lanes), f32),) + (array((8, lanes), bf16),) * (planes - 1),
    )(keep, in_plane(fold, 2))
    got = [swap(sent, "depth", d, planes) for d, sent in enumerate(sends, 1)]
    grad_input, *got = lax.optimization_barrier((grad_input, *got))
    voxels = count * SIDES * width * rows
    mine = call(
        functools.partial(sum_kernel, float(1.0 / voxels**0.5)),
        "plane_sum", 4, 8 * total * 4, 8 * total * 14, array((8, lanes), bf16),
    )(own, *got)
    grad_weight = call(
        join_kernel, "join", 4, 8 * total, 8 * total * 14, array((channels // count, total), f32)
    )(mine, in_plane(mine, 1))
    shape = features.shape
    return act.reshape(shape), grad_input.reshape(shape), grad_weight


def padded_2(cells, sides, width):
    for axis, dim in sides:
        count = lax.axis_size(axis)
        ends = count - 1
        head = lax.slice_in_dim(cells, 0, width, axis=dim)
        tail = lax.slice_in_dim(cells, cells.shape[dim] - width, cells.shape[dim], axis=dim)
        cells = jnp.concatenate(
            [
                lax.ppermute(tail, axis, [(i, (i + 1) % count) for i in range(ends)]),
                cells,
                lax.ppermute(head, axis, [((i + 1) % count, i) for i in range(ends)]),
            ],
            axis=dim,
        )
    return cells


def gather_taps(padded, width_x, width_y, depth_z, channels, flip):
    pieces = []
    for shift_x in range(3):
        for shift_y in range(3):
            for shift_z in range(3):
                start_x = 2 - shift_x if flip else shift_x
                start_y = 2 - shift_y if flip else shift_y
                start_z = 2 - shift_z if flip else shift_z
                piece = padded[
                    start_x : start_x + width_x,
                    start_y : start_y + width_y,
                    start_z : start_z + depth_z,
                    :,
                ]
                pieces.append(piece.reshape(-1, channels))
    return jnp.concatenate(pieces, axis=1)


def summed_local(features, weight, voxel_mask, cotangent):
    width_x, width_y, depth_z, channels = features.shape
    masked = features * voxel_mask.astype(jnp.bfloat16)[..., None]
    padded = padded_2(masked, (("wide", 0), ("narrow", 1)), 1)
    padded = jnp.pad(padded, ((0, 0), (0, 0), (1, 1), (0, 0)))
    columns = gather_taps(padded, width_x, width_y, depth_z, channels, False)
    pre = jnp.dot(columns, weight, preferred_element_type=jnp.float32)
    live = voxel_mask.reshape(-1, 1).astype(jnp.float32)
    sig = jax.nn.sigmoid(pre)
    activation = (
        (pre * sig * live).astype(jnp.bfloat16).reshape(width_x, width_y, depth_z, channels)
    )
    slope = sig * (1.0 + pre * (1.0 - sig))
    grad_pre = (cotangent.reshape(-1, channels).astype(jnp.float32) * live * slope).astype(
        jnp.bfloat16
    )
    taps = weight.reshape(27, channels, channels)
    grid = grad_pre.reshape(width_x, width_y, depth_z, channels)
    grad_pad = padded_2(grid, (("wide", 0), ("narrow", 1)), 1)
    grad_pad = jnp.pad(grad_pad, ((0, 0), (0, 0), (1, 1), (0, 0)))
    grad_columns = gather_taps(grad_pad, width_x, width_y, depth_z, channels, True)
    flipped = jnp.transpose(taps, (0, 2, 1)).reshape(27 * channels, channels)
    grad_field = jnp.dot(grad_columns, flipped, preferred_element_type=jnp.float32)
    grad_input = (
        (grad_field * live).astype(jnp.bfloat16).reshape(width_x, width_y, depth_z, channels)
    )
    scale = 1.0 / jnp.sqrt(
        jnp.float32(width_x * width_y * depth_z * lax.axis_size("wide") * lax.axis_size("narrow"))
    )
    whole = lax.dot_general(
        grad_pre, columns, (((0,), (0,)), ((), ())), preferred_element_type=jnp.float32
    )
    piece_flat = lax.psum_scatter(
        whole.reshape(-1), ("wide", "narrow"), scatter_dimension=0, tiled=True
    )
    gathered = lax.all_gather(piece_flat, "narrow", axis=0, tiled=True)
    summed = gathered.reshape(channels // lax.axis_size("wide"), 27 * channels)
    grad_weight = summed * scale
    return (activation, grad_input, grad_weight)


def sharded(body, mesh, wide):
    return jax.shard_map(
        body,
        mesh=mesh,
        in_specs=(
            P(wide, "narrow", None, None),
            P(),
            P(wide, "narrow", None),
            P(wide, "narrow", None, None),
        ),
        out_specs=(
            P(wide, "narrow", None, None),
            P(wide, "narrow", None, None),
            P(wide, None),
        ),
        check_vma=False,
    )


def solution(mesh):
    wide, narrow = mesh.shape["wide"], mesh.shape["narrow"]
    if wide != 4 * QUAD or narrow != SIDES:
        return sharded(summed_local, mesh, "wide")
    planes = Mesh(
        mesh.devices.reshape(wide // QUAD, QUAD, narrow), ("depth", "quad", "narrow")
    )
    return sharded(planes_local, planes, WIDE)
```

```python
import functools

import jax
import jax.numpy as jnp
from jax import lax
from jax.experimental import pallas as pl
from jax.experimental.pallas import tpu as pltpu
from jax.sharding import Mesh
from jax.sharding import PartitionSpec as P

WIDE = ("depth", "quad")
QUAD = 4
SIDES = 2
MEMBERS = QUAD * SIDES
CHIPS = (0, 1, 4, 5)
OFFSETS = (-1, 0, 1)
DEPTH = 8


def position():
    quad, side = lax.axis_index("quad"), lax.axis_index("narrow")
    return lax.axis_index("depth"), quad * SIDES + side, quad, side


def shift_z(field, step):
    if step == 0:
        return field
    depth = field.shape[1]
    moved = pltpu.roll(field, (-step) % depth, 1)
    z = lax.broadcasted_iota(jnp.int32, field.shape, 1) + step
    return jnp.where((z >= 0) & (z < depth), moved, 0.0)


def pick_kernel(planes, out_ref):
    index = lax.broadcasted_iota(jnp.int32, out_ref.shape, 0)
    column = lax.broadcasted_iota(jnp.int32, out_ref.shape, 1)
    per = out_ref.shape[1] // (planes * QUAD)
    share = per // SIDES
    group = planes * share
    quad, side = index // (SIDES * group), index // group % SIDES
    plane, row = index // share % planes, index % share
    channel = per * (QUAD * plane + quad) + share * side + row
    out_ref[...] = jnp.where(channel == column, 1.0, 0.0).astype(jnp.bfloat16)


def dense(total):
    tiles = -(-total // 128)
    moved = tiles // 4
    return (tiles - moved) * 128, moved * 128


def fold_rows(block, total):
    kept, moved = dense(total)
    tail = block[:, kept : kept + moved]
    row = lax.broadcasted_iota(jnp.int32, tail.shape, 0)
    pieces = []
    for k in range(3):
        spare = jnp.where(row == 6, pltpu.roll(tail, 6 - k, 0), pltpu.roll(tail, 4 - k, 0))
        pieces.append(jnp.where(row < 6, block[:, k * moved : (k + 1) * moved], spare))
    return jnp.concatenate(pieces + [block[:, 3 * moved : kept]], axis=1)


def unfold_rows(block, total):
    kept, moved = dense(total)
    row = lax.broadcasted_iota(jnp.int32, (8, moved), 0)
    tail = jnp.zeros((8, moved), block.dtype)
    for k in range(3):
        piece = block[:, k * moved : (k + 1) * moved]
        tail = jnp.where(row == k, pltpu.roll(piece, 2 + k, 0), tail)
        tail = jnp.where(row == 3 + k, pltpu.roll(piece, 4 + k, 0), tail)
    return jnp.concatenate([block, tail], axis=1)[:, :total]


def prepare_kernel(features, cot, mask, first, masked_ref, cot_ref, live_ref, near_ref, far_ref):
    width, rows, channels = features.shape
    f32 = jnp.float32
    flat = mask[...].astype(f32).reshape(width * rows // DEPTH, DEPTH)
    live = jnp.broadcast_to(flat[:, :, None], flat.shape + (channels,)).reshape(features.shape)
    live_ref[...] = live[:, :, :128]
    masked_ref[...] = (features[...].astype(f32) * live).astype(jnp.bfloat16)
    cot_ref[...] = (cot[...].astype(f32) * live).astype(jnp.bfloat16)
    odd = lax.rem(position()[2], 2)
    for ref, upper in ((near_ref, 1 - odd), (far_ref, odd)):
        ref[0:2] = masked_ref[pl.ds(upper * (width - 2), 2)]
        ref[2:3] = cot_ref[pl.ds(upper * (width - 1), 1)]


def rows_of_128(masked, out_ref):
    width = masked.shape[0]
    half = width // 2
    rest = jnp.concatenate([masked[:half, :, 128:], masked[half:, :, 128:]], axis=2)
    out_ref[:width] = masked[:, :, :128]
    out_ref[width : width + half] = rest


def pack_kernel(masked, after, packed_ref):
    rows_of_128(masked, packed_ref)


def across_kernel(masked, cot, across_ref):
    width, rows, channels = masked.shape
    rows_of_128(masked, across_ref)
    count = across_ref.shape[0] - 2
    ahead = position()[3] == 0
    grown = cot[...].astype(jnp.float32)
    strip = jnp.where(ahead, grown[:, rows - DEPTH :], grown[:, :DEPTH])
    strip = strip.reshape(width * DEPTH, channels)
    rest = jnp.concatenate([strip[:, 128:], jnp.zeros_like(strip[:, 128:])], axis=1)
    across_ref[count] = strip[:, :128].astype(jnp.bfloat16)
    across_ref[count + 1] = rest.astype(jnp.bfloat16)


def corner_kernel(near, far, out_ref, edge):
    _, rows, channels = near.shape
    _, _, quad, side = position()
    odd = lax.rem(quad, 2)
    edge[odd] = far[...]
    edge[1 - odd] = near[...]
    halo = 2 * DEPTH
    ahead = side == 0
    held = edge[...].astype(jnp.float32)
    strip = jnp.where(ahead, held[:, :2, rows - halo :], held[:, :2, :halo])
    cots = jnp.where(ahead, held[:, 2, rows - DEPTH :], held[:, 2, :DEPTH])
    out_ref[: 4 * halo] = strip.reshape(4 * halo, channels).astype(jnp.bfloat16)
    out_ref[4 * halo :] = cots.reshape(2 * DEPTH, channels).astype(jnp.bfloat16)


def turn_kernel(weight, out_ref):
    step = 2 * weight.shape[0]
    total = weight.shape[1]
    for start in range(0, total, step):
        stop = min(start + step, total)
        out_ref[start:stop, :] = weight[:, start:stop].T


def forward_kernel(
    masked, cot, near, far, across, corner, live, weight, pick, *refs
):
    act_ref, gp_ref = refs[:2]
    slice_refs = refs[2 : 2 + len(CHIPS)]
    ext, edge, cols, slices = refs[2 + len(CHIPS) :]
    width, rows, channels = masked.shape
    f32 = jnp.float32
    plane, me, quad, side = position()
    use_low = side.astype(f32)
    use_high = (1 - side).astype(f32)
    place = plane * QUAD + quad
    use_left = (place > 0).astype(f32)
    use_right = (place < QUAD * lax.axis_size("depth") - 1).astype(f32)
    halo = 2 * DEPTH
    tall = rows + 2 * halo
    mid = rows + 2 * DEPTH
    span = width + 4
    odd = lax.rem(quad, 2)
    edge[odd] = far[...]
    edge[1 - odd] = near[...]
    left, right = edge[0].astype(f32) * use_left, edge[1].astype(f32) * use_right
    corners = corner[: 4 * halo].astype(f32).reshape(2, 2, halo, channels)
    lower, upper = corners[0] * use_left, corners[1] * use_right
    ends = corner[4 * halo :].astype(f32).reshape(2, 1, DEPTH, channels)
    ext[0:2, halo : halo + rows, :] = left[0:2]
    ext[2 : 2 + width, halo : halo + rows, :] = masked[...].astype(f32)
    ext[2 + width :, halo : halo + rows, :] = right[0:2]
    half = width // 2
    ahead = side == 0
    held = across[...].astype(f32)
    brick = jnp.where(ahead, held[: width + half, :halo], held[: width + half, rows - halo :])
    rest = jnp.concatenate([brick[width:, :, :64], brick[width:, :, 64:]], axis=0)
    beside = jnp.concatenate([brick[:width], rest], axis=2)
    for use, start in ((use_low, 0), (use_high, halo + rows)):
        at = slice(start, start + halo)
        ext[0:2, at, :] = lower * use
        ext[2 : 2 + width, at, :] = beside * use
        ext[2 + width :, at, :] = upper * use
    field = ext[...].reshape(span * tall // DEPTH, DEPTH, channels)
    for c in OFFSETS:
        moved = shift_z(field, c).reshape(span, tall, channels)
        for b in OFFSETS:
            at = ((b + 1) * 3 + c + 1) * channels
            start = DEPTH * (b + 1)
            cols[:, :, at : at + channels] = moved[:, start : start + mid].astype(jnp.bfloat16)
    nine = 9 * channels
    pre = jnp.zeros(((width + 2) * mid, channels), f32)
    for a in range(3):
        pre += jnp.dot(
            cols[a : a + width + 2].reshape((width + 2) * mid, nine),
            weight[a * nine : (a + 1) * nine, :],
            preferred_element_type=f32,
        )
    sig = jax.nn.sigmoid(pre)
    act = (pre * sig).reshape(width + 2, mid, channels)[1 : 1 + width, DEPTH : DEPTH + rows]
    act_ref[...] = (act * live[:, :, 0:1]).astype(jnp.bfloat16)
    slope = (sig * (1.0 + pre * (1.0 - sig))).reshape(width + 2, mid, channels)
    beyond = jnp.concatenate(
        [
            ends[0] * use_left,
            jnp.concatenate([held[width + half], held[width + half + 1, :, :64]], axis=1).reshape(
                width, DEPTH, channels
            ),
            ends[1] * use_right,
        ],
        axis=0,
    )
    centre = jnp.concatenate([left[2:3], cot[...].astype(f32), right[2:3]], axis=0)
    full = jnp.concatenate([beyond * use_low, centre, beyond * use_high], axis=1)
    grad = full * slope
    gp_ref[...] = grad.astype(jnp.bfloat16)
    inner = grad[:, DEPTH : DEPTH + rows].astype(jnp.bfloat16)
    turned = lax.dot_general(
        pick[...],
        inner.reshape((width + 2) * rows, channels),
        (((1,), (1,)), ((), ())),
        preferred_element_type=f32,
    )
    slices[...] = turned.reshape(slices.shape)
    chip = me - lax.rem(quad, 2) * SIDES
    for distance, ref in zip(CHIPS, slice_refs):
        both = [slices[chip ^ distance], slices[(chip ^ distance) + SIDES]]
        ref[...] = jnp.concatenate(both, axis=0).astype(jnp.bfloat16)


def input_kernel(gp, live, turned, out_ref, cols, weight):
    width, rows, channels = out_ref.shape
    f32 = jnp.float32
    tall = rows + 2 * DEPTH
    for tap in range(27):
        weight[tap * channels : (tap + 1) * channels, :] = turned[
            :, tap * channels : (tap + 1) * channels
        ]
    field = gp[...].astype(f32).reshape((width + 2) * tall // DEPTH, DEPTH, channels)
    for c in OFFSETS:
        moved = shift_z(field, -c).reshape(width + 2, tall, channels)
        for b in OFFSETS:
            at = ((b + 1) * 3 + c + 1) * channels
            start = DEPTH * (1 - b)
            cols[:, :, at : at + channels] = moved[:, start : start + rows].astype(jnp.bfloat16)
    nine = 9 * channels
    total = jnp.zeros((width * rows, channels), f32)
    for a in range(3):
        total += jnp.dot(
            cols[2 - a : 2 - a + width].reshape(width * rows, nine),
            weight[a * nine : (a + 1) * nine, :],
            preferred_element_type=f32,
        )
    out_ref[...] = (total.reshape(width, rows, channels) * live[:, :, 0:1]).astype(jnp.bfloat16)


def kernel_grad_kernel(*refs):
    chips = len(CHIPS)
    received, bricks = refs[:chips], refs[chips : 2 * chips]
    keep_ref, send_ref, slices, cols, part, stage, masked, sems = refs[2 * chips :]
    f32 = jnp.float32
    group, lanes = received[0].shape
    blocks, per, lane, channels = masked.shape
    half = lane // 2
    _, _, quad, side = position()
    copies = []
    for i, distance in enumerate(CHIPS):
        to = stage.at[distance // 4, side ^ (distance % 2)]
        packed = bricks[i].at[pl.ds(0, stage.shape[2])]
        copies.append(pltpu.make_async_copy(packed, to, sems.at[i]))
        copies[i].start()
        slices[distance // 4, side ^ (distance % 2)] = received[i][...]
    at = lax.broadcasted_iota(jnp.int32, (group, lane), 1)
    y, z = at // DEPTH, at % DEPTH
    tall = lane // DEPTH
    for block in range(blocks):
        first = slices[block, 0].astype(f32)
        second = slices[block, 1].astype(f32)
        for k in range(per + 2):
            one = first[:, k // 2 * lane : (k // 2 + 1) * lane]
            two = second[:, k // 2 * lane : (k // 2 + 1) * lane]
            if k % 2 == 0:
                base = jnp.where(at < half, one, pltpu.roll(two, half, 1))
            else:
                base = jnp.where(at < half, pltpu.roll(one, half, 1), two)
            pieces = []
            for b in OFFSETS:
                for c in OFFSETS:
                    step = (DEPTH * b + c) % lane
                    moved = base if step == 0 else pltpu.roll(base, step, 1)
                    keep = (y - b >= 0) & (y - b < tall) & (z - c >= 0) & (z - c < DEPTH)
                    pieces.append(jnp.where(keep, moved, 0.0))
            slab = block * (per + 2) + k
            cols[:, slab * lane : (slab + 1) * lane] = jnp.concatenate(pieces, axis=0).astype(
                jnp.bfloat16
            )
    for copy in copies:
        copy.wait()
    for block in range(blocks):
        for sided in range(SIDES):
            at_rows = pl.ds(sided * half, half)
            for x in range(per):
                shift = 64 * (x // (per // 2))
                rest = stage[block, sided, per + x % (per // 2)]
                masked[block, x, at_rows, :128] = stage[block, sided, x]
                masked[block, x, at_rows, 128:] = rest[:, shift : shift + 64]
    for a in range(3):
        got = jnp.zeros((cols.shape[0], channels), f32)
        for block in range(blocks):
            start = (block * (per + 2) + 2 - a) * lane
            got += jnp.dot(
                cols[:, start : start + per * lane],
                masked[block].reshape(per * lane, channels),
                preferred_element_type=f32,
            )
        got = got.reshape(9, group, channels)
        part[:, a * 9 * channels : (a + 1) * 9 * channels] = jnp.concatenate(
            [got[tap] for tap in range(9)], axis=1
        )
    core = lax.rem(quad, 2)
    half = group // 2
    keep_ref[...] = part[pl.ds(pl.multiple_of(core * half, 8), half)]
    send_ref[...] = part[pl.ds(pl.multiple_of((1 - core) * half, 8), half)].astype(jnp.bfloat16)


def fold_kernel(keep, other, own_ref, *refs):
    *send_refs, both, rows = refs
    planes, eight, _ = rows.shape
    count, total = keep.shape
    share = count // planes
    both[:count, :total] = keep[...] + other[...].astype(jnp.float32)
    both[:, total:] = jnp.zeros((both.shape[0], both.shape[1] - total), jnp.float32)
    for to in range(planes):
        rows[to] = fold_rows(both[share * to : share * to + eight, :], total)
    plane = position()[0]
    own_ref[...] = rows[plane]
    for distance, ref in enumerate(send_refs, 1):
        ref[...] = rows[plane ^ distance].astype(jnp.bfloat16)


def sum_kernel(scale, own, one, two, three, out_ref):
    f32 = jnp.float32
    total = own[...] + one[...].astype(f32) + two[...].astype(f32) + three[...].astype(f32)
    out_ref[...] = (total * scale).astype(out_ref.dtype)


def join_kernel(mine, other, out_ref):
    share = out_ref.shape[0] // SIDES
    ahead = position()[3] == 0
    total = out_ref.shape[1]
    here = unfold_rows(mine[...].astype(jnp.float32), total)
    there = unfold_rows(other[...].astype(jnp.float32), total)
    first = jnp.where(ahead, here, there)
    second = jnp.where(ahead, there, here)
    out_ref[0:share] = first[:share]
    out_ref[share:] = second[:share]


def call(body, name, mebibytes, flops, moved, out_shape, scratch=(), in_specs=None):
    spec = pl.BlockSpec(memory_space=pltpu.VMEM)

    def run(*operands):
        return pl.pallas_call(
            body,
            out_shape=out_shape,
            in_specs=in_specs or [spec] * len(operands),
            out_specs=jax.tree.map(lambda _: spec, out_shape),
            scratch_shapes=scratch,
            compiler_params=pltpu.CompilerParams(vmem_limit_bytes=mebibytes << 20),
            cost_estimate=pl.CostEstimate(flops=flops, bytes_accessed=moved, transcendentals=0),
            name=name,
        )(*operands)

    return run


def planes_local(features, weight, voxel_mask, cotangent):
    bf16 = jnp.bfloat16
    f32 = jnp.float32
    array = jax.ShapeDtypeStruct
    width, wide_y, depth, channels = features.shape
    rows = wide_y * depth
    planes = lax.axis_size("depth")
    count = planes * QUAD
    total = 27 * channels
    halo = 2 * DEPTH
    span = (width + 2) * rows
    share = channels // count // SIDES
    group = planes * share

    def swap(piece, axes, distance, size):
        return lax.ppermute(piece, axes, [(i, i ^ distance) for i in range(size)])

    def in_plane(piece, distance):
        return swap(piece, ("quad", "narrow"), distance, MEMBERS)

    brick = array((width, rows, channels), bf16)
    slab = array((3, rows, channels), bf16)
    pick = call(
        functools.partial(pick_kernel, planes), "pick", 4, 1 << 32, 1 << 16,
        array((MEMBERS * group, channels), bf16),
    )()
    vmem = pl.BlockSpec(memory_space=pltpu.VMEM)
    masked, cot, live, near, far = call(
        prepare_kernel, "prepare", 16, 1 << 20, 1 << 20,
        (brick, brick, array((width, rows, 128), f32), slab, slab),
        (),
        [vmem] * 3 + [pl.BlockSpec(memory_space=pl.ANY)],
    )(
        features.reshape(width, rows, channels),
        cotangent.reshape(width, rows, channels),
        voxel_mask,
        pick,
    )
    near = swap(near, WIDE, 1, count)
    ends = [min(max(((i + 1) ^ 1) - 1, 0), count - 1) for i in range(count)]
    far = lax.ppermute(far, WIDE, list(enumerate(ends)))
    weight_rows = call(
        turn_kernel, "turn", 8, 1 << 34, 4 << 20, array((total, channels), bf16)
    )(weight.T)
    slabs = width * channels // 128
    across = call(
        across_kernel, "across", 4, 1 << 16, 1 << 19, array((slabs + 2, rows, 128), bf16)
    )(masked, cot)
    across = in_plane(across, CHIPS[1])
    near, far, weight_rows = lax.optimization_barrier((near, far, weight_rows))
    corner = call(
        corner_kernel, "corner", 4, 1 << 16, 1 << 18,
        array((4 * halo + 2 * DEPTH, channels), bf16),
        (pltpu.VMEM((2,) + slab.shape, bf16),),
    )(near, far)
    packed = call(
        pack_kernel, "pack", 4, 1 << 16, 1 << 19, array((slabs, rows, 128), bf16), (),
        [vmem, pl.BlockSpec(memory_space=pl.ANY)],
    )(masked, corner)
    corner = in_plane(corner, 1)
    bricks = [packed, across] + [in_plane(packed, distance) for distance in CHIPS[2:]]

    mid = rows + 2 * DEPTH
    act, gp, *slices = call(
        forward_kernel, "forward", 28, 1 << 32, 1 << 20,
        (brick, array((width + 2, mid, channels), bf16))
        + (array((2 * group, span), bf16),) * len(CHIPS),
        (
            pltpu.VMEM((width + 4, rows + 2 * halo, channels), f32),
            pltpu.VMEM((2,) + slab.shape, bf16),
            pltpu.VMEM((width + 4, mid, 9 * channels), bf16),
            pltpu.VMEM((MEMBERS, group, span), f32),
        ),
    )(masked, cot, near, far, across, corner, live, weight_rows, pick)
    slices = [slices[0]] + [in_plane(part, d) for part, d in zip(slices[1:], CHIPS[1:])]

    grad_input = call(
        input_kernel, "input_gradient", 20, 2 * 512 * 5184 * 256, 4 << 20, brick,
        (
            pltpu.VMEM((width + 2, rows, 9 * channels), bf16),
            pltpu.VMEM((total, channels), bf16),
        ),
    )(gp, live, weight.T)

    blocks = QUAD // 2
    chips = len(CHIPS)
    lanes = dense(total)[0]
    keep, fold = call(
        kernel_grad_kernel, "kernel_gradient", 28, 2 * 432 * 3 * 2048 * 256, 4 << 20,
        (array((group, total), f32), array((group, total), bf16)),
        (
            pltpu.VMEM((blocks, SIDES, 2 * group, span), bf16),
            pltpu.VMEM((9 * 2 * group, blocks * (width + 2) * SIDES * rows), bf16),
            pltpu.VMEM((2 * group, total), f32),
            pltpu.VMEM((blocks, SIDES) + packed.shape, bf16),
            pltpu.VMEM((blocks, width, SIDES * rows, channels), bf16),
            pltpu.SemaphoreType.DMA((chips,)),
        ),
        [vmem] * chips + [pl.BlockSpec(memory_space=pl.ANY)] * chips,
    )(*slices, *bricks)
    own, *sends = call(
        fold_kernel, "fold", 8, 8 * total * 4, 8 * total * 40,
        (array((8, lanes), f32),) + (array((8, lanes), bf16),) * (planes - 1),
        (
            pltpu.VMEM((group + 8, sum(dense(total))), f32),
            pltpu.VMEM((planes, 8, lanes), f32),
        ),
    )(keep, in_plane(fold, 2))
    got = [swap(sent, "depth", d, planes) for d, sent in enumerate(sends, 1)]
    grad_input, *got = lax.optimization_barrier((grad_input, *got))
    voxels = count * SIDES * width * rows
    mine = call(
        functools.partial(sum_kernel, float(1.0 / voxels**0.5)),
        "plane_sum", 4, 8 * total * 4, 8 * total * 14, array((8, lanes), bf16),
    )(own, *got)
    grad_weight = call(
        join_kernel, "join", 4, 8 * total, 8 * total * 14, array((channels // count, total), f32)
    )(mine, in_plane(mine, 1))
    shape = features.shape
    return act.reshape(shape), grad_input.reshape(shape), grad_weight


def padded_2(cells, sides, width):
    for axis, dim in sides:
        count = lax.axis_size(axis)
        ends = count - 1
        head = lax.slice_in_dim(cells, 0, width, axis=dim)
        tail = lax.slice_in_dim(cells, cells.shape[dim] - width, cells.shape[dim], axis=dim)
        cells = jnp.concatenate(
            [
                lax.ppermute(tail, axis, [(i, (i + 1) % count) for i in range(ends)]),
                cells,
                lax.ppermute(head, axis, [((i + 1) % count, i) for i in range(ends)]),
            ],
            axis=dim,
        )
    return cells


def gather_taps(padded, width_x, width_y, depth_z, channels, flip):
    pieces = []
    for shift_x in range(3):
        for shift_y in range(3):
            for shift_z in range(3):
                start_x = 2 - shift_x if flip else shift_x
                start_y = 2 - shift_y if flip else shift_y
                start_z = 2 - shift_z if flip else shift_z
                piece = padded[
                    start_x : start_x + width_x,
                    start_y : start_y + width_y,
                    start_z : start_z + depth_z,
                    :,
                ]
                pieces.append(piece.reshape(-1, channels))
    return jnp.concatenate(pieces, axis=1)


def summed_local(features, weight, voxel_mask, cotangent):
    width_x, width_y, depth_z, channels = features.shape
    masked = features * voxel_mask.astype(jnp.bfloat16)[..., None]
    padded = padded_2(masked, (("wide", 0), ("narrow", 1)), 1)
    padded = jnp.pad(padded, ((0, 0), (0, 0), (1, 1), (0, 0)))
    columns = gather_taps(padded, width_x, width_y, depth_z, channels, False)
    pre = jnp.dot(columns, weight, preferred_element_type=jnp.float32)
    live = voxel_mask.reshape(-1, 1).astype(jnp.float32)
    sig = jax.nn.sigmoid(pre)
    activation = (
        (pre * sig * live).astype(jnp.bfloat16).reshape(width_x, width_y, depth_z, channels)
    )
    slope = sig * (1.0 + pre * (1.0 - sig))
    grad_pre = (cotangent.reshape(-1, channels).astype(jnp.float32) * live * slope).astype(
        jnp.bfloat16
    )
    taps = weight.reshape(27, channels, channels)
    grid = grad_pre.reshape(width_x, width_y, depth_z, channels)
    grad_pad = padded_2(grid, (("wide", 0), ("narrow", 1)), 1)
    grad_pad = jnp.pad(grad_pad, ((0, 0), (0, 0), (1, 1), (0, 0)))
    grad_columns = gather_taps(grad_pad, width_x, width_y, depth_z, channels, True)
    flipped = jnp.transpose(taps, (0, 2, 1)).reshape(27 * channels, channels)
    grad_field = jnp.dot(grad_columns, flipped, preferred_element_type=jnp.float32)
    grad_input = (
        (grad_field * live).astype(jnp.bfloat16).reshape(width_x, width_y, depth_z, channels)
    )
    scale = 1.0 / jnp.sqrt(
        jnp.float32(width_x * width_y * depth_z * lax.axis_size("wide") * lax.axis_size("narrow"))
    )
    whole = lax.dot_general(
        grad_pre, columns, (((0,), (0,)), ((), ())), preferred_element_type=jnp.float32
    )
    piece_flat = lax.psum_scatter(
        whole.reshape(-1), ("wide", "narrow"), scatter_dimension=0, tiled=True
    )
    gathered = lax.all_gather(piece_flat, "narrow", axis=0, tiled=True)
    summed = gathered.reshape(channels // lax.axis_size("wide"), 27 * channels)
    grad_weight = summed * scale
    return (activation, grad_input, grad_weight)


def sharded(body, mesh, wide):
    return jax.shard_map(
        body,
        mesh=mesh,
        in_specs=(
            P(wide, "narrow", None, None),
            P(),
            P(wide, "narrow", None),
            P(wide, "narrow", None, None),
        ),
        out_specs=(
            P(wide, "narrow", None, None),
            P(wide, "narrow", None, None),
            P(wide, None),
        ),
        check_vma=False,
    )


def solution(mesh):
    wide, narrow = mesh.shape["wide"], mesh.shape["narrow"]
    if wide != 4 * QUAD or narrow != SIDES:
        return sharded(summed_local, mesh, "wide")
    planes = Mesh(
        mesh.devices.reshape(wide // QUAD, QUAD, narrow), ("depth", "quad", "narrow")
    )
    return sharded(planes_local, planes, WIDE)
```

```python
import functools

import jax
import jax.numpy as jnp
from jax import lax
from jax.experimental import pallas as pl
from jax.experimental.pallas import tpu as pltpu
from jax.sharding import Mesh
from jax.sharding import PartitionSpec as P

WIDE = ("depth", "quad")
QUAD = 4
SIDES = 2
MEMBERS = QUAD * SIDES
CHIPS = (0, 1, 4, 5)
OFFSETS = (-1, 0, 1)
DEPTH = 8


def position():
    quad, side = lax.axis_index("quad"), lax.axis_index("narrow")
    return lax.axis_index("depth"), quad * SIDES + side, quad, side


def shift_z(field, step):
    if step == 0:
        return field
    depth = field.shape[1]
    moved = pltpu.roll(field, (-step) % depth, 1)
    z = lax.broadcasted_iota(jnp.int32, field.shape, 1) + step
    return jnp.where((z >= 0) & (z < depth), moved, 0.0)


def pick_kernel(planes, out_ref):
    index = lax.broadcasted_iota(jnp.int32, out_ref.shape, 0)
    column = lax.broadcasted_iota(jnp.int32, out_ref.shape, 1)
    per = out_ref.shape[1] // (planes * QUAD)
    share = per // SIDES
    group = planes * share
    quad, side = index // (SIDES * group), index // group % SIDES
    plane, row = index // share % planes, index % share
    channel = per * (QUAD * plane + quad) + share * side + row
    out_ref[...] = jnp.where(channel == column, 1.0, 0.0).astype(jnp.bfloat16)


def dense(total):
    tiles = -(-total // 128)
    moved = tiles // 4
    return (tiles - moved) * 128, moved * 128


def fold_rows(block, total):
    kept, moved = dense(total)
    tail = block[:, kept : kept + moved]
    row = lax.broadcasted_iota(jnp.int32, tail.shape, 0)
    pieces = []
    for k in range(3):
        spare = jnp.where(row == 6, pltpu.roll(tail, 6 - k, 0), pltpu.roll(tail, 4 - k, 0))
        pieces.append(jnp.where(row < 6, block[:, k * moved : (k + 1) * moved], spare))
    return jnp.concatenate(pieces + [block[:, 3 * moved : kept]], axis=1)


def unfold_rows(block, total):
    kept, moved = dense(total)
    row = lax.broadcasted_iota(jnp.int32, (8, moved), 0)
    tail = jnp.zeros((8, moved), block.dtype)
    for k in range(3):
        piece = block[:, k * moved : (k + 1) * moved]
        tail = jnp.where(row == k, pltpu.roll(piece, 2 + k, 0), tail)
        tail = jnp.where(row == 3 + k, pltpu.roll(piece, 4 + k, 0), tail)
    return jnp.concatenate([block, tail], axis=1)[:, :total]


def prepare_kernel(features, cot, mask, first, masked_ref, cot_ref, live_ref, near_ref, far_ref):
    width, rows, channels = features.shape
    f32 = jnp.float32
    flat = mask[...].astype(f32).reshape(width * rows // DEPTH, DEPTH)
    live = jnp.broadcast_to(flat[:, :, None], flat.shape + (channels,)).reshape(features.shape)
    live_ref[...] = live[:, :, :128]
    masked_ref[...] = (features[...].astype(f32) * live).astype(jnp.bfloat16)
    cot_ref[...] = (cot[...].astype(f32) * live).astype(jnp.bfloat16)
    odd = lax.rem(position()[2], 2)
    for ref, upper in ((near_ref, 1 - odd), (far_ref, odd)):
        ref[0:2] = masked_ref[pl.ds(upper * (width - 2), 2)]
        ref[2:3] = cot_ref[pl.ds(upper * (width - 1), 1)]


def rows_of_128(masked, out_ref):
    width = masked.shape[0]
    half = width // 2
    rest = jnp.concatenate([masked[:half, :, 128:], masked[half:, :, 128:]], axis=2)
    out_ref[:width] = masked[:, :, :128]
    out_ref[width : width + half] = rest


def pack_kernel(masked, packed_ref):
    rows_of_128(masked, packed_ref)


def across_kernel(masked, cot, across_ref):
    width, rows, channels = masked.shape
    rows_of_128(masked, across_ref)
    count = across_ref.shape[0] - 2
    ahead = position()[3] == 0
    grown = cot[...].astype(jnp.float32)
    strip = jnp.where(ahead, grown[:, rows - DEPTH :], grown[:, :DEPTH])
    strip = strip.reshape(width * DEPTH, channels)
    rest = jnp.concatenate([strip[:, 128:], jnp.zeros_like(strip[:, 128:])], axis=1)
    across_ref[count] = strip[:, :128].astype(jnp.bfloat16)
    across_ref[count + 1] = rest.astype(jnp.bfloat16)


def corner_kernel(near, far, out_ref, edge):
    _, rows, channels = near.shape
    _, _, quad, side = position()
    odd = lax.rem(quad, 2)
    edge[odd] = far[...]
    edge[1 - odd] = near[...]
    halo = 2 * DEPTH
    ahead = side == 0
    held = edge[...].astype(jnp.float32)
    strip = jnp.where(ahead, held[:, :2, rows - halo :], held[:, :2, :halo])
    cots = jnp.where(ahead, held[:, 2, rows - DEPTH :], held[:, 2, :DEPTH])
    out_ref[: 4 * halo] = strip.reshape(4 * halo, channels).astype(jnp.bfloat16)
    out_ref[4 * halo :] = cots.reshape(2 * DEPTH, channels).astype(jnp.bfloat16)


def turn_kernel(weight, out_ref):
    step = 2 * weight.shape[0]
    total = weight.shape[1]
    for start in range(0, total, step):
        stop = min(start + step, total)
        out_ref[start:stop, :] = weight[:, start:stop].T


def forward_kernel(
    masked, cot, near, far, across, corner, live, weight, pick, *refs
):
    act_ref, gp_ref = refs[:2]
    slice_refs = refs[2 : 2 + len(CHIPS)]
    ext, edge, cols, slices = refs[2 + len(CHIPS) :]
    width, rows, channels = masked.shape
    f32 = jnp.float32
    plane, me, quad, side = position()
    use_low = side.astype(f32)
    use_high = (1 - side).astype(f32)
    place = plane * QUAD + quad
    use_left = (place > 0).astype(f32)
    use_right = (place < QUAD * lax.axis_size("depth") - 1).astype(f32)
    halo = 2 * DEPTH
    tall = rows + 2 * halo
    mid = rows + 2 * DEPTH
    span = width + 4
    odd = lax.rem(quad, 2)
    edge[odd] = far[...]
    edge[1 - odd] = near[...]
    left, right = edge[0].astype(f32) * use_left, edge[1].astype(f32) * use_right
    corners = corner[: 4 * halo].astype(f32).reshape(2, 2, halo, channels)
    lower, upper = corners[0] * use_left, corners[1] * use_right
    ends = corner[4 * halo :].astype(f32).reshape(2, 1, DEPTH, channels)
    ext[0:2, halo : halo + rows, :] = left[0:2]
    ext[2 : 2 + width, halo : halo + rows, :] = masked[...].astype(f32)
    ext[2 + width :, halo : halo + rows, :] = right[0:2]
    half = width // 2
    ahead = side == 0
    held = across[...].astype(f32)
    brick = jnp.where(ahead, held[: width + half, :halo], held[: width + half, rows - halo :])
    rest = jnp.concatenate([brick[width:, :, :64], brick[width:, :, 64:]], axis=0)
    beside = jnp.concatenate([brick[:width], rest], axis=2)
    for use, start in ((use_low, 0), (use_high, halo + rows)):
        at = slice(start, start + halo)
        ext[0:2, at, :] = lower * use
        ext[2 : 2 + width, at, :] = beside * use
        ext[2 + width :, at, :] = upper * use
    field = ext[...].reshape(span * tall // DEPTH, DEPTH, channels)
    for c in OFFSETS:
        moved = shift_z(field, c).reshape(span, tall, channels)
        for b in OFFSETS:
            at = ((b + 1) * 3 + c + 1) * channels
            start = DEPTH * (b + 1)
            cols[:, :, at : at + channels] = moved[:, start : start + mid].astype(jnp.bfloat16)
    nine = 9 * channels
    pre = jnp.zeros(((width + 2) * mid, channels), f32)
    for a in range(3):
        pre += jnp.dot(
            cols[a : a + width + 2].reshape((width + 2) * mid, nine),
            weight[a * nine : (a + 1) * nine, :],
            preferred_element_type=f32,
        )
    sig = jax.nn.sigmoid(pre)
    act = (pre * sig).reshape(width + 2, mid, channels)[1 : 1 + width, DEPTH : DEPTH + rows]
    act_ref[...] = (act * live[:, :, 0:1]).astype(jnp.bfloat16)
    slope = (sig * (1.0 + pre * (1.0 - sig))).reshape(width + 2, mid, channels)
    beyond = jnp.concatenate(
        [
            ends[0] * use_left,
            jnp.concatenate([held[width + half], held[width + half + 1, :, :64]], axis=1).reshape(
                width, DEPTH, channels
            ),
            ends[1] * use_right,
        ],
        axis=0,
    )
    centre = jnp.concatenate([left[2:3], cot[...].astype(f32), right[2:3]], axis=0)
    full = jnp.concatenate([beyond * use_low, centre, beyond * use_high], axis=1)
    grad = full * slope
    gp_ref[...] = grad.astype(jnp.bfloat16)
    inner = grad[:, DEPTH : DEPTH + rows].astype(jnp.bfloat16)
    turned = lax.dot_general(
        pick[...],
        inner.reshape((width + 2) * rows, channels),
        (((1,), (1,)), ((), ())),
        preferred_element_type=f32,
    )
    slices[...] = turned.reshape(slices.shape)
    chip = me - lax.rem(quad, 2) * SIDES
    for distance, ref in zip(CHIPS, slice_refs):
        both = [slices[chip ^ distance], slices[(chip ^ distance) + SIDES]]
        ref[...] = jnp.concatenate(both, axis=0).astype(jnp.bfloat16)


def input_kernel(gp, live, turned, out_ref, cols, weight):
    width, rows, channels = out_ref.shape
    f32 = jnp.float32
    tall = rows + 2 * DEPTH
    for tap in range(27):
        weight[tap * channels : (tap + 1) * channels, :] = turned[
            :, tap * channels : (tap + 1) * channels
        ]
    field = gp[...].astype(f32).reshape((width + 2) * tall // DEPTH, DEPTH, channels)
    for c in OFFSETS:
        moved = shift_z(field, -c).reshape(width + 2, tall, channels)
        for b in OFFSETS:
            at = ((b + 1) * 3 + c + 1) * channels
            start = DEPTH * (1 - b)
            cols[:, :, at : at + channels] = moved[:, start : start + rows].astype(jnp.bfloat16)
    nine = 9 * channels
    total = jnp.zeros((width * rows, channels), f32)
    for a in range(3):
        total += jnp.dot(
            cols[2 - a : 2 - a + width].reshape(width * rows, nine),
            weight[a * nine : (a + 1) * nine, :],
            preferred_element_type=f32,
        )
    out_ref[...] = (total.reshape(width, rows, channels) * live[:, :, 0:1]).astype(jnp.bfloat16)


def kernel_grad_kernel(*refs):
    chips = len(CHIPS)
    received, bricks = refs[:chips], refs[chips : 2 * chips]
    keep_ref, send_ref, slices, cols, part, stage, masked, sems = refs[2 * chips :]
    f32 = jnp.float32
    group, lanes = received[0].shape
    blocks, per, lane, channels = masked.shape
    half = lane // 2
    _, _, quad, side = position()
    copies = []
    for i, distance in enumerate(CHIPS):
        to = stage.at[distance // 4, side ^ (distance % 2)]
        packed = bricks[i].at[pl.ds(0, stage.shape[2])]
        copies.append(pltpu.make_async_copy(packed, to, sems.at[i]))
        copies[i].start()
        slices[distance // 4, side ^ (distance % 2)] = received[i][...]
    at = lax.broadcasted_iota(jnp.int32, (group, lane), 1)
    y, z = at // DEPTH, at % DEPTH
    tall = lane // DEPTH
    for block in range(blocks):
        first = slices[block, 0].astype(f32)
        second = slices[block, 1].astype(f32)
        for k in range(per + 2):
            one = first[:, k // 2 * lane : (k // 2 + 1) * lane]
            two = second[:, k // 2 * lane : (k // 2 + 1) * lane]
            if k % 2 == 0:
                base = jnp.where(at < half, one, pltpu.roll(two, half, 1))
            else:
                base = jnp.where(at < half, pltpu.roll(one, half, 1), two)
            pieces = []
            for b in OFFSETS:
                for c in OFFSETS:
                    step = (DEPTH * b + c) % lane
                    moved = base if step == 0 else pltpu.roll(base, step, 1)
                    keep = (y - b >= 0) & (y - b < tall) & (z - c >= 0) & (z - c < DEPTH)
                    pieces.append(jnp.where(keep, moved, 0.0))
            slab = block * (per + 2) + k
            cols[:, slab * lane : (slab + 1) * lane] = jnp.concatenate(pieces, axis=0).astype(
                jnp.bfloat16
            )
    for copy in copies:
        copy.wait()
    for block in range(blocks):
        for sided in range(SIDES):
            at_rows = pl.ds(sided * half, half)
            for x in range(per):
                shift = 64 * (x // (per // 2))
                rest = stage[block, sided, per + x % (per // 2)]
                masked[block, x, at_rows, :128] = stage[block, sided, x]
                masked[block, x, at_rows, 128:] = rest[:, shift : shift + 64]
    for a in range(3):
        got = jnp.zeros((cols.shape[0], channels), f32)
        for block in range(blocks):
            start = (block * (per + 2) + 2 - a) * lane
            got += jnp.dot(
                cols[:, start : start + per * lane],
                masked[block].reshape(per * lane, channels),
                preferred_element_type=f32,
            )
        got = got.reshape(9, group, channels)
        part[:, a * 9 * channels : (a + 1) * 9 * channels] = jnp.concatenate(
            [got[tap] for tap in range(9)], axis=1
        )
    core = lax.rem(quad, 2)
    half = group // 2
    keep_ref[...] = part[pl.ds(pl.multiple_of(core * half, 8), half)]
    send_ref[...] = part[pl.ds(pl.multiple_of((1 - core) * half, 8), half)].astype(jnp.bfloat16)


def fold_kernel(keep, other, own_ref, *refs):
    *send_refs, both, rows = refs
    planes, eight, _ = rows.shape
    count, total = keep.shape
    share = count // planes
    both[:count, :total] = keep[...] + other[...].astype(jnp.float32)
    both[:, total:] = jnp.zeros((both.shape[0], both.shape[1] - total), jnp.float32)
    for to in range(planes):
        rows[to] = fold_rows(both[share * to : share * to + eight, :], total)
    plane = position()[0]
    own_ref[...] = rows[plane]
    for distance, ref in enumerate(send_refs, 1):
        ref[...] = rows[plane ^ distance].astype(jnp.bfloat16)


def sum_kernel(scale, own, one, two, three, out_ref):
    f32 = jnp.float32
    total = own[...] + one[...].astype(f32) + two[...].astype(f32) + three[...].astype(f32)
    out_ref[...] = (total * scale).astype(out_ref.dtype)


def join_kernel(mine, other, out_ref):
    share = out_ref.shape[0] // SIDES
    ahead = position()[3] == 0
    total = out_ref.shape[1]
    here = unfold_rows(mine[...].astype(jnp.float32), total)
    there = unfold_rows(other[...].astype(jnp.float32), total)
    first = jnp.where(ahead, here, there)
    second = jnp.where(ahead, there, here)
    out_ref[0:share] = first[:share]
    out_ref[share:] = second[:share]


def call(body, name, mebibytes, flops, moved, out_shape, scratch=(), in_specs=None):
    spec = pl.BlockSpec(memory_space=pltpu.VMEM)

    def run(*operands):
        return pl.pallas_call(
            body,
            out_shape=out_shape,
            in_specs=in_specs or [spec] * len(operands),
            out_specs=jax.tree.map(lambda _: spec, out_shape),
            scratch_shapes=scratch,
            compiler_params=pltpu.CompilerParams(vmem_limit_bytes=mebibytes << 20),
            cost_estimate=pl.CostEstimate(flops=flops, bytes_accessed=moved, transcendentals=0),
            name=name,
        )(*operands)

    return run


def planes_local(features, weight, voxel_mask, cotangent):
    bf16 = jnp.bfloat16
    f32 = jnp.float32
    array = jax.ShapeDtypeStruct
    width, wide_y, depth, channels = features.shape
    rows = wide_y * depth
    planes = lax.axis_size("depth")
    count = planes * QUAD
    total = 27 * channels
    halo = 2 * DEPTH
    span = (width + 2) * rows
    share = channels // count // SIDES
    group = planes * share

    def swap(piece, axes, distance, size):
        return lax.ppermute(piece, axes, [(i, i ^ distance) for i in range(size)])

    def in_plane(piece, distance):
        return swap(piece, ("quad", "narrow"), distance, MEMBERS)

    brick = array((width, rows, channels), bf16)
    slab = array((3, rows, channels), bf16)
    pick = call(
        functools.partial(pick_kernel, planes), "pick", 4, 1 << 32, 1 << 16,
        array((MEMBERS * group, channels), bf16),
    )()
    vmem = pl.BlockSpec(memory_space=pltpu.VMEM)
    masked, cot, live, near, far = call(
        prepare_kernel, "prepare", 16, 1 << 20, 1 << 20,
        (brick, brick, array((width, rows, 128), f32), slab, slab),
        (),
        [vmem] * 3 + [pl.BlockSpec(memory_space=pl.ANY)],
    )(
        features.reshape(width, rows, channels),
        cotangent.reshape(width, rows, channels),
        voxel_mask,
        pick,
    )
    near = swap(near, WIDE, 1, count)
    ends = [min(max(((i + 1) ^ 1) - 1, 0), count - 1) for i in range(count)]
    far = lax.ppermute(far, WIDE, list(enumerate(ends)))
    weight_rows = call(
        turn_kernel, "turn", 8, 1 << 20, 4 << 20, array((total, channels), bf16)
    )(weight.T)
    slabs = width * channels // 128
    across = call(
        across_kernel, "across", 4, 1 << 16, 1 << 19, array((slabs + 2, rows, 128), bf16)
    )(masked, cot)
    across = in_plane(across, CHIPS[1])
    near, far, weight_rows = lax.optimization_barrier((near, far, weight_rows))
    corner = call(
        corner_kernel, "corner", 4, 1 << 16, 1 << 18,
        array((4 * halo + 2 * DEPTH, channels), bf16),
        (pltpu.VMEM((2,) + slab.shape, bf16),),
    )(near, far)
    packed = call(
        pack_kernel, "pack", 4, 1 << 16, 1 << 19, array((slabs, rows, 128), bf16)
    )(masked)
    corner = in_plane(corner, 1)
    bricks = [packed, across] + [in_plane(packed, distance) for distance in CHIPS[2:]]

    mid = rows + 2 * DEPTH
    act, gp, *slices = call(
        forward_kernel, "forward", 28, 1 << 32, 1 << 20,
        (brick, array((width + 2, mid, channels), bf16))
        + (array((2 * group, span), bf16),) * len(CHIPS),
        (
            pltpu.VMEM((width + 4, rows + 2 * halo, channels), f32),
            pltpu.VMEM((2,) + slab.shape, bf16),
            pltpu.VMEM((width + 4, mid, 9 * channels), bf16),
            pltpu.VMEM((MEMBERS, group, span), f32),
        ),
    )(masked, cot, near, far, across, corner, live, weight_rows, pick)
    slices = [slices[0]] + [in_plane(part, d) for part, d in zip(slices[1:], CHIPS[1:])]

    grad_input = call(
        input_kernel, "input_gradient", 20, 2 * 512 * 5184 * 256, 4 << 20, brick,
        (
            pltpu.VMEM((width + 2, rows, 9 * channels), bf16),
            pltpu.VMEM((total, channels), bf16),
        ),
    )(gp, live, weight.T)

    blocks = QUAD // 2
    chips = len(CHIPS)
    lanes = dense(total)[0]
    keep, fold = call(
        kernel_grad_kernel, "kernel_gradient", 28, 2 * 432 * 3 * 2048 * 256, 4 << 20,
        (array((group, total), f32), array((group, total), bf16)),
        (
            pltpu.VMEM((blocks, SIDES, 2 * group, span), bf16),
            pltpu.VMEM((9 * 2 * group, blocks * (width + 2) * SIDES * rows), bf16),
            pltpu.VMEM((2 * group, total), f32),
            pltpu.VMEM((blocks, SIDES) + packed.shape, bf16),
            pltpu.VMEM((blocks, width, SIDES * rows, channels), bf16),
            pltpu.SemaphoreType.DMA((chips,)),
        ),
        [vmem] * chips + [pl.BlockSpec(memory_space=pl.ANY)] * chips,
    )(*slices, *bricks)
    own, *sends = call(
        fold_kernel, "fold", 8, 8 * total * 4, 8 * total * 40,
        (array((8, lanes), f32),) + (array((8, lanes), bf16),) * (planes - 1),
        (
            pltpu.VMEM((group + 8, sum(dense(total))), f32),
            pltpu.VMEM((planes, 8, lanes), f32),
        ),
    )(keep, in_plane(fold, 2))
    got = [swap(sent, "depth", d, planes) for d, sent in enumerate(sends, 1)]
    grad_input, *got = lax.optimization_barrier((grad_input, *got))
    voxels = count * SIDES * width * rows
    mine = call(
        functools.partial(sum_kernel, float(1.0 / voxels**0.5)),
        "plane_sum", 4, 8 * total * 4, 8 * total * 14, array((8, lanes), bf16),
    )(own, *got)
    grad_weight = call(
        join_kernel, "join", 4, 8 * total, 8 * total * 14, array((channels // count, total), f32)
    )(mine, in_plane(mine, 1))
    shape = features.shape
    return act.reshape(shape), grad_input.reshape(shape), grad_weight


def padded_2(cells, sides, width):
    for axis, dim in sides:
        count = lax.axis_size(axis)
        ends = count - 1
        head = lax.slice_in_dim(cells, 0, width, axis=dim)
        tail = lax.slice_in_dim(cells, cells.shape[dim] - width, cells.shape[dim], axis=dim)
        cells = jnp.concatenate(
            [
                lax.ppermute(tail, axis, [(i, (i + 1) % count) for i in range(ends)]),
                cells,
                lax.ppermute(head, axis, [((i + 1) % count, i) for i in range(ends)]),
            ],
            axis=dim,
        )
    return cells


def gather_taps(padded, width_x, width_y, depth_z, channels, flip):
    pieces = []
    for shift_x in range(3):
        for shift_y in range(3):
            for shift_z in range(3):
                start_x = 2 - shift_x if flip else shift_x
                start_y = 2 - shift_y if flip else shift_y
                start_z = 2 - shift_z if flip else shift_z
                piece = padded[
                    start_x : start_x + width_x,
                    start_y : start_y + width_y,
                    start_z : start_z + depth_z,
                    :,
                ]
                pieces.append(piece.reshape(-1, channels))
    return jnp.concatenate(pieces, axis=1)


def summed_local(features, weight, voxel_mask, cotangent):
    width_x, width_y, depth_z, channels = features.shape
    masked = features * voxel_mask.astype(jnp.bfloat16)[..., None]
    padded = padded_2(masked, (("wide", 0), ("narrow", 1)), 1)
    padded = jnp.pad(padded, ((0, 0), (0, 0), (1, 1), (0, 0)))
    columns = gather_taps(padded, width_x, width_y, depth_z, channels, False)
    pre = jnp.dot(columns, weight, preferred_element_type=jnp.float32)
    live = voxel_mask.reshape(-1, 1).astype(jnp.float32)
    sig = jax.nn.sigmoid(pre)
    activation = (
        (pre * sig * live).astype(jnp.bfloat16).reshape(width_x, width_y, depth_z, channels)
    )
    slope = sig * (1.0 + pre * (1.0 - sig))
    grad_pre = (cotangent.reshape(-1, channels).astype(jnp.float32) * live * slope).astype(
        jnp.bfloat16
    )
    taps = weight.reshape(27, channels, channels)
    grid = grad_pre.reshape(width_x, width_y, depth_z, channels)
    grad_pad = padded_2(grid, (("wide", 0), ("narrow", 1)), 1)
    grad_pad = jnp.pad(grad_pad, ((0, 0), (0, 0), (1, 1), (0, 0)))
    grad_columns = gather_taps(grad_pad, width_x, width_y, depth_z, channels, True)
    flipped = jnp.transpose(taps, (0, 2, 1)).reshape(27 * channels, channels)
    grad_field = jnp.dot(grad_columns, flipped, preferred_element_type=jnp.float32)
    grad_input = (
        (grad_field * live).astype(jnp.bfloat16).reshape(width_x, width_y, depth_z, channels)
    )
    scale = 1.0 / jnp.sqrt(
        jnp.float32(width_x * width_y * depth_z * lax.axis_size("wide") * lax.axis_size("narrow"))
    )
    whole = lax.dot_general(
        grad_pre, columns, (((0,), (0,)), ((), ())), preferred_element_type=jnp.float32
    )
    piece_flat = lax.psum_scatter(
        whole.reshape(-1), ("wide", "narrow"), scatter_dimension=0, tiled=True
    )
    gathered = lax.all_gather(piece_flat, "narrow", axis=0, tiled=True)
    summed = gathered.reshape(channels // lax.axis_size("wide"), 27 * channels)
    grad_weight = summed * scale
    return (activation, grad_input, grad_weight)


def sharded(body, mesh, wide):
    return jax.shard_map(
        body,
        mesh=mesh,
        in_specs=(
            P(wide, "narrow", None, None),
            P(),
            P(wide, "narrow", None),
            P(wide, "narrow", None, None),
        ),
        out_specs=(
            P(wide, "narrow", None, None),
            P(wide, "narrow", None, None),
            P(wide, None),
        ),
        check_vma=False,
    )


def solution(mesh):
    wide, narrow = mesh.shape["wide"], mesh.shape["narrow"]
    if wide != 4 * QUAD or narrow != SIDES:
        return sharded(summed_local, mesh, "wide")
    planes = Mesh(
        mesh.devices.reshape(wide // QUAD, QUAD, narrow), ("depth", "quad", "narrow")
    )
    return sharded(planes_local, planes, WIDE)
```

```python
import functools

import jax
import jax.numpy as jnp
from jax import lax
from jax.experimental import pallas as pl
from jax.experimental.pallas import tpu as pltpu
from jax.sharding import Mesh
from jax.sharding import PartitionSpec as P

WIDE = ("depth", "quad")
QUAD = 4
SIDES = 2
MEMBERS = QUAD * SIDES
CHIPS = (0, 1, 4, 5)
OFFSETS = (-1, 0, 1)
DEPTH = 8


def position():
    quad, side = lax.axis_index("quad"), lax.axis_index("narrow")
    return lax.axis_index("depth"), quad * SIDES + side, quad, side


def shift_z(field, step):
    if step == 0:
        return field
    depth = field.shape[1]
    moved = pltpu.roll(field, (-step) % depth, 1)
    z = lax.broadcasted_iota(jnp.int32, field.shape, 1) + step
    return jnp.where((z >= 0) & (z < depth), moved, 0.0)


def pick_kernel(planes, out_ref):
    index = lax.broadcasted_iota(jnp.int32, out_ref.shape, 0)
    column = lax.broadcasted_iota(jnp.int32, out_ref.shape, 1)
    per = out_ref.shape[1] // (planes * QUAD)
    share = per // SIDES
    group = planes * share
    quad, side = index // (SIDES * group), index // group % SIDES
    plane, row = index // share % planes, index % share
    channel = per * (QUAD * plane + quad) + share * side + row
    out_ref[...] = jnp.where(channel == column, 1.0, 0.0).astype(jnp.bfloat16)


def dense(total):
    tiles = -(-total // 128)
    moved = tiles // 4
    return (tiles - moved) * 128, moved * 128


def fold_rows(block, total):
    kept, moved = dense(total)
    tail = block[:, kept : kept + moved]
    row = lax.broadcasted_iota(jnp.int32, tail.shape, 0)
    pieces = []
    for k in range(3):
        spare = jnp.where(row == 6, pltpu.roll(tail, 6 - k, 0), pltpu.roll(tail, 4 - k, 0))
        pieces.append(jnp.where(row < 6, block[:, k * moved : (k + 1) * moved], spare))
    return jnp.concatenate(pieces + [block[:, 3 * moved : kept]], axis=1)


def unfold_rows(block, total):
    kept, moved = dense(total)
    row = lax.broadcasted_iota(jnp.int32, (8, moved), 0)
    tail = jnp.zeros((8, moved), block.dtype)
    for k in range(3):
        piece = block[:, k * moved : (k + 1) * moved]
        tail = jnp.where(row == k, pltpu.roll(piece, 2 + k, 0), tail)
        tail = jnp.where(row == 3 + k, pltpu.roll(piece, 4 + k, 0), tail)
    return jnp.concatenate([block, tail], axis=1)[:, :total]


def prepare_kernel(features, cot, mask, first, masked_ref, cot_ref, live_ref, near_ref, far_ref):
    width, rows, channels = features.shape
    f32 = jnp.float32
    flat = mask[...].astype(f32).reshape(width * rows // DEPTH, DEPTH)
    live = jnp.broadcast_to(flat[:, :, None], flat.shape + (channels,)).reshape(features.shape)
    live_ref[...] = live[:, :, :128]
    masked_ref[...] = (features[...].astype(f32) * live).astype(jnp.bfloat16)
    cot_ref[...] = (cot[...].astype(f32) * live).astype(jnp.bfloat16)
    odd = lax.rem(position()[2], 2)
    for ref, upper in ((near_ref, 1 - odd), (far_ref, odd)):
        ref[0:2] = masked_ref[pl.ds(upper * (width - 2), 2)]
        ref[2:3] = cot_ref[pl.ds(upper * (width - 1), 1)]


def rows_of_128(masked, out_ref):
    width = masked.shape[0]
    half = width // 2
    rest = jnp.concatenate([masked[:half, :, 128:], masked[half:, :, 128:]], axis=2)
    out_ref[:width] = masked[:, :, :128]
    out_ref[width : width + half] = rest


def pack_kernel(masked, after, packed_ref):
    rows_of_128(masked, packed_ref)


def across_kernel(masked, cot, across_ref):
    width, rows, channels = masked.shape
    rows_of_128(masked, across_ref)
    count = across_ref.shape[0] - 2
    ahead = position()[3] == 0
    grown = cot[...].astype(jnp.float32)
    strip = jnp.where(ahead, grown[:, rows - DEPTH :], grown[:, :DEPTH])
    strip = strip.reshape(width * DEPTH, channels)
    rest = jnp.concatenate([strip[:, 128:], jnp.zeros_like(strip[:, 128:])], axis=1)
    across_ref[count] = strip[:, :128].astype(jnp.bfloat16)
    across_ref[count + 1] = rest.astype(jnp.bfloat16)


def corner_kernel(near, far, out_ref, edge):
    _, rows, channels = near.shape
    _, _, quad, side = position()
    odd = lax.rem(quad, 2)
    edge[odd] = far[...]
    edge[1 - odd] = near[...]
    halo = 2 * DEPTH
    ahead = side == 0
    held = edge[...].astype(jnp.float32)
    strip = jnp.where(ahead, held[:, :2, rows - halo :], held[:, :2, :halo])
    cots = jnp.where(ahead, held[:, 2, rows - DEPTH :], held[:, 2, :DEPTH])
    out_ref[: 4 * halo] = strip.reshape(4 * halo, channels).astype(jnp.bfloat16)
    out_ref[4 * halo :] = cots.reshape(2 * DEPTH, channels).astype(jnp.bfloat16)


def turn_kernel(weight, out_ref):
    step = 2 * weight.shape[0]
    total = weight.shape[1]
    for start in range(0, total, step):
        stop = min(start + step, total)
        out_ref[start:stop, :] = weight[:, start:stop].T


def forward_kernel(
    masked, cot, near, far, across, corner, live, weight, pick, *refs
):
    act_ref, gp_ref = refs[:2]
    slice_refs = refs[2 : 2 + len(CHIPS)]
    ext, edge, cols, slices = refs[2 + len(CHIPS) :]
    width, rows, channels = masked.shape
    f32 = jnp.float32
    plane, me, quad, side = position()
    use_low = side.astype(f32)
    use_high = (1 - side).astype(f32)
    place = plane * QUAD + quad
    use_left = (place > 0).astype(f32)
    use_right = (place < QUAD * lax.axis_size("depth") - 1).astype(f32)
    halo = 2 * DEPTH
    tall = rows + 2 * halo
    mid = rows + 2 * DEPTH
    span = width + 4
    odd = lax.rem(quad, 2)
    edge[odd] = far[...]
    edge[1 - odd] = near[...]
    left, right = edge[0].astype(f32) * use_left, edge[1].astype(f32) * use_right
    corners = corner[: 4 * halo].astype(f32).reshape(2, 2, halo, channels)
    lower, upper = corners[0] * use_left, corners[1] * use_right
    ends = corner[4 * halo :].astype(f32).reshape(2, 1, DEPTH, channels)
    ext[0:2, halo : halo + rows, :] = left[0:2]
    ext[2 : 2 + width, halo : halo + rows, :] = masked[...].astype(f32)
    ext[2 + width :, halo : halo + rows, :] = right[0:2]
    half = width // 2
    ahead = side == 0
    held = across[...].astype(f32)
    brick = jnp.where(ahead, held[: width + half, :halo], held[: width + half, rows - halo :])
    rest = jnp.concatenate([brick[width:, :, :64], brick[width:, :, 64:]], axis=0)
    beside = jnp.concatenate([brick[:width], rest], axis=2)
    for use, start in ((use_low, 0), (use_high, halo + rows)):
        at = slice(start, start + halo)
        ext[0:2, at, :] = lower * use
        ext[2 : 2 + width, at, :] = beside * use
        ext[2 + width :, at, :] = upper * use
    field = ext[...].reshape(span * tall // DEPTH, DEPTH, channels)
    for c in OFFSETS:
        moved = shift_z(field, c).reshape(span, tall, channels)
        for b in OFFSETS:
            at = ((b + 1) * 3 + c + 1) * channels
            start = DEPTH * (b + 1)
            cols[:, :, at : at + channels] = moved[:, start : start + mid].astype(jnp.bfloat16)
    nine = 9 * channels
    pre = jnp.zeros(((width + 2) * mid, channels), f32)
    for a in range(3):
        pre += jnp.dot(
            cols[a : a + width + 2].reshape((width + 2) * mid, nine),
            weight[a * nine : (a + 1) * nine, :],
            preferred_element_type=f32,
        )
    sig = jax.nn.sigmoid(pre)
    act = (pre * sig).reshape(width + 2, mid, channels)[1 : 1 + width, DEPTH : DEPTH + rows]
    act_ref[...] = (act * live[:, :, 0:1]).astype(jnp.bfloat16)
    slope = (sig * (1.0 + pre * (1.0 - sig))).reshape(width + 2, mid, channels)
    beyond = jnp.concatenate(
        [
            ends[0] * use_left,
            jnp.concatenate([held[width + half], held[width + half + 1, :, :64]], axis=1).reshape(
                width, DEPTH, channels
            ),
            ends[1] * use_right,
        ],
        axis=0,
    )
    centre = jnp.concatenate([left[2:3], cot[...].astype(f32), right[2:3]], axis=0)
    full = jnp.concatenate([beyond * use_low, centre, beyond * use_high], axis=1)
    grad = full * slope
    gp_ref[...] = grad.astype(jnp.bfloat16)
    inner = grad[:, DEPTH : DEPTH + rows].astype(jnp.bfloat16)
    turned = lax.dot_general(
        pick[...],
        inner.reshape((width + 2) * rows, channels),
        (((1,), (1,)), ((), ())),
        preferred_element_type=f32,
    )
    slices[...] = turned.reshape(slices.shape)
    chip = me - lax.rem(quad, 2) * SIDES
    for distance, ref in zip(CHIPS, slice_refs):
        both = [slices[chip ^ distance], slices[(chip ^ distance) + SIDES]]
        ref[...] = jnp.concatenate(both, axis=0).astype(jnp.bfloat16)


def input_kernel(gp, live, turned, out_ref, cols, weight):
    width, rows, channels = out_ref.shape
    f32 = jnp.float32
    tall = rows + 2 * DEPTH
    for tap in range(27):
        weight[tap * channels : (tap + 1) * channels, :] = turned[
            :, tap * channels : (tap + 1) * channels
        ]
    field = gp[...].astype(f32).reshape((width + 2) * tall // DEPTH, DEPTH, channels)
    for c in OFFSETS:
        moved = shift_z(field, -c).reshape(width + 2, tall, channels)
        for b in OFFSETS:
            at = ((b + 1) * 3 + c + 1) * channels
            start = DEPTH * (1 - b)
            cols[:, :, at : at + channels] = moved[:, start : start + rows].astype(jnp.bfloat16)
    nine = 9 * channels
    total = jnp.zeros((width * rows, channels), f32)
    for a in range(3):
        total += jnp.dot(
            cols[2 - a : 2 - a + width].reshape(width * rows, nine),
            weight[a * nine : (a + 1) * nine, :],
            preferred_element_type=f32,
        )
    out_ref[...] = (total.reshape(width, rows, channels) * live[:, :, 0:1]).astype(jnp.bfloat16)


def kernel_grad_kernel(*refs):
    chips = len(CHIPS)
    received, bricks = refs[:chips], refs[chips : 2 * chips]
    keep_ref, send_ref, slices, cols, part, stage, masked, sems = refs[2 * chips :]
    f32 = jnp.float32
    group, lanes = received[0].shape
    blocks, per, lane, channels = masked.shape
    half = lane // 2
    _, _, quad, side = position()
    copies = []
    for i, distance in enumerate(CHIPS):
        to = stage.at[distance // 4, side ^ (distance % 2)]
        packed = bricks[i].at[pl.ds(0, stage.shape[2])]
        copies.append(pltpu.make_async_copy(packed, to, sems.at[i]))
        copies[i].start()
        slices[distance // 4, side ^ (distance % 2)] = received[i][...]
    at = lax.broadcasted_iota(jnp.int32, (group, lane), 1)
    y, z = at // DEPTH, at % DEPTH
    tall = lane // DEPTH
    for block in range(blocks):
        first = slices[block, 0].astype(f32)
        second = slices[block, 1].astype(f32)
        for k in range(per + 2):
            one = first[:, k // 2 * lane : (k // 2 + 1) * lane]
            two = second[:, k // 2 * lane : (k // 2 + 1) * lane]
            if k % 2 == 0:
                base = jnp.where(at < half, one, pltpu.roll(two, half, 1))
            else:
                base = jnp.where(at < half, pltpu.roll(one, half, 1), two)
            pieces = []
            for b in OFFSETS:
                for c in OFFSETS:
                    step = (DEPTH * b + c) % lane
                    moved = base if step == 0 else pltpu.roll(base, step, 1)
                    keep = (y - b >= 0) & (y - b < tall) & (z - c >= 0) & (z - c < DEPTH)
                    pieces.append(jnp.where(keep, moved, 0.0))
            slab = block * (per + 2) + k
            cols[:, slab * lane : (slab + 1) * lane] = jnp.concatenate(pieces, axis=0).astype(
                jnp.bfloat16
            )
    for copy in copies:
        copy.wait()
    for block in range(blocks):
        for sided in range(SIDES):
            at_rows = pl.ds(sided * half, half)
            for x in range(per):
                shift = 64 * (x // (per // 2))
                rest = stage[block, sided, per + x % (per // 2)]
                masked[block, x, at_rows, :128] = stage[block, sided, x]
                masked[block, x, at_rows, 128:] = rest[:, shift : shift + 64]
    for a in range(3):
        got = jnp.zeros((cols.shape[0], channels), f32)
        for block in range(blocks):
            start = (block * (per + 2) + 2 - a) * lane
            got += jnp.dot(
                cols[:, start : start + per * lane],
                masked[block].reshape(per * lane, channels),
                preferred_element_type=f32,
            )
        got = got.reshape(9, group, channels)
        part[:, a * 9 * channels : (a + 1) * 9 * channels] = jnp.concatenate(
            [got[tap] for tap in range(9)], axis=1
        )
    core = lax.rem(quad, 2)
    half = group // 2
    keep_ref[...] = part[pl.ds(pl.multiple_of(core * half, 8), half)]
    send_ref[...] = part[pl.ds(pl.multiple_of((1 - core) * half, 8), half)].astype(jnp.bfloat16)


def fold_kernel(keep, other, own_ref, *refs):
    *send_refs, both, rows = refs
    planes, eight, _ = rows.shape
    count, total = keep.shape
    share = count // planes
    both[:count, :total] = keep[...] + other[...].astype(jnp.float32)
    both[:, total:] = jnp.zeros((both.shape[0], both.shape[1] - total), jnp.float32)
    for to in range(planes):
        rows[to] = fold_rows(both[share * to : share * to + eight, :], total)
    plane = position()[0]
    own_ref[...] = rows[plane]
    for distance, ref in enumerate(send_refs, 1):
        ref[...] = rows[plane ^ distance].astype(jnp.bfloat16)


def sum_kernel(scale, own, one, two, three, out_ref):
    f32 = jnp.float32
    total = own[...] + one[...].astype(f32) + two[...].astype(f32) + three[...].astype(f32)
    out_ref[...] = (total * scale).astype(out_ref.dtype)


def join_kernel(mine, other, out_ref):
    share = out_ref.shape[0] // SIDES
    ahead = position()[3] == 0
    total = out_ref.shape[1]
    here = unfold_rows(mine[...].astype(jnp.float32), total)
    there = unfold_rows(other[...].astype(jnp.float32), total)
    first = jnp.where(ahead, here, there)
    second = jnp.where(ahead, there, here)
    out_ref[0:share] = first[:share]
    out_ref[share:] = second[:share]


def call(body, name, mebibytes, flops, moved, out_shape, scratch=(), in_specs=None):
    spec = pl.BlockSpec(memory_space=pltpu.VMEM)

    def run(*operands):
        return pl.pallas_call(
            body,
            out_shape=out_shape,
            in_specs=in_specs or [spec] * len(operands),
            out_specs=jax.tree.map(lambda _: spec, out_shape),
            scratch_shapes=scratch,
            compiler_params=pltpu.CompilerParams(vmem_limit_bytes=mebibytes << 20),
            cost_estimate=pl.CostEstimate(flops=flops, bytes_accessed=moved, transcendentals=0),
            name=name,
        )(*operands)

    return run


def planes_local(features, weight, voxel_mask, cotangent):
    bf16 = jnp.bfloat16
    f32 = jnp.float32
    array = jax.ShapeDtypeStruct
    width, wide_y, depth, channels = features.shape
    rows = wide_y * depth
    planes = lax.axis_size("depth")
    count = planes * QUAD
    total = 27 * channels
    halo = 2 * DEPTH
    span = (width + 2) * rows
    share = channels // count // SIDES
    group = planes * share

    def swap(piece, axes, distance, size):
        return lax.ppermute(piece, axes, [(i, i ^ distance) for i in range(size)])

    def in_plane(piece, distance):
        return swap(piece, ("quad", "narrow"), distance, MEMBERS)

    brick = array((width, rows, channels), bf16)
    slab = array((3, rows, channels), bf16)
    pick = call(
        functools.partial(pick_kernel, planes), "pick", 4, 1 << 32, 1 << 16,
        array((MEMBERS * group, channels), bf16),
    )()
    vmem = pl.BlockSpec(memory_space=pltpu.VMEM)
    masked, cot, live, near, far = call(
        prepare_kernel, "prepare", 16, 1 << 20, 1 << 20,
        (brick, brick, array((width, rows, 128), f32), slab, slab),
        (),
        [vmem] * 3 + [pl.BlockSpec(memory_space=pl.ANY)],
    )(
        features.reshape(width, rows, channels),
        cotangent.reshape(width, rows, channels),
        voxel_mask,
        pick,
    )
    near = swap(near, WIDE, 1, count)
    ends = [min(max(((i + 1) ^ 1) - 1, 0), count - 1) for i in range(count)]
    far = lax.ppermute(far, WIDE, list(enumerate(ends)))
    weight_rows = call(
        turn_kernel, "turn", 8, 1 << 20, 4 << 20, array((total, channels), bf16)
    )(weight.T)
    slabs = width * channels // 128
    across = call(
        across_kernel, "across", 4, 1 << 16, 1 << 19, array((slabs + 2, rows, 128), bf16)
    )(masked, cot)
    across = in_plane(across, CHIPS[1])
    packed = call(
        pack_kernel, "pack", 4, 1 << 16, 1 << 19, array((slabs, rows, 128), bf16), (),
        [vmem, pl.BlockSpec(memory_space=pl.ANY)],
    )(masked, weight_rows)
    near, far, weight_rows, late = lax.optimization_barrier((near, far, weight_rows, packed))
    corner = call(
        corner_kernel, "corner", 4, 1 << 16, 1 << 18,
        array((4 * halo + 2 * DEPTH, channels), bf16),
        (pltpu.VMEM((2,) + slab.shape, bf16),),
    )(near, far)
    corner = in_plane(corner, 1)
    bricks = [packed, across, in_plane(packed, CHIPS[2]), in_plane(late, CHIPS[3])]

    mid = rows + 2 * DEPTH
    act, gp, *slices = call(
        forward_kernel, "forward", 28, 3 << 29, 1 << 20,
        (brick, array((width + 2, mid, channels), bf16))
        + (array((2 * group, span), bf16),) * len(CHIPS),
        (
            pltpu.VMEM((width + 4, rows + 2 * halo, channels), f32),
            pltpu.VMEM((2,) + slab.shape, bf16),
            pltpu.VMEM((width + 4, mid, 9 * channels), bf16),
            pltpu.VMEM((MEMBERS, group, span), f32),
        ),
    )(masked, cot, near, far, across, corner, live, weight_rows, pick)
    bricks[2], *slices = lax.optimization_barrier((bricks[2], *slices))
    slices = [slices[0]] + [in_plane(part, d) for part, d in zip(slices[1:], CHIPS[1:])]

    grad_input = call(
        input_kernel, "input_gradient", 20, 2 * 512 * 5184 * 256, 4 << 20, brick,
        (
            pltpu.VMEM((width + 2, rows, 9 * channels), bf16),
            pltpu.VMEM((total, channels), bf16),
        ),
    )(gp, live, weight.T)

    blocks = QUAD // 2
    chips = len(CHIPS)
    lanes = dense(total)[0]
    keep, fold = call(
        kernel_grad_kernel, "kernel_gradient", 28, 2 * 432 * 3 * 2048 * 256, 4 << 20,
        (array((group, total), f32), array((group, total), bf16)),
        (
            pltpu.VMEM((blocks, SIDES, 2 * group, span), bf16),
            pltpu.VMEM((9 * 2 * group, blocks * (width + 2) * SIDES * rows), bf16),
            pltpu.VMEM((2 * group, total), f32),
            pltpu.VMEM((blocks, SIDES) + packed.shape, bf16),
            pltpu.VMEM((blocks, width, SIDES * rows, channels), bf16),
            pltpu.SemaphoreType.DMA((chips,)),
        ),
        [vmem] * chips + [pl.BlockSpec(memory_space=pl.ANY)] * chips,
    )(*slices, *bricks)
    own, *sends = call(
        fold_kernel, "fold", 8, 8 * total * 4, 8 * total * 40,
        (array((8, lanes), f32),) + (array((8, lanes), bf16),) * (planes - 1),
        (
            pltpu.VMEM((group + 8, sum(dense(total))), f32),
            pltpu.VMEM((planes, 8, lanes), f32),
        ),
    )(keep, in_plane(fold, 2))
    got = [swap(sent, "depth", d, planes) for d, sent in enumerate(sends, 1)]
    grad_input, *got = lax.optimization_barrier((grad_input, *got))
    voxels = count * SIDES * width * rows
    mine = call(
        functools.partial(sum_kernel, float(1.0 / voxels**0.5)),
        "plane_sum", 4, 8 * total * 4, 8 * total * 14, array((8, lanes), bf16),
    )(own, *got)
    grad_weight = call(
        join_kernel, "join", 4, 8 * total, 8 * total * 14, array((channels // count, total), f32)
    )(mine, in_plane(mine, 1))
    shape = features.shape
    return act.reshape(shape), grad_input.reshape(shape), grad_weight


def padded_2(cells, sides, width):
    for axis, dim in sides:
        count = lax.axis_size(axis)
        ends = count - 1
        head = lax.slice_in_dim(cells, 0, width, axis=dim)
        tail = lax.slice_in_dim(cells, cells.shape[dim] - width, cells.shape[dim], axis=dim)
        cells = jnp.concatenate(
            [
                lax.ppermute(tail, axis, [(i, (i + 1) % count) for i in range(ends)]),
                cells,
                lax.ppermute(head, axis, [((i + 1) % count, i) for i in range(ends)]),
            ],
            axis=dim,
        )
    return cells


def gather_taps(padded, width_x, width_y, depth_z, channels, flip):
    pieces = []
    for shift_x in range(3):
        for shift_y in range(3):
            for shift_z in range(3):
                start_x = 2 - shift_x if flip else shift_x
                start_y = 2 - shift_y if flip else shift_y
                start_z = 2 - shift_z if flip else shift_z
                piece = padded[
                    start_x : start_x + width_x,
                    start_y : start_y + width_y,
                    start_z : start_z + depth_z,
                    :,
                ]
                pieces.append(piece.reshape(-1, channels))
    return jnp.concatenate(pieces, axis=1)


def summed_local(features, weight, voxel_mask, cotangent):
    width_x, width_y, depth_z, channels = features.shape
    masked = features * voxel_mask.astype(jnp.bfloat16)[..., None]
    padded = padded_2(masked, (("wide", 0), ("narrow", 1)), 1)
    padded = jnp.pad(padded, ((0, 0), (0, 0), (1, 1), (0, 0)))
    columns = gather_taps(padded, width_x, width_y, depth_z, channels, False)
    pre = jnp.dot(columns, weight, preferred_element_type=jnp.float32)
    live = voxel_mask.reshape(-1, 1).astype(jnp.float32)
    sig = jax.nn.sigmoid(pre)
    activation = (
        (pre * sig * live).astype(jnp.bfloat16).reshape(width_x, width_y, depth_z, channels)
    )
    slope = sig * (1.0 + pre * (1.0 - sig))
    grad_pre = (cotangent.reshape(-1, channels).astype(jnp.float32) * live * slope).astype(
        jnp.bfloat16
    )
    taps = weight.reshape(27, channels, channels)
    grid = grad_pre.reshape(width_x, width_y, depth_z, channels)
    grad_pad = padded_2(grid, (("wide", 0), ("narrow", 1)), 1)
    grad_pad = jnp.pad(grad_pad, ((0, 0), (0, 0), (1, 1), (0, 0)))
    grad_columns = gather_taps(grad_pad, width_x, width_y, depth_z, channels, True)
    flipped = jnp.transpose(taps, (0, 2, 1)).reshape(27 * channels, channels)
    grad_field = jnp.dot(grad_columns, flipped, preferred_element_type=jnp.float32)
    grad_input = (
        (grad_field * live).astype(jnp.bfloat16).reshape(width_x, width_y, depth_z, channels)
    )
    scale = 1.0 / jnp.sqrt(
        jnp.float32(width_x * width_y * depth_z * lax.axis_size("wide") * lax.axis_size("narrow"))
    )
    whole = lax.dot_general(
        grad_pre, columns, (((0,), (0,)), ((), ())), preferred_element_type=jnp.float32
    )
    piece_flat = lax.psum_scatter(
        whole.reshape(-1), ("wide", "narrow"), scatter_dimension=0, tiled=True
    )
    gathered = lax.all_gather(piece_flat, "narrow", axis=0, tiled=True)
    summed = gathered.reshape(channels // lax.axis_size("wide"), 27 * channels)
    grad_weight = summed * scale
    return (activation, grad_input, grad_weight)


def sharded(body, mesh, wide):
    return jax.shard_map(
        body,
        mesh=mesh,
        in_specs=(
            P(wide, "narrow", None, None),
            P(),
            P(wide, "narrow", None),
            P(wide, "narrow", None, None),
        ),
        out_specs=(
            P(wide, "narrow", None, None),
            P(wide, "narrow", None, None),
            P(wide, None),
        ),
        check_vma=False,
    )


def solution(mesh):
    wide, narrow = mesh.shape["wide"], mesh.shape["narrow"]
    if wide != 4 * QUAD or narrow != SIDES:
        return sharded(summed_local, mesh, "wide")
    planes = Mesh(
        mesh.devices.reshape(wide // QUAD, QUAD, narrow), ("depth", "quad", "narrow")
    )
    return sharded(planes_local, planes, WIDE)
```

```python
import functools

import jax
import jax.numpy as jnp
from jax import lax
from jax.experimental import pallas as pl
from jax.experimental.pallas import tpu as pltpu
from jax.sharding import Mesh
from jax.sharding import PartitionSpec as P

WIDE = ("depth", "quad")
QUAD = 4
SIDES = 2
MEMBERS = QUAD * SIDES
CHIPS = (0, 1, 4, 5)
OFFSETS = (-1, 0, 1)
DEPTH = 8


def position():
    quad, side = lax.axis_index("quad"), lax.axis_index("narrow")
    return lax.axis_index("depth"), quad * SIDES + side, quad, side


def shift_z(field, step):
    if step == 0:
        return field
    depth = field.shape[1]
    moved = pltpu.roll(field, (-step) % depth, 1)
    z = lax.broadcasted_iota(jnp.int32, field.shape, 1) + step
    return jnp.where((z >= 0) & (z < depth), moved, 0.0)


def pick_kernel(planes, out_ref):
    index = lax.broadcasted_iota(jnp.int32, out_ref.shape, 0)
    column = lax.broadcasted_iota(jnp.int32, out_ref.shape, 1)
    per = out_ref.shape[1] // (planes * QUAD)
    share = per // SIDES
    group = planes * share
    quad, side = index // (SIDES * group), index // group % SIDES
    plane, row = index // share % planes, index % share
    channel = per * (QUAD * plane + quad) + share * side + row
    out_ref[...] = jnp.where(channel == column, 1.0, 0.0).astype(jnp.bfloat16)


def dense(total):
    tiles = -(-total // 128)
    moved = tiles // 4
    return (tiles - moved) * 128, moved * 128


def fold_rows(block, total):
    kept, moved = dense(total)
    tail = block[:, kept : kept + moved]
    row = lax.broadcasted_iota(jnp.int32, tail.shape, 0)
    pieces = []
    for k in range(3):
        spare = jnp.where(row == 6, pltpu.roll(tail, 6 - k, 0), pltpu.roll(tail, 4 - k, 0))
        pieces.append(jnp.where(row < 6, block[:, k * moved : (k + 1) * moved], spare))
    return jnp.concatenate(pieces + [block[:, 3 * moved : kept]], axis=1)


def unfold_rows(block, total):
    kept, moved = dense(total)
    row = lax.broadcasted_iota(jnp.int32, (8, moved), 0)
    tail = jnp.zeros((8, moved), block.dtype)
    for k in range(3):
        piece = block[:, k * moved : (k + 1) * moved]
        tail = jnp.where(row == k, pltpu.roll(piece, 2 + k, 0), tail)
        tail = jnp.where(row == 3 + k, pltpu.roll(piece, 4 + k, 0), tail)
    return jnp.concatenate([block, tail], axis=1)[:, :total]


def prepare_kernel(features, cot, mask, first, masked_ref, cot_ref, live_ref, near_ref, far_ref):
    width, rows, channels = features.shape
    f32 = jnp.float32
    flat = mask[...].astype(f32).reshape(width * rows // DEPTH, DEPTH)
    live = jnp.broadcast_to(flat[:, :, None], flat.shape + (channels,)).reshape(features.shape)
    live_ref[...] = live[:, :, :128]
    masked_ref[...] = (features[...].astype(f32) * live).astype(jnp.bfloat16)
    cot_ref[...] = (cot[...].astype(f32) * live).astype(jnp.bfloat16)
    odd = lax.rem(position()[2], 2)
    for ref, upper in ((near_ref, 1 - odd), (far_ref, odd)):
        ref[0:2] = masked_ref[pl.ds(upper * (width - 2), 2)]
        ref[2:3] = cot_ref[pl.ds(upper * (width - 1), 1)]


def rows_of_128(masked, out_ref):
    width = masked.shape[0]
    half = width // 2
    rest = jnp.concatenate([masked[:half, :, 128:], masked[half:, :, 128:]], axis=2)
    out_ref[:width] = masked[:, :, :128]
    out_ref[width : width + half] = rest


def pack_kernel(masked, after, packed_ref):
    rows_of_128(masked, packed_ref)


def across_kernel(masked, cot, across_ref):
    width, rows, channels = masked.shape
    rows_of_128(masked, across_ref)
    count = across_ref.shape[0] - 2
    ahead = position()[3] == 0
    grown = cot[...].astype(jnp.float32)
    strip = jnp.where(ahead, grown[:, rows - DEPTH :], grown[:, :DEPTH])
    strip = strip.reshape(width * DEPTH, channels)
    rest = jnp.concatenate([strip[:, 128:], jnp.zeros_like(strip[:, 128:])], axis=1)
    across_ref[count] = strip[:, :128].astype(jnp.bfloat16)
    across_ref[count + 1] = rest.astype(jnp.bfloat16)


def corner_kernel(near, far, out_ref, edge):
    _, rows, channels = near.shape
    _, _, quad, side = position()
    odd = lax.rem(quad, 2)
    edge[odd] = far[...]
    edge[1 - odd] = near[...]
    halo = 2 * DEPTH
    ahead = side == 0
    held = edge[...].astype(jnp.float32)
    strip = jnp.where(ahead, held[:, :2, rows - halo :], held[:, :2, :halo])
    cots = jnp.where(ahead, held[:, 2, rows - DEPTH :], held[:, 2, :DEPTH])
    out_ref[: 4 * halo] = strip.reshape(4 * halo, channels).astype(jnp.bfloat16)
    out_ref[4 * halo :] = cots.reshape(2 * DEPTH, channels).astype(jnp.bfloat16)


def turn_kernel(weight, out_ref):
    step = 2 * weight.shape[0]
    total = weight.shape[1]
    for start in range(0, total, step):
        stop = min(start + step, total)
        out_ref[start:stop, :] = weight[:, start:stop].T


def forward_kernel(
    masked, cot, near, far, across, corner, live, weight, pick, *refs
):
    act_ref, gp_ref = refs[:2]
    slice_refs = refs[2 : 2 + len(CHIPS)]
    ext, edge, cols, slices = refs[2 + len(CHIPS) :]
    width, rows, channels = masked.shape
    f32 = jnp.float32
    plane, me, quad, side = position()
    use_low = side.astype(f32)
    use_high = (1 - side).astype(f32)
    place = plane * QUAD + quad
    use_left = (place > 0).astype(f32)
    use_right = (place < QUAD * lax.axis_size("depth") - 1).astype(f32)
    halo = 2 * DEPTH
    tall = rows + 2 * halo
    mid = rows + 2 * DEPTH
    span = width + 4
    odd = lax.rem(quad, 2)
    edge[odd] = far[...]
    edge[1 - odd] = near[...]
    left, right = edge[0].astype(f32) * use_left, edge[1].astype(f32) * use_right
    corners = corner[: 4 * halo].astype(f32).reshape(2, 2, halo, channels)
    lower, upper = corners[0] * use_left, corners[1] * use_right
    ends = corner[4 * halo :].astype(f32).reshape(2, 1, DEPTH, channels)
    ext[0:2, halo : halo + rows, :] = left[0:2]
    ext[2 : 2 + width, halo : halo + rows, :] = masked[...].astype(f32)
    ext[2 + width :, halo : halo + rows, :] = right[0:2]
    half = width // 2
    ahead = side == 0
    held = across[...].astype(f32)
    brick = jnp.where(ahead, held[: width + half, :halo], held[: width + half, rows - halo :])
    rest = jnp.concatenate([brick[width:, :, :64], brick[width:, :, 64:]], axis=0)
    beside = jnp.concatenate([brick[:width], rest], axis=2)
    for use, start in ((use_low, 0), (use_high, halo + rows)):
        at = slice(start, start + halo)
        ext[0:2, at, :] = lower * use
        ext[2 : 2 + width, at, :] = beside * use
        ext[2 + width :, at, :] = upper * use
    field = ext[...].reshape(span * tall // DEPTH, DEPTH, channels)
    for c in OFFSETS:
        moved = shift_z(field, c).reshape(span, tall, channels)
        for b in OFFSETS:
            at = ((b + 1) * 3 + c + 1) * channels
            start = DEPTH * (b + 1)
            cols[:, :, at : at + channels] = moved[:, start : start + mid].astype(jnp.bfloat16)
    nine = 9 * channels
    pre = jnp.zeros(((width + 2) * mid, channels), f32)
    for a in range(3):
        pre += jnp.dot(
            cols[a : a + width + 2].reshape((width + 2) * mid, nine),
            weight[a * nine : (a + 1) * nine, :],
            preferred_element_type=f32,
        )
    sig = jax.nn.sigmoid(pre)
    act = (pre * sig).reshape(width + 2, mid, channels)[1 : 1 + width, DEPTH : DEPTH + rows]
    act_ref[...] = (act * live[:, :, 0:1]).astype(jnp.bfloat16)
    slope = (sig * (1.0 + pre * (1.0 - sig))).reshape(width + 2, mid, channels)
    beyond = jnp.concatenate(
        [
            ends[0] * use_left,
            jnp.concatenate([held[width + half], held[width + half + 1, :, :64]], axis=1).reshape(
                width, DEPTH, channels
            ),
            ends[1] * use_right,
        ],
        axis=0,
    )
    centre = jnp.concatenate([left[2:3], cot[...].astype(f32), right[2:3]], axis=0)
    full = jnp.concatenate([beyond * use_low, centre, beyond * use_high], axis=1)
    grad = full * slope
    gp_ref[...] = grad.astype(jnp.bfloat16)
    inner = grad[:, DEPTH : DEPTH + rows].astype(jnp.bfloat16)
    turned = lax.dot_general(
        pick[...],
        inner.reshape((width + 2) * rows, channels),
        (((1,), (1,)), ((), ())),
        preferred_element_type=f32,
    )
    slices[...] = turned.reshape(slices.shape)
    chip = me - lax.rem(quad, 2) * SIDES
    for distance, ref in zip(CHIPS, slice_refs):
        both = [slices[chip ^ distance], slices[(chip ^ distance) + SIDES]]
        ref[...] = jnp.concatenate(both, axis=0).astype(jnp.bfloat16)


def input_kernel(gp, live, turned, out_ref, cols, weight):
    width, rows, channels = out_ref.shape
    f32 = jnp.float32
    tall = rows + 2 * DEPTH
    for tap in range(27):
        weight[tap * channels : (tap + 1) * channels, :] = turned[
            :, tap * channels : (tap + 1) * channels
        ]
    field = gp[...].astype(f32).reshape((width + 2) * tall // DEPTH, DEPTH, channels)
    for c in OFFSETS:
        moved = shift_z(field, -c).reshape(width + 2, tall, channels)
        for b in OFFSETS:
            at = ((b + 1) * 3 + c + 1) * channels
            start = DEPTH * (1 - b)
            cols[:, :, at : at + channels] = moved[:, start : start + rows].astype(jnp.bfloat16)
    nine = 9 * channels
    total = jnp.zeros((width * rows, channels), f32)
    for a in range(3):
        total += jnp.dot(
            cols[2 - a : 2 - a + width].reshape(width * rows, nine),
            weight[a * nine : (a + 1) * nine, :],
            preferred_element_type=f32,
        )
    out_ref[...] = (total.reshape(width, rows, channels) * live[:, :, 0:1]).astype(jnp.bfloat16)


def kernel_grad_kernel(*refs):
    chips = len(CHIPS)
    received, bricks = refs[:chips], refs[chips : 2 * chips]
    keep_ref, send_ref, slices, cols, part, masked = refs[2 * chips :]
    f32 = jnp.float32
    group, lanes = received[0].shape
    blocks, per, lane, channels = masked.shape
    half = lane // 2
    _, _, quad, side = position()
    for i, distance in enumerate(CHIPS):
        block, sided = distance // 4, side ^ (distance % 2)
        slices[block, sided] = received[i][...]
        at_rows = pl.ds(pl.multiple_of(sided * half, half), half)
        for x in range(per):
            shift = 64 * (x // (per // 2))
            rest = bricks[i][per + x % (per // 2)]
            masked[block, x, at_rows, :128] = bricks[i][x]
            masked[block, x, at_rows, 128:] = rest[:, shift : shift + 64]
    at = lax.broadcasted_iota(jnp.int32, (group, lane), 1)
    y, z = at // DEPTH, at % DEPTH
    tall = lane // DEPTH
    for block in range(blocks):
        first = slices[block, 0].astype(f32)
        second = slices[block, 1].astype(f32)
        for k in range(per + 2):
            one = first[:, k // 2 * lane : (k // 2 + 1) * lane]
            two = second[:, k // 2 * lane : (k // 2 + 1) * lane]
            if k % 2 == 0:
                base = jnp.where(at < half, one, pltpu.roll(two, half, 1))
            else:
                base = jnp.where(at < half, pltpu.roll(one, half, 1), two)
            pieces = []
            for b in OFFSETS:
                for c in OFFSETS:
                    step = (DEPTH * b + c) % lane
                    moved = base if step == 0 else pltpu.roll(base, step, 1)
                    keep = (y - b >= 0) & (y - b < tall) & (z - c >= 0) & (z - c < DEPTH)
                    pieces.append(jnp.where(keep, moved, 0.0))
            slab = block * (per + 2) + k
            cols[:, slab * lane : (slab + 1) * lane] = jnp.concatenate(pieces, axis=0).astype(
                jnp.bfloat16
            )
    for a in range(3):
        got = jnp.zeros((cols.shape[0], channels), f32)
        for block in range(blocks):
            start = (block * (per + 2) + 2 - a) * lane
            got += jnp.dot(
                cols[:, start : start + per * lane],
                masked[block].reshape(per * lane, channels),
                preferred_element_type=f32,
            )
        got = got.reshape(9, group, channels)
        part[:, a * 9 * channels : (a + 1) * 9 * channels] = jnp.concatenate(
            [got[tap] for tap in range(9)], axis=1
        )
    core = lax.rem(quad, 2)
    half = group // 2
    keep_ref[...] = part[pl.ds(pl.multiple_of(core * half, 8), half)]
    send_ref[...] = part[pl.ds(pl.multiple_of((1 - core) * half, 8), half)].astype(jnp.bfloat16)


def fold_kernel(keep, other, own_ref, *refs):
    *send_refs, both, rows = refs
    planes, eight, _ = rows.shape
    count, total = keep.shape
    share = count // planes
    both[:count, :total] = keep[...] + other[...].astype(jnp.float32)
    both[:, total:] = jnp.zeros((both.shape[0], both.shape[1] - total), jnp.float32)
    for to in range(planes):
        rows[to] = fold_rows(both[share * to : share * to + eight, :], total)
    plane = position()[0]
    own_ref[...] = rows[plane]
    for distance, ref in enumerate(send_refs, 1):
        ref[...] = rows[plane ^ distance].astype(jnp.bfloat16)


def sum_kernel(scale, own, one, two, three, out_ref):
    f32 = jnp.float32
    total = own[...] + one[...].astype(f32) + two[...].astype(f32) + three[...].astype(f32)
    out_ref[...] = (total * scale).astype(out_ref.dtype)


def join_kernel(mine, other, out_ref):
    share = out_ref.shape[0] // SIDES
    ahead = position()[3] == 0
    total = out_ref.shape[1]
    here = unfold_rows(mine[...].astype(jnp.float32), total)
    there = unfold_rows(other[...].astype(jnp.float32), total)
    first = jnp.where(ahead, here, there)
    second = jnp.where(ahead, there, here)
    out_ref[0:share] = first[:share]
    out_ref[share:] = second[:share]


def call(body, name, mebibytes, flops, moved, out_shape, scratch=(), in_specs=None):
    spec = pl.BlockSpec(memory_space=pltpu.VMEM)

    def run(*operands):
        return pl.pallas_call(
            body,
            out_shape=out_shape,
            in_specs=in_specs or [spec] * len(operands),
            out_specs=jax.tree.map(lambda _: spec, out_shape),
            scratch_shapes=scratch,
            compiler_params=pltpu.CompilerParams(vmem_limit_bytes=mebibytes << 20),
            cost_estimate=pl.CostEstimate(flops=flops, bytes_accessed=moved, transcendentals=0),
            name=name,
        )(*operands)

    return run


def planes_local(features, weight, voxel_mask, cotangent):
    bf16 = jnp.bfloat16
    f32 = jnp.float32
    array = jax.ShapeDtypeStruct
    width, wide_y, depth, channels = features.shape
    rows = wide_y * depth
    planes = lax.axis_size("depth")
    count = planes * QUAD
    total = 27 * channels
    halo = 2 * DEPTH
    span = (width + 2) * rows
    share = channels // count // SIDES
    group = planes * share

    def swap(piece, axes, distance, size):
        return lax.ppermute(piece, axes, [(i, i ^ distance) for i in range(size)])

    def in_plane(piece, distance):
        return swap(piece, ("quad", "narrow"), distance, MEMBERS)

    brick = array((width, rows, channels), bf16)
    slab = array((3, rows, channels), bf16)
    pick = call(
        functools.partial(pick_kernel, planes), "pick", 4, 1 << 32, 1 << 16,
        array((MEMBERS * group, channels), bf16),
    )()
    vmem = pl.BlockSpec(memory_space=pltpu.VMEM)
    masked, cot, live, near, far = call(
        prepare_kernel, "prepare", 16, 1 << 20, 1 << 20,
        (brick, brick, array((width, rows, 128), f32), slab, slab),
        (),
        [vmem] * 3 + [pl.BlockSpec(memory_space=pl.ANY)],
    )(
        features.reshape(width, rows, channels),
        cotangent.reshape(width, rows, channels),
        voxel_mask,
        pick,
    )
    near = swap(near, WIDE, 1, count)
    steps = [(i, i + 2 - 4 * (i % 2)) for i in range(count)]
    steps = [(i, j) for i, j in steps if 0 <= j < count]
    far = lax.ppermute(swap(far, WIDE, 1, count), WIDE, steps)
    weight_rows = call(
        turn_kernel, "turn", 8, 1 << 20, 4 << 20, array((total, channels), bf16)
    )(weight.T)
    slabs = width * channels // 128
    across = call(
        across_kernel, "across", 4, 1 << 16, 1 << 19, array((slabs + 2, rows, 128), bf16)
    )(masked, cot)
    across = in_plane(across, CHIPS[1])
    packed = call(
        pack_kernel, "pack", 4, 1 << 16, 1 << 19, array((slabs, rows, 128), bf16), (),
        [vmem, pl.BlockSpec(memory_space=pl.ANY)],
    )(masked, weight_rows)
    near, far, weight_rows, late = lax.optimization_barrier((near, far, weight_rows, packed))
    corner = call(
        corner_kernel, "corner", 4, 1 << 16, 1 << 18,
        array((4 * halo + 2 * DEPTH, channels), bf16),
        (pltpu.VMEM((2,) + slab.shape, bf16),),
    )(near, far)
    corner = in_plane(corner, 1)
    bricks = [packed, across, in_plane(packed, CHIPS[2]), in_plane(late, CHIPS[3])]

    mid = rows + 2 * DEPTH
    act, gp, *slices = call(
        forward_kernel, "forward", 28, 3 << 29, 1 << 20,
        (brick, array((width + 2, mid, channels), bf16))
        + (array((2 * group, span), bf16),) * len(CHIPS),
        (
            pltpu.VMEM((width + 4, rows + 2 * halo, channels), f32),
            pltpu.VMEM((2,) + slab.shape, bf16),
            pltpu.VMEM((width + 4, mid, 9 * channels), bf16),
            pltpu.VMEM((MEMBERS, group, span), f32),
        ),
    )(masked, cot, near, far, across, corner, live, weight_rows, pick)
    bricks[2], *slices = lax.optimization_barrier((bricks[2], *slices))
    slices = [slices[0]] + [in_plane(part, d) for part, d in zip(slices[1:], CHIPS[1:])]

    grad_input = call(
        input_kernel, "input_gradient", 20, 2 * 512 * 5184 * 256, 4 << 20, brick,
        (
            pltpu.VMEM((width + 2, rows, 9 * channels), bf16),
            pltpu.VMEM((total, channels), bf16),
        ),
    )(gp, live, weight.T)

    blocks = QUAD // 2
    chips = len(CHIPS)
    lanes = dense(total)[0]
    keep, fold = call(
        kernel_grad_kernel, "kernel_gradient", 28, 2 * 432 * 3 * 2048 * 256, 4 << 20,
        (array((group, total), f32), array((group, total), bf16)),
        (
            pltpu.VMEM((blocks, SIDES, 2 * group, span), bf16),
            pltpu.VMEM((9 * 2 * group, blocks * (width + 2) * SIDES * rows), bf16),
            pltpu.VMEM((2 * group, total), f32),
            pltpu.VMEM((blocks, width, SIDES * rows, channels), bf16),
        ),
    )(*slices, *bricks)
    own, *sends = call(
        fold_kernel, "fold", 8, 8 * total * 4, 8 * total * 40,
        (array((8, lanes), f32),) + (array((8, lanes), bf16),) * (planes - 1),
        (
            pltpu.VMEM((group + 8, sum(dense(total))), f32),
            pltpu.VMEM((planes, 8, lanes), f32),
        ),
    )(keep, in_plane(fold, 2))
    got = [swap(sent, "depth", d, planes) for d, sent in list(enumerate(sends, 1))[::-1]]
    grad_input, *got = lax.optimization_barrier((grad_input, *got))
    voxels = count * SIDES * width * rows
    mine = call(
        functools.partial(sum_kernel, float(1.0 / voxels**0.5)),
        "plane_sum", 4, 8 * total * 4, 8 * total * 14, array((8, lanes), bf16),
    )(own, *got)
    grad_weight = call(
        join_kernel, "join", 4, 8 * total, 8 * total * 14, array((channels // count, total), f32)
    )(mine, in_plane(mine, 1))
    shape = features.shape
    return act.reshape(shape), grad_input.reshape(shape), grad_weight


def padded_2(cells, sides, width):
    for axis, dim in sides:
        count = lax.axis_size(axis)
        ends = count - 1
        head = lax.slice_in_dim(cells, 0, width, axis=dim)
        tail = lax.slice_in_dim(cells, cells.shape[dim] - width, cells.shape[dim], axis=dim)
        cells = jnp.concatenate(
            [
                lax.ppermute(tail, axis, [(i, (i + 1) % count) for i in range(ends)]),
                cells,
                lax.ppermute(head, axis, [((i + 1) % count, i) for i in range(ends)]),
            ],
            axis=dim,
        )
    return cells


def gather_taps(padded, width_x, width_y, depth_z, channels, flip):
    pieces = []
    for shift_x in range(3):
        for shift_y in range(3):
            for shift_z in range(3):
                start_x = 2 - shift_x if flip else shift_x
                start_y = 2 - shift_y if flip else shift_y
                start_z = 2 - shift_z if flip else shift_z
                piece = padded[
                    start_x : start_x + width_x,
                    start_y : start_y + width_y,
                    start_z : start_z + depth_z,
                    :,
                ]
                pieces.append(piece.reshape(-1, channels))
    return jnp.concatenate(pieces, axis=1)


def summed_local(features, weight, voxel_mask, cotangent):
    width_x, width_y, depth_z, channels = features.shape
    masked = features * voxel_mask.astype(jnp.bfloat16)[..., None]
    padded = padded_2(masked, (("wide", 0), ("narrow", 1)), 1)
    padded = jnp.pad(padded, ((0, 0), (0, 0), (1, 1), (0, 0)))
    columns = gather_taps(padded, width_x, width_y, depth_z, channels, False)
    pre = jnp.dot(columns, weight, preferred_element_type=jnp.float32)
    live = voxel_mask.reshape(-1, 1).astype(jnp.float32)
    sig = jax.nn.sigmoid(pre)
    activation = (
        (pre * sig * live).astype(jnp.bfloat16).reshape(width_x, width_y, depth_z, channels)
    )
    slope = sig * (1.0 + pre * (1.0 - sig))
    grad_pre = (cotangent.reshape(-1, channels).astype(jnp.float32) * live * slope).astype(
        jnp.bfloat16
    )
    taps = weight.reshape(27, channels, channels)
    grid = grad_pre.reshape(width_x, width_y, depth_z, channels)
    grad_pad = padded_2(grid, (("wide", 0), ("narrow", 1)), 1)
    grad_pad = jnp.pad(grad_pad, ((0, 0), (0, 0), (1, 1), (0, 0)))
    grad_columns = gather_taps(grad_pad, width_x, width_y, depth_z, channels, True)
    flipped = jnp.transpose(taps, (0, 2, 1)).reshape(27 * channels, channels)
    grad_field = jnp.dot(grad_columns, flipped, preferred_element_type=jnp.float32)
    grad_input = (
        (grad_field * live).astype(jnp.bfloat16).reshape(width_x, width_y, depth_z, channels)
    )
    scale = 1.0 / jnp.sqrt(
        jnp.float32(width_x * width_y * depth_z * lax.axis_size("wide") * lax.axis_size("narrow"))
    )
    whole = lax.dot_general(
        grad_pre, columns, (((0,), (0,)), ((), ())), preferred_element_type=jnp.float32
    )
    piece_flat = lax.psum_scatter(
        whole.reshape(-1), ("wide", "narrow"), scatter_dimension=0, tiled=True
    )
    gathered = lax.all_gather(piece_flat, "narrow", axis=0, tiled=True)
    summed = gathered.reshape(channels // lax.axis_size("wide"), 27 * channels)
    grad_weight = summed * scale
    return (activation, grad_input, grad_weight)


def sharded(body, mesh, wide):
    return jax.shard_map(
        body,
        mesh=mesh,
        in_specs=(
            P(wide, "narrow", None, None),
            P(),
            P(wide, "narrow", None),
            P(wide, "narrow", None, None),
        ),
        out_specs=(
            P(wide, "narrow", None, None),
            P(wide, "narrow", None, None),
            P(wide, None),
        ),
        check_vma=False,
    )


def solution(mesh):
    wide, narrow = mesh.shape["wide"], mesh.shape["narrow"]
    if wide != 4 * QUAD or narrow != SIDES:
        return sharded(summed_local, mesh, "wide")
    planes = Mesh(
        mesh.devices.reshape(wide // QUAD, QUAD, narrow), ("depth", "quad", "narrow")
    )
    return sharded(planes_local, planes, WIDE)
```

```python
import functools

import jax
import jax.numpy as jnp
from jax import lax
from jax.experimental import pallas as pl
from jax.experimental.pallas import tpu as pltpu
from jax.sharding import Mesh
from jax.sharding import PartitionSpec as P

WIDE = ("depth", "quad")
QUAD = 4
SIDES = 2
MEMBERS = QUAD * SIDES
CHIPS = (0, 1, 4, 5)
OFFSETS = (-1, 0, 1)
DEPTH = 8


def position():
    quad, side = lax.axis_index("quad"), lax.axis_index("narrow")
    return lax.axis_index("depth"), quad * SIDES + side, quad, side


def shift_z(field, step):
    if step == 0:
        return field
    depth = field.shape[1]
    moved = pltpu.roll(field, (-step) % depth, 1)
    z = lax.broadcasted_iota(jnp.int32, field.shape, 1) + step
    return jnp.where((z >= 0) & (z < depth), moved, 0.0)


def pick_kernel(planes, out_ref):
    index = lax.broadcasted_iota(jnp.int32, out_ref.shape, 0)
    column = lax.broadcasted_iota(jnp.int32, out_ref.shape, 1)
    per = out_ref.shape[1] // (planes * QUAD)
    share = per // SIDES
    group = planes * share
    quad, side = index // (SIDES * group), index // group % SIDES
    plane, row = index // share % planes, index % share
    channel = per * (QUAD * plane + quad) + share * side + row
    out_ref[...] = jnp.where(channel == column, 1.0, 0.0).astype(jnp.bfloat16)


def dense(total):
    tiles = -(-total // 128)
    moved = tiles // 4
    return (tiles - moved) * 128, moved * 128


def fold_rows(block, total):
    kept, moved = dense(total)
    tail = block[:, kept : kept + moved]
    row = lax.broadcasted_iota(jnp.int32, tail.shape, 0)
    pieces = []
    for k in range(3):
        spare = jnp.where(row == 6, pltpu.roll(tail, 6 - k, 0), pltpu.roll(tail, 4 - k, 0))
        pieces.append(jnp.where(row < 6, block[:, k * moved : (k + 1) * moved], spare))
    return jnp.concatenate(pieces + [block[:, 3 * moved : kept]], axis=1)


def unfold_rows(block, total):
    kept, moved = dense(total)
    row = lax.broadcasted_iota(jnp.int32, (8, moved), 0)
    tail = jnp.zeros((8, moved), block.dtype)
    for k in range(3):
        piece = block[:, k * moved : (k + 1) * moved]
        tail = jnp.where(row == k, pltpu.roll(piece, 2 + k, 0), tail)
        tail = jnp.where(row == 3 + k, pltpu.roll(piece, 4 + k, 0), tail)
    return jnp.concatenate([block, tail], axis=1)[:, :total]


def prepare_kernel(features, cot, mask, first, masked_ref, cot_ref, live_ref, near_ref, far_ref):
    width, rows, channels = features.shape
    f32 = jnp.float32
    flat = mask[...].astype(f32).reshape(width * rows // DEPTH, DEPTH)
    live = jnp.broadcast_to(flat[:, :, None], flat.shape + (channels,)).reshape(features.shape)
    live_ref[...] = live[:, :, :128]
    masked_ref[...] = (features[...].astype(f32) * live).astype(jnp.bfloat16)
    cot_ref[...] = (cot[...].astype(f32) * live).astype(jnp.bfloat16)
    odd = lax.rem(position()[2], 2)
    for ref, upper in ((near_ref, 1 - odd), (far_ref, odd)):
        ref[0:2] = masked_ref[pl.ds(upper * (width - 2), 2)]
        ref[2:3] = cot_ref[pl.ds(upper * (width - 1), 1)]


def rows_of_128(masked, out_ref):
    width = masked.shape[0]
    half = width // 2
    rest = jnp.concatenate([masked[:half, :, 128:], masked[half:, :, 128:]], axis=2)
    out_ref[:width] = masked[:, :, :128]
    out_ref[width : width + half] = rest


def pack_kernel(masked, after, packed_ref):
    rows_of_128(masked, packed_ref)


def across_kernel(masked, cot, across_ref):
    width, rows, channels = masked.shape
    rows_of_128(masked, across_ref)
    count = across_ref.shape[0] - 2
    ahead = position()[3] == 0
    grown = cot[...].astype(jnp.float32)
    strip = jnp.where(ahead, grown[:, rows - DEPTH :], grown[:, :DEPTH])
    strip = strip.reshape(width * DEPTH, channels)
    rest = jnp.concatenate([strip[:, 128:], jnp.zeros_like(strip[:, 128:])], axis=1)
    across_ref[count] = strip[:, :128].astype(jnp.bfloat16)
    across_ref[count + 1] = rest.astype(jnp.bfloat16)


def corner_kernel(near, far, out_ref, edge):
    _, rows, channels = near.shape
    _, _, quad, side = position()
    odd = lax.rem(quad, 2)
    edge[odd] = far[...]
    edge[1 - odd] = near[...]
    halo = 2 * DEPTH
    ahead = side == 0
    held = edge[...].astype(jnp.float32)
    strip = jnp.where(ahead, held[:, :2, rows - halo :], held[:, :2, :halo])
    cots = jnp.where(ahead, held[:, 2, rows - DEPTH :], held[:, 2, :DEPTH])
    out_ref[: 4 * halo] = strip.reshape(4 * halo, channels).astype(jnp.bfloat16)
    out_ref[4 * halo :] = cots.reshape(2 * DEPTH, channels).astype(jnp.bfloat16)


def turn_kernel(weight, out_ref):
    step = 2 * weight.shape[0]
    total = weight.shape[1]
    for start in range(0, total, step):
        stop = min(start + step, total)
        out_ref[start:stop, :] = weight[:, start:stop].T


def forward_kernel(
    masked, cot, near, far, across, corner, live, weight, pick, *refs
):
    act_ref, gp_ref = refs[:2]
    slice_refs = refs[2 : 2 + len(CHIPS)]
    ext, edge, cols, slices = refs[2 + len(CHIPS) :]
    width, rows, channels = masked.shape
    f32 = jnp.float32
    plane, me, quad, side = position()
    use_low = side.astype(f32)
    use_high = (1 - side).astype(f32)
    place = plane * QUAD + quad
    use_left = (place > 0).astype(f32)
    use_right = (place < QUAD * lax.axis_size("depth") - 1).astype(f32)
    halo = 2 * DEPTH
    tall = rows + 2 * halo
    mid = rows + 2 * DEPTH
    span = width + 4
    odd = lax.rem(quad, 2)
    edge[odd] = far[...]
    edge[1 - odd] = near[...]
    left, right = edge[0].astype(f32) * use_left, edge[1].astype(f32) * use_right
    corners = corner[: 4 * halo].astype(f32).reshape(2, 2, halo, channels)
    lower, upper = corners[0] * use_left, corners[1] * use_right
    ends = corner[4 * halo :].astype(f32).reshape(2, 1, DEPTH, channels)
    ext[0:2, halo : halo + rows, :] = left[0:2]
    ext[2 : 2 + width, halo : halo + rows, :] = masked[...].astype(f32)
    ext[2 + width :, halo : halo + rows, :] = right[0:2]
    half = width // 2
    ahead = side == 0
    held = across[...].astype(f32)
    brick = jnp.where(ahead, held[: width + half, :halo], held[: width + half, rows - halo :])
    rest = jnp.concatenate([brick[width:, :, :64], brick[width:, :, 64:]], axis=0)
    beside = jnp.concatenate([brick[:width], rest], axis=2)
    for use, start in ((use_low, 0), (use_high, halo + rows)):
        at = slice(start, start + halo)
        ext[0:2, at, :] = lower * use
        ext[2 : 2 + width, at, :] = beside * use
        ext[2 + width :, at, :] = upper * use
    field = ext[...].reshape(span * tall // DEPTH, DEPTH, channels)
    for c in OFFSETS:
        moved = shift_z(field, c).reshape(span, tall, channels)
        for b in OFFSETS:
            at = ((b + 1) * 3 + c + 1) * channels
            start = DEPTH * (b + 1)
            cols[:, :, at : at + channels] = moved[:, start : start + mid].astype(jnp.bfloat16)
    nine = 9 * channels
    pre = jnp.zeros(((width + 2) * mid, channels), f32)
    for a in range(3):
        pre += jnp.dot(
            cols[a : a + width + 2].reshape((width + 2) * mid, nine),
            weight[a * nine : (a + 1) * nine, :],
            preferred_element_type=f32,
        )
    sig = jax.nn.sigmoid(pre)
    act = (pre * sig).reshape(width + 2, mid, channels)[1 : 1 + width, DEPTH : DEPTH + rows]
    act_ref[...] = (act * live[:, :, 0:1]).astype(jnp.bfloat16)
    slope = (sig * (1.0 + pre * (1.0 - sig))).reshape(width + 2, mid, channels)
    beyond = jnp.concatenate(
        [
            ends[0] * use_left,
            jnp.concatenate([held[width + half], held[width + half + 1, :, :64]], axis=1).reshape(
                width, DEPTH, channels
            ),
            ends[1] * use_right,
        ],
        axis=0,
    )
    centre = jnp.concatenate([left[2:3], cot[...].astype(f32), right[2:3]], axis=0)
    full = jnp.concatenate([beyond * use_low, centre, beyond * use_high], axis=1)
    grad = full * slope
    gp_ref[...] = grad.astype(jnp.bfloat16)
    inner = grad[:, DEPTH : DEPTH + rows].astype(jnp.bfloat16)
    turned = lax.dot_general(
        pick[...],
        inner.reshape((width + 2) * rows, channels),
        (((1,), (1,)), ((), ())),
        preferred_element_type=f32,
    )
    slices[...] = turned.reshape(slices.shape)
    chip = me - lax.rem(quad, 2) * SIDES
    for distance, ref in zip(CHIPS, slice_refs):
        both = [slices[chip ^ distance], slices[(chip ^ distance) + SIDES]]
        ref[...] = jnp.concatenate(both, axis=0).astype(jnp.bfloat16)


def input_kernel(gp, live, turned, out_ref, cols, weight):
    width, rows, channels = out_ref.shape
    f32 = jnp.float32
    tall = rows + 2 * DEPTH
    for tap in range(27):
        weight[tap * channels : (tap + 1) * channels, :] = turned[
            :, tap * channels : (tap + 1) * channels
        ]
    field = gp[...].astype(f32).reshape((width + 2) * tall // DEPTH, DEPTH, channels)
    for c in OFFSETS:
        moved = shift_z(field, -c).reshape(width + 2, tall, channels)
        for b in OFFSETS:
            at = ((b + 1) * 3 + c + 1) * channels
            start = DEPTH * (1 - b)
            cols[:, :, at : at + channels] = moved[:, start : start + rows].astype(jnp.bfloat16)
    nine = 9 * channels
    total = jnp.zeros((width * rows, channels), f32)
    for a in range(3):
        total += jnp.dot(
            cols[2 - a : 2 - a + width].reshape(width * rows, nine),
            weight[a * nine : (a + 1) * nine, :],
            preferred_element_type=f32,
        )
    out_ref[...] = (total.reshape(width, rows, channels) * live[:, :, 0:1]).astype(jnp.bfloat16)


def kernel_grad_kernel(*refs):
    chips = len(CHIPS)
    received, bricks = refs[:chips], refs[chips : 2 * chips]
    keep_ref, send_ref, slices, cols, part, masked = refs[2 * chips :]
    f32 = jnp.float32
    group, lanes = received[0].shape
    blocks, per, lane, channels = masked.shape
    half = lane // 2
    _, _, quad, side = position()
    for i, distance in enumerate(CHIPS):
        block, sided = distance // 4, side ^ (distance % 2)
        slices[block, sided] = received[i][...]
        at_rows = pl.ds(pl.multiple_of(sided * half, half), half)
        for x in range(per):
            shift = 64 * (x // (per // 2))
            rest = bricks[i][per + x % (per // 2)]
            masked[block, x, at_rows, :128] = bricks[i][x]
            masked[block, x, at_rows, 128:] = rest[:, shift : shift + 64]
    at = lax.broadcasted_iota(jnp.int32, (group, lane), 1)
    y, z = at // DEPTH, at % DEPTH
    tall = lane // DEPTH
    for block in range(blocks):
        first = slices[block, 0].astype(f32)
        second = slices[block, 1].astype(f32)
        for k in range(per + 2):
            one = first[:, k // 2 * lane : (k // 2 + 1) * lane]
            two = second[:, k // 2 * lane : (k // 2 + 1) * lane]
            if k % 2 == 0:
                base = jnp.where(at < half, one, pltpu.roll(two, half, 1))
            else:
                base = jnp.where(at < half, pltpu.roll(one, half, 1), two)
            pieces = []
            for b in OFFSETS:
                for c in OFFSETS:
                    step = (DEPTH * b + c) % lane
                    moved = base if step == 0 else pltpu.roll(base, step, 1)
                    keep = (y - b >= 0) & (y - b < tall) & (z - c >= 0) & (z - c < DEPTH)
                    pieces.append(jnp.where(keep, moved, 0.0))
            slab = block * (per + 2) + k
            cols[:, slab * lane : (slab + 1) * lane] = jnp.concatenate(pieces, axis=0).astype(
                jnp.bfloat16
            )
    for a in range(3):
        got = jnp.zeros((cols.shape[0], channels), f32)
        for block in range(blocks):
            start = (block * (per + 2) + 2 - a) * lane
            got += jnp.dot(
                cols[:, start : start + per * lane],
                masked[block].reshape(per * lane, channels),
                preferred_element_type=f32,
            )
        got = got.reshape(9, group, channels)
        part[:, a * 9 * channels : (a + 1) * 9 * channels] = jnp.concatenate(
            [got[tap] for tap in range(9)], axis=1
        )
    core = lax.rem(quad, 2)
    half = group // 2
    keep_ref[...] = part[pl.ds(pl.multiple_of(core * half, 8), half)]
    send_ref[...] = part[pl.ds(pl.multiple_of((1 - core) * half, 8), half)].astype(jnp.bfloat16)


def fold_kernel(keep, other, own_ref, *refs):
    *send_refs, both, rows = refs
    planes, eight, _ = rows.shape
    count, total = keep.shape
    share = count // planes
    both[:count, :total] = keep[...] + other[...].astype(jnp.float32)
    both[:, total:] = jnp.zeros((both.shape[0], both.shape[1] - total), jnp.float32)
    for to in range(planes):
        rows[to] = fold_rows(both[share * to : share * to + eight, :], total)
    plane = position()[0]
    own_ref[...] = rows[plane]
    for distance, ref in enumerate(send_refs, 1):
        ref[...] = rows[plane ^ distance].astype(jnp.bfloat16)


def sum_kernel(scale, own, one, two, three, out_ref):
    f32 = jnp.float32
    total = own[...] + one[...].astype(f32) + two[...].astype(f32) + three[...].astype(f32)
    out_ref[...] = (total * scale).astype(out_ref.dtype)


def join_kernel(mine, other, out_ref):
    share = out_ref.shape[0] // SIDES
    ahead = position()[3] == 0
    total = out_ref.shape[1]
    here = unfold_rows(mine[...].astype(jnp.float32), total)
    there = unfold_rows(other[...].astype(jnp.float32), total)
    first = jnp.where(ahead, here, there)
    second = jnp.where(ahead, there, here)
    out_ref[0:share] = first[:share]
    out_ref[share:] = second[:share]


def call(body, name, mebibytes, flops, moved, out_shape, scratch=(), in_specs=None):
    spec = pl.BlockSpec(memory_space=pltpu.VMEM)

    def run(*operands):
        return pl.pallas_call(
            body,
            out_shape=out_shape,
            in_specs=in_specs or [spec] * len(operands),
            out_specs=jax.tree.map(lambda _: spec, out_shape),
            scratch_shapes=scratch,
            compiler_params=pltpu.CompilerParams(vmem_limit_bytes=mebibytes << 20),
            cost_estimate=pl.CostEstimate(flops=flops, bytes_accessed=moved, transcendentals=0),
            name=name,
        )(*operands)

    return run


def planes_local(features, weight, voxel_mask, cotangent):
    bf16 = jnp.bfloat16
    f32 = jnp.float32
    array = jax.ShapeDtypeStruct
    width, wide_y, depth, channels = features.shape
    rows = wide_y * depth
    planes = lax.axis_size("depth")
    count = planes * QUAD
    total = 27 * channels
    halo = 2 * DEPTH
    span = (width + 2) * rows
    share = channels // count // SIDES
    group = planes * share

    def swap(piece, axes, distance, size):
        return lax.ppermute(piece, axes, [(i, i ^ distance) for i in range(size)])

    def in_plane(piece, distance):
        return swap(piece, ("quad", "narrow"), distance, MEMBERS)

    brick = array((width, rows, channels), bf16)
    slab = array((3, rows, channels), bf16)
    pick = call(
        functools.partial(pick_kernel, planes), "pick", 4, 1 << 32, 1 << 16,
        array((MEMBERS * group, channels), bf16),
    )()
    vmem = pl.BlockSpec(memory_space=pltpu.VMEM)
    masked, cot, live, near, far = call(
        prepare_kernel, "prepare", 16, 1 << 20, 1 << 20,
        (brick, brick, array((width, rows, 128), f32), slab, slab),
        (),
        [vmem] * 3 + [pl.BlockSpec(memory_space=pl.ANY)],
    )(
        features.reshape(width, rows, channels),
        cotangent.reshape(width, rows, channels),
        voxel_mask,
        pick,
    )
    near = swap(near, WIDE, 1, count)
    ends = [min(max(((i + 1) ^ 1) - 1, 0), count - 1) for i in range(count)]
    far = lax.ppermute(far, WIDE, list(enumerate(ends)))
    weight_rows = call(
        turn_kernel, "turn", 8, 1 << 20, 4 << 20, array((total, channels), bf16)
    )(weight.T)
    slabs = width * channels // 128
    across = call(
        across_kernel, "across", 4, 1 << 16, 1 << 19, array((slabs + 2, rows, 128), bf16)
    )(masked, cot)
    across = in_plane(across, CHIPS[1])
    packed = call(
        pack_kernel, "pack", 4, 1 << 16, 1 << 19, array((slabs, rows, 128), bf16), (),
        [vmem, pl.BlockSpec(memory_space=pl.ANY)],
    )(masked, weight_rows)
    near, far, weight_rows, late = lax.optimization_barrier((near, far, weight_rows, packed))
    corner = call(
        corner_kernel, "corner", 4, 1 << 16, 1 << 18,
        array((4 * halo + 2 * DEPTH, channels), bf16),
        (pltpu.VMEM((2,) + slab.shape, bf16),),
    )(near, far)
    corner = in_plane(corner, 1)
    bricks = [packed, across, in_plane(packed, CHIPS[2]), in_plane(late, CHIPS[3])]

    mid = rows + 2 * DEPTH
    act, gp, *slices = call(
        forward_kernel, "forward", 28, 3 << 29, 1 << 20,
        (brick, array((width + 2, mid, channels), bf16))
        + (array((2 * group, span), bf16),) * len(CHIPS),
        (
            pltpu.VMEM((width + 4, rows + 2 * halo, channels), f32),
            pltpu.VMEM((2,) + slab.shape, bf16),
            pltpu.VMEM((width + 4, mid, 9 * channels), bf16),
            pltpu.VMEM((MEMBERS, group, span), f32),
        ),
    )(masked, cot, near, far, across, corner, live, weight_rows, pick)
    bricks[2], *slices = lax.optimization_barrier((bricks[2], *slices))
    slices = [slices[0]] + [in_plane(part, d) for part, d in zip(slices[1:], CHIPS[1:])]

    grad_input = call(
        input_kernel, "input_gradient", 20, 2 * 512 * 5184 * 256, 4 << 20, brick,
        (
            pltpu.VMEM((width + 2, rows, 9 * channels), bf16),
            pltpu.VMEM((total, channels), bf16),
        ),
    )(gp, live, weight.T)

    blocks = QUAD // 2
    chips = len(CHIPS)
    lanes = dense(total)[0]
    keep, fold = call(
        kernel_grad_kernel, "kernel_gradient", 28, 2 * 432 * 3 * 2048 * 256, 4 << 20,
        (array((group, total), f32), array((group, total), bf16)),
        (
            pltpu.VMEM((blocks, SIDES, 2 * group, span), bf16),
            pltpu.VMEM((9 * 2 * group, blocks * (width + 2) * SIDES * rows), bf16),
            pltpu.VMEM((2 * group, total), f32),
            pltpu.VMEM((blocks, width, SIDES * rows, channels), bf16),
        ),
    )(*slices, *bricks)
    own, *sends = call(
        fold_kernel, "fold", 8, 8 * total * 4, 8 * total * 40,
        (array((8, lanes), f32),) + (array((8, lanes), bf16),) * (planes - 1),
        (
            pltpu.VMEM((group + 8, sum(dense(total))), f32),
            pltpu.VMEM((planes, 8, lanes), f32),
        ),
    )(keep, in_plane(fold, 2))
    got = [swap(sent, "depth", d, planes) for d, sent in list(enumerate(sends, 1))[::-1]]
    grad_input, *got = lax.optimization_barrier((grad_input, *got))
    voxels = count * SIDES * width * rows
    mine = call(
        functools.partial(sum_kernel, float(1.0 / voxels**0.5)),
        "plane_sum", 4, 8 * total * 4, 8 * total * 14, array((8, lanes), bf16),
    )(own, *got)
    grad_weight = call(
        join_kernel, "join", 4, 8 * total, 8 * total * 14, array((channels // count, total), f32)
    )(mine, in_plane(mine, 1))
    shape = features.shape
    return act.reshape(shape), grad_input.reshape(shape), grad_weight


def padded_2(cells, sides, width):
    for axis, dim in sides:
        count = lax.axis_size(axis)
        ends = count - 1
        head = lax.slice_in_dim(cells, 0, width, axis=dim)
        tail = lax.slice_in_dim(cells, cells.shape[dim] - width, cells.shape[dim], axis=dim)
        cells = jnp.concatenate(
            [
                lax.ppermute(tail, axis, [(i, (i + 1) % count) for i in range(ends)]),
                cells,
                lax.ppermute(head, axis, [((i + 1) % count, i) for i in range(ends)]),
            ],
            axis=dim,
        )
    return cells


def gather_taps(padded, width_x, width_y, depth_z, channels, flip):
    pieces = []
    for shift_x in range(3):
        for shift_y in range(3):
            for shift_z in range(3):
                start_x = 2 - shift_x if flip else shift_x
                start_y = 2 - shift_y if flip else shift_y
                start_z = 2 - shift_z if flip else shift_z
                piece = padded[
                    start_x : start_x + width_x,
                    start_y : start_y + width_y,
                    start_z : start_z + depth_z,
                    :,
                ]
                pieces.append(piece.reshape(-1, channels))
    return jnp.concatenate(pieces, axis=1)


def summed_local(features, weight, voxel_mask, cotangent):
    width_x, width_y, depth_z, channels = features.shape
    masked = features * voxel_mask.astype(jnp.bfloat16)[..., None]
    padded = padded_2(masked, (("wide", 0), ("narrow", 1)), 1)
    padded = jnp.pad(padded, ((0, 0), (0, 0), (1, 1), (0, 0)))
    columns = gather_taps(padded, width_x, width_y, depth_z, channels, False)
    pre = jnp.dot(columns, weight, preferred_element_type=jnp.float32)
    live = voxel_mask.reshape(-1, 1).astype(jnp.float32)
    sig = jax.nn.sigmoid(pre)
    activation = (
        (pre * sig * live).astype(jnp.bfloat16).reshape(width_x, width_y, depth_z, channels)
    )
    slope = sig * (1.0 + pre * (1.0 - sig))
    grad_pre = (cotangent.reshape(-1, channels).astype(jnp.float32) * live * slope).astype(
        jnp.bfloat16
    )
    taps = weight.reshape(27, channels, channels)
    grid = grad_pre.reshape(width_x, width_y, depth_z, channels)
    grad_pad = padded_2(grid, (("wide", 0), ("narrow", 1)), 1)
    grad_pad = jnp.pad(grad_pad, ((0, 0), (0, 0), (1, 1), (0, 0)))
    grad_columns = gather_taps(grad_pad, width_x, width_y, depth_z, channels, True)
    flipped = jnp.transpose(taps, (0, 2, 1)).reshape(27 * channels, channels)
    grad_field = jnp.dot(grad_columns, flipped, preferred_element_type=jnp.float32)
    grad_input = (
        (grad_field * live).astype(jnp.bfloat16).reshape(width_x, width_y, depth_z, channels)
    )
    scale = 1.0 / jnp.sqrt(
        jnp.float32(width_x * width_y * depth_z * lax.axis_size("wide") * lax.axis_size("narrow"))
    )
    whole = lax.dot_general(
        grad_pre, columns, (((0,), (0,)), ((), ())), preferred_element_type=jnp.float32
    )
    piece_flat = lax.psum_scatter(
        whole.reshape(-1), ("wide", "narrow"), scatter_dimension=0, tiled=True
    )
    gathered = lax.all_gather(piece_flat, "narrow", axis=0, tiled=True)
    summed = gathered.reshape(channels // lax.axis_size("wide"), 27 * channels)
    grad_weight = summed * scale
    return (activation, grad_input, grad_weight)


def sharded(body, mesh, wide):
    return jax.shard_map(
        body,
        mesh=mesh,
        in_specs=(
            P(wide, "narrow", None, None),
            P(),
            P(wide, "narrow", None),
            P(wide, "narrow", None, None),
        ),
        out_specs=(
            P(wide, "narrow", None, None),
            P(wide, "narrow", None, None),
            P(wide, None),
        ),
        check_vma=False,
    )


def solution(mesh):
    wide, narrow = mesh.shape["wide"], mesh.shape["narrow"]
    if wide != 4 * QUAD or narrow != SIDES:
        return sharded(summed_local, mesh, "wide")
    planes = Mesh(
        mesh.devices.reshape(wide // QUAD, QUAD, narrow), ("depth", "quad", "narrow")
    )
    return sharded(planes_local, planes, WIDE)
```

```python
import functools

import jax
import jax.numpy as jnp
from jax import lax
from jax.experimental import pallas as pl
from jax.experimental.pallas import tpu as pltpu
from jax.sharding import Mesh
from jax.sharding import PartitionSpec as P

WIDE = ("depth", "quad")
QUAD = 4
SIDES = 2
MEMBERS = QUAD * SIDES
CHIPS = (0, 1, 4, 5)
OFFSETS = (-1, 0, 1)
DEPTH = 8


def position():
    quad, side = lax.axis_index("quad"), lax.axis_index("narrow")
    return lax.axis_index("depth"), quad * SIDES + side, quad, side


def shift_z(field, step):
    if step == 0:
        return field
    depth = field.shape[1]
    moved = pltpu.roll(field, (-step) % depth, 1)
    z = lax.broadcasted_iota(jnp.int32, field.shape, 1) + step
    return jnp.where((z >= 0) & (z < depth), moved, 0.0)


def pick_kernel(planes, out_ref):
    index = lax.broadcasted_iota(jnp.int32, out_ref.shape, 0)
    column = lax.broadcasted_iota(jnp.int32, out_ref.shape, 1)
    per = out_ref.shape[1] // (planes * QUAD)
    share = per // SIDES
    group = planes * share
    quad, side = index // (SIDES * group), index // group % SIDES
    plane, row = index // share % planes, index % share
    channel = per * (QUAD * plane + quad) + share * side + row
    out_ref[...] = jnp.where(channel == column, 1.0, 0.0).astype(jnp.bfloat16)


def dense(total):
    tiles = -(-total // 128)
    moved = tiles // 4
    return (tiles - moved) * 128, moved * 128


def fold_rows(block, total):
    kept, moved = dense(total)
    tail = block[:, kept : kept + moved]
    row = lax.broadcasted_iota(jnp.int32, tail.shape, 0)
    pieces = []
    for k in range(3):
        spare = jnp.where(row == 6, pltpu.roll(tail, 6 - k, 0), pltpu.roll(tail, 4 - k, 0))
        pieces.append(jnp.where(row < 6, block[:, k * moved : (k + 1) * moved], spare))
    return jnp.concatenate(pieces + [block[:, 3 * moved : kept]], axis=1)


def unfold_rows(block, total):
    kept, moved = dense(total)
    row = lax.broadcasted_iota(jnp.int32, (8, moved), 0)
    tail = jnp.zeros((8, moved), block.dtype)
    for k in range(3):
        piece = block[:, k * moved : (k + 1) * moved]
        tail = jnp.where(row == k, pltpu.roll(piece, 2 + k, 0), tail)
        tail = jnp.where(row == 3 + k, pltpu.roll(piece, 4 + k, 0), tail)
    return jnp.concatenate([block, tail], axis=1)[:, :total]


def rows_of_128(block):
    half = block.shape[0] // 2
    rest = jnp.concatenate([block[:half, 128:], block[half:, 128:]], axis=1)
    return jnp.concatenate([block[:, :128], rest], axis=0)


def rows_of_192(block):
    count = block.shape[0] * 2 // 3
    rest = jnp.concatenate([block[count:, :64], block[count:, 64:]], axis=0)
    return jnp.concatenate([block[:count], rest], axis=1)


def prepare_kernel(features, cot, mask, first, masked_ref, cot_ref, live_ref, near_ref, far_ref):
    width, rows, channels = features.shape
    f32 = jnp.float32
    flat = mask[...].astype(f32).reshape(width * rows // DEPTH, DEPTH)
    live = jnp.broadcast_to(flat[:, :, None], flat.shape + (channels,)).reshape(features.shape)
    live_ref[...] = live[:, :, :128]
    masked_ref[...] = (features[...].astype(f32) * live).astype(jnp.bfloat16)
    cot_ref[...] = (cot[...].astype(f32) * live).astype(jnp.bfloat16)
    odd = lax.rem(position()[2], 2)
    for ref, upper in ((near_ref, 1 - odd), (far_ref, odd)):
        slabs = [
            masked_ref[pl.ds(upper * (width - 2), 2)],
            cot_ref[pl.ds(upper * (width - 1), 1)],
        ]
        slabs = jnp.concatenate(slabs, axis=0).astype(f32).reshape(3 * rows, channels)
        ref[...] = rows_of_128(slabs).astype(jnp.bfloat16)


def pack_kernel(masked, after, packed_ref):
    count, channels = packed_ref.shape[0] * 128 // masked.shape[2], masked.shape[2]
    block = masked[...].reshape(count, channels)
    packed_ref[...] = rows_of_128(block)


def across_kernel(masked, cot, across_ref):
    width, rows, channels = masked.shape
    packed = rows_of_128(masked[...].reshape(width * rows, channels))
    across_ref[: packed.shape[0]] = packed
    ahead = position()[3] == 0
    grown = cot[...].astype(jnp.float32)
    strip = jnp.where(ahead, grown[:, rows - DEPTH :], grown[:, :DEPTH])
    strip = rows_of_128(strip.reshape(width * DEPTH, channels))
    across_ref[packed.shape[0] :] = strip.astype(jnp.bfloat16)


def corner_kernel(near, far, out_ref, edge):
    _, slabs, rows, channels = edge.shape
    _, _, quad, side = position()
    odd = lax.rem(quad, 2)
    f32 = jnp.float32
    edge[odd] = rows_of_192(far[...].astype(f32)).reshape(edge.shape[1:])
    edge[1 - odd] = rows_of_192(near[...].astype(f32)).reshape(edge.shape[1:])
    halo = 2 * DEPTH
    ahead = side == 0
    strip = jnp.where(ahead, edge[:, :2, rows - halo :], edge[:, :2, :halo])
    cots = jnp.where(ahead, edge[:, 2, rows - DEPTH :], edge[:, 2, :DEPTH])
    both = [strip.reshape(4 * halo, channels), cots.reshape(2 * DEPTH, channels)]
    both = rows_of_128(jnp.concatenate(both, axis=0))
    blank = jnp.zeros((out_ref.shape[0] - both.shape[0], 128), f32)
    out_ref[...] = jnp.concatenate([both, blank], axis=0).astype(jnp.bfloat16)


def turn_kernel(weight, out_ref):
    step = 2 * weight.shape[0]
    total = weight.shape[1]
    for start in range(0, total, step):
        stop = min(start + step, total)
        out_ref[start:stop, :] = weight[:, start:stop].T


def forward_kernel(
    masked, cot, near, far, across, corner, live, weight, pick, *refs
):
    act_ref, gp_ref = refs[:2]
    slice_refs = refs[2 : 2 + len(CHIPS)]
    ext, edge, cols, slices = refs[2 + len(CHIPS) :]
    width, rows, channels = masked.shape
    f32 = jnp.float32
    plane, me, quad, side = position()
    use_low = side.astype(f32)
    use_high = (1 - side).astype(f32)
    place = plane * QUAD + quad
    use_left = (place > 0).astype(f32)
    use_right = (place < QUAD * lax.axis_size("depth") - 1).astype(f32)
    halo = 2 * DEPTH
    tall = rows + 2 * halo
    mid = rows + 2 * DEPTH
    span = width + 4
    odd = lax.rem(quad, 2)
    edge[odd] = rows_of_192(far[...].astype(f32)).reshape(edge.shape[1:])
    edge[1 - odd] = rows_of_192(near[...].astype(f32)).reshape(edge.shape[1:])
    left, right = edge[0] * use_left, edge[1] * use_right
    count = 4 * halo + 2 * DEPTH
    both = rows_of_192(corner[...].astype(f32)[: count * channels // 128])
    corners = both[: 4 * halo].reshape(2, 2, halo, channels)
    lower, upper = corners[0] * use_left, corners[1] * use_right
    ends = both[4 * halo :].reshape(2, 1, DEPTH, channels)
    ext[0:2, halo : halo + rows, :] = left[0:2]
    ext[2 : 2 + width, halo : halo + rows, :] = masked[...].astype(f32)
    ext[2 + width :, halo : halo + rows, :] = right[0:2]
    half = width // 2
    ahead = side == 0
    count = width * rows * channels // 128
    held = across[:count].astype(f32).reshape(width + half, rows, 128)
    brick = jnp.where(ahead, held[:, :halo], held[:, rows - halo :])
    rest = jnp.concatenate([brick[width:, :, :64], brick[width:, :, 64:]], axis=0)
    beside = jnp.concatenate([brick[:width], rest], axis=2)
    for use, start in ((use_low, 0), (use_high, halo + rows)):
        at = slice(start, start + halo)
        ext[0:2, at, :] = lower * use
        ext[2 : 2 + width, at, :] = beside * use
        ext[2 + width :, at, :] = upper * use
    field = ext[...].reshape(span * tall // DEPTH, DEPTH, channels)
    for c in OFFSETS:
        moved = shift_z(field, c).reshape(span, tall, channels)
        for b in OFFSETS:
            at = ((b + 1) * 3 + c + 1) * channels
            start = DEPTH * (b + 1)
            cols[:, :, at : at + channels] = moved[:, start : start + mid].astype(jnp.bfloat16)
    nine = 9 * channels
    pre = jnp.zeros(((width + 2) * mid, channels), f32)
    for a in range(3):
        pre += jnp.dot(
            cols[a : a + width + 2].reshape((width + 2) * mid, nine),
            weight[a * nine : (a + 1) * nine, :],
            preferred_element_type=f32,
        )
    sig = 0.5 * jnp.tanh(0.5 * pre) + 0.5
    act = (pre * sig).reshape(width + 2, mid, channels)[1 : 1 + width, DEPTH : DEPTH + rows]
    act_ref[...] = (act * live[:, :, 0:1]).astype(jnp.bfloat16)
    slope = (sig * (1.0 + pre * (1.0 - sig))).reshape(width + 2, mid, channels)
    beyond = jnp.concatenate(
        [
            ends[0] * use_left,
            rows_of_192(across[count:].astype(f32)).reshape(width, DEPTH, channels),
            ends[1] * use_right,
        ],
        axis=0,
    )
    centre = jnp.concatenate([left[2:3], cot[...].astype(f32), right[2:3]], axis=0)
    full = jnp.concatenate([beyond * use_low, centre, beyond * use_high], axis=1)
    grad = full * slope
    gp_ref[...] = grad.astype(jnp.bfloat16)
    inner = grad[:, DEPTH : DEPTH + rows].astype(jnp.bfloat16)
    turned = lax.dot_general(
        pick[...],
        inner.reshape((width + 2) * rows, channels),
        (((1,), (1,)), ((), ())),
        preferred_element_type=f32,
    )
    slices[...] = turned.reshape(slices.shape)
    chip = me - lax.rem(quad, 2) * SIDES
    for distance, ref in zip(CHIPS, slice_refs):
        both = [slices[chip ^ distance], slices[(chip ^ distance) + SIDES]]
        ref[...] = jnp.concatenate(both, axis=0).astype(jnp.bfloat16)


def input_kernel(gp, live, turned, out_ref, cols, weight):
    width, rows, channels = out_ref.shape
    f32 = jnp.float32
    tall = rows + 2 * DEPTH
    for tap in range(27):
        weight[tap * channels : (tap + 1) * channels, :] = turned[
            :, tap * channels : (tap + 1) * channels
        ]
    field = gp[...].astype(f32).reshape((width + 2) * tall // DEPTH, DEPTH, channels)
    for c in OFFSETS:
        moved = shift_z(field, -c).reshape(width + 2, tall, channels)
        for b in OFFSETS:
            at = ((b + 1) * 3 + c + 1) * channels
            start = DEPTH * (1 - b)
            cols[:, :, at : at + channels] = moved[:, start : start + rows].astype(jnp.bfloat16)
    nine = 9 * channels
    total = jnp.zeros((width * rows, channels), f32)
    for a in range(3):
        total += jnp.dot(
            cols[2 - a : 2 - a + width].reshape(width * rows, nine),
            weight[a * nine : (a + 1) * nine, :],
            preferred_element_type=f32,
        )
    out_ref[...] = (total.reshape(width, rows, channels) * live[:, :, 0:1]).astype(jnp.bfloat16)


def kernel_grad_kernel(*refs):
    chips = len(CHIPS)
    received, bricks = refs[:chips], refs[chips : 2 * chips]
    keep_ref, send_ref, slices, cols, part, masked = refs[2 * chips :]
    f32 = jnp.float32
    group, lanes = received[0].shape
    blocks, per, lane, channels = masked.shape
    half = lane // 2
    _, _, quad, side = position()
    for i, distance in enumerate(CHIPS):
        block, sided = distance // 4, side ^ (distance % 2)
        slices[block, sided] = received[i][...]
        at_rows = pl.ds(pl.multiple_of(sided * half, half), half)
        for x in range(per):
            shift = 64 * (x // (per // 2))
            rest = bricks[i][pl.ds((per + x % (per // 2)) * half, half)]
            masked[block, x, at_rows, :128] = bricks[i][pl.ds(x * half, half)]
            masked[block, x, at_rows, 128:] = rest[:, shift : shift + 64]
    at = lax.broadcasted_iota(jnp.int32, (group, lane), 1)
    y, z = at // DEPTH, at % DEPTH
    tall = lane // DEPTH
    for block in range(blocks):
        first = slices[block, 0].astype(f32)
        second = slices[block, 1].astype(f32)
        for k in range(per + 2):
            one = first[:, k // 2 * lane : (k // 2 + 1) * lane]
            two = second[:, k // 2 * lane : (k // 2 + 1) * lane]
            if k % 2 == 0:
                base = jnp.where(at < half, one, pltpu.roll(two, half, 1))
            else:
                base = jnp.where(at < half, pltpu.roll(one, half, 1), two)
            pieces = []
            for b in OFFSETS:
                for c in OFFSETS:
                    step = (DEPTH * b + c) % lane
                    moved = base if step == 0 else pltpu.roll(base, step, 1)
                    keep = (y - b >= 0) & (y - b < tall) & (z - c >= 0) & (z - c < DEPTH)
                    pieces.append(jnp.where(keep, moved, 0.0))
            slab = block * (per + 2) + k
            cols[:, slab * lane : (slab + 1) * lane] = jnp.concatenate(pieces, axis=0).astype(
                jnp.bfloat16
            )
    for a in range(3):
        got = jnp.zeros((cols.shape[0], channels), f32)
        for block in range(blocks):
            start = (block * (per + 2) + 2 - a) * lane
            got += jnp.dot(
                cols[:, start : start + per * lane],
                masked[block].reshape(per * lane, channels),
                preferred_element_type=f32,
            )
        got = got.reshape(9, group, channels)
        part[:, a * 9 * channels : (a + 1) * 9 * channels] = jnp.concatenate(
            [got[tap] for tap in range(9)], axis=1
        )
    core = lax.rem(quad, 2)
    half = group // 2
    keep_ref[...] = part[pl.ds(pl.multiple_of(core * half, 8), half)]
    send_ref[...] = part[pl.ds(pl.multiple_of((1 - core) * half, 8), half)].astype(jnp.bfloat16)


def fold_kernel(keep, other, own_ref, *refs):
    *send_refs, both, rows = refs
    planes, eight, _ = rows.shape
    count, total = keep.shape
    share = count // planes
    both[:count, :total] = keep[...] + other[...].astype(jnp.float32)
    both[:, total:] = jnp.zeros((both.shape[0], both.shape[1] - total), jnp.float32)
    for to in range(planes):
        rows[to] = fold_rows(both[share * to : share * to + eight, :], total)
    plane = position()[0]
    own_ref[...] = rows[plane]
    for distance, ref in enumerate(send_refs, 1):
        ref[...] = rows[plane ^ distance].astype(jnp.bfloat16)


def sum_kernel(scale, own, one, two, three, out_ref):
    f32 = jnp.float32
    total = own[...] + one[...].astype(f32) + two[...].astype(f32) + three[...].astype(f32)
    out_ref[...] = (total * scale).astype(out_ref.dtype)


def join_kernel(mine, other, out_ref):
    share = out_ref.shape[0] // SIDES
    ahead = position()[3] == 0
    total = out_ref.shape[1]
    here = unfold_rows(mine[...].astype(jnp.float32), total)
    there = unfold_rows(other[...].astype(jnp.float32), total)
    first = jnp.where(ahead, here, there)
    second = jnp.where(ahead, there, here)
    out_ref[0:share] = first[:share]
    out_ref[share:] = second[:share]


def call(body, name, mebibytes, flops, moved, out_shape, scratch=(), in_specs=None):
    spec = pl.BlockSpec(memory_space=pltpu.VMEM)

    def run(*operands):
        return pl.pallas_call(
            body,
            out_shape=out_shape,
            in_specs=in_specs or [spec] * len(operands),
            out_specs=jax.tree.map(lambda _: spec, out_shape),
            scratch_shapes=scratch,
            compiler_params=pltpu.CompilerParams(vmem_limit_bytes=mebibytes << 20),
            cost_estimate=pl.CostEstimate(flops=flops, bytes_accessed=moved, transcendentals=0),
            name=name,
        )(*operands)

    return run


def planes_local(features, weight, voxel_mask, cotangent):
    bf16 = jnp.bfloat16
    f32 = jnp.float32
    array = jax.ShapeDtypeStruct
    width, wide_y, depth, channels = features.shape
    rows = wide_y * depth
    planes = lax.axis_size("depth")
    count = planes * QUAD
    total = 27 * channels
    halo = 2 * DEPTH
    span = (width + 2) * rows
    share = channels // count // SIDES
    group = planes * share

    def swap(piece, axes, distance, size):
        return lax.ppermute(piece, axes, [(i, i ^ distance) for i in range(size)])

    def in_plane(piece, distance):
        return swap(piece, ("quad", "narrow"), distance, MEMBERS)

    brick = array((width, rows, channels), bf16)
    slab = array((3 * rows * channels // 128, 128), bf16)
    slabs = (2, 3, rows, channels)
    pick = call(
        functools.partial(pick_kernel, planes), "pick", 4, 1 << 32, 1 << 16,
        array((MEMBERS * group, channels), bf16),
    )()
    vmem = pl.BlockSpec(memory_space=pltpu.VMEM)
    masked, cot, live, near, far = call(
        prepare_kernel, "prepare", 16, 1 << 20, 1 << 20,
        (brick, brick, array((width, rows, 128), f32), slab, slab),
        (),
        [vmem] * 3 + [pl.BlockSpec(memory_space=pl.ANY)],
    )(
        features.reshape(width, rows, channels),
        cotangent.reshape(width, rows, channels),
        voxel_mask,
        pick,
    )
    near = swap(near, WIDE, 1, count)
    ends = [min(max(((i + 1) ^ 1) - 1, 0), count - 1) for i in range(count)]
    far = lax.ppermute(far, WIDE, list(enumerate(ends)))
    weight_rows = call(
        turn_kernel, "turn", 8, 1 << 20, 4 << 20, array((total, channels), bf16)
    )(weight.T)
    count_128 = width * rows * channels // 128
    strip_128 = width * DEPTH * channels // 128
    across = call(
        across_kernel, "across", 4, 1 << 16, 1 << 19, array((count_128 + strip_128, 128), bf16)
    )(masked, cot)
    across = in_plane(across, CHIPS[1])
    packed = call(
        pack_kernel, "pack", 4, 1 << 16, 1 << 19, array((count_128, 128), bf16), (),
        [vmem, pl.BlockSpec(memory_space=pl.ANY)],
    )(masked, weight_rows)
    near, far, weight_rows, late = lax.optimization_barrier((near, far, weight_rows, packed))
    corner = call(
        corner_kernel, "corner", 4, 1 << 16, 1 << 18,
        array((128, 128), bf16),
        (pltpu.VMEM(slabs, f32),),
    )(near, far)
    corner = in_plane(corner, 1)
    bricks = [packed, across, in_plane(packed, CHIPS[2]), in_plane(late, CHIPS[3])]

    mid = rows + 2 * DEPTH
    act, gp, *slices = call(
        forward_kernel, "forward", 28, 3 << 29, 1 << 20,
        (brick, array((width + 2, mid, channels), bf16))
        + (array((2 * group, span), bf16),) * len(CHIPS),
        (
            pltpu.VMEM((width + 4, rows + 2 * halo, channels), f32),
            pltpu.VMEM(slabs, f32),
            pltpu.VMEM((width + 4, mid, 9 * channels), bf16),
            pltpu.VMEM((MEMBERS, group, span), f32),
        ),
    )(masked, cot, near, far, across, corner, live, weight_rows, pick)
    bricks[2], *slices = lax.optimization_barrier((bricks[2], *slices))
    slices = [slices[0]] + [in_plane(part, d) for part, d in zip(slices[1:], CHIPS[1:])]

    grad_input = call(
        input_kernel, "input_gradient", 20, 2 * 512 * 5184 * 256, 4 << 20, brick,
        (
            pltpu.VMEM((width + 2, rows, 9 * channels), bf16),
            pltpu.VMEM((total, channels), bf16),
        ),
    )(gp, live, weight.T)

    blocks = QUAD // 2
    chips = len(CHIPS)
    lanes = dense(total)[0]
    keep, fold = call(
        kernel_grad_kernel, "kernel_gradient", 28, 2 * 432 * 3 * 2048 * 256, 4 << 20,
        (array((group, total), f32), array((group, total), bf16)),
        (
            pltpu.VMEM((blocks, SIDES, 2 * group, span), bf16),
            pltpu.VMEM((9 * 2 * group, blocks * (width + 2) * SIDES * rows), bf16),
            pltpu.VMEM((2 * group, total), f32),
            pltpu.VMEM((blocks, width, SIDES * rows, channels), bf16),
        ),
    )(*slices, *bricks)
    own, *sends = call(
        fold_kernel, "fold", 8, 8 * total * 4, 8 * total * 40,
        (array((8, lanes), f32),) + (array((8, lanes), bf16),) * (planes - 1),
        (
            pltpu.VMEM((group + 8, sum(dense(total))), f32),
            pltpu.VMEM((planes, 8, lanes), f32),
        ),
    )(keep, in_plane(fold, 2))
    got = [swap(sent, "depth", d, planes) for d, sent in list(enumerate(sends, 1))[::-1]]
    grad_input, *got = lax.optimization_barrier((grad_input, *got))
    voxels = count * SIDES * width * rows
    mine = call(
        functools.partial(sum_kernel, float(1.0 / voxels**0.5)),
        "plane_sum", 4, 8 * total * 4, 8 * total * 14, array((8, lanes), bf16),
    )(own, *got)
    grad_weight = call(
        join_kernel, "join", 4, 8 * total, 8 * total * 14, array((channels // count, total), f32)
    )(mine, in_plane(mine, 1))
    shape = features.shape
    return act.reshape(shape), grad_input.reshape(shape), grad_weight


def padded_2(cells, sides, width):
    for axis, dim in sides:
        count = lax.axis_size(axis)
        ends = count - 1
        head = lax.slice_in_dim(cells, 0, width, axis=dim)
        tail = lax.slice_in_dim(cells, cells.shape[dim] - width, cells.shape[dim], axis=dim)
        cells = jnp.concatenate(
            [
                lax.ppermute(tail, axis, [(i, (i + 1) % count) for i in range(ends)]),
                cells,
                lax.ppermute(head, axis, [((i + 1) % count, i) for i in range(ends)]),
            ],
            axis=dim,
        )
    return cells


def gather_taps(padded, width_x, width_y, depth_z, channels, flip):
    pieces = []
    for shift_x in range(3):
        for shift_y in range(3):
            for shift_z in range(3):
                start_x = 2 - shift_x if flip else shift_x
                start_y = 2 - shift_y if flip else shift_y
                start_z = 2 - shift_z if flip else shift_z
                piece = padded[
                    start_x : start_x + width_x,
                    start_y : start_y + width_y,
                    start_z : start_z + depth_z,
                    :,
                ]
                pieces.append(piece.reshape(-1, channels))
    return jnp.concatenate(pieces, axis=1)


def summed_local(features, weight, voxel_mask, cotangent):
    width_x, width_y, depth_z, channels = features.shape
    masked = features * voxel_mask.astype(jnp.bfloat16)[..., None]
    padded = padded_2(masked, (("wide", 0), ("narrow", 1)), 1)
    padded = jnp.pad(padded, ((0, 0), (0, 0), (1, 1), (0, 0)))
    columns = gather_taps(padded, width_x, width_y, depth_z, channels, False)
    pre = jnp.dot(columns, weight, preferred_element_type=jnp.float32)
    live = voxel_mask.reshape(-1, 1).astype(jnp.float32)
    sig = jax.nn.sigmoid(pre)
    activation = (
        (pre * sig * live).astype(jnp.bfloat16).reshape(width_x, width_y, depth_z, channels)
    )
    slope = sig * (1.0 + pre * (1.0 - sig))
    grad_pre = (cotangent.reshape(-1, channels).astype(jnp.float32) * live * slope).astype(
        jnp.bfloat16
    )
    taps = weight.reshape(27, channels, channels)
    grid = grad_pre.reshape(width_x, width_y, depth_z, channels)
    grad_pad = padded_2(grid, (("wide", 0), ("narrow", 1)), 1)
    grad_pad = jnp.pad(grad_pad, ((0, 0), (0, 0), (1, 1), (0, 0)))
    grad_columns = gather_taps(grad_pad, width_x, width_y, depth_z, channels, True)
    flipped = jnp.transpose(taps, (0, 2, 1)).reshape(27 * channels, channels)
    grad_field = jnp.dot(grad_columns, flipped, preferred_element_type=jnp.float32)
    grad_input = (
        (grad_field * live).astype(jnp.bfloat16).reshape(width_x, width_y, depth_z, channels)
    )
    scale = 1.0 / jnp.sqrt(
        jnp.float32(width_x * width_y * depth_z * lax.axis_size("wide") * lax.axis_size("narrow"))
    )
    whole = lax.dot_general(
        grad_pre, columns, (((0,), (0,)), ((), ())), preferred_element_type=jnp.float32
    )
    piece_flat = lax.psum_scatter(
        whole.reshape(-1), ("wide", "narrow"), scatter_dimension=0, tiled=True
    )
    gathered = lax.all_gather(piece_flat, "narrow", axis=0, tiled=True)
    summed = gathered.reshape(channels // lax.axis_size("wide"), 27 * channels)
    grad_weight = summed * scale
    return (activation, grad_input, grad_weight)


def sharded(body, mesh, wide):
    return jax.shard_map(
        body,
        mesh=mesh,
        in_specs=(
            P(wide, "narrow", None, None),
            P(),
            P(wide, "narrow", None),
            P(wide, "narrow", None, None),
        ),
        out_specs=(
            P(wide, "narrow", None, None),
            P(wide, "narrow", None, None),
            P(wide, None),
        ),
        check_vma=False,
    )


def solution(mesh):
    wide, narrow = mesh.shape["wide"], mesh.shape["narrow"]
    if wide != 4 * QUAD or narrow != SIDES:
        return sharded(summed_local, mesh, "wide")
    planes = Mesh(
        mesh.devices.reshape(wide // QUAD, QUAD, narrow), ("depth", "quad", "narrow")
    )
    return sharded(planes_local, planes, WIDE)
```

```python
import functools

import jax
import jax.numpy as jnp
from jax import lax
from jax.experimental import pallas as pl
from jax.experimental.pallas import tpu as pltpu
from jax.sharding import Mesh
from jax.sharding import PartitionSpec as P

WIDE = ("depth", "quad")
QUAD = 4
SIDES = 2
MEMBERS = QUAD * SIDES
CHIPS = (0, 1, 4, 5)
OFFSETS = (-1, 0, 1)
DEPTH = 8


def position():
    quad, side = lax.axis_index("quad"), lax.axis_index("narrow")
    return lax.axis_index("depth"), quad * SIDES + side, quad, side


def shift_z(field, step):
    if step == 0:
        return field
    depth = field.shape[1]
    moved = pltpu.roll(field, (-step) % depth, 1)
    z = lax.broadcasted_iota(jnp.int32, field.shape, 1) + step
    return jnp.where((z >= 0) & (z < depth), moved, 0.0)


def pick_kernel(planes, out_ref):
    index = lax.broadcasted_iota(jnp.int32, out_ref.shape, 0)
    column = lax.broadcasted_iota(jnp.int32, out_ref.shape, 1)
    per = out_ref.shape[1] // (planes * QUAD)
    share = per // SIDES
    group = planes * share
    quad, side = index // (SIDES * group), index // group % SIDES
    plane, row = index // share % planes, index % share
    channel = per * (QUAD * plane + quad) + share * side + row
    out_ref[...] = jnp.where(channel == column, 1.0, 0.0).astype(jnp.bfloat16)


def dense(total):
    tiles = -(-total // 128)
    moved = tiles // 4
    return (tiles - moved) * 128, moved * 128


def fold_rows(block, total):
    kept, moved = dense(total)
    tail = block[:, kept : kept + moved]
    row = lax.broadcasted_iota(jnp.int32, tail.shape, 0)
    pieces = []
    for k in range(3):
        spare = jnp.where(row == 6, pltpu.roll(tail, 6 - k, 0), pltpu.roll(tail, 4 - k, 0))
        pieces.append(jnp.where(row < 6, block[:, k * moved : (k + 1) * moved], spare))
    return jnp.concatenate(pieces + [block[:, 3 * moved : kept]], axis=1)


def unfold_rows(block, total):
    kept, moved = dense(total)
    row = lax.broadcasted_iota(jnp.int32, (8, moved), 0)
    tail = jnp.zeros((8, moved), block.dtype)
    for k in range(3):
        piece = block[:, k * moved : (k + 1) * moved]
        tail = jnp.where(row == k, pltpu.roll(piece, 2 + k, 0), tail)
        tail = jnp.where(row == 3 + k, pltpu.roll(piece, 4 + k, 0), tail)
    return jnp.concatenate([block, tail], axis=1)[:, :total]


def rows_of_128(block):
    half = block.shape[0] // 2
    rest = jnp.concatenate([block[:half, 128:], block[half:, 128:]], axis=1)
    return jnp.concatenate([block[:, :128], rest], axis=0)


def rows_of_192(block):
    count = block.shape[0] * 2 // 3
    rest = jnp.concatenate([block[count:, :64], block[count:, 64:]], axis=0)
    return jnp.concatenate([block[:count], rest], axis=1)


def prepare_kernel(features, cot, mask, first, masked_ref, cot_ref, live_ref, near_ref, far_ref):
    width, rows, channels = features.shape
    f32 = jnp.float32
    flat = mask[...].astype(f32).reshape(width * rows // DEPTH, DEPTH)
    live = jnp.broadcast_to(flat[:, :, None], flat.shape + (channels,)).reshape(features.shape)
    live_ref[...] = live[:, :, :128]
    masked_ref[...] = (features[...].astype(f32) * live).astype(jnp.bfloat16)
    cot_ref[...] = (cot[...].astype(f32) * live).astype(jnp.bfloat16)
    odd = lax.rem(position()[2], 2)
    for ref, upper in ((near_ref, 1 - odd), (far_ref, odd)):
        slabs = [
            masked_ref[pl.ds(upper * (width - 2), 2)],
            cot_ref[pl.ds(upper * (width - 1), 1)],
        ]
        slabs = jnp.concatenate(slabs, axis=0).astype(f32).reshape(3 * rows, channels)
        ref[...] = rows_of_128(slabs).astype(jnp.bfloat16)


def pack_kernel(masked, after, packed_ref):
    count, channels = packed_ref.shape[0] * 128 // masked.shape[2], masked.shape[2]
    block = masked[...].reshape(count, channels)
    packed_ref[...] = rows_of_128(block)


def across_kernel(masked, cot, across_ref):
    width, rows, channels = masked.shape
    packed = rows_of_128(masked[...].reshape(width * rows, channels))
    across_ref[: packed.shape[0]] = packed
    ahead = position()[3] == 0
    grown = cot[...].astype(jnp.float32)
    strip = jnp.where(ahead, grown[:, rows - DEPTH :], grown[:, :DEPTH])
    strip = rows_of_128(strip.reshape(width * DEPTH, channels))
    across_ref[packed.shape[0] :] = strip.astype(jnp.bfloat16)


def corner_kernel(near, far, out_ref, edge):
    _, slabs, rows, channels = edge.shape
    _, _, quad, side = position()
    odd = lax.rem(quad, 2)
    f32 = jnp.float32
    edge[odd] = rows_of_192(far[...].astype(f32)).reshape(edge.shape[1:])
    edge[1 - odd] = rows_of_192(near[...].astype(f32)).reshape(edge.shape[1:])
    halo = 2 * DEPTH
    ahead = side == 0
    strip = jnp.where(ahead, edge[:, :2, rows - halo :], edge[:, :2, :halo])
    cots = jnp.where(ahead, edge[:, 2, rows - DEPTH :], edge[:, 2, :DEPTH])
    both = [strip.reshape(4 * halo, channels), cots.reshape(2 * DEPTH, channels)]
    both = rows_of_128(jnp.concatenate(both, axis=0))
    blank = jnp.zeros((out_ref.shape[0] - both.shape[0], 128), f32)
    out_ref[...] = jnp.concatenate([both, blank], axis=0).astype(jnp.bfloat16)


def turn_kernel(weight, out_ref):
    step = 2 * weight.shape[0]
    total = weight.shape[1]
    for start in range(0, total, step):
        stop = min(start + step, total)
        out_ref[start:stop, :] = weight[:, start:stop].T


def bulk_kernel(masked, near, far, across, weight, pre_ref, ext, edge, cols):
    width, rows, channels = masked.shape
    f32 = jnp.float32
    plane, _, quad, side = position()
    use_low = side.astype(f32)
    use_high = (1 - side).astype(f32)
    place = plane * QUAD + quad
    use_left = (place > 0).astype(f32)
    use_right = (place < QUAD * lax.axis_size("depth") - 1).astype(f32)
    halo = 2 * DEPTH
    tall = rows + 2 * halo
    mid = rows + 2 * DEPTH
    span = width + 4
    odd = lax.rem(quad, 2)
    edge[odd] = rows_of_192(far[...].astype(f32)).reshape(edge.shape[1:])
    edge[1 - odd] = rows_of_192(near[...].astype(f32)).reshape(edge.shape[1:])
    ext[0:2, halo : halo + rows, :] = edge[0, 0:2] * use_left
    ext[2 : 2 + width, halo : halo + rows, :] = masked[...].astype(f32)
    ext[2 + width :, halo : halo + rows, :] = edge[1, 0:2] * use_right
    half = width // 2
    count = width * rows * channels // 128
    held = across[:count].astype(f32).reshape(width + half, rows, 128)
    brick = jnp.where(side == 0, held[:, :halo], held[:, rows - halo :])
    rest = jnp.concatenate([brick[width:, :, :64], brick[width:, :, 64:]], axis=0)
    beside = jnp.concatenate([brick[:width], rest], axis=2)
    blank = jnp.zeros((2, halo, channels), f32)
    for use, start in ((use_low, 0), (use_high, halo + rows)):
        at = slice(start, start + halo)
        ext[0:2, at, :] = blank
        ext[2 : 2 + width, at, :] = beside * use
        ext[2 + width :, at, :] = blank
    field = ext[...].reshape(span * tall // DEPTH, DEPTH, channels)
    for c in OFFSETS:
        moved = shift_z(field, c).reshape(span, tall, channels)
        for b in OFFSETS:
            at = ((b + 1) * 3 + c + 1) * channels
            start = DEPTH * (b + 1)
            cols[:, :, at : at + channels] = moved[:, start : start + mid].astype(jnp.bfloat16)
    nine = 9 * channels
    pre = jnp.zeros(((width + 2) * mid, channels), f32)
    for a in range(3):
        pre += jnp.dot(
            cols[a : a + width + 2].reshape((width + 2) * mid, nine),
            weight[a * nine : (a + 1) * nine, :],
            preferred_element_type=f32,
        )
    pre_ref[...] = pre.reshape(pre_ref.shape)


def forward_kernel(bulk, cot, near, far, across, corner, live, weight, pick, *refs):
    act_ref, gp_ref = refs[:2]
    slice_refs = refs[2 : 2 + len(CHIPS)]
    edge, cols, total, slices = refs[2 + len(CHIPS) :]
    width, rows, channels = cot.shape
    f32 = jnp.float32
    plane, me, quad, side = position()
    use_low = side.astype(f32)
    use_high = (1 - side).astype(f32)
    place = plane * QUAD + quad
    use_left = (place > 0).astype(f32)
    use_right = (place < QUAD * lax.axis_size("depth") - 1).astype(f32)
    halo = 2 * DEPTH
    mid = rows + 2 * DEPTH
    count = 4 * halo + 2 * DEPTH
    both = rows_of_192(corner[...].astype(f32)[: count * channels // 128])
    corners = both[: 4 * halo].reshape(2, 2, halo, channels)
    corners = jnp.concatenate([corners[0] * use_left, corners[1] * use_right], axis=0)
    sources = ((0, 1, None, None), (1, None, None, 2), (None, None, 2, 3))
    blank = jnp.zeros((DEPTH, channels), f32)
    for c in OFFSETS:
        moved = shift_z(corners.reshape(8, DEPTH, channels), c)
        for b in OFFSETS:
            low = {-1: (0, 1), 0: (1, None), 1: (None, None)}[b]
            high = {-1: (None, None), 0: (None, 0), 1: (0, 1)}[b]
            at = ((b + 1) * 3 + c + 1) * channels
            parts = []
            for slab in range(4):
                for below, above in zip(low, high):
                    part = blank if below is None else moved[2 * slab + below] * use_low
                    if above is not None:
                        part = part + moved[2 * slab + above] * use_high
                    parts.append(part)
            for a in range(3):
                rows_a = []
                for source in sources[a]:
                    pair = [blank] * 2 if source is None else parts[2 * source : 2 * source + 2]
                    rows_a += pair
                cols[a, :, at : at + channels] = jnp.concatenate(rows_a, axis=0).astype(
                    jnp.bfloat16
                )
    nine = 9 * channels
    share = jnp.zeros((4 * halo, channels), f32)
    for a in range(3):
        share += jnp.dot(
            cols[a], weight[a * nine : (a + 1) * nine, :], preferred_element_type=f32
        )
    share = share.reshape(4, halo, channels)
    total[...] = bulk[...]
    at = pl.ds(pl.multiple_of((1 - side) * (mid - halo), DEPTH), halo)
    total[0:2, at, :] += share[0:2]
    total[width : width + 2, at, :] += share[2:4]
    pre = total[...].reshape((width + 2) * mid, channels)
    sig = 0.5 * jnp.tanh(0.5 * pre) + 0.5
    act = (pre * sig).reshape(width + 2, mid, channels)[1 : 1 + width, DEPTH : DEPTH + rows]
    act_ref[...] = (act * live[:, :, 0:1]).astype(jnp.bfloat16)
    slope = (sig * (1.0 + pre * (1.0 - sig))).reshape(width + 2, mid, channels)
    ends = both[4 * halo :].reshape(2, 1, DEPTH, channels)
    strip = across[width * rows * channels // 128 :].astype(f32)
    beyond = jnp.concatenate(
        [
            ends[0] * use_left,
            rows_of_192(strip).reshape(width, DEPTH, channels),
            ends[1] * use_right,
        ],
        axis=0,
    )
    odd = lax.rem(quad, 2)
    edge[odd] = rows_of_192(far[...].astype(f32))[2 * rows :]
    edge[1 - odd] = rows_of_192(near[...].astype(f32))[2 * rows :]
    centre = [edge[0:1] * use_left, cot[...].astype(f32), edge[1:2] * use_right]
    centre = jnp.concatenate(centre, axis=0)
    full = jnp.concatenate([beyond * use_low, centre, beyond * use_high], axis=1)
    grad = full * slope
    gp_ref[...] = grad.astype(jnp.bfloat16)
    inner = grad[:, DEPTH : DEPTH + rows].astype(jnp.bfloat16)
    turned = lax.dot_general(
        pick[...],
        inner.reshape((width + 2) * rows, channels),
        (((1,), (1,)), ((), ())),
        preferred_element_type=f32,
    )
    slices[...] = turned.reshape(slices.shape)
    chip = me - lax.rem(quad, 2) * SIDES
    for distance, ref in zip(CHIPS, slice_refs):
        both = [slices[chip ^ distance], slices[(chip ^ distance) + SIDES]]
        ref[...] = jnp.concatenate(both, axis=0).astype(jnp.bfloat16)


def input_kernel(gp, live, turned, out_ref, cols, weight):
    width, rows, channels = out_ref.shape
    f32 = jnp.float32
    tall = rows + 2 * DEPTH
    for tap in range(27):
        weight[tap * channels : (tap + 1) * channels, :] = turned[
            :, tap * channels : (tap + 1) * channels
        ]
    field = gp[...].astype(f32).reshape((width + 2) * tall // DEPTH, DEPTH, channels)
    for c in OFFSETS:
        moved = shift_z(field, -c).reshape(width + 2, tall, channels)
        for b in OFFSETS:
            at = ((b + 1) * 3 + c + 1) * channels
            start = DEPTH * (1 - b)
            cols[:, :, at : at + channels] = moved[:, start : start + rows].astype(jnp.bfloat16)
    nine = 9 * channels
    total = jnp.zeros((width * rows, channels), f32)
    for a in range(3):
        total += jnp.dot(
            cols[2 - a : 2 - a + width].reshape(width * rows, nine),
            weight[a * nine : (a + 1) * nine, :],
            preferred_element_type=f32,
        )
    out_ref[...] = (total.reshape(width, rows, channels) * live[:, :, 0:1]).astype(jnp.bfloat16)


def kernel_grad_kernel(*refs):
    chips = len(CHIPS)
    received, bricks = refs[:chips], refs[chips : 2 * chips]
    keep_ref, send_ref, slices, cols, part, masked = refs[2 * chips :]
    f32 = jnp.float32
    group, lanes = received[0].shape
    blocks, per, lane, channels = masked.shape
    half = lane // 2
    _, _, quad, side = position()
    for i, distance in enumerate(CHIPS):
        block, sided = distance // 4, side ^ (distance % 2)
        slices[block, sided] = received[i][...]
        at_rows = pl.ds(pl.multiple_of(sided * half, half), half)
        for x in range(per):
            shift = 64 * (x // (per // 2))
            rest = bricks[i][pl.ds((per + x % (per // 2)) * half, half)]
            masked[block, x, at_rows, :128] = bricks[i][pl.ds(x * half, half)]
            masked[block, x, at_rows, 128:] = rest[:, shift : shift + 64]
    at = lax.broadcasted_iota(jnp.int32, (group, lane), 1)
    y, z = at // DEPTH, at % DEPTH
    tall = lane // DEPTH
    for block in range(blocks):
        first = slices[block, 0].astype(f32)
        second = slices[block, 1].astype(f32)
        for k in range(per + 2):
            one = first[:, k // 2 * lane : (k // 2 + 1) * lane]
            two = second[:, k // 2 * lane : (k // 2 + 1) * lane]
            if k % 2 == 0:
                base = jnp.where(at < half, one, pltpu.roll(two, half, 1))
            else:
                base = jnp.where(at < half, pltpu.roll(one, half, 1), two)
            pieces = []
            for b in OFFSETS:
                for c in OFFSETS:
                    step = (DEPTH * b + c) % lane
                    moved = base if step == 0 else pltpu.roll(base, step, 1)
                    keep = (y - b >= 0) & (y - b < tall) & (z - c >= 0) & (z - c < DEPTH)
                    pieces.append(jnp.where(keep, moved, 0.0))
            slab = block * (per + 2) + k
            cols[:, slab * lane : (slab + 1) * lane] = jnp.concatenate(pieces, axis=0).astype(
                jnp.bfloat16
            )
    for a in range(3):
        got = jnp.zeros((cols.shape[0], channels), f32)
        for block in range(blocks):
            start = (block * (per + 2) + 2 - a) * lane
            got += jnp.dot(
                cols[:, start : start + per * lane],
                masked[block].reshape(per * lane, channels),
                preferred_element_type=f32,
            )
        got = got.reshape(9, group, channels)
        part[:, a * 9 * channels : (a + 1) * 9 * channels] = jnp.concatenate(
            [got[tap] for tap in range(9)], axis=1
        )
    core = lax.rem(quad, 2)
    half = group // 2
    keep_ref[...] = part[pl.ds(pl.multiple_of(core * half, 8), half)]
    send_ref[...] = part[pl.ds(pl.multiple_of((1 - core) * half, 8), half)].astype(jnp.bfloat16)


def fold_kernel(keep, other, own_ref, *refs):
    *send_refs, both, rows = refs
    planes, eight, _ = rows.shape
    count, total = keep.shape
    share = count // planes
    both[:count, :total] = keep[...] + other[...].astype(jnp.float32)
    both[:, total:] = jnp.zeros((both.shape[0], both.shape[1] - total), jnp.float32)
    for to in range(planes):
        rows[to] = fold_rows(both[share * to : share * to + eight, :], total)
    plane = position()[0]
    own_ref[...] = rows[plane]
    for distance, ref in enumerate(send_refs, 1):
        ref[...] = rows[plane ^ distance].astype(jnp.bfloat16)


def sum_kernel(scale, own, one, two, three, out_ref):
    f32 = jnp.float32
    total = own[...] + one[...].astype(f32) + two[...].astype(f32) + three[...].astype(f32)
    out_ref[...] = (total * scale).astype(out_ref.dtype)


def join_kernel(mine, other, out_ref):
    share = out_ref.shape[0] // SIDES
    ahead = position()[3] == 0
    total = out_ref.shape[1]
    here = unfold_rows(mine[...].astype(jnp.float32), total)
    there = unfold_rows(other[...].astype(jnp.float32), total)
    first = jnp.where(ahead, here, there)
    second = jnp.where(ahead, there, here)
    out_ref[0:share] = first[:share]
    out_ref[share:] = second[:share]


def call(body, name, mebibytes, flops, moved, out_shape, scratch=(), in_specs=None):
    spec = pl.BlockSpec(memory_space=pltpu.VMEM)

    def run(*operands):
        return pl.pallas_call(
            body,
            out_shape=out_shape,
            in_specs=in_specs or [spec] * len(operands),
            out_specs=jax.tree.map(lambda _: spec, out_shape),
            scratch_shapes=scratch,
            compiler_params=pltpu.CompilerParams(vmem_limit_bytes=mebibytes << 20),
            cost_estimate=pl.CostEstimate(flops=flops, bytes_accessed=moved, transcendentals=0),
            name=name,
        )(*operands)

    return run


def planes_local(features, weight, voxel_mask, cotangent):
    bf16 = jnp.bfloat16
    f32 = jnp.float32
    array = jax.ShapeDtypeStruct
    width, wide_y, depth, channels = features.shape
    rows = wide_y * depth
    planes = lax.axis_size("depth")
    count = planes * QUAD
    total = 27 * channels
    halo = 2 * DEPTH
    span = (width + 2) * rows
    share = channels // count // SIDES
    group = planes * share

    def swap(piece, axes, distance, size):
        return lax.ppermute(piece, axes, [(i, i ^ distance) for i in range(size)])

    def in_plane(piece, distance):
        return swap(piece, ("quad", "narrow"), distance, MEMBERS)

    brick = array((width, rows, channels), bf16)
    slab = array((3 * rows * channels // 128, 128), bf16)
    slabs = (2, 3, rows, channels)
    pick = call(
        functools.partial(pick_kernel, planes), "pick", 4, 1 << 32, 1 << 16,
        array((MEMBERS * group, channels), bf16),
    )()
    vmem = pl.BlockSpec(memory_space=pltpu.VMEM)
    masked, cot, live, near, far = call(
        prepare_kernel, "prepare", 16, 1 << 20, 1 << 20,
        (brick, brick, array((width, rows, 128), f32), slab, slab),
        (),
        [vmem] * 3 + [pl.BlockSpec(memory_space=pl.ANY)],
    )(
        features.reshape(width, rows, channels),
        cotangent.reshape(width, rows, channels),
        voxel_mask,
        pick,
    )
    near = swap(near, WIDE, 1, count)
    ends = [min(max(((i + 1) ^ 1) - 1, 0), count - 1) for i in range(count)]
    far = lax.ppermute(far, WIDE, list(enumerate(ends)))
    weight_rows = call(
        turn_kernel, "turn", 8, 1 << 20, 4 << 20, array((total, channels), bf16)
    )(weight.T)
    count_128 = width * rows * channels // 128
    strip_128 = width * DEPTH * channels // 128
    across = call(
        across_kernel, "across", 4, 1 << 16, 1 << 19, array((count_128 + strip_128, 128), bf16)
    )(masked, cot)
    across = in_plane(across, CHIPS[1])
    packed = call(
        pack_kernel, "pack", 4, 1 << 16, 1 << 19, array((count_128, 128), bf16), (),
        [vmem, pl.BlockSpec(memory_space=pl.ANY)],
    )(masked, weight_rows)
    near, far, weight_rows = lax.optimization_barrier((near, far, weight_rows))
    corner = call(
        corner_kernel, "corner", 4, 1 << 16, 1 << 18,
        array((128, 128), bf16),
        (pltpu.VMEM(slabs, f32),),
    )(near, far)
    corner = in_plane(corner, 1)
    mid = rows + 2 * DEPTH
    bulk = call(
        bulk_kernel, "bulk", 24, 3 << 29, 1 << 20, array((width + 2, mid, channels), f32),
        (
            pltpu.VMEM((width + 4, rows + 2 * halo, channels), f32),
            pltpu.VMEM(slabs, f32),
            pltpu.VMEM((width + 4, mid, 9 * channels), bf16),
        ),
    )(masked, near, far, across, weight_rows)
    late, bulk = lax.optimization_barrier((packed, bulk))
    bricks = [packed, across, in_plane(packed, CHIPS[2]), in_plane(late, CHIPS[3])]

    act, gp, *slices = call(
        forward_kernel, "forward", 24, 3 << 29, 1 << 20,
        (brick, array((width + 2, mid, channels), bf16))
        + (array((2 * group, span), bf16),) * len(CHIPS),
        (
            pltpu.VMEM((2, rows, channels), f32),
            pltpu.VMEM((3, 4 * halo, 9 * channels), bf16),
            pltpu.VMEM((width + 2, mid, channels), f32),
            pltpu.VMEM((MEMBERS, group, span), f32),
        ),
    )(bulk, cot, near, far, across, corner, live, weight_rows, pick)
    bricks[2], *slices = lax.optimization_barrier((bricks[2], *slices))
    for place in (3, 2, 1):
        slices[place] = in_plane(slices[place], CHIPS[place])

    grad_input = call(
        input_kernel, "input_gradient", 20, 2 * 512 * 5184 * 256, 4 << 20, brick,
        (
            pltpu.VMEM((width + 2, rows, 9 * channels), bf16),
            pltpu.VMEM((total, channels), bf16),
        ),
    )(gp, live, weight.T)

    blocks = QUAD // 2
    chips = len(CHIPS)
    lanes = dense(total)[0]
    keep, fold = call(
        kernel_grad_kernel, "kernel_gradient", 28, 2 * 432 * 3 * 2048 * 256, 4 << 20,
        (array((group, total), f32), array((group, total), bf16)),
        (
            pltpu.VMEM((blocks, SIDES, 2 * group, span), bf16),
            pltpu.VMEM((9 * 2 * group, blocks * (width + 2) * SIDES * rows), bf16),
            pltpu.VMEM((2 * group, total), f32),
            pltpu.VMEM((blocks, width, SIDES * rows, channels), bf16),
        ),
    )(*slices, *bricks)
    own, *sends = call(
        fold_kernel, "fold", 8, 8 * total * 4, 8 * total * 40,
        (array((8, lanes), f32),) + (array((8, lanes), bf16),) * (planes - 1),
        (
            pltpu.VMEM((group + 8, sum(dense(total))), f32),
            pltpu.VMEM((planes, 8, lanes), f32),
        ),
    )(keep, in_plane(fold, 2))
    got = [swap(sent, "depth", d, planes) for d, sent in list(enumerate(sends, 1))[::-1]]
    grad_input, *got = lax.optimization_barrier((grad_input, *got))
    voxels = count * SIDES * width * rows
    mine = call(
        functools.partial(sum_kernel, float(1.0 / voxels**0.5)),
        "plane_sum", 4, 8 * total * 4, 8 * total * 14, array((8, lanes), bf16),
    )(own, *got)
    grad_weight = call(
        join_kernel, "join", 4, 8 * total, 8 * total * 14, array((channels // count, total), f32)
    )(mine, in_plane(mine, 1))
    shape = features.shape
    return act.reshape(shape), grad_input.reshape(shape), grad_weight


def padded_2(cells, sides, width):
    for axis, dim in sides:
        count = lax.axis_size(axis)
        ends = count - 1
        head = lax.slice_in_dim(cells, 0, width, axis=dim)
        tail = lax.slice_in_dim(cells, cells.shape[dim] - width, cells.shape[dim], axis=dim)
        cells = jnp.concatenate(
            [
                lax.ppermute(tail, axis, [(i, (i + 1) % count) for i in range(ends)]),
                cells,
                lax.ppermute(head, axis, [((i + 1) % count, i) for i in range(ends)]),
            ],
            axis=dim,
        )
    return cells


def gather_taps(padded, width_x, width_y, depth_z, channels, flip):
    pieces = []
    for shift_x in range(3):
        for shift_y in range(3):
            for shift_z in range(3):
                start_x = 2 - shift_x if flip else shift_x
                start_y = 2 - shift_y if flip else shift_y
                start_z = 2 - shift_z if flip else shift_z
                piece = padded[
                    start_x : start_x + width_x,
                    start_y : start_y + width_y,
                    start_z : start_z + depth_z,
                    :,
                ]
                pieces.append(piece.reshape(-1, channels))
    return jnp.concatenate(pieces, axis=1)


def summed_local(features, weight, voxel_mask, cotangent):
    width_x, width_y, depth_z, channels = features.shape
    masked = features * voxel_mask.astype(jnp.bfloat16)[..., None]
    padded = padded_2(masked, (("wide", 0), ("narrow", 1)), 1)
    padded = jnp.pad(padded, ((0, 0), (0, 0), (1, 1), (0, 0)))
    columns = gather_taps(padded, width_x, width_y, depth_z, channels, False)
    pre = jnp.dot(columns, weight, preferred_element_type=jnp.float32)
    live = voxel_mask.reshape(-1, 1).astype(jnp.float32)
    sig = jax.nn.sigmoid(pre)
    activation = (
        (pre * sig * live).astype(jnp.bfloat16).reshape(width_x, width_y, depth_z, channels)
    )
    slope = sig * (1.0 + pre * (1.0 - sig))
    grad_pre = (cotangent.reshape(-1, channels).astype(jnp.float32) * live * slope).astype(
        jnp.bfloat16
    )
    taps = weight.reshape(27, channels, channels)
    grid = grad_pre.reshape(width_x, width_y, depth_z, channels)
    grad_pad = padded_2(grid, (("wide", 0), ("narrow", 1)), 1)
    grad_pad = jnp.pad(grad_pad, ((0, 0), (0, 0), (1, 1), (0, 0)))
    grad_columns = gather_taps(grad_pad, width_x, width_y, depth_z, channels, True)
    flipped = jnp.transpose(taps, (0, 2, 1)).reshape(27 * channels, channels)
    grad_field = jnp.dot(grad_columns, flipped, preferred_element_type=jnp.float32)
    grad_input = (
        (grad_field * live).astype(jnp.bfloat16).reshape(width_x, width_y, depth_z, channels)
    )
    scale = 1.0 / jnp.sqrt(
        jnp.float32(width_x * width_y * depth_z * lax.axis_size("wide") * lax.axis_size("narrow"))
    )
    whole = lax.dot_general(
        grad_pre, columns, (((0,), (0,)), ((), ())), preferred_element_type=jnp.float32
    )
    piece_flat = lax.psum_scatter(
        whole.reshape(-1), ("wide", "narrow"), scatter_dimension=0, tiled=True
    )
    gathered = lax.all_gather(piece_flat, "narrow", axis=0, tiled=True)
    summed = gathered.reshape(channels // lax.axis_size("wide"), 27 * channels)
    grad_weight = summed * scale
    return (activation, grad_input, grad_weight)


def sharded(body, mesh, wide):
    return jax.shard_map(
        body,
        mesh=mesh,
        in_specs=(
            P(wide, "narrow", None, None),
            P(),
            P(wide, "narrow", None),
            P(wide, "narrow", None, None),
        ),
        out_specs=(
            P(wide, "narrow", None, None),
            P(wide, "narrow", None, None),
            P(wide, None),
        ),
        check_vma=False,
    )


def solution(mesh):
    wide, narrow = mesh.shape["wide"], mesh.shape["narrow"]
    if wide != 4 * QUAD or narrow != SIDES:
        return sharded(summed_local, mesh, "wide")
    planes = Mesh(
        mesh.devices.reshape(wide // QUAD, QUAD, narrow), ("depth", "quad", "narrow")
    )
    return sharded(planes_local, planes, WIDE)
```

```python
import functools

import jax
import jax.numpy as jnp
from jax import lax
from jax.experimental import pallas as pl
from jax.experimental.pallas import tpu as pltpu
from jax.sharding import Mesh
from jax.sharding import PartitionSpec as P

WIDE = ("depth", "quad")
QUAD = 4
SIDES = 2
MEMBERS = QUAD * SIDES
CHIPS = (0, 1, 4, 5)
OFFSETS = (-1, 0, 1)
DEPTH = 8


def position():
    quad, side = lax.axis_index("quad"), lax.axis_index("narrow")
    return lax.axis_index("depth"), quad * SIDES + side, quad, side


def shift_z(field, step):
    if step == 0:
        return field
    depth = field.shape[1]
    moved = pltpu.roll(field, (-step) % depth, 1)
    z = lax.broadcasted_iota(jnp.int32, field.shape, 1) + step
    return jnp.where((z >= 0) & (z < depth), moved, 0.0)


def pick_kernel(planes, out_ref):
    index = lax.broadcasted_iota(jnp.int32, out_ref.shape, 0)
    column = lax.broadcasted_iota(jnp.int32, out_ref.shape, 1)
    per = out_ref.shape[1] // (planes * QUAD)
    share = per // SIDES
    group = planes * share
    quad, side = index // (SIDES * group), index // group % SIDES
    plane, row = index // share % planes, index % share
    channel = per * (QUAD * plane + quad) + share * side + row
    out_ref[...] = jnp.where(channel == column, 1.0, 0.0).astype(jnp.bfloat16)


def dense(total):
    tiles = -(-total // 128)
    moved = tiles // 4
    return (tiles - moved) * 128, moved * 128


def fold_rows(block, total):
    kept, moved = dense(total)
    tail = block[:, kept : kept + moved]
    row = lax.broadcasted_iota(jnp.int32, tail.shape, 0)
    pieces = []
    for k in range(3):
        spare = jnp.where(row == 6, pltpu.roll(tail, 6 - k, 0), pltpu.roll(tail, 4 - k, 0))
        pieces.append(jnp.where(row < 6, block[:, k * moved : (k + 1) * moved], spare))
    return jnp.concatenate(pieces + [block[:, 3 * moved : kept]], axis=1)


def unfold_rows(block, total):
    kept, moved = dense(total)
    row = lax.broadcasted_iota(jnp.int32, (8, moved), 0)
    tail = jnp.zeros((8, moved), block.dtype)
    for k in range(3):
        piece = block[:, k * moved : (k + 1) * moved]
        tail = jnp.where(row == k, pltpu.roll(piece, 2 + k, 0), tail)
        tail = jnp.where(row == 3 + k, pltpu.roll(piece, 4 + k, 0), tail)
    return jnp.concatenate([block, tail], axis=1)[:, :total]


def rows_of_128(block):
    half = block.shape[0] // 2
    rest = jnp.concatenate([block[:half, 128:], block[half:, 128:]], axis=1)
    return jnp.concatenate([block[:, :128], rest], axis=0)


def rows_of_192(block):
    count = block.shape[0] * 2 // 3
    rest = jnp.concatenate([block[count:, :64], block[count:, 64:]], axis=0)
    return jnp.concatenate([block[:count], rest], axis=1)


def prepare_kernel(features, cot, mask, first, masked_ref, cot_ref, live_ref, near_ref, far_ref):
    width, rows, channels = features.shape
    f32 = jnp.float32
    flat = mask[...].astype(f32).reshape(width * rows // DEPTH, DEPTH)
    live = jnp.broadcast_to(flat[:, :, None], flat.shape + (channels,)).reshape(features.shape)
    live_ref[...] = live[:, :, :128]
    masked_ref[...] = (features[...].astype(f32) * live).astype(jnp.bfloat16)
    cot_ref[...] = (cot[...].astype(f32) * live).astype(jnp.bfloat16)
    odd = lax.rem(position()[2], 2)
    for ref, upper in ((near_ref, 1 - odd), (far_ref, odd)):
        slabs = [
            masked_ref[pl.ds(upper * (width - 2), 2)],
            cot_ref[pl.ds(upper * (width - 1), 1)],
        ]
        slabs = jnp.concatenate(slabs, axis=0).astype(f32).reshape(3 * rows, channels)
        ref[...] = rows_of_128(slabs).astype(jnp.bfloat16)


def pack_kernel(masked, after, packed_ref):
    count, channels = packed_ref.shape[0] * 128 // masked.shape[2], masked.shape[2]
    block = masked[...].reshape(count, channels)
    packed_ref[...] = rows_of_128(block)


def across_kernel(masked, cot, across_ref):
    width, rows, channels = masked.shape
    packed = rows_of_128(masked[...].reshape(width * rows, channels))
    across_ref[: packed.shape[0]] = packed
    ahead = position()[3] == 0
    grown = cot[...].astype(jnp.float32)
    strip = jnp.where(ahead, grown[:, rows - DEPTH :], grown[:, :DEPTH])
    strip = rows_of_128(strip.reshape(width * DEPTH, channels))
    across_ref[packed.shape[0] :] = strip.astype(jnp.bfloat16)


def corner_kernel(near, far, out_ref, edge):
    _, slabs, rows, channels = edge.shape
    _, _, quad, side = position()
    odd = lax.rem(quad, 2)
    f32 = jnp.float32
    edge[odd] = rows_of_192(far[...].astype(f32)).reshape(edge.shape[1:])
    edge[1 - odd] = rows_of_192(near[...].astype(f32)).reshape(edge.shape[1:])
    halo = 2 * DEPTH
    ahead = side == 0
    strip = jnp.where(ahead, edge[:, :2, rows - halo :], edge[:, :2, :halo])
    cots = jnp.where(ahead, edge[:, 2, rows - DEPTH :], edge[:, 2, :DEPTH])
    both = [strip.reshape(4 * halo, channels), cots.reshape(2 * DEPTH, channels)]
    both = rows_of_128(jnp.concatenate(both, axis=0))
    blank = jnp.zeros((out_ref.shape[0] - both.shape[0], 128), f32)
    out_ref[...] = jnp.concatenate([both, blank], axis=0).astype(jnp.bfloat16)


def turn_kernel(weight, out_ref):
    step = 2 * weight.shape[0]
    total = weight.shape[1]
    for start in range(0, total, step):
        stop = min(start + step, total)
        out_ref[start:stop, :] = weight[:, start:stop].T


def bulk_kernel(masked, near, far, across, weight, pre_ref, ext, edge, cols):
    width, rows, channels = masked.shape
    f32 = jnp.float32
    plane, _, quad, side = position()
    use_low = side.astype(f32)
    use_high = (1 - side).astype(f32)
    place = plane * QUAD + quad
    use_left = (place > 0).astype(f32)
    use_right = (place < QUAD * lax.axis_size("depth") - 1).astype(f32)
    halo = 2 * DEPTH
    tall = rows + 2 * halo
    mid = rows + 2 * DEPTH
    span = width + 4
    odd = lax.rem(quad, 2)
    edge[odd] = rows_of_192(far[...].astype(f32)).reshape(edge.shape[1:])
    edge[1 - odd] = rows_of_192(near[...].astype(f32)).reshape(edge.shape[1:])
    ext[0:2, halo : halo + rows, :] = edge[0, 0:2] * use_left
    ext[2 : 2 + width, halo : halo + rows, :] = masked[...].astype(f32)
    ext[2 + width :, halo : halo + rows, :] = edge[1, 0:2] * use_right
    half = width // 2
    count = width * rows * channels // 128
    held = across[:count].astype(f32).reshape(width + half, rows, 128)
    brick = jnp.where(side == 0, held[:, :halo], held[:, rows - halo :])
    rest = jnp.concatenate([brick[width:, :, :64], brick[width:, :, 64:]], axis=0)
    beside = jnp.concatenate([brick[:width], rest], axis=2)
    blank = jnp.zeros((2, halo, channels), f32)
    for use, start in ((use_low, 0), (use_high, halo + rows)):
        at = slice(start, start + halo)
        ext[0:2, at, :] = blank
        ext[2 : 2 + width, at, :] = beside * use
        ext[2 + width :, at, :] = blank
    field = ext[...].reshape(span * tall // DEPTH, DEPTH, channels)
    for c in OFFSETS:
        moved = shift_z(field, c).reshape(span, tall, channels)
        for b in OFFSETS:
            at = ((b + 1) * 3 + c + 1) * channels
            start = DEPTH * (b + 1)
            cols[:, :, at : at + channels] = moved[:, start : start + mid].astype(jnp.bfloat16)
    nine = 9 * channels
    pre = jnp.zeros(((width + 2) * mid, channels), f32)
    for a in range(3):
        pre += jnp.dot(
            cols[a : a + width + 2].reshape((width + 2) * mid, nine),
            weight[a * nine : (a + 1) * nine, :],
            preferred_element_type=f32,
        )
    pre_ref[...] = pre.reshape(pre_ref.shape)


def forward_kernel(bulk, cot, near, far, across, corner, live, weight, pick, *refs):
    act_ref, gp_ref = refs[:2]
    slice_refs = refs[2 : 2 + len(CHIPS)]
    edge, cols, total, slices = refs[2 + len(CHIPS) :]
    width, rows, channels = cot.shape
    f32 = jnp.float32
    plane, me, quad, side = position()
    use_low = side.astype(f32)
    use_high = (1 - side).astype(f32)
    place = plane * QUAD + quad
    use_left = (place > 0).astype(f32)
    use_right = (place < QUAD * lax.axis_size("depth") - 1).astype(f32)
    halo = 2 * DEPTH
    mid = rows + 2 * DEPTH
    count = 4 * halo + 2 * DEPTH
    both = rows_of_192(corner[...].astype(f32)[: count * channels // 128])
    corners = both[: 4 * halo].reshape(2, 2, halo, channels)
    corners = jnp.concatenate([corners[0] * use_left, corners[1] * use_right], axis=0)
    sources = ((0, 1, None, None), (1, None, None, 2), (None, None, 2, 3))
    blank = jnp.zeros((DEPTH, channels), f32)
    for c in OFFSETS:
        moved = shift_z(corners.reshape(8, DEPTH, channels), c)
        for b in OFFSETS:
            low = {-1: (0, 1), 0: (1, None), 1: (None, None)}[b]
            high = {-1: (None, None), 0: (None, 0), 1: (0, 1)}[b]
            at = ((b + 1) * 3 + c + 1) * channels
            parts = []
            for slab in range(4):
                for below, above in zip(low, high):
                    part = blank if below is None else moved[2 * slab + below] * use_low
                    if above is not None:
                        part = part + moved[2 * slab + above] * use_high
                    parts.append(part)
            for a in range(3):
                rows_a = []
                for source in sources[a]:
                    pair = [blank] * 2 if source is None else parts[2 * source : 2 * source + 2]
                    rows_a += pair
                cols[a, :, at : at + channels] = jnp.concatenate(rows_a, axis=0).astype(
                    jnp.bfloat16
                )
    nine = 9 * channels
    share = jnp.zeros((4 * halo, channels), f32)
    for a in range(3):
        share += jnp.dot(
            cols[a], weight[a * nine : (a + 1) * nine, :], preferred_element_type=f32
        )
    share = share.reshape(4, halo, channels)
    total[...] = bulk[...]
    at = pl.ds(pl.multiple_of((1 - side) * (mid - halo), DEPTH), halo)
    total[0:2, at, :] += share[0:2]
    total[width : width + 2, at, :] += share[2:4]
    pre = total[...].reshape((width + 2) * mid, channels)
    sig = 0.5 * jnp.tanh(0.5 * pre) + 0.5
    act = (pre * sig).reshape(width + 2, mid, channels)[1 : 1 + width, DEPTH : DEPTH + rows]
    act_ref[...] = (act * live[:, :, 0:1]).astype(jnp.bfloat16)
    slope = (sig * (1.0 + pre * (1.0 - sig))).reshape(width + 2, mid, channels)
    ends = both[4 * halo :].reshape(2, 1, DEPTH, channels)
    strip = across[width * rows * channels // 128 :].astype(f32)
    beyond = jnp.concatenate(
        [
            ends[0] * use_left,
            rows_of_192(strip).reshape(width, DEPTH, channels),
            ends[1] * use_right,
        ],
        axis=0,
    )
    odd = lax.rem(quad, 2)
    edge[odd] = rows_of_192(far[...].astype(f32))[2 * rows :]
    edge[1 - odd] = rows_of_192(near[...].astype(f32))[2 * rows :]
    centre = [edge[0:1] * use_left, cot[...].astype(f32), edge[1:2] * use_right]
    centre = jnp.concatenate(centre, axis=0)
    full = jnp.concatenate([beyond * use_low, centre, beyond * use_high], axis=1)
    grad = full * slope
    gp_ref[...] = grad.astype(jnp.bfloat16)
    inner = grad[:, DEPTH : DEPTH + rows].astype(jnp.bfloat16)
    turned = lax.dot_general(
        pick[...],
        inner.reshape((width + 2) * rows, channels),
        (((1,), (1,)), ((), ())),
        preferred_element_type=f32,
    )
    slices[...] = turned.reshape(slices.shape)
    chip = me - lax.rem(quad, 2) * SIDES
    for distance, ref in zip(CHIPS, slice_refs):
        both = [slices[chip ^ distance], slices[(chip ^ distance) + SIDES]]
        ref[...] = jnp.concatenate(both, axis=0).astype(jnp.bfloat16)


def input_kernel(gp, live, turned, out_ref, cols, weight):
    width, rows, channels = out_ref.shape
    f32 = jnp.float32
    tall = rows + 2 * DEPTH
    for tap in range(27):
        weight[tap * channels : (tap + 1) * channels, :] = turned[
            :, tap * channels : (tap + 1) * channels
        ]
    field = gp[...].astype(f32).reshape((width + 2) * tall // DEPTH, DEPTH, channels)
    for c in OFFSETS:
        moved = shift_z(field, -c).reshape(width + 2, tall, channels)
        for b in OFFSETS:
            at = ((b + 1) * 3 + c + 1) * channels
            start = DEPTH * (1 - b)
            cols[:, :, at : at + channels] = moved[:, start : start + rows].astype(jnp.bfloat16)
    nine = 9 * channels
    total = jnp.zeros((width * rows, channels), f32)
    for a in range(3):
        total += jnp.dot(
            cols[2 - a : 2 - a + width].reshape(width * rows, nine),
            weight[a * nine : (a + 1) * nine, :],
            preferred_element_type=f32,
        )
    out_ref[...] = (total.reshape(width, rows, channels) * live[:, :, 0:1]).astype(jnp.bfloat16)


def kernel_grad_kernel(*refs):
    chips = len(CHIPS)
    received, bricks = refs[:chips], refs[chips : 2 * chips]
    keep_ref, send_ref, slices, cols, part, masked = refs[2 * chips :]
    f32 = jnp.float32
    group, lanes = received[0].shape
    blocks, per, lane, channels = masked.shape
    half = lane // 2
    _, _, quad, side = position()
    for i, distance in enumerate(CHIPS):
        block, sided = distance // 4, side ^ (distance % 2)
        slices[block, sided] = received[i][...]
        at_rows = pl.ds(pl.multiple_of(sided * half, half), half)
        for x in range(per):
            shift = 64 * (x // (per // 2))
            rest = bricks[i][pl.ds((per + x % (per // 2)) * half, half)]
            masked[block, x, at_rows, :128] = bricks[i][pl.ds(x * half, half)]
            masked[block, x, at_rows, 128:] = rest[:, shift : shift + 64]
    at = lax.broadcasted_iota(jnp.int32, (group, lane), 1)
    y, z = at // DEPTH, at % DEPTH
    tall = lane // DEPTH
    for block in range(blocks):
        first = slices[block, 0].astype(f32)
        second = slices[block, 1].astype(f32)
        for k in range(per + 2):
            one = first[:, k // 2 * lane : (k // 2 + 1) * lane]
            two = second[:, k // 2 * lane : (k // 2 + 1) * lane]
            if k % 2 == 0:
                base = jnp.where(at < half, one, pltpu.roll(two, half, 1))
            else:
                base = jnp.where(at < half, pltpu.roll(one, half, 1), two)
            pieces = []
            for b in OFFSETS:
                for c in OFFSETS:
                    step = (DEPTH * b + c) % lane
                    moved = base if step == 0 else pltpu.roll(base, step, 1)
                    keep = (y - b >= 0) & (y - b < tall) & (z - c >= 0) & (z - c < DEPTH)
                    pieces.append(jnp.where(keep, moved, 0.0))
            slab = block * (per + 2) + k
            cols[:, slab * lane : (slab + 1) * lane] = jnp.concatenate(pieces, axis=0).astype(
                jnp.bfloat16
            )
    for a in range(3):
        got = jnp.zeros((cols.shape[0], channels), f32)
        for block in range(blocks):
            start = (block * (per + 2) + 2 - a) * lane
            got += jnp.dot(
                cols[:, start : start + per * lane],
                masked[block].reshape(per * lane, channels),
                preferred_element_type=f32,
            )
        got = got.reshape(9, group, channels)
        part[:, a * 9 * channels : (a + 1) * 9 * channels] = jnp.concatenate(
            [got[tap] for tap in range(9)], axis=1
        )
    core = lax.rem(quad, 2)
    half = group // 2
    keep_ref[...] = part[pl.ds(pl.multiple_of(core * half, 8), half)]
    send_ref[...] = part[pl.ds(pl.multiple_of((1 - core) * half, 8), half)].astype(jnp.bfloat16)


def fold_kernel(keep, other, own_ref, *refs):
    *send_refs, both, rows = refs
    planes, eight, _ = rows.shape
    count, total = keep.shape
    share = count // planes
    both[:count, :total] = keep[...] + other[...].astype(jnp.float32)
    both[:, total:] = jnp.zeros((both.shape[0], both.shape[1] - total), jnp.float32)
    for to in range(planes):
        rows[to] = fold_rows(both[share * to : share * to + eight, :], total)
    plane = position()[0]
    own_ref[...] = rows[plane]
    for distance, ref in enumerate(send_refs, 1):
        ref[...] = rows[plane ^ distance].astype(jnp.bfloat16)


def sum_kernel(scale, own, one, two, three, out_ref):
    f32 = jnp.float32
    total = own[...] + one[...].astype(f32) + two[...].astype(f32) + three[...].astype(f32)
    out_ref[...] = (total * scale).astype(out_ref.dtype)


def join_kernel(mine, other, out_ref):
    share = out_ref.shape[0] // SIDES
    ahead = position()[3] == 0
    total = out_ref.shape[1]
    here = unfold_rows(mine[...].astype(jnp.float32), total)
    there = unfold_rows(other[...].astype(jnp.float32), total)
    first = jnp.where(ahead, here, there)
    second = jnp.where(ahead, there, here)
    out_ref[0:share] = first[:share]
    out_ref[share:] = second[:share]


def call(body, name, mebibytes, flops, moved, out_shape, scratch=(), in_specs=None):
    spec = pl.BlockSpec(memory_space=pltpu.VMEM)

    def run(*operands):
        return pl.pallas_call(
            body,
            out_shape=out_shape,
            in_specs=in_specs or [spec] * len(operands),
            out_specs=jax.tree.map(lambda _: spec, out_shape),
            scratch_shapes=scratch,
            compiler_params=pltpu.CompilerParams(vmem_limit_bytes=mebibytes << 20),
            cost_estimate=pl.CostEstimate(flops=flops, bytes_accessed=moved, transcendentals=0),
            name=name,
        )(*operands)

    return run


def planes_local(features, weight, voxel_mask, cotangent):
    bf16 = jnp.bfloat16
    f32 = jnp.float32
    array = jax.ShapeDtypeStruct
    width, wide_y, depth, channels = features.shape
    rows = wide_y * depth
    planes = lax.axis_size("depth")
    count = planes * QUAD
    total = 27 * channels
    halo = 2 * DEPTH
    span = (width + 2) * rows
    share = channels // count // SIDES
    group = planes * share

    def swap(piece, axes, distance, size):
        return lax.ppermute(piece, axes, [(i, i ^ distance) for i in range(size)])

    def in_plane(piece, distance):
        return swap(piece, ("quad", "narrow"), distance, MEMBERS)

    brick = array((width, rows, channels), bf16)
    slab = array((3 * rows * channels // 128, 128), bf16)
    slabs = (2, 3, rows, channels)
    pick = call(
        functools.partial(pick_kernel, planes), "pick", 4, 1 << 32, 1 << 16,
        array((MEMBERS * group, channels), bf16),
    )()
    vmem = pl.BlockSpec(memory_space=pltpu.VMEM)
    masked, cot, live, near, far = call(
        prepare_kernel, "prepare", 16, 1 << 20, 1 << 20,
        (brick, brick, array((width, rows, 128), f32), slab, slab),
        (),
        [vmem] * 3 + [pl.BlockSpec(memory_space=pl.ANY)],
    )(
        features.reshape(width, rows, channels),
        cotangent.reshape(width, rows, channels),
        voxel_mask,
        pick,
    )
    near = swap(near, WIDE, 1, count)
    ends = [min(max(((i + 1) ^ 1) - 1, 0), count - 1) for i in range(count)]
    far = lax.ppermute(far, WIDE, list(enumerate(ends)))
    weight_rows = call(
        turn_kernel, "turn", 8, 1 << 20, 4 << 20, array((total, channels), bf16)
    )(weight.T)
    count_128 = width * rows * channels // 128
    strip_128 = width * DEPTH * channels // 128
    across = call(
        across_kernel, "across", 4, 1 << 16, 1 << 19, array((count_128 + strip_128, 128), bf16)
    )(masked, cot)
    across = in_plane(across, CHIPS[1])
    packed = call(
        pack_kernel, "pack", 4, 1 << 16, 1 << 19, array((count_128, 128), bf16), (),
        [vmem, pl.BlockSpec(memory_space=pl.ANY)],
    )(masked, weight_rows)
    near, far, weight_rows, late = lax.optimization_barrier((near, far, weight_rows, packed))
    corner = call(
        corner_kernel, "corner", 4, 1 << 16, 1 << 18,
        array((128, 128), bf16),
        (pltpu.VMEM(slabs, f32),),
    )(near, far)
    corner = in_plane(corner, 1)
    mid = rows + 2 * DEPTH
    bulk = call(
        bulk_kernel, "bulk", 24, 3 << 29, 1 << 20, array((width + 2, mid, channels), f32),
        (
            pltpu.VMEM((width + 4, rows + 2 * halo, channels), f32),
            pltpu.VMEM(slabs, f32),
            pltpu.VMEM((width + 4, mid, 9 * channels), bf16),
        ),
    )(masked, near, far, across, weight_rows)
    bricks = [packed, across, in_plane(packed, CHIPS[2]), in_plane(late, CHIPS[3])]

    act, gp, *slices = call(
        forward_kernel, "forward", 24, 3 << 29, 1 << 20,
        (brick, array((width + 2, mid, channels), bf16))
        + (array((2 * group, span), bf16),) * len(CHIPS),
        (
            pltpu.VMEM((2, rows, channels), f32),
            pltpu.VMEM((3, 4 * halo, 9 * channels), bf16),
            pltpu.VMEM((width + 2, mid, channels), f32),
            pltpu.VMEM((MEMBERS, group, span), f32),
        ),
    )(bulk, cot, near, far, across, corner, live, weight_rows, pick)
    bricks[2], *slices = lax.optimization_barrier((bricks[2], *slices))
    for place in (3, 2, 1):
        slices[place] = in_plane(slices[place], CHIPS[place])

    grad_input = call(
        input_kernel, "input_gradient", 20, 2 * 512 * 5184 * 256, 4 << 20, brick,
        (
            pltpu.VMEM((width + 2, rows, 9 * channels), bf16),
            pltpu.VMEM((total, channels), bf16),
        ),
    )(gp, live, weight.T)

    blocks = QUAD // 2
    chips = len(CHIPS)
    lanes = dense(total)[0]
    keep, fold = call(
        kernel_grad_kernel, "kernel_gradient", 28, 2 * 432 * 3 * 2048 * 256, 4 << 20,
        (array((group, total), f32), array((group, total), bf16)),
        (
            pltpu.VMEM((blocks, SIDES, 2 * group, span), bf16),
            pltpu.VMEM((9 * 2 * group, blocks * (width + 2) * SIDES * rows), bf16),
            pltpu.VMEM((2 * group, total), f32),
            pltpu.VMEM((blocks, width, SIDES * rows, channels), bf16),
        ),
    )(*slices, *bricks)
    own, *sends = call(
        fold_kernel, "fold", 8, 8 * total * 4, 8 * total * 40,
        (array((8, lanes), f32),) + (array((8, lanes), bf16),) * (planes - 1),
        (
            pltpu.VMEM((group + 8, sum(dense(total))), f32),
            pltpu.VMEM((planes, 8, lanes), f32),
        ),
    )(keep, in_plane(fold, 2))
    got = [swap(sent, "depth", d, planes) for d, sent in list(enumerate(sends, 1))[::-1]]
    grad_input, *got = lax.optimization_barrier((grad_input, *got))
    voxels = count * SIDES * width * rows
    mine = call(
        functools.partial(sum_kernel, float(1.0 / voxels**0.5)),
        "plane_sum", 4, 8 * total * 4, 8 * total * 14, array((8, lanes), bf16),
    )(own, *got)
    grad_weight = call(
        join_kernel, "join", 4, 8 * total, 8 * total * 14, array((channels // count, total), f32)
    )(mine, in_plane(mine, 1))
    shape = features.shape
    return act.reshape(shape), grad_input.reshape(shape), grad_weight


def padded_2(cells, sides, width):
    for axis, dim in sides:
        count = lax.axis_size(axis)
        ends = count - 1
        head = lax.slice_in_dim(cells, 0, width, axis=dim)
        tail = lax.slice_in_dim(cells, cells.shape[dim] - width, cells.shape[dim], axis=dim)
        cells = jnp.concatenate(
            [
                lax.ppermute(tail, axis, [(i, (i + 1) % count) for i in range(ends)]),
                cells,
                lax.ppermute(head, axis, [((i + 1) % count, i) for i in range(ends)]),
            ],
            axis=dim,
        )
    return cells


def gather_taps(padded, width_x, width_y, depth_z, channels, flip):
    pieces = []
    for shift_x in range(3):
        for shift_y in range(3):
            for shift_z in range(3):
                start_x = 2 - shift_x if flip else shift_x
                start_y = 2 - shift_y if flip else shift_y
                start_z = 2 - shift_z if flip else shift_z
                piece = padded[
                    start_x : start_x + width_x,
                    start_y : start_y + width_y,
                    start_z : start_z + depth_z,
                    :,
                ]
                pieces.append(piece.reshape(-1, channels))
    return jnp.concatenate(pieces, axis=1)


def summed_local(features, weight, voxel_mask, cotangent):
    width_x, width_y, depth_z, channels = features.shape
    masked = features * voxel_mask.astype(jnp.bfloat16)[..., None]
    padded = padded_2(masked, (("wide", 0), ("narrow", 1)), 1)
    padded = jnp.pad(padded, ((0, 0), (0, 0), (1, 1), (0, 0)))
    columns = gather_taps(padded, width_x, width_y, depth_z, channels, False)
    pre = jnp.dot(columns, weight, preferred_element_type=jnp.float32)
    live = voxel_mask.reshape(-1, 1).astype(jnp.float32)
    sig = jax.nn.sigmoid(pre)
    activation = (
        (pre * sig * live).astype(jnp.bfloat16).reshape(width_x, width_y, depth_z, channels)
    )
    slope = sig * (1.0 + pre * (1.0 - sig))
    grad_pre = (cotangent.reshape(-1, channels).astype(jnp.float32) * live * slope).astype(
        jnp.bfloat16
    )
    taps = weight.reshape(27, channels, channels)
    grid = grad_pre.reshape(width_x, width_y, depth_z, channels)
    grad_pad = padded_2(grid, (("wide", 0), ("narrow", 1)), 1)
    grad_pad = jnp.pad(grad_pad, ((0, 0), (0, 0), (1, 1), (0, 0)))
    grad_columns = gather_taps(grad_pad, width_x, width_y, depth_z, channels, True)
    flipped = jnp.transpose(taps, (0, 2, 1)).reshape(27 * channels, channels)
    grad_field = jnp.dot(grad_columns, flipped, preferred_element_type=jnp.float32)
    grad_input = (
        (grad_field * live).astype(jnp.bfloat16).reshape(width_x, width_y, depth_z, channels)
    )
    scale = 1.0 / jnp.sqrt(
        jnp.float32(width_x * width_y * depth_z * lax.axis_size("wide") * lax.axis_size("narrow"))
    )
    whole = lax.dot_general(
        grad_pre, columns, (((0,), (0,)), ((), ())), preferred_element_type=jnp.float32
    )
    piece_flat = lax.psum_scatter(
        whole.reshape(-1), ("wide", "narrow"), scatter_dimension=0, tiled=True
    )
    gathered = lax.all_gather(piece_flat, "narrow", axis=0, tiled=True)
    summed = gathered.reshape(channels // lax.axis_size("wide"), 27 * channels)
    grad_weight = summed * scale
    return (activation, grad_input, grad_weight)


def sharded(body, mesh, wide):
    return jax.shard_map(
        body,
        mesh=mesh,
        in_specs=(
            P(wide, "narrow", None, None),
            P(),
            P(wide, "narrow", None),
            P(wide, "narrow", None, None),
        ),
        out_specs=(
            P(wide, "narrow", None, None),
            P(wide, "narrow", None, None),
            P(wide, None),
        ),
        check_vma=False,
    )


def solution(mesh):
    wide, narrow = mesh.shape["wide"], mesh.shape["narrow"]
    if wide != 4 * QUAD or narrow != SIDES:
        return sharded(summed_local, mesh, "wide")
    planes = Mesh(
        mesh.devices.reshape(wide // QUAD, QUAD, narrow), ("depth", "quad", "narrow")
    )
    return sharded(planes_local, planes, WIDE)
```

```python
import functools

import jax
import jax.numpy as jnp
from jax import lax
from jax.experimental import pallas as pl
from jax.experimental.pallas import tpu as pltpu
from jax.sharding import Mesh
from jax.sharding import PartitionSpec as P

WIDE = ("depth", "quad")
QUAD = 4
SIDES = 2
MEMBERS = QUAD * SIDES
CHIPS = (0, 1, 4, 5)
OFFSETS = (-1, 0, 1)
DEPTH = 8


def position():
    quad, side = lax.axis_index("quad"), lax.axis_index("narrow")
    return lax.axis_index("depth"), quad * SIDES + side, quad, side


def shift_z(field, step):
    if step == 0:
        return field
    depth = field.shape[1]
    moved = pltpu.roll(field, (-step) % depth, 1)
    z = lax.broadcasted_iota(jnp.int32, field.shape, 1) + step
    return jnp.where((z >= 0) & (z < depth), moved, 0.0)


def pick_kernel(planes, out_ref):
    index = lax.broadcasted_iota(jnp.int32, out_ref.shape, 0)
    column = lax.broadcasted_iota(jnp.int32, out_ref.shape, 1)
    per = out_ref.shape[1] // (planes * QUAD)
    share = per // SIDES
    group = planes * share
    quad, side = index // (SIDES * group), index // group % SIDES
    plane, row = index // share % planes, index % share
    channel = per * (QUAD * plane + quad) + share * side + row
    out_ref[...] = jnp.where(channel == column, 1.0, 0.0).astype(jnp.bfloat16)


def dense(total):
    tiles = -(-total // 128)
    moved = tiles // 4
    return (tiles - moved) * 128, moved * 128


def fold_rows(block, total):
    kept, moved = dense(total)
    tail = block[:, kept : kept + moved]
    row = lax.broadcasted_iota(jnp.int32, tail.shape, 0)
    pieces = []
    for k in range(3):
        spare = jnp.where(row == 6, pltpu.roll(tail, 6 - k, 0), pltpu.roll(tail, 4 - k, 0))
        pieces.append(jnp.where(row < 6, block[:, k * moved : (k + 1) * moved], spare))
    return jnp.concatenate(pieces + [block[:, 3 * moved : kept]], axis=1)


def unfold_rows(block, total):
    kept, moved = dense(total)
    row = lax.broadcasted_iota(jnp.int32, (8, moved), 0)
    tail = jnp.zeros((8, moved), block.dtype)
    for k in range(3):
        piece = block[:, k * moved : (k + 1) * moved]
        tail = jnp.where(row == k, pltpu.roll(piece, 2 + k, 0), tail)
        tail = jnp.where(row == 3 + k, pltpu.roll(piece, 4 + k, 0), tail)
    return jnp.concatenate([block, tail], axis=1)[:, :total]


def rows_of_128(block):
    half = block.shape[0] // 2
    rest = jnp.concatenate([block[:half, 128:], block[half:, 128:]], axis=1)
    return jnp.concatenate([block[:, :128], rest], axis=0)


def rows_of_192(block):
    count = block.shape[0] * 2 // 3
    rest = jnp.concatenate([block[count:, :64], block[count:, 64:]], axis=0)
    return jnp.concatenate([block[:count], rest], axis=1)


def prepare_kernel(features, cot, mask, first, masked_ref, cot_ref, live_ref, near_ref, far_ref):
    width, rows, channels = features.shape
    f32 = jnp.float32
    flat = mask[...].astype(f32).reshape(width * rows // DEPTH, DEPTH)
    live = jnp.broadcast_to(flat[:, :, None], flat.shape + (channels,)).reshape(features.shape)
    live_ref[...] = live[:, :, :128]
    masked_ref[...] = (features[...].astype(f32) * live).astype(jnp.bfloat16)
    cot_ref[...] = (cot[...].astype(f32) * live).astype(jnp.bfloat16)
    odd = lax.rem(position()[2], 2)
    for ref, upper in ((near_ref, 1 - odd), (far_ref, odd)):
        slabs = [
            masked_ref[pl.ds(upper * (width - 2), 2)],
            cot_ref[pl.ds(upper * (width - 1), 1)],
        ]
        slabs = jnp.concatenate(slabs, axis=0).astype(f32).reshape(3 * rows, channels)
        ref[...] = rows_of_128(slabs).astype(jnp.bfloat16)


def pack_kernel(masked, after, packed_ref):
    count, channels = packed_ref.shape[0] * 128 // masked.shape[2], masked.shape[2]
    block = masked[...].reshape(count, channels)
    packed_ref[...] = rows_of_128(block)


def across_kernel(masked, cot, across_ref):
    width, rows, channels = masked.shape
    packed = rows_of_128(masked[...].reshape(width * rows, channels))
    across_ref[: packed.shape[0]] = packed
    ahead = position()[3] == 0
    grown = cot[...].astype(jnp.float32)
    strip = jnp.where(ahead, grown[:, rows - DEPTH :], grown[:, :DEPTH])
    strip = rows_of_128(strip.reshape(width * DEPTH, channels))
    across_ref[packed.shape[0] :] = strip.astype(jnp.bfloat16)


def corner_kernel(near, far, out_ref, edge):
    _, slabs, rows, channels = edge.shape
    _, _, quad, side = position()
    odd = lax.rem(quad, 2)
    f32 = jnp.float32
    edge[odd] = rows_of_192(far[...].astype(f32)).reshape(edge.shape[1:])
    edge[1 - odd] = rows_of_192(near[...].astype(f32)).reshape(edge.shape[1:])
    halo = 2 * DEPTH
    ahead = side == 0
    strip = jnp.where(ahead, edge[:, :2, rows - halo :], edge[:, :2, :halo])
    cots = jnp.where(ahead, edge[:, 2, rows - DEPTH :], edge[:, 2, :DEPTH])
    both = [strip.reshape(4 * halo, channels), cots.reshape(2 * DEPTH, channels)]
    both = rows_of_128(jnp.concatenate(both, axis=0))
    blank = jnp.zeros((out_ref.shape[0] - both.shape[0], 128), f32)
    out_ref[...] = jnp.concatenate([both, blank], axis=0).astype(jnp.bfloat16)


def turn_kernel(weight, out_ref):
    step = 2 * weight.shape[0]
    total = weight.shape[1]
    for start in range(0, total, step):
        stop = min(start + step, total)
        out_ref[start:stop, :] = weight[:, start:stop].T


def bulk_kernel(masked, near, far, across, weight, pre_ref, ext, edge, cols):
    width, rows, channels = masked.shape
    f32 = jnp.float32
    plane, _, quad, side = position()
    use_low = side.astype(f32)
    use_high = (1 - side).astype(f32)
    place = plane * QUAD + quad
    use_left = (place > 0).astype(f32)
    use_right = (place < QUAD * lax.axis_size("depth") - 1).astype(f32)
    halo = 2 * DEPTH
    tall = rows + 2 * halo
    mid = rows + 2 * DEPTH
    span = width + 4
    odd = lax.rem(quad, 2)
    edge[odd] = rows_of_192(far[...].astype(f32)).reshape(edge.shape[1:])
    edge[1 - odd] = rows_of_192(near[...].astype(f32)).reshape(edge.shape[1:])
    ext[0:2, halo : halo + rows, :] = edge[0, 0:2] * use_left
    ext[2 : 2 + width, halo : halo + rows, :] = masked[...].astype(f32)
    ext[2 + width :, halo : halo + rows, :] = edge[1, 0:2] * use_right
    half = width // 2
    count = width * rows * channels // 128
    held = across[:count].astype(f32).reshape(width + half, rows, 128)
    brick = jnp.where(side == 0, held[:, :halo], held[:, rows - halo :])
    rest = jnp.concatenate([brick[width:, :, :64], brick[width:, :, 64:]], axis=0)
    beside = jnp.concatenate([brick[:width], rest], axis=2)
    blank = jnp.zeros((2, halo, channels), f32)
    for use, start in ((use_low, 0), (use_high, halo + rows)):
        at = slice(start, start + halo)
        ext[0:2, at, :] = blank
        ext[2 : 2 + width, at, :] = beside * use
        ext[2 + width :, at, :] = blank
    field = ext[...].reshape(span * tall // DEPTH, DEPTH, channels)
    for c in OFFSETS:
        moved = shift_z(field, c).reshape(span, tall, channels)
        for b in OFFSETS:
            at = ((b + 1) * 3 + c + 1) * channels
            start = DEPTH * (b + 1)
            cols[:, :, at : at + channels] = moved[:, start : start + mid].astype(jnp.bfloat16)
    nine = 9 * channels
    pre = jnp.zeros(((width + 2) * mid, channels), f32)
    for a in range(3):
        pre += jnp.dot(
            cols[a : a + width + 2].reshape((width + 2) * mid, nine),
            weight[a * nine : (a + 1) * nine, :],
            preferred_element_type=f32,
        )
    pre_ref[...] = pre.reshape(pre_ref.shape)


def forward_kernel(bulk, cot, near, far, across, corner, live, weight, pick, *refs):
    act_ref, gp_ref = refs[:2]
    slice_refs = refs[2 : 2 + len(CHIPS)]
    edge, cols, total, slices = refs[2 + len(CHIPS) :]
    width, rows, channels = cot.shape
    f32 = jnp.float32
    plane, me, quad, side = position()
    use_low = side.astype(f32)
    use_high = (1 - side).astype(f32)
    place = plane * QUAD + quad
    use_left = (place > 0).astype(f32)
    use_right = (place < QUAD * lax.axis_size("depth") - 1).astype(f32)
    halo = 2 * DEPTH
    mid = rows + 2 * DEPTH
    count = 4 * halo + 2 * DEPTH
    both = rows_of_192(corner[...].astype(f32)[: count * channels // 128])
    corners = both[: 4 * halo].reshape(2, 2, halo, channels)
    corners = jnp.concatenate([corners[0] * use_left, corners[1] * use_right], axis=0)
    sources = ((0, 1, None, None), (1, None, None, 2), (None, None, 2, 3))
    blank = jnp.zeros((DEPTH, channels), f32)
    for c in OFFSETS:
        moved = shift_z(corners.reshape(8, DEPTH, channels), c)
        for b in OFFSETS:
            low = {-1: (0, 1), 0: (1, None), 1: (None, None)}[b]
            high = {-1: (None, None), 0: (None, 0), 1: (0, 1)}[b]
            at = ((b + 1) * 3 + c + 1) * channels
            parts = []
            for slab in range(4):
                for below, above in zip(low, high):
                    part = blank if below is None else moved[2 * slab + below] * use_low
                    if above is not None:
                        part = part + moved[2 * slab + above] * use_high
                    parts.append(part)
            for a in range(3):
                rows_a = []
                for source in sources[a]:
                    pair = [blank] * 2 if source is None else parts[2 * source : 2 * source + 2]
                    rows_a += pair
                cols[a, :, at : at + channels] = jnp.concatenate(rows_a, axis=0).astype(
                    jnp.bfloat16
                )
    nine = 9 * channels
    share = jnp.zeros((4 * halo, channels), f32)
    for a in range(3):
        share += jnp.dot(
            cols[a], weight[a * nine : (a + 1) * nine, :], preferred_element_type=f32
        )
    share = share.reshape(4, halo, channels)
    total[...] = bulk[...]
    at = pl.ds(pl.multiple_of((1 - side) * (mid - halo), DEPTH), halo)
    total[0:2, at, :] += share[0:2]
    total[width : width + 2, at, :] += share[2:4]
    pre = total[...].reshape((width + 2) * mid, channels)
    sig = 0.5 * jnp.tanh(0.5 * pre) + 0.5
    act = (pre * sig).reshape(width + 2, mid, channels)[1 : 1 + width, DEPTH : DEPTH + rows]
    act_ref[...] = (act * live[:, :, 0:1]).astype(jnp.bfloat16)
    slope = (sig * (1.0 + pre * (1.0 - sig))).reshape(width + 2, mid, channels)
    ends = both[4 * halo :].reshape(2, 1, DEPTH, channels)
    strip = across[width * rows * channels // 128 :].astype(f32)
    beyond = jnp.concatenate(
        [
            ends[0] * use_left,
            rows_of_192(strip).reshape(width, DEPTH, channels),
            ends[1] * use_right,
        ],
        axis=0,
    )
    odd = lax.rem(quad, 2)
    edge[odd] = rows_of_192(far[...].astype(f32))[2 * rows :]
    edge[1 - odd] = rows_of_192(near[...].astype(f32))[2 * rows :]
    centre = [edge[0:1] * use_left, cot[...].astype(f32), edge[1:2] * use_right]
    centre = jnp.concatenate(centre, axis=0)
    full = jnp.concatenate([beyond * use_low, centre, beyond * use_high], axis=1)
    grad = full * slope
    gp_ref[...] = grad.astype(jnp.bfloat16)
    inner = grad[:, DEPTH : DEPTH + rows].astype(jnp.bfloat16)
    turned = lax.dot_general(
        pick[...],
        inner.reshape((width + 2) * rows, channels),
        (((1,), (1,)), ((), ())),
        preferred_element_type=f32,
    )
    slices[...] = turned.reshape(slices.shape)
    chip = me - lax.rem(quad, 2) * SIDES
    for distance, ref in zip(CHIPS, slice_refs):
        both = [slices[chip ^ distance], slices[(chip ^ distance) + SIDES]]
        ref[...] = jnp.concatenate(both, axis=0).astype(jnp.bfloat16)


def input_kernel(gp, live, turned, out_ref, cols, weight):
    width, rows, channels = out_ref.shape
    f32 = jnp.float32
    tall = rows + 2 * DEPTH
    for tap in range(27):
        weight[tap * channels : (tap + 1) * channels, :] = turned[
            :, tap * channels : (tap + 1) * channels
        ]
    field = gp[...].astype(f32).reshape((width + 2) * tall // DEPTH, DEPTH, channels)
    for c in OFFSETS:
        moved = shift_z(field, -c).reshape(width + 2, tall, channels)
        for b in OFFSETS:
            at = ((b + 1) * 3 + c + 1) * channels
            start = DEPTH * (1 - b)
            cols[:, :, at : at + channels] = moved[:, start : start + rows].astype(jnp.bfloat16)
    nine = 9 * channels
    total = jnp.zeros((width * rows, channels), f32)
    for a in range(3):
        total += jnp.dot(
            cols[2 - a : 2 - a + width].reshape(width * rows, nine),
            weight[a * nine : (a + 1) * nine, :],
            preferred_element_type=f32,
        )
    out_ref[...] = (total.reshape(width, rows, channels) * live[:, :, 0:1]).astype(jnp.bfloat16)


def pair_product(received, bricks, cols, masked):
    f32 = jnp.float32
    group, lanes = received[0].shape
    per, lane, channels = masked.shape
    half = lane // 2
    side = position()[3]
    for i, brick in enumerate(bricks):
        at_rows = pl.ds(pl.multiple_of((side ^ i) * half, half), half)
        for x in range(per):
            shift = 64 * (x // (per // 2))
            rest = brick[pl.ds((per + x % (per // 2)) * half, half)]
            masked[x, at_rows, :128] = brick[pl.ds(x * half, half)]
            masked[x, at_rows, 128:] = rest[:, shift : shift + 64]
    at = lax.broadcasted_iota(jnp.int32, (group, lane), 1)
    y, z = at // DEPTH, at % DEPTH
    tall = lane // DEPTH
    own, other = (ref[...].astype(f32) for ref in received)
    first = jnp.where(side == 0, own, other)
    second = jnp.where(side == 0, other, own)
    for k in range(per + 2):
        one = first[:, k // 2 * lane : (k // 2 + 1) * lane]
        two = second[:, k // 2 * lane : (k // 2 + 1) * lane]
        if k % 2 == 0:
            base = jnp.where(at < half, one, pltpu.roll(two, half, 1))
        else:
            base = jnp.where(at < half, pltpu.roll(one, half, 1), two)
        pieces = []
        for b in OFFSETS:
            for c in OFFSETS:
                step = (DEPTH * b + c) % lane
                moved = base if step == 0 else pltpu.roll(base, step, 1)
                keep = (y - b >= 0) & (y - b < tall) & (z - c >= 0) & (z - c < DEPTH)
                pieces.append(jnp.where(keep, moved, 0.0))
        cols[:, k * lane : (k + 1) * lane] = jnp.concatenate(pieces, axis=0).astype(jnp.bfloat16)
    field = masked[...].reshape(per * lane, channels)
    for a in range(3):
        start = (2 - a) * lane
        got = jnp.dot(
            cols[:, start : start + per * lane], field, preferred_element_type=f32
        ).reshape(9, group, channels)
        yield a, jnp.concatenate([got[tap] for tap in range(9)], axis=1)


def first_pair_kernel(own, other, brick, across, part_ref, cols, masked):
    for a, rows in pair_product((own, other), (brick, across), cols, masked):
        width = rows.shape[1]
        part_ref[:, a * width : (a + 1) * width] = rows


def second_pair_kernel(
    before, own, other, brick, across, keep_ref, send_ref, part, cols, masked
):
    for a, rows in pair_product((own, other), (brick, across), cols, masked):
        width = rows.shape[1]
        at = slice(a * width, (a + 1) * width)
        part[:, at] = before[:, at] + rows
    core = lax.rem(position()[2], 2)
    half = part.shape[0] // 2
    keep_ref[...] = part[pl.ds(pl.multiple_of(core * half, 8), half)]
    send_ref[...] = part[pl.ds(pl.multiple_of((1 - core) * half, 8), half)].astype(jnp.bfloat16)


def fold_kernel(keep, other, own_ref, *refs):
    *send_refs, both, rows = refs
    planes, eight, _ = rows.shape
    count, total = keep.shape
    share = count // planes
    both[:count, :total] = keep[...] + other[...].astype(jnp.float32)
    both[:, total:] = jnp.zeros((both.shape[0], both.shape[1] - total), jnp.float32)
    for to in range(planes):
        rows[to] = fold_rows(both[share * to : share * to + eight, :], total)
    plane = position()[0]
    own_ref[...] = rows[plane]
    for distance, ref in enumerate(send_refs, 1):
        ref[...] = rows[plane ^ distance].astype(jnp.bfloat16)


def sum_kernel(scale, own, one, two, three, out_ref):
    f32 = jnp.float32
    total = own[...] + one[...].astype(f32) + two[...].astype(f32) + three[...].astype(f32)
    out_ref[...] = (total * scale).astype(out_ref.dtype)


def join_kernel(mine, other, out_ref):
    share = out_ref.shape[0] // SIDES
    ahead = position()[3] == 0
    total = out_ref.shape[1]
    here = unfold_rows(mine[...].astype(jnp.float32), total)
    there = unfold_rows(other[...].astype(jnp.float32), total)
    first = jnp.where(ahead, here, there)
    second = jnp.where(ahead, there, here)
    out_ref[0:share] = first[:share]
    out_ref[share:] = second[:share]


def call(body, name, mebibytes, flops, moved, out_shape, scratch=(), in_specs=None):
    spec = pl.BlockSpec(memory_space=pltpu.VMEM)

    def run(*operands):
        return pl.pallas_call(
            body,
            out_shape=out_shape,
            in_specs=in_specs or [spec] * len(operands),
            out_specs=jax.tree.map(lambda _: spec, out_shape),
            scratch_shapes=scratch,
            compiler_params=pltpu.CompilerParams(vmem_limit_bytes=mebibytes << 20),
            cost_estimate=pl.CostEstimate(flops=flops, bytes_accessed=moved, transcendentals=0),
            name=name,
        )(*operands)

    return run


def planes_local(features, weight, voxel_mask, cotangent):
    bf16 = jnp.bfloat16
    f32 = jnp.float32
    array = jax.ShapeDtypeStruct
    width, wide_y, depth, channels = features.shape
    rows = wide_y * depth
    planes = lax.axis_size("depth")
    count = planes * QUAD
    total = 27 * channels
    halo = 2 * DEPTH
    span = (width + 2) * rows
    share = channels // count // SIDES
    group = planes * share

    def swap(piece, axes, distance, size):
        return lax.ppermute(piece, axes, [(i, i ^ distance) for i in range(size)])

    def in_plane(piece, distance):
        return swap(piece, ("quad", "narrow"), distance, MEMBERS)

    brick = array((width, rows, channels), bf16)
    slab = array((3 * rows * channels // 128, 128), bf16)
    slabs = (2, 3, rows, channels)
    pick = call(
        functools.partial(pick_kernel, planes), "pick", 4, 1 << 32, 1 << 16,
        array((MEMBERS * group, channels), bf16),
    )()
    vmem = pl.BlockSpec(memory_space=pltpu.VMEM)
    masked, cot, live, near, far = call(
        prepare_kernel, "prepare", 16, 1 << 20, 1 << 20,
        (brick, brick, array((width, rows, 128), f32), slab, slab),
        (),
        [vmem] * 3 + [pl.BlockSpec(memory_space=pl.ANY)],
    )(
        features.reshape(width, rows, channels),
        cotangent.reshape(width, rows, channels),
        voxel_mask,
        pick,
    )
    near = swap(near, WIDE, 1, count)
    ends = [min(max(((i + 1) ^ 1) - 1, 0), count - 1) for i in range(count)]
    far = lax.ppermute(far, WIDE, list(enumerate(ends)))
    weight_rows = call(
        turn_kernel, "turn", 8, 1 << 20, 4 << 20, array((total, channels), bf16)
    )(weight.T)
    count_128 = width * rows * channels // 128
    strip_128 = width * DEPTH * channels // 128
    across = call(
        across_kernel, "across", 4, 1 << 16, 1 << 19, array((count_128 + strip_128, 128), bf16)
    )(masked, cot)
    across = in_plane(across, CHIPS[1])
    packed = call(
        pack_kernel, "pack", 4, 1 << 16, 1 << 19, array((count_128, 128), bf16), (),
        [vmem, pl.BlockSpec(memory_space=pl.ANY)],
    )(masked, weight_rows)
    near, far, weight_rows, late = lax.optimization_barrier((near, far, weight_rows, packed))
    corner = call(
        corner_kernel, "corner", 4, 1 << 16, 1 << 18,
        array((128, 128), bf16),
        (pltpu.VMEM(slabs, f32),),
    )(near, far)
    corner = in_plane(corner, 1)
    mid = rows + 2 * DEPTH
    bulk = call(
        bulk_kernel, "bulk", 24, 3 << 29, 1 << 20, array((width + 2, mid, channels), f32),
        (
            pltpu.VMEM((width + 4, rows + 2 * halo, channels), f32),
            pltpu.VMEM(slabs, f32),
            pltpu.VMEM((width + 4, mid, 9 * channels), bf16),
        ),
    )(masked, near, far, across, weight_rows)
    bricks = [packed, across, in_plane(packed, CHIPS[2]), in_plane(late, CHIPS[3])]

    act, gp, *slices = call(
        forward_kernel, "forward", 24, 3 << 29, 1 << 20,
        (brick, array((width + 2, mid, channels), bf16))
        + (array((2 * group, span), bf16),) * len(CHIPS),
        (
            pltpu.VMEM((2, rows, channels), f32),
            pltpu.VMEM((3, 4 * halo, 9 * channels), bf16),
            pltpu.VMEM((width + 2, mid, channels), f32),
            pltpu.VMEM((MEMBERS, group, span), f32),
        ),
    )(bulk, cot, near, far, across, corner, live, weight_rows, pick)
    bricks[2], *slices = lax.optimization_barrier((bricks[2], *slices))
    for place in (3, 2, 1):
        slices[place] = in_plane(slices[place], CHIPS[place])

    grad_input = call(
        input_kernel, "input_gradient", 20, 2 * 512 * 5184 * 256, 4 << 20, brick,
        (
            pltpu.VMEM((width + 2, rows, 9 * channels), bf16),
            pltpu.VMEM((total, channels), bf16),
        ),
    )(gp, live, weight.T)

    lanes = dense(total)[0]
    scratch = (
        pltpu.VMEM((9 * 2 * group, (width + 2) * SIDES * rows), bf16),
        pltpu.VMEM((width, SIDES * rows, channels), bf16),
    )
    part = call(
        first_pair_kernel, "first_pair", 16, 1 << 30, 2 << 20,
        array((2 * group, total), f32), scratch,
    )(*slices[:2], *bricks[:2])
    keep, fold = call(
        second_pair_kernel, "second_pair", 16, 1 << 30, 2 << 20,
        (array((group, total), f32), array((group, total), bf16)),
        (pltpu.VMEM((2 * group, total), f32),) + scratch,
    )(part, *slices[2:], *bricks[2:])
    own, *sends = call(
        fold_kernel, "fold", 8, 8 * total * 4, 8 * total * 40,
        (array((8, lanes), f32),) + (array((8, lanes), bf16),) * (planes - 1),
        (
            pltpu.VMEM((group + 8, sum(dense(total))), f32),
            pltpu.VMEM((planes, 8, lanes), f32),
        ),
    )(keep, in_plane(fold, 2))
    got = [swap(sent, "depth", d, planes) for d, sent in list(enumerate(sends, 1))[::-1]]
    grad_input, *got = lax.optimization_barrier((grad_input, *got))
    voxels = count * SIDES * width * rows
    mine = call(
        functools.partial(sum_kernel, float(1.0 / voxels**0.5)),
        "plane_sum", 4, 8 * total * 4, 8 * total * 14, array((8, lanes), bf16),
    )(own, *got)
    grad_weight = call(
        join_kernel, "join", 4, 8 * total, 8 * total * 14, array((channels // count, total), f32)
    )(mine, in_plane(mine, 1))
    shape = features.shape
    return act.reshape(shape), grad_input.reshape(shape), grad_weight


def padded_2(cells, sides, width):
    for axis, dim in sides:
        count = lax.axis_size(axis)
        ends = count - 1
        head = lax.slice_in_dim(cells, 0, width, axis=dim)
        tail = lax.slice_in_dim(cells, cells.shape[dim] - width, cells.shape[dim], axis=dim)
        cells = jnp.concatenate(
            [
                lax.ppermute(tail, axis, [(i, (i + 1) % count) for i in range(ends)]),
                cells,
                lax.ppermute(head, axis, [((i + 1) % count, i) for i in range(ends)]),
            ],
            axis=dim,
        )
    return cells


def gather_taps(padded, width_x, width_y, depth_z, channels, flip):
    pieces = []
    for shift_x in range(3):
        for shift_y in range(3):
            for shift_z in range(3):
                start_x = 2 - shift_x if flip else shift_x
                start_y = 2 - shift_y if flip else shift_y
                start_z = 2 - shift_z if flip else shift_z
                piece = padded[
                    start_x : start_x + width_x,
                    start_y : start_y + width_y,
                    start_z : start_z + depth_z,
                    :,
                ]
                pieces.append(piece.reshape(-1, channels))
    return jnp.concatenate(pieces, axis=1)


def summed_local(features, weight, voxel_mask, cotangent):
    width_x, width_y, depth_z, channels = features.shape
    masked = features * voxel_mask.astype(jnp.bfloat16)[..., None]
    padded = padded_2(masked, (("wide", 0), ("narrow", 1)), 1)
    padded = jnp.pad(padded, ((0, 0), (0, 0), (1, 1), (0, 0)))
    columns = gather_taps(padded, width_x, width_y, depth_z, channels, False)
    pre = jnp.dot(columns, weight, preferred_element_type=jnp.float32)
    live = voxel_mask.reshape(-1, 1).astype(jnp.float32)
    sig = jax.nn.sigmoid(pre)
    activation = (
        (pre * sig * live).astype(jnp.bfloat16).reshape(width_x, width_y, depth_z, channels)
    )
    slope = sig * (1.0 + pre * (1.0 - sig))
    grad_pre = (cotangent.reshape(-1, channels).astype(jnp.float32) * live * slope).astype(
        jnp.bfloat16
    )
    taps = weight.reshape(27, channels, channels)
    grid = grad_pre.reshape(width_x, width_y, depth_z, channels)
    grad_pad = padded_2(grid, (("wide", 0), ("narrow", 1)), 1)
    grad_pad = jnp.pad(grad_pad, ((0, 0), (0, 0), (1, 1), (0, 0)))
    grad_columns = gather_taps(grad_pad, width_x, width_y, depth_z, channels, True)
    flipped = jnp.transpose(taps, (0, 2, 1)).reshape(27 * channels, channels)
    grad_field = jnp.dot(grad_columns, flipped, preferred_element_type=jnp.float32)
    grad_input = (
        (grad_field * live).astype(jnp.bfloat16).reshape(width_x, width_y, depth_z, channels)
    )
    scale = 1.0 / jnp.sqrt(
        jnp.float32(width_x * width_y * depth_z * lax.axis_size("wide") * lax.axis_size("narrow"))
    )
    whole = lax.dot_general(
        grad_pre, columns, (((0,), (0,)), ((), ())), preferred_element_type=jnp.float32
    )
    piece_flat = lax.psum_scatter(
        whole.reshape(-1), ("wide", "narrow"), scatter_dimension=0, tiled=True
    )
    gathered = lax.all_gather(piece_flat, "narrow", axis=0, tiled=True)
    summed = gathered.reshape(channels // lax.axis_size("wide"), 27 * channels)
    grad_weight = summed * scale
    return (activation, grad_input, grad_weight)


def sharded(body, mesh, wide):
    return jax.shard_map(
        body,
        mesh=mesh,
        in_specs=(
            P(wide, "narrow", None, None),
            P(),
            P(wide, "narrow", None),
            P(wide, "narrow", None, None),
        ),
        out_specs=(
            P(wide, "narrow", None, None),
            P(wide, "narrow", None, None),
            P(wide, None),
        ),
        check_vma=False,
    )


def solution(mesh):
    wide, narrow = mesh.shape["wide"], mesh.shape["narrow"]
    if wide != 4 * QUAD or narrow != SIDES:
        return sharded(summed_local, mesh, "wide")
    planes = Mesh(
        mesh.devices.reshape(wide // QUAD, QUAD, narrow), ("depth", "quad", "narrow")
    )
    return sharded(planes_local, planes, WIDE)
```

```python
import functools

import jax
import jax.numpy as jnp
from jax import lax
from jax.experimental import pallas as pl
from jax.experimental.pallas import tpu as pltpu
from jax.sharding import Mesh
from jax.sharding import PartitionSpec as P

WIDE = ("depth", "quad")
QUAD = 4
SIDES = 2
MEMBERS = QUAD * SIDES
CHIPS = (0, 1, 4, 5)
OFFSETS = (-1, 0, 1)
DEPTH = 8


def position():
    quad, side = lax.axis_index("quad"), lax.axis_index("narrow")
    return lax.axis_index("depth"), quad * SIDES + side, quad, side


def shift_z(field, step):
    if step == 0:
        return field
    depth = field.shape[1]
    moved = pltpu.roll(field, (-step) % depth, 1)
    z = lax.broadcasted_iota(jnp.int32, field.shape, 1) + step
    return jnp.where((z >= 0) & (z < depth), moved, 0.0)


def pick_kernel(planes, out_ref):
    index = lax.broadcasted_iota(jnp.int32, out_ref.shape, 0)
    column = lax.broadcasted_iota(jnp.int32, out_ref.shape, 1)
    per = out_ref.shape[1] // (planes * QUAD)
    share = per // SIDES
    group = planes * share
    quad, side = index // (SIDES * group), index // group % SIDES
    plane, row = index // share % planes, index % share
    channel = per * (QUAD * plane + quad) + share * side + row
    out_ref[...] = jnp.where(channel == column, 1.0, 0.0).astype(jnp.bfloat16)


def dense(total):
    tiles = -(-total // 128)
    moved = tiles // 4
    return (tiles - moved) * 128, moved * 128


def fold_rows(block, total):
    kept, moved = dense(total)
    tail = block[:, kept : kept + moved]
    row = lax.broadcasted_iota(jnp.int32, tail.shape, 0)
    pieces = []
    for k in range(3):
        spare = jnp.where(row == 6, pltpu.roll(tail, 6 - k, 0), pltpu.roll(tail, 4 - k, 0))
        pieces.append(jnp.where(row < 6, block[:, k * moved : (k + 1) * moved], spare))
    return jnp.concatenate(pieces + [block[:, 3 * moved : kept]], axis=1)


def unfold_rows(block, total):
    kept, moved = dense(total)
    row = lax.broadcasted_iota(jnp.int32, (8, moved), 0)
    tail = jnp.zeros((8, moved), block.dtype)
    for k in range(3):
        piece = block[:, k * moved : (k + 1) * moved]
        tail = jnp.where(row == k, pltpu.roll(piece, 2 + k, 0), tail)
        tail = jnp.where(row == 3 + k, pltpu.roll(piece, 4 + k, 0), tail)
    return jnp.concatenate([block, tail], axis=1)[:, :total]


def rows_of_128(block):
    half = block.shape[0] // 2
    rest = jnp.concatenate([block[:half, 128:], block[half:, 128:]], axis=1)
    return jnp.concatenate([block[:, :128], rest], axis=0)


def rows_of_192(block):
    count = block.shape[0] * 2 // 3
    rest = jnp.concatenate([block[count:, :64], block[count:, 64:]], axis=0)
    return jnp.concatenate([block[:count], rest], axis=1)


def prepare_kernel(features, cot, mask, first, masked_ref, cot_ref, live_ref, near_ref, far_ref):
    width, rows, channels = features.shape
    f32 = jnp.float32
    flat = mask[...].astype(f32).reshape(width * rows // DEPTH, DEPTH)
    live = jnp.broadcast_to(flat[:, :, None], flat.shape + (channels,)).reshape(features.shape)
    live_ref[...] = live[:, :, :128]
    masked_ref[...] = (features[...].astype(f32) * live).astype(jnp.bfloat16)
    cot_ref[...] = (cot[...].astype(f32) * live).astype(jnp.bfloat16)
    odd = lax.rem(position()[2], 2)
    for ref, upper in ((near_ref, 1 - odd), (far_ref, odd)):
        slabs = [
            masked_ref[pl.ds(upper * (width - 2), 2)],
            cot_ref[pl.ds(upper * (width - 1), 1)],
        ]
        slabs = jnp.concatenate(slabs, axis=0).astype(f32).reshape(3 * rows, channels)
        ref[...] = rows_of_128(slabs).astype(jnp.bfloat16)


def pack_kernel(masked, after, packed_ref):
    count, channels = packed_ref.shape[0] * 128 // masked.shape[2], masked.shape[2]
    block = masked[...].reshape(count, channels)
    packed_ref[...] = rows_of_128(block)


def across_kernel(masked, cot, across_ref):
    width, rows, channels = masked.shape
    packed = rows_of_128(masked[...].reshape(width * rows, channels))
    across_ref[: packed.shape[0]] = packed
    ahead = position()[3] == 0
    grown = cot[...].astype(jnp.float32)
    strip = jnp.where(ahead, grown[:, rows - DEPTH :], grown[:, :DEPTH])
    strip = rows_of_128(strip.reshape(width * DEPTH, channels))
    across_ref[packed.shape[0] :] = strip.astype(jnp.bfloat16)


def corner_kernel(near, far, out_ref, edge):
    _, slabs, rows, channels = edge.shape
    _, _, quad, side = position()
    odd = lax.rem(quad, 2)
    f32 = jnp.float32
    edge[odd] = rows_of_192(far[...].astype(f32)).reshape(edge.shape[1:])
    edge[1 - odd] = rows_of_192(near[...].astype(f32)).reshape(edge.shape[1:])
    halo = 2 * DEPTH
    ahead = side == 0
    strip = jnp.where(ahead, edge[:, :2, rows - halo :], edge[:, :2, :halo])
    cots = jnp.where(ahead, edge[:, 2, rows - DEPTH :], edge[:, 2, :DEPTH])
    both = [strip.reshape(4 * halo, channels), cots.reshape(2 * DEPTH, channels)]
    both = rows_of_128(jnp.concatenate(both, axis=0))
    blank = jnp.zeros((out_ref.shape[0] - both.shape[0], 128), f32)
    out_ref[...] = jnp.concatenate([both, blank], axis=0).astype(jnp.bfloat16)


def turn_kernel(weight, out_ref):
    step = 2 * weight.shape[0]
    total = weight.shape[1]
    for start in range(0, total, step):
        stop = min(start + step, total)
        out_ref[start:stop, :] = weight[:, start:stop].T


def bulk_kernel(masked, near, far, across, weight, pre_ref, ext, edge, cols):
    width, rows, channels = masked.shape
    f32 = jnp.float32
    plane, _, quad, side = position()
    use_low = side.astype(f32)
    use_high = (1 - side).astype(f32)
    place = plane * QUAD + quad
    use_left = (place > 0).astype(f32)
    use_right = (place < QUAD * lax.axis_size("depth") - 1).astype(f32)
    halo = 2 * DEPTH
    tall = rows + 2 * halo
    mid = rows + 2 * DEPTH
    span = width + 4
    odd = lax.rem(quad, 2)
    edge[odd] = rows_of_192(far[...].astype(f32)).reshape(edge.shape[1:])
    edge[1 - odd] = rows_of_192(near[...].astype(f32)).reshape(edge.shape[1:])
    ext[0:2, halo : halo + rows, :] = edge[0, 0:2] * use_left
    ext[2 : 2 + width, halo : halo + rows, :] = masked[...].astype(f32)
    ext[2 + width :, halo : halo + rows, :] = edge[1, 0:2] * use_right
    half = width // 2
    count = width * rows * channels // 128
    held = across[:count].astype(f32).reshape(width + half, rows, 128)
    brick = jnp.where(side == 0, held[:, :halo], held[:, rows - halo :])
    rest = jnp.concatenate([brick[width:, :, :64], brick[width:, :, 64:]], axis=0)
    beside = jnp.concatenate([brick[:width], rest], axis=2)
    blank = jnp.zeros((2, halo, channels), f32)
    for use, start in ((use_low, 0), (use_high, halo + rows)):
        at = slice(start, start + halo)
        ext[0:2, at, :] = blank
        ext[2 : 2 + width, at, :] = beside * use
        ext[2 + width :, at, :] = blank
    field = ext[...].reshape(span * tall // DEPTH, DEPTH, channels)
    for c in OFFSETS:
        moved = shift_z(field, c).reshape(span, tall, channels)
        for b in OFFSETS:
            at = ((b + 1) * 3 + c + 1) * channels
            start = DEPTH * (b + 1)
            cols[:, :, at : at + channels] = moved[:, start : start + mid].astype(jnp.bfloat16)
    nine = 9 * channels
    pre = jnp.zeros(((width + 2) * mid, channels), f32)
    for a in range(3):
        pre += jnp.dot(
            cols[a : a + width + 2].reshape((width + 2) * mid, nine),
            weight[a * nine : (a + 1) * nine, :],
            preferred_element_type=f32,
        )
    pre_ref[...] = pre.reshape(pre_ref.shape)


def forward_kernel(bulk, cot, near, far, across, corner, live, weight, pick, *refs):
    act_ref, gp_ref = refs[:2]
    slice_refs = refs[2 : 2 + len(CHIPS)]
    edge, cols, total, slices = refs[2 + len(CHIPS) :]
    width, rows, channels = cot.shape
    f32 = jnp.float32
    plane, me, quad, side = position()
    use_low = side.astype(f32)
    use_high = (1 - side).astype(f32)
    place = plane * QUAD + quad
    use_left = (place > 0).astype(f32)
    use_right = (place < QUAD * lax.axis_size("depth") - 1).astype(f32)
    halo = 2 * DEPTH
    mid = rows + 2 * DEPTH
    count = 4 * halo + 2 * DEPTH
    both = rows_of_192(corner[...].astype(f32)[: count * channels // 128])
    corners = both[: 4 * halo].reshape(2, 2, halo, channels)
    corners = jnp.concatenate([corners[0] * use_left, corners[1] * use_right], axis=0)
    sources = ((0, 1, None, None), (1, None, None, 2), (None, None, 2, 3))
    blank = jnp.zeros((DEPTH, channels), f32)
    six = 6 * channels
    for c in OFFSETS:
        moved = shift_z(corners.reshape(8, DEPTH, channels), c)
        for b, low, high in ((0, (0, 1), (None, 0)), (1, (1, None), (0, 1))):
            at = (b * 3 + c + 1) * channels
            parts = []
            for slab in range(4):
                for below, above in zip(low, high):
                    part = blank if below is None else moved[2 * slab + below] * use_low
                    if above is not None:
                        part = part + moved[2 * slab + above] * use_high
                    parts.append(part)
            for a in range(3):
                rows_a = []
                for source in sources[a]:
                    pair = [blank] * 2 if source is None else parts[2 * source : 2 * source + 2]
                    rows_a += pair
                cols[a, :, at : at + channels] = jnp.concatenate(rows_a, axis=0).astype(
                    jnp.bfloat16
                )
    share = jnp.zeros((4 * halo, channels), f32)
    for a in range(3):
        taps = pl.ds(pl.multiple_of((3 * a + 1 - side) * 3 * channels, 16), six)
        share += jnp.dot(cols[a], weight[taps], preferred_element_type=f32)
    share = share.reshape(4, halo, channels)
    total[...] = bulk[...]
    at = pl.ds(pl.multiple_of((1 - side) * (mid - halo), DEPTH), halo)
    total[0:2, at, :] += share[0:2]
    total[width : width + 2, at, :] += share[2:4]
    pre = total[...].reshape((width + 2) * mid, channels)
    sig = 0.5 * jnp.tanh(0.5 * pre) + 0.5
    act = (pre * sig).reshape(width + 2, mid, channels)[1 : 1 + width, DEPTH : DEPTH + rows]
    act_ref[...] = (act * live[:, :, 0:1]).astype(jnp.bfloat16)
    slope = (sig * (1.0 + pre * (1.0 - sig))).reshape(width + 2, mid, channels)
    ends = both[4 * halo :].reshape(2, 1, DEPTH, channels)
    strip = across[width * rows * channels // 128 :].astype(f32)
    beyond = jnp.concatenate(
        [
            ends[0] * use_left,
            rows_of_192(strip).reshape(width, DEPTH, channels),
            ends[1] * use_right,
        ],
        axis=0,
    )
    odd = lax.rem(quad, 2)
    edge[odd] = rows_of_192(far[...].astype(f32))[2 * rows :]
    edge[1 - odd] = rows_of_192(near[...].astype(f32))[2 * rows :]
    centre = [edge[0:1] * use_left, cot[...].astype(f32), edge[1:2] * use_right]
    centre = jnp.concatenate(centre, axis=0)
    full = jnp.concatenate([beyond * use_low, centre, beyond * use_high], axis=1)
    grad = full * slope
    gp_ref[...] = grad.astype(jnp.bfloat16)
    inner = grad[:, DEPTH : DEPTH + rows].astype(jnp.bfloat16)
    turned = lax.dot_general(
        pick[...],
        inner.reshape((width + 2) * rows, channels),
        (((1,), (1,)), ((), ())),
        preferred_element_type=f32,
    )
    slices[...] = turned.reshape(slices.shape)
    chip = me - lax.rem(quad, 2) * SIDES
    for distance, ref in zip(CHIPS, slice_refs):
        both = [slices[chip ^ distance], slices[(chip ^ distance) + SIDES]]
        ref[...] = jnp.concatenate(both, axis=0).astype(jnp.bfloat16)


def input_kernel(gp, live, turned, out_ref, cols, weight):
    width, rows, channels = out_ref.shape
    f32 = jnp.float32
    tall = rows + 2 * DEPTH
    for tap in range(27):
        weight[tap * channels : (tap + 1) * channels, :] = turned[
            :, tap * channels : (tap + 1) * channels
        ]
    field = gp[...].astype(f32).reshape((width + 2) * tall // DEPTH, DEPTH, channels)
    for c in OFFSETS:
        moved = shift_z(field, -c).reshape(width + 2, tall, channels)
        for b in OFFSETS:
            at = ((b + 1) * 3 + c + 1) * channels
            start = DEPTH * (1 - b)
            cols[:, :, at : at + channels] = moved[:, start : start + rows].astype(jnp.bfloat16)
    nine = 9 * channels
    total = jnp.zeros((width * rows, channels), f32)
    for a in range(3):
        total += jnp.dot(
            cols[2 - a : 2 - a + width].reshape(width * rows, nine),
            weight[a * nine : (a + 1) * nine, :],
            preferred_element_type=f32,
        )
    out_ref[...] = (total.reshape(width, rows, channels) * live[:, :, 0:1]).astype(jnp.bfloat16)


def pair_product(received, bricks, cols, masked):
    f32 = jnp.float32
    group, lanes = received[0].shape
    per, lane, channels = masked.shape
    half = lane // 2
    side = position()[3]
    for i, brick in enumerate(bricks):
        at_rows = pl.ds(pl.multiple_of((side ^ i) * half, half), half)
        for x in range(per):
            shift = 64 * (x // (per // 2))
            rest = brick[pl.ds((per + x % (per // 2)) * half, half)]
            masked[x, at_rows, :128] = brick[pl.ds(x * half, half)]
            masked[x, at_rows, 128:] = rest[:, shift : shift + 64]
    at = lax.broadcasted_iota(jnp.int32, (group, lane), 1)
    y, z = at // DEPTH, at % DEPTH
    tall = lane // DEPTH
    own, other = (ref[...].astype(f32) for ref in received)
    first = jnp.where(side == 0, own, other)
    second = jnp.where(side == 0, other, own)
    for k in range(per + 2):
        one = first[:, k // 2 * lane : (k // 2 + 1) * lane]
        two = second[:, k // 2 * lane : (k // 2 + 1) * lane]
        if k % 2 == 0:
            base = jnp.where(at < half, one, pltpu.roll(two, half, 1))
        else:
            base = jnp.where(at < half, pltpu.roll(one, half, 1), two)
        pieces = []
        for b in OFFSETS:
            for c in OFFSETS:
                step = (DEPTH * b + c) % lane
                moved = base if step == 0 else pltpu.roll(base, step, 1)
                keep = (y - b >= 0) & (y - b < tall) & (z - c >= 0) & (z - c < DEPTH)
                pieces.append(jnp.where(keep, moved, 0.0))
        cols[:, k * lane : (k + 1) * lane] = jnp.concatenate(pieces, axis=0).astype(jnp.bfloat16)
    field = masked[...].reshape(per * lane, channels)
    for a in range(3):
        start = (2 - a) * lane
        got = jnp.dot(
            cols[:, start : start + per * lane], field, preferred_element_type=f32
        ).reshape(9, group, channels)
        yield a, jnp.concatenate([got[tap] for tap in range(9)], axis=1)


def first_pair_kernel(other, own, across, brick, part_ref, cols, masked):
    for a, rows in pair_product((own, other), (brick, across), cols, masked):
        width = rows.shape[1]
        part_ref[:, a * width : (a + 1) * width] = rows


def second_pair_kernel(
    before, own, other, brick, across, keep_ref, send_ref, part, cols, masked
):
    for a, rows in pair_product((own, other), (brick, across), cols, masked):
        width = rows.shape[1]
        at = slice(a * width, (a + 1) * width)
        part[:, at] = before[:, at] + rows
    core = lax.rem(position()[2], 2)
    half = part.shape[0] // 2
    keep_ref[...] = part[pl.ds(pl.multiple_of(core * half, 8), half)]
    send_ref[...] = part[pl.ds(pl.multiple_of((1 - core) * half, 8), half)].astype(jnp.bfloat16)


def fold_kernel(keep, other, own_ref, *refs):
    *send_refs, both, rows = refs
    planes, eight, _ = rows.shape
    count, total = keep.shape
    share = count // planes
    both[:count, :total] = keep[...] + other[...].astype(jnp.float32)
    both[:, total:] = jnp.zeros((both.shape[0], both.shape[1] - total), jnp.float32)
    for to in range(planes):
        rows[to] = fold_rows(both[share * to : share * to + eight, :], total)
    plane = position()[0]
    own_ref[...] = rows[plane]
    for distance, ref in enumerate(send_refs, 1):
        ref[...] = rows[plane ^ distance].astype(jnp.bfloat16)


def sum_kernel(scale, own, one, two, three, out_ref):
    f32 = jnp.float32
    total = own[...] + one[...].astype(f32) + two[...].astype(f32) + three[...].astype(f32)
    out_ref[...] = (total * scale).astype(out_ref.dtype)


def join_kernel(mine, other, out_ref):
    share = out_ref.shape[0] // SIDES
    ahead = position()[3] == 0
    total = out_ref.shape[1]
    here = unfold_rows(mine[...].astype(jnp.float32), total)
    there = unfold_rows(other[...].astype(jnp.float32), total)
    first = jnp.where(ahead, here, there)
    second = jnp.where(ahead, there, here)
    out_ref[0:share] = first[:share]
    out_ref[share:] = second[:share]


def call(body, name, mebibytes, flops, moved, out_shape, scratch=(), in_specs=None):
    spec = pl.BlockSpec(memory_space=pltpu.VMEM)

    def run(*operands):
        return pl.pallas_call(
            body,
            out_shape=out_shape,
            in_specs=in_specs or [spec] * len(operands),
            out_specs=jax.tree.map(lambda _: spec, out_shape),
            scratch_shapes=scratch,
            compiler_params=pltpu.CompilerParams(vmem_limit_bytes=mebibytes << 20),
            cost_estimate=pl.CostEstimate(flops=flops, bytes_accessed=moved, transcendentals=0),
            name=name,
        )(*operands)

    return run


def planes_local(features, weight, voxel_mask, cotangent):
    bf16 = jnp.bfloat16
    f32 = jnp.float32
    array = jax.ShapeDtypeStruct
    width, wide_y, depth, channels = features.shape
    rows = wide_y * depth
    planes = lax.axis_size("depth")
    count = planes * QUAD
    total = 27 * channels
    halo = 2 * DEPTH
    span = (width + 2) * rows
    share = channels // count // SIDES
    group = planes * share

    def swap(piece, axes, distance, size):
        return lax.ppermute(piece, axes, [(i, i ^ distance) for i in range(size)])

    def in_plane(piece, distance):
        return swap(piece, ("quad", "narrow"), distance, MEMBERS)

    brick = array((width, rows, channels), bf16)
    slab = array((3 * rows * channels // 128, 128), bf16)
    slabs = (2, 3, rows, channels)
    pick = call(
        functools.partial(pick_kernel, planes), "pick", 4, 1 << 32, 1 << 16,
        array((MEMBERS * group, channels), bf16),
    )()
    vmem = pl.BlockSpec(memory_space=pltpu.VMEM)
    masked, cot, live, near, far = call(
        prepare_kernel, "prepare", 16, 1 << 20, 1 << 20,
        (brick, brick, array((width, rows, 128), f32), slab, slab),
        (),
        [vmem] * 3 + [pl.BlockSpec(memory_space=pl.ANY)],
    )(
        features.reshape(width, rows, channels),
        cotangent.reshape(width, rows, channels),
        voxel_mask,
        pick,
    )
    near = swap(near, WIDE, 1, count)
    ends = [min(max(((i + 1) ^ 1) - 1, 0), count - 1) for i in range(count)]
    far = lax.ppermute(far, WIDE, list(enumerate(ends)))
    weight_rows = call(
        turn_kernel, "turn", 8, 1 << 20, 4 << 20, array((total, channels), bf16)
    )(weight.T)
    count_128 = width * rows * channels // 128
    strip_128 = width * DEPTH * channels // 128
    across = call(
        across_kernel, "across", 4, 1 << 16, 1 << 19, array((count_128 + strip_128, 128), bf16)
    )(masked, cot)
    across = in_plane(across, CHIPS[1])
    packed = call(
        pack_kernel, "pack", 4, 1 << 16, 1 << 19, array((count_128, 128), bf16), (),
        [vmem, pl.BlockSpec(memory_space=pl.ANY)],
    )(masked, weight_rows)
    near, far, weight_rows, late = lax.optimization_barrier((near, far, weight_rows, packed))
    corner = call(
        corner_kernel, "corner", 4, 1 << 16, 1 << 18,
        array((128, 128), bf16),
        (pltpu.VMEM(slabs, f32),),
    )(near, far)
    corner = in_plane(corner, 1)
    mid = rows + 2 * DEPTH
    bulk = call(
        bulk_kernel, "bulk", 24, 3 << 29, 1 << 20, array((width + 2, mid, channels), f32),
        (
            pltpu.VMEM((width + 4, rows + 2 * halo, channels), f32),
            pltpu.VMEM(slabs, f32),
            pltpu.VMEM((width + 4, mid, 9 * channels), bf16),
        ),
    )(masked, near, far, across, weight_rows)
    bricks = [packed, across, in_plane(packed, CHIPS[2]), in_plane(late, CHIPS[3])]

    act, gp, *slices = call(
        forward_kernel, "forward", 24, 3 << 29, 1 << 20,
        (brick, array((width + 2, mid, channels), bf16))
        + (array((2 * group, span), bf16),) * len(CHIPS),
        (
            pltpu.VMEM((2, rows, channels), f32),
            pltpu.VMEM((3, 4 * halo, 6 * channels), bf16),
            pltpu.VMEM((width + 2, mid, channels), f32),
            pltpu.VMEM((MEMBERS, group, span), f32),
        ),
    )(bulk, cot, near, far, across, corner, live, weight_rows, pick)
    bricks[2], *slices = lax.optimization_barrier((bricks[2], *slices))
    for place in (3, 2, 1):
        slices[place] = in_plane(slices[place], CHIPS[place])

    grad_input = call(
        input_kernel, "input_gradient", 20, 2 * 512 * 5184 * 256, 4 << 20, brick,
        (
            pltpu.VMEM((width + 2, rows, 9 * channels), bf16),
            pltpu.VMEM((total, channels), bf16),
        ),
    )(gp, live, weight.T)

    lanes = dense(total)[0]
    scratch = (
        pltpu.VMEM((9 * 2 * group, (width + 2) * SIDES * rows), bf16),
        pltpu.VMEM((width, SIDES * rows, channels), bf16),
    )
    part = call(
        first_pair_kernel, "first_pair", 16, 1 << 30, 2 << 20,
        array((2 * group, total), f32), scratch,
    )(*slices[3:1:-1], *bricks[3:1:-1])
    keep, fold = call(
        second_pair_kernel, "second_pair", 16, 1 << 30, 2 << 20,
        (array((group, total), f32), array((group, total), bf16)),
        (pltpu.VMEM((2 * group, total), f32),) + scratch,
    )(part, *slices[:2], *bricks[:2])
    own, *sends = call(
        fold_kernel, "fold", 8, 8 * total * 4, 8 * total * 40,
        (array((8, lanes), f32),) + (array((8, lanes), bf16),) * (planes - 1),
        (
            pltpu.VMEM((group + 8, sum(dense(total))), f32),
            pltpu.VMEM((planes, 8, lanes), f32),
        ),
    )(keep, in_plane(fold, 2))
    got = [swap(sent, "depth", d, planes) for d, sent in list(enumerate(sends, 1))[::-1]]
    grad_input, *got = lax.optimization_barrier((grad_input, *got))
    voxels = count * SIDES * width * rows
    mine = call(
        functools.partial(sum_kernel, float(1.0 / voxels**0.5)),
        "plane_sum", 4, 8 * total * 4, 8 * total * 14, array((8, lanes), bf16),
    )(own, *got)
    grad_weight = call(
        join_kernel, "join", 4, 8 * total, 8 * total * 14, array((channels // count, total), f32)
    )(mine, in_plane(mine, 1))
    shape = features.shape
    return act.reshape(shape), grad_input.reshape(shape), grad_weight


def padded_2(cells, sides, width):
    for axis, dim in sides:
        count = lax.axis_size(axis)
        ends = count - 1
        head = lax.slice_in_dim(cells, 0, width, axis=dim)
        tail = lax.slice_in_dim(cells, cells.shape[dim] - width, cells.shape[dim], axis=dim)
        cells = jnp.concatenate(
            [
                lax.ppermute(tail, axis, [(i, (i + 1) % count) for i in range(ends)]),
                cells,
                lax.ppermute(head, axis, [((i + 1) % count, i) for i in range(ends)]),
            ],
            axis=dim,
        )
    return cells


def gather_taps(padded, width_x, width_y, depth_z, channels, flip):
    pieces = []
    for shift_x in range(3):
        for shift_y in range(3):
            for shift_z in range(3):
                start_x = 2 - shift_x if flip else shift_x
                start_y = 2 - shift_y if flip else shift_y
                start_z = 2 - shift_z if flip else shift_z
                piece = padded[
                    start_x : start_x + width_x,
                    start_y : start_y + width_y,
                    start_z : start_z + depth_z,
                    :,
                ]
                pieces.append(piece.reshape(-1, channels))
    return jnp.concatenate(pieces, axis=1)


def summed_local(features, weight, voxel_mask, cotangent):
    width_x, width_y, depth_z, channels = features.shape
    masked = features * voxel_mask.astype(jnp.bfloat16)[..., None]
    padded = padded_2(masked, (("wide", 0), ("narrow", 1)), 1)
    padded = jnp.pad(padded, ((0, 0), (0, 0), (1, 1), (0, 0)))
    columns = gather_taps(padded, width_x, width_y, depth_z, channels, False)
    pre = jnp.dot(columns, weight, preferred_element_type=jnp.float32)
    live = voxel_mask.reshape(-1, 1).astype(jnp.float32)
    sig = jax.nn.sigmoid(pre)
    activation = (
        (pre * sig * live).astype(jnp.bfloat16).reshape(width_x, width_y, depth_z, channels)
    )
    slope = sig * (1.0 + pre * (1.0 - sig))
    grad_pre = (cotangent.reshape(-1, channels).astype(jnp.float32) * live * slope).astype(
        jnp.bfloat16
    )
    taps = weight.reshape(27, channels, channels)
    grid = grad_pre.reshape(width_x, width_y, depth_z, channels)
    grad_pad = padded_2(grid, (("wide", 0), ("narrow", 1)), 1)
    grad_pad = jnp.pad(grad_pad, ((0, 0), (0, 0), (1, 1), (0, 0)))
    grad_columns = gather_taps(grad_pad, width_x, width_y, depth_z, channels, True)
    flipped = jnp.transpose(taps, (0, 2, 1)).reshape(27 * channels, channels)
    grad_field = jnp.dot(grad_columns, flipped, preferred_element_type=jnp.float32)
    grad_input = (
        (grad_field * live).astype(jnp.bfloat16).reshape(width_x, width_y, depth_z, channels)
    )
    scale = 1.0 / jnp.sqrt(
        jnp.float32(width_x * width_y * depth_z * lax.axis_size("wide") * lax.axis_size("narrow"))
    )
    whole = lax.dot_general(
        grad_pre, columns, (((0,), (0,)), ((), ())), preferred_element_type=jnp.float32
    )
    piece_flat = lax.psum_scatter(
        whole.reshape(-1), ("wide", "narrow"), scatter_dimension=0, tiled=True
    )
    gathered = lax.all_gather(piece_flat, "narrow", axis=0, tiled=True)
    summed = gathered.reshape(channels // lax.axis_size("wide"), 27 * channels)
    grad_weight = summed * scale
    return (activation, grad_input, grad_weight)


def sharded(body, mesh, wide):
    return jax.shard_map(
        body,
        mesh=mesh,
        in_specs=(
            P(wide, "narrow", None, None),
            P(),
            P(wide, "narrow", None),
            P(wide, "narrow", None, None),
        ),
        out_specs=(
            P(wide, "narrow", None, None),
            P(wide, "narrow", None, None),
            P(wide, None),
        ),
        check_vma=False,
    )


def solution(mesh):
    wide, narrow = mesh.shape["wide"], mesh.shape["narrow"]
    if wide != 4 * QUAD or narrow != SIDES:
        return sharded(summed_local, mesh, "wide")
    planes = Mesh(
        mesh.devices.reshape(wide // QUAD, QUAD, narrow), ("depth", "quad", "narrow")
    )
    return sharded(planes_local, planes, WIDE)
```

```python
import functools

import jax
import jax.numpy as jnp
from jax import lax
from jax.experimental import pallas as pl
from jax.experimental.pallas import tpu as pltpu
from jax.sharding import Mesh
from jax.sharding import PartitionSpec as P

WIDE = ("depth", "quad")
QUAD = 4
SIDES = 2
MEMBERS = QUAD * SIDES
CHIPS = (0, 1, 4, 5)
OFFSETS = (-1, 0, 1)
DEPTH = 8


def position():
    quad, side = lax.axis_index("quad"), lax.axis_index("narrow")
    return lax.axis_index("depth"), quad * SIDES + side, quad, side


def shift_z(field, step):
    if step == 0:
        return field
    depth = field.shape[1]
    moved = pltpu.roll(field, (-step) % depth, 1)
    z = lax.broadcasted_iota(jnp.int32, field.shape, 1) + step
    return jnp.where((z >= 0) & (z < depth), moved, 0.0)


def pick_kernel(planes, out_ref):
    index = lax.broadcasted_iota(jnp.int32, out_ref.shape, 0)
    column = lax.broadcasted_iota(jnp.int32, out_ref.shape, 1)
    per = out_ref.shape[1] // (planes * QUAD)
    share = per // SIDES
    group = planes * share
    quad, side = index // (SIDES * group), index // group % SIDES
    plane, row = index // share % planes, index % share
    channel = per * (QUAD * plane + quad) + share * side + row
    out_ref[...] = jnp.where(channel == column, 1.0, 0.0).astype(jnp.bfloat16)


def dense(total):
    tiles = -(-total // 128)
    moved = tiles // 4
    return (tiles - moved) * 128, moved * 128


def fold_rows(block, total):
    kept, moved = dense(total)
    tail = block[:, kept : kept + moved]
    row = lax.broadcasted_iota(jnp.int32, tail.shape, 0)
    pieces = []
    for k in range(3):
        spare = jnp.where(row == 6, pltpu.roll(tail, 6 - k, 0), pltpu.roll(tail, 4 - k, 0))
        pieces.append(jnp.where(row < 6, block[:, k * moved : (k + 1) * moved], spare))
    return jnp.concatenate(pieces + [block[:, 3 * moved : kept]], axis=1)


def unfold_rows(block, total):
    kept, moved = dense(total)
    row = lax.broadcasted_iota(jnp.int32, (8, moved), 0)
    tail = jnp.zeros((8, moved), block.dtype)
    for k in range(3):
        piece = block[:, k * moved : (k + 1) * moved]
        tail = jnp.where(row == k, pltpu.roll(piece, 2 + k, 0), tail)
        tail = jnp.where(row == 3 + k, pltpu.roll(piece, 4 + k, 0), tail)
    return jnp.concatenate([block, tail], axis=1)[:, :total]


def rows_of_128(block):
    half = block.shape[0] // 2
    rest = jnp.concatenate([block[:half, 128:], block[half:, 128:]], axis=1)
    return jnp.concatenate([block[:, :128], rest], axis=0)


def rows_of_192(block):
    count = block.shape[0] * 2 // 3
    rest = jnp.concatenate([block[count:, :64], block[count:, 64:]], axis=0)
    return jnp.concatenate([block[:count], rest], axis=1)


def prepare_kernel(features, cot, mask, first, masked_ref, cot_ref, live_ref, near_ref, far_ref):
    width, rows, channels = features.shape
    f32 = jnp.float32
    flat = mask[...].astype(f32).reshape(width * rows // DEPTH, DEPTH)
    live = jnp.broadcast_to(flat[:, :, None], flat.shape + (channels,)).reshape(features.shape)
    live_ref[...] = live[:, :, :128]
    masked_ref[...] = (features[...].astype(f32) * live).astype(jnp.bfloat16)
    cot_ref[...] = (cot[...].astype(f32) * live).astype(jnp.bfloat16)
    odd = lax.rem(position()[2], 2)
    for ref, upper in ((near_ref, 1 - odd), (far_ref, odd)):
        slabs = [
            masked_ref[pl.ds(upper * (width - 2), 2)],
            cot_ref[pl.ds(upper * (width - 1), 1)],
        ]
        slabs = jnp.concatenate(slabs, axis=0).astype(f32).reshape(3 * rows, channels)
        ref[...] = rows_of_128(slabs).astype(jnp.bfloat16)


def pack_kernel(masked, after, packed_ref):
    count, channels = packed_ref.shape[0] * 128 // masked.shape[2], masked.shape[2]
    block = masked[...].reshape(count, channels)
    packed_ref[...] = rows_of_128(block)


def across_kernel(masked, cot, across_ref):
    width, rows, channels = masked.shape
    packed = rows_of_128(masked[...].reshape(width * rows, channels))
    across_ref[: packed.shape[0]] = packed
    ahead = position()[3] == 0
    grown = cot[...].astype(jnp.float32)
    strip = jnp.where(ahead, grown[:, rows - DEPTH :], grown[:, :DEPTH])
    strip = rows_of_128(strip.reshape(width * DEPTH, channels))
    across_ref[packed.shape[0] :] = strip.astype(jnp.bfloat16)


def corner_kernel(near, far, out_ref, edge):
    _, slabs, rows, channels = edge.shape
    _, _, quad, side = position()
    odd = lax.rem(quad, 2)
    f32 = jnp.float32
    edge[odd] = rows_of_192(far[...].astype(f32)).reshape(edge.shape[1:])
    edge[1 - odd] = rows_of_192(near[...].astype(f32)).reshape(edge.shape[1:])
    halo = 2 * DEPTH
    ahead = side == 0
    strip = jnp.where(ahead, edge[:, :2, rows - halo :], edge[:, :2, :halo])
    cots = jnp.where(ahead, edge[:, 2, rows - DEPTH :], edge[:, 2, :DEPTH])
    both = [strip.reshape(4 * halo, channels), cots.reshape(2 * DEPTH, channels)]
    both = rows_of_128(jnp.concatenate(both, axis=0))
    blank = jnp.zeros((out_ref.shape[0] - both.shape[0], 128), f32)
    out_ref[...] = jnp.concatenate([both, blank], axis=0).astype(jnp.bfloat16)


def turn_kernel(weight, out_ref):
    step = 2 * weight.shape[0]
    total = weight.shape[1]
    for start in range(0, total, step):
        stop = min(start + step, total)
        out_ref[start:stop, :] = weight[:, start:stop].T


def bulk_kernel(masked, near, far, across, weight, pre_ref, ext, edge, cols):
    width, rows, channels = masked.shape
    f32 = jnp.float32
    plane, _, quad, side = position()
    use_low = side.astype(f32)
    use_high = (1 - side).astype(f32)
    place = plane * QUAD + quad
    use_left = (place > 0).astype(f32)
    use_right = (place < QUAD * lax.axis_size("depth") - 1).astype(f32)
    halo = 2 * DEPTH
    tall = rows + 2 * halo
    mid = rows + 2 * DEPTH
    span = width + 4
    odd = lax.rem(quad, 2)
    edge[odd] = rows_of_192(far[...].astype(f32)).reshape(edge.shape[1:])
    edge[1 - odd] = rows_of_192(near[...].astype(f32)).reshape(edge.shape[1:])
    ext[0:2, halo : halo + rows, :] = edge[0, 0:2] * use_left
    ext[2 : 2 + width, halo : halo + rows, :] = masked[...].astype(f32)
    ext[2 + width :, halo : halo + rows, :] = edge[1, 0:2] * use_right
    half = width // 2
    count = width * rows * channels // 128
    held = across[:count].astype(f32).reshape(width + half, rows, 128)
    brick = jnp.where(side == 0, held[:, :halo], held[:, rows - halo :])
    rest = jnp.concatenate([brick[width:, :, :64], brick[width:, :, 64:]], axis=0)
    beside = jnp.concatenate([brick[:width], rest], axis=2)
    blank = jnp.zeros((2, halo, channels), f32)
    for use, start in ((use_low, 0), (use_high, halo + rows)):
        at = slice(start, start + halo)
        ext[0:2, at, :] = blank
        ext[2 : 2 + width, at, :] = beside * use
        ext[2 + width :, at, :] = blank
    field = ext[...].reshape(span * tall // DEPTH, DEPTH, channels)
    for c in OFFSETS:
        moved = shift_z(field, c).reshape(span, tall, channels)
        for b in OFFSETS:
            at = ((b + 1) * 3 + c + 1) * channels
            start = DEPTH * (b + 1)
            cols[:, :, at : at + channels] = moved[:, start : start + mid].astype(jnp.bfloat16)
    nine = 9 * channels
    pre = jnp.zeros(((width + 2) * mid, channels), f32)
    for a in range(3):
        pre += jnp.dot(
            cols[a : a + width + 2].reshape((width + 2) * mid, nine),
            weight[a * nine : (a + 1) * nine, :],
            preferred_element_type=f32,
        )
    pre_ref[...] = pre.reshape(pre_ref.shape)


def forward_kernel(bulk, cot, near, far, across, corner, live, weight, pick, *refs):
    act_ref, gp_ref = refs[:2]
    slice_refs = refs[2 : 2 + len(CHIPS)]
    edge, cols, total, slices = refs[2 + len(CHIPS) :]
    width, rows, channels = cot.shape
    f32 = jnp.float32
    plane, me, quad, side = position()
    use_low = side.astype(f32)
    use_high = (1 - side).astype(f32)
    place = plane * QUAD + quad
    use_left = (place > 0).astype(f32)
    use_right = (place < QUAD * lax.axis_size("depth") - 1).astype(f32)
    halo = 2 * DEPTH
    mid = rows + 2 * DEPTH
    count = 4 * halo + 2 * DEPTH
    both = rows_of_192(corner[...].astype(f32)[: count * channels // 128])
    corners = both[: 4 * halo].reshape(2, 2, halo, channels)
    corners = jnp.concatenate([corners[0] * use_left, corners[1] * use_right], axis=0)
    sources = ((0, 1, None, None), (1, None, None, 2), (None, None, 2, 3))
    blank = jnp.zeros((DEPTH, channels), f32)
    six = 6 * channels
    for c in OFFSETS:
        moved = shift_z(corners.reshape(8, DEPTH, channels), c)
        for b, low, high in ((0, (0, 1), (None, 0)), (1, (1, None), (0, 1))):
            at = (b * 3 + c + 1) * channels
            parts = []
            for slab in range(4):
                for below, above in zip(low, high):
                    part = blank if below is None else moved[2 * slab + below] * use_low
                    if above is not None:
                        part = part + moved[2 * slab + above] * use_high
                    parts.append(part)
            for a in range(3):
                rows_a = []
                for source in sources[a]:
                    pair = [blank] * 2 if source is None else parts[2 * source : 2 * source + 2]
                    rows_a += pair
                cols[a, :, at : at + channels] = jnp.concatenate(rows_a, axis=0).astype(
                    jnp.bfloat16
                )
    share = jnp.zeros((4 * halo, channels), f32)
    for a in range(3):
        taps = pl.ds(pl.multiple_of((3 * a + 1 - side) * 3 * channels, 16), six)
        share += jnp.dot(cols[a], weight[taps], preferred_element_type=f32)
    share = share.reshape(4, halo, channels)
    total[...] = bulk[...]
    at = pl.ds(pl.multiple_of((1 - side) * (mid - halo), DEPTH), halo)
    total[0:2, at, :] += share[0:2]
    total[width : width + 2, at, :] += share[2:4]
    pre = total[...].reshape((width + 2) * mid, channels)
    sig = 0.5 * jnp.tanh(0.5 * pre) + 0.5
    act = (pre * sig).reshape(width + 2, mid, channels)[1 : 1 + width, DEPTH : DEPTH + rows]
    act_ref[...] = (act * live[:, :, 0:1]).astype(jnp.bfloat16)
    slope = (sig * (1.0 + pre * (1.0 - sig))).reshape(width + 2, mid, channels)
    ends = both[4 * halo :].reshape(2, 1, DEPTH, channels)
    strip = across[width * rows * channels // 128 :].astype(f32)
    beyond = jnp.concatenate(
        [
            ends[0] * use_left,
            rows_of_192(strip).reshape(width, DEPTH, channels),
            ends[1] * use_right,
        ],
        axis=0,
    )
    odd = lax.rem(quad, 2)
    edge[odd] = rows_of_192(far[...].astype(f32))[2 * rows :]
    edge[1 - odd] = rows_of_192(near[...].astype(f32))[2 * rows :]
    centre = [edge[0:1] * use_left, cot[...].astype(f32), edge[1:2] * use_right]
    centre = jnp.concatenate(centre, axis=0)
    full = jnp.concatenate([beyond * use_low, centre, beyond * use_high], axis=1)
    grad = full * slope
    gp_ref[...] = grad.astype(jnp.bfloat16)
    inner = grad[:, DEPTH : DEPTH + rows].astype(jnp.bfloat16)
    turned = lax.dot_general(
        pick[...],
        inner.reshape((width + 2) * rows, channels),
        (((1,), (1,)), ((), ())),
        preferred_element_type=f32,
    )
    slices[...] = turned.reshape(slices.shape)
    chip = me - lax.rem(quad, 2) * SIDES
    for distance, ref in zip(CHIPS, slice_refs):
        both = [slices[chip ^ distance], slices[(chip ^ distance) + SIDES]]
        ref[...] = jnp.concatenate(both, axis=0).astype(jnp.bfloat16)


def input_kernel(gp, live, turned, out_ref, cols, weight):
    width, rows, channels = out_ref.shape
    f32 = jnp.float32
    tall = rows + 2 * DEPTH
    for tap in range(27):
        weight[tap * channels : (tap + 1) * channels, :] = turned[
            :, tap * channels : (tap + 1) * channels
        ]
    field = gp[...].astype(f32).reshape((width + 2) * tall // DEPTH, DEPTH, channels)
    for c in OFFSETS:
        moved = shift_z(field, -c).reshape(width + 2, tall, channels)
        for b in OFFSETS:
            at = ((b + 1) * 3 + c + 1) * channels
            start = DEPTH * (1 - b)
            cols[:, :, at : at + channels] = moved[:, start : start + rows].astype(jnp.bfloat16)
    nine = 9 * channels
    total = jnp.zeros((width * rows, channels), f32)
    for a in range(3):
        total += jnp.dot(
            cols[2 - a : 2 - a + width].reshape(width * rows, nine),
            weight[a * nine : (a + 1) * nine, :],
            preferred_element_type=f32,
        )
    out_ref[...] = (total.reshape(width, rows, channels) * live[:, :, 0:1]).astype(jnp.bfloat16)


def pair_product(received, bricks, cols, masked):
    f32 = jnp.float32
    group, lanes = received[0].shape
    per, lane, channels = masked.shape
    half = lane // 2
    side = position()[3]
    for i, brick in enumerate(bricks):
        at_rows = pl.ds(pl.multiple_of((side ^ i) * half, half), half)
        for x in range(per):
            shift = 64 * (x // (per // 2))
            rest = brick[pl.ds((per + x % (per // 2)) * half, half)]
            masked[x, at_rows, :128] = brick[pl.ds(x * half, half)]
            masked[x, at_rows, 128:] = rest[:, shift : shift + 64]
    at = lax.broadcasted_iota(jnp.int32, (group, lane), 1)
    y, z = at // DEPTH, at % DEPTH
    tall = lane // DEPTH
    own, other = (ref[...].astype(f32) for ref in received)
    first = jnp.where(side == 0, own, other)
    second = jnp.where(side == 0, other, own)
    for k in range(per + 2):
        one = first[:, k // 2 * lane : (k // 2 + 1) * lane]
        two = second[:, k // 2 * lane : (k // 2 + 1) * lane]
        if k % 2 == 0:
            base = jnp.where(at < half, one, pltpu.roll(two, half, 1))
        else:
            base = jnp.where(at < half, pltpu.roll(one, half, 1), two)
        pieces = []
        for b in OFFSETS:
            for c in OFFSETS:
                step = (DEPTH * b + c) % lane
                moved = base if step == 0 else pltpu.roll(base, step, 1)
                keep = (y - b >= 0) & (y - b < tall) & (z - c >= 0) & (z - c < DEPTH)
                pieces.append(jnp.where(keep, moved, 0.0))
        cols[:, k * lane : (k + 1) * lane] = jnp.concatenate(pieces, axis=0).astype(jnp.bfloat16)
    field = masked[...].reshape(per * lane, channels)
    for a in range(3):
        start = (2 - a) * lane
        got = jnp.dot(
            cols[:, start : start + per * lane], field, preferred_element_type=f32
        ).reshape(9, group, channels)
        yield a, jnp.concatenate([got[tap] for tap in range(9)], axis=1)


def first_pair_kernel(own, other, brick, across, part_ref, cols, masked):
    for a, rows in pair_product((own, other), (brick, across), cols, masked):
        width = rows.shape[1]
        part_ref[:, a * width : (a + 1) * width] = rows


def second_pair_kernel(
    before, other, own, across, brick, keep_ref, send_ref, part, cols, masked
):
    for a, rows in pair_product((own, other), (brick, across), cols, masked):
        width = rows.shape[1]
        at = slice(a * width, (a + 1) * width)
        part[:, at] = before[:, at] + rows
    core = lax.rem(position()[2], 2)
    half = part.shape[0] // 2
    keep_ref[...] = part[pl.ds(pl.multiple_of(core * half, 8), half)]
    send_ref[...] = part[pl.ds(pl.multiple_of((1 - core) * half, 8), half)].astype(jnp.bfloat16)


def fold_kernel(keep, other, own_ref, *refs):
    *send_refs, both, rows = refs
    planes, eight, _ = rows.shape
    count, total = keep.shape
    share = count // planes
    both[:count, :total] = keep[...] + other[...].astype(jnp.float32)
    both[:, total:] = jnp.zeros((both.shape[0], both.shape[1] - total), jnp.float32)
    for to in range(planes):
        rows[to] = fold_rows(both[share * to : share * to + eight, :], total)
    plane = position()[0]
    own_ref[...] = rows[plane]
    for distance, ref in enumerate(send_refs, 1):
        ref[...] = rows[plane ^ distance].astype(jnp.bfloat16)


def sum_kernel(scale, own, one, two, three, out_ref):
    f32 = jnp.float32
    total = own[...] + one[...].astype(f32) + two[...].astype(f32) + three[...].astype(f32)
    out_ref[...] = (total * scale).astype(out_ref.dtype)


def join_kernel(mine, other, out_ref):
    share = out_ref.shape[0] // SIDES
    ahead = position()[3] == 0
    total = out_ref.shape[1]
    here = unfold_rows(mine[...].astype(jnp.float32), total)
    there = unfold_rows(other[...].astype(jnp.float32), total)
    first = jnp.where(ahead, here, there)
    second = jnp.where(ahead, there, here)
    out_ref[0:share] = first[:share]
    out_ref[share:] = second[:share]


def call(body, name, mebibytes, flops, moved, out_shape, scratch=(), in_specs=None):
    spec = pl.BlockSpec(memory_space=pltpu.VMEM)

    def run(*operands):
        return pl.pallas_call(
            body,
            out_shape=out_shape,
            in_specs=in_specs or [spec] * len(operands),
            out_specs=jax.tree.map(lambda _: spec, out_shape),
            scratch_shapes=scratch,
            compiler_params=pltpu.CompilerParams(vmem_limit_bytes=mebibytes << 20),
            cost_estimate=pl.CostEstimate(flops=flops, bytes_accessed=moved, transcendentals=0),
            name=name,
        )(*operands)

    return run


def planes_local(features, weight, voxel_mask, cotangent):
    bf16 = jnp.bfloat16
    f32 = jnp.float32
    array = jax.ShapeDtypeStruct
    width, wide_y, depth, channels = features.shape
    rows = wide_y * depth
    planes = lax.axis_size("depth")
    count = planes * QUAD
    total = 27 * channels
    halo = 2 * DEPTH
    span = (width + 2) * rows
    share = channels // count // SIDES
    group = planes * share

    def swap(piece, axes, distance, size):
        return lax.ppermute(piece, axes, [(i, i ^ distance) for i in range(size)])

    def in_plane(piece, distance):
        return swap(piece, ("quad", "narrow"), distance, MEMBERS)

    brick = array((width, rows, channels), bf16)
    slab = array((3 * rows * channels // 128, 128), bf16)
    slabs = (2, 3, rows, channels)
    pick = call(
        functools.partial(pick_kernel, planes), "pick", 4, 1 << 32, 1 << 16,
        array((MEMBERS * group, channels), bf16),
    )()
    vmem = pl.BlockSpec(memory_space=pltpu.VMEM)
    masked, cot, live, near, far = call(
        prepare_kernel, "prepare", 16, 1 << 20, 1 << 20,
        (brick, brick, array((width, rows, 128), f32), slab, slab),
        (),
        [vmem] * 3 + [pl.BlockSpec(memory_space=pl.ANY)],
    )(
        features.reshape(width, rows, channels),
        cotangent.reshape(width, rows, channels),
        voxel_mask,
        pick,
    )
    near = swap(near, WIDE, 1, count)
    ends = [min(max(((i + 1) ^ 1) - 1, 0), count - 1) for i in range(count)]
    far = lax.ppermute(far, WIDE, list(enumerate(ends)))
    weight_rows = call(
        turn_kernel, "turn", 8, 1 << 20, 4 << 20, array((total, channels), bf16)
    )(weight.T)
    count_128 = width * rows * channels // 128
    strip_128 = width * DEPTH * channels // 128
    across = call(
        across_kernel, "across", 4, 1 << 16, 1 << 19, array((count_128 + strip_128, 128), bf16)
    )(masked, cot)
    across = in_plane(across, CHIPS[1])
    packed = call(
        pack_kernel, "pack", 4, 1 << 16, 1 << 19, array((count_128, 128), bf16), (),
        [vmem, pl.BlockSpec(memory_space=pl.ANY)],
    )(masked, weight_rows)
    near, far, weight_rows, late = lax.optimization_barrier((near, far, weight_rows, packed))
    corner = call(
        corner_kernel, "corner", 4, 1 << 16, 1 << 18,
        array((128, 128), bf16),
        (pltpu.VMEM(slabs, f32),),
    )(near, far)
    corner = in_plane(corner, 1)
    mid = rows + 2 * DEPTH
    bulk = call(
        bulk_kernel, "bulk", 24, 3 << 29, 1 << 20, array((width + 2, mid, channels), f32),
        (
            pltpu.VMEM((width + 4, rows + 2 * halo, channels), f32),
            pltpu.VMEM(slabs, f32),
            pltpu.VMEM((width + 4, mid, 9 * channels), bf16),
        ),
    )(masked, near, far, across, weight_rows)
    bricks = [packed, across, in_plane(packed, CHIPS[2]), in_plane(late, CHIPS[3])]

    act, gp, *slices = call(
        forward_kernel, "forward", 24, 3 << 29, 1 << 20,
        (brick, array((width + 2, mid, channels), bf16))
        + (array((2 * group, span), bf16),) * len(CHIPS),
        (
            pltpu.VMEM((2, rows, channels), f32),
            pltpu.VMEM((3, 4 * halo, 6 * channels), bf16),
            pltpu.VMEM((width + 2, mid, channels), f32),
            pltpu.VMEM((MEMBERS, group, span), f32),
        ),
    )(bulk, cot, near, far, across, corner, live, weight_rows, pick)
    bricks[2], *slices = lax.optimization_barrier((bricks[2], *slices))
    for place in (3, 2, 1):
        slices[place] = in_plane(slices[place], CHIPS[place])

    grad_input = call(
        input_kernel, "input_gradient", 20, 2 * 512 * 5184 * 256, 4 << 20, brick,
        (
            pltpu.VMEM((width + 2, rows, 9 * channels), bf16),
            pltpu.VMEM((total, channels), bf16),
        ),
    )(gp, live, weight.T)

    lanes = dense(total)[0]
    scratch = (
        pltpu.VMEM((9 * 2 * group, (width + 2) * SIDES * rows), bf16),
        pltpu.VMEM((width, SIDES * rows, channels), bf16),
    )
    part = call(
        first_pair_kernel, "first_pair", 16, 1 << 30, 2 << 20,
        array((2 * group, total), f32), scratch,
    )(*slices[:2], *bricks[:2])
    keep, fold = call(
        second_pair_kernel, "second_pair", 16, 1 << 30, 2 << 20,
        (array((group, total), f32), array((group, total), bf16)),
        (pltpu.VMEM((2 * group, total), f32),) + scratch,
    )(part, *slices[3:1:-1], *bricks[3:1:-1])
    own, *sends = call(
        fold_kernel, "fold", 8, 8 * total * 4, 8 * total * 40,
        (array((8, lanes), f32),) + (array((8, lanes), bf16),) * (planes - 1),
        (
            pltpu.VMEM((group + 8, sum(dense(total))), f32),
            pltpu.VMEM((planes, 8, lanes), f32),
        ),
    )(keep, in_plane(fold, 2))
    got = [swap(sent, "depth", d, planes) for d, sent in list(enumerate(sends, 1))[::-1]]
    grad_input, *got = lax.optimization_barrier((grad_input, *got))
    voxels = count * SIDES * width * rows
    mine = call(
        functools.partial(sum_kernel, float(1.0 / voxels**0.5)),
        "plane_sum", 4, 8 * total * 4, 8 * total * 14, array((8, lanes), bf16),
    )(own, *got)
    grad_weight = call(
        join_kernel, "join", 4, 8 * total, 8 * total * 14, array((channels // count, total), f32)
    )(mine, in_plane(mine, 1))
    shape = features.shape
    return act.reshape(shape), grad_input.reshape(shape), grad_weight


def padded_2(cells, sides, width):
    for axis, dim in sides:
        count = lax.axis_size(axis)
        ends = count - 1
        head = lax.slice_in_dim(cells, 0, width, axis=dim)
        tail = lax.slice_in_dim(cells, cells.shape[dim] - width, cells.shape[dim], axis=dim)
        cells = jnp.concatenate(
            [
                lax.ppermute(tail, axis, [(i, (i + 1) % count) for i in range(ends)]),
                cells,
                lax.ppermute(head, axis, [((i + 1) % count, i) for i in range(ends)]),
            ],
            axis=dim,
        )
    return cells


def gather_taps(padded, width_x, width_y, depth_z, channels, flip):
    pieces = []
    for shift_x in range(3):
        for shift_y in range(3):
            for shift_z in range(3):
                start_x = 2 - shift_x if flip else shift_x
                start_y = 2 - shift_y if flip else shift_y
                start_z = 2 - shift_z if flip else shift_z
                piece = padded[
                    start_x : start_x + width_x,
                    start_y : start_y + width_y,
                    start_z : start_z + depth_z,
                    :,
                ]
                pieces.append(piece.reshape(-1, channels))
    return jnp.concatenate(pieces, axis=1)


def summed_local(features, weight, voxel_mask, cotangent):
    width_x, width_y, depth_z, channels = features.shape
    masked = features * voxel_mask.astype(jnp.bfloat16)[..., None]
    padded = padded_2(masked, (("wide", 0), ("narrow", 1)), 1)
    padded = jnp.pad(padded, ((0, 0), (0, 0), (1, 1), (0, 0)))
    columns = gather_taps(padded, width_x, width_y, depth_z, channels, False)
    pre = jnp.dot(columns, weight, preferred_element_type=jnp.float32)
    live = voxel_mask.reshape(-1, 1).astype(jnp.float32)
    sig = jax.nn.sigmoid(pre)
    activation = (
        (pre * sig * live).astype(jnp.bfloat16).reshape(width_x, width_y, depth_z, channels)
    )
    slope = sig * (1.0 + pre * (1.0 - sig))
    grad_pre = (cotangent.reshape(-1, channels).astype(jnp.float32) * live * slope).astype(
        jnp.bfloat16
    )
    taps = weight.reshape(27, channels, channels)
    grid = grad_pre.reshape(width_x, width_y, depth_z, channels)
    grad_pad = padded_2(grid, (("wide", 0), ("narrow", 1)), 1)
    grad_pad = jnp.pad(grad_pad, ((0, 0), (0, 0), (1, 1), (0, 0)))
    grad_columns = gather_taps(grad_pad, width_x, width_y, depth_z, channels, True)
    flipped = jnp.transpose(taps, (0, 2, 1)).reshape(27 * channels, channels)
    grad_field = jnp.dot(grad_columns, flipped, preferred_element_type=jnp.float32)
    grad_input = (
        (grad_field * live).astype(jnp.bfloat16).reshape(width_x, width_y, depth_z, channels)
    )
    scale = 1.0 / jnp.sqrt(
        jnp.float32(width_x * width_y * depth_z * lax.axis_size("wide") * lax.axis_size("narrow"))
    )
    whole = lax.dot_general(
        grad_pre, columns, (((0,), (0,)), ((), ())), preferred_element_type=jnp.float32
    )
    piece_flat = lax.psum_scatter(
        whole.reshape(-1), ("wide", "narrow"), scatter_dimension=0, tiled=True
    )
    gathered = lax.all_gather(piece_flat, "narrow", axis=0, tiled=True)
    summed = gathered.reshape(channels // lax.axis_size("wide"), 27 * channels)
    grad_weight = summed * scale
    return (activation, grad_input, grad_weight)


def sharded(body, mesh, wide):
    return jax.shard_map(
        body,
        mesh=mesh,
        in_specs=(
            P(wide, "narrow", None, None),
            P(),
            P(wide, "narrow", None),
            P(wide, "narrow", None, None),
        ),
        out_specs=(
            P(wide, "narrow", None, None),
            P(wide, "narrow", None, None),
            P(wide, None),
        ),
        check_vma=False,
    )


def solution(mesh):
    wide, narrow = mesh.shape["wide"], mesh.shape["narrow"]
    if wide != 4 * QUAD or narrow != SIDES:
        return sharded(summed_local, mesh, "wide")
    planes = Mesh(
        mesh.devices.reshape(wide // QUAD, QUAD, narrow), ("depth", "quad", "narrow")
    )
    return sharded(planes_local, planes, WIDE)
```

```python
import functools

import jax
import jax.numpy as jnp
from jax import lax
from jax.experimental import pallas as pl
from jax.experimental.pallas import tpu as pltpu
from jax.sharding import Mesh
from jax.sharding import PartitionSpec as P

WIDE = ("depth", "quad")
QUAD = 4
SIDES = 2
MEMBERS = QUAD * SIDES
CHIPS = (0, 1, 4, 5)
OFFSETS = (-1, 0, 1)
DEPTH = 8


def position():
    quad, side = lax.axis_index("quad"), lax.axis_index("narrow")
    return lax.axis_index("depth"), quad * SIDES + side, quad, side


def shift_z(field, step):
    if step == 0:
        return field
    depth = field.shape[1]
    moved = pltpu.roll(field, (-step) % depth, 1)
    z = lax.broadcasted_iota(jnp.int32, field.shape, 1) + step
    return jnp.where((z >= 0) & (z < depth), moved, 0.0)


def pick_kernel(planes, out_ref):
    index = lax.broadcasted_iota(jnp.int32, out_ref.shape, 0)
    column = lax.broadcasted_iota(jnp.int32, out_ref.shape, 1)
    per = out_ref.shape[1] // (planes * QUAD)
    share = per // SIDES
    group = planes * share
    quad, side = index // (SIDES * group), index // group % SIDES
    plane, row = index // share % planes, index % share
    channel = per * (QUAD * plane + quad) + share * side + row
    out_ref[...] = jnp.where(channel == column, 1.0, 0.0).astype(jnp.bfloat16)


def dense(total):
    tiles = -(-total // 128)
    moved = tiles // 4
    return (tiles - moved) * 128, moved * 128


def fold_rows(block, total):
    kept, moved = dense(total)
    tail = block[:, kept : kept + moved]
    row = lax.broadcasted_iota(jnp.int32, tail.shape, 0)
    pieces = []
    for k in range(3):
        spare = jnp.where(row == 6, pltpu.roll(tail, 6 - k, 0), pltpu.roll(tail, 4 - k, 0))
        pieces.append(jnp.where(row < 6, block[:, k * moved : (k + 1) * moved], spare))
    return jnp.concatenate(pieces + [block[:, 3 * moved : kept]], axis=1)


def unfold_rows(block, total):
    kept, moved = dense(total)
    row = lax.broadcasted_iota(jnp.int32, (8, moved), 0)
    tail = jnp.zeros((8, moved), block.dtype)
    for k in range(3):
        piece = block[:, k * moved : (k + 1) * moved]
        tail = jnp.where(row == k, pltpu.roll(piece, 2 + k, 0), tail)
        tail = jnp.where(row == 3 + k, pltpu.roll(piece, 4 + k, 0), tail)
    return jnp.concatenate([block, tail], axis=1)[:, :total]


def rows_of_128(block):
    half = block.shape[0] // 2
    rest = jnp.concatenate([block[:half, 128:], block[half:, 128:]], axis=1)
    return jnp.concatenate([block[:, :128], rest], axis=0)


def rows_of_192(block):
    count = block.shape[0] * 2 // 3
    rest = jnp.concatenate([block[count:, :64], block[count:, 64:]], axis=0)
    return jnp.concatenate([block[:count], rest], axis=1)


def prepare_kernel(features, cot, mask, first, masked_ref, cot_ref, live_ref, near_ref, far_ref):
    width, rows, channels = features.shape
    f32 = jnp.float32
    flat = mask[...].astype(f32).reshape(width * rows // DEPTH, DEPTH)
    live = jnp.broadcast_to(flat[:, :, None], flat.shape + (channels,)).reshape(features.shape)
    live_ref[...] = live[:, :, :128]
    masked_ref[...] = (features[...].astype(f32) * live).astype(jnp.bfloat16)
    cot_ref[...] = (cot[...].astype(f32) * live).astype(jnp.bfloat16)
    odd = lax.rem(position()[2], 2)
    for ref, upper in ((near_ref, 1 - odd), (far_ref, odd)):
        slabs = [
            masked_ref[pl.ds(upper * (width - 2), 2)],
            cot_ref[pl.ds(upper * (width - 1), 1)],
        ]
        slabs = jnp.concatenate(slabs, axis=0).astype(f32).reshape(3 * rows, channels)
        ref[...] = rows_of_128(slabs).astype(jnp.bfloat16)


def pack_kernel(masked, after, packed_ref):
    count, channels = packed_ref.shape[0] * 128 // masked.shape[2], masked.shape[2]
    block = masked[...].reshape(count, channels)
    packed_ref[...] = rows_of_128(block)


def across_kernel(masked, cot, across_ref):
    width, rows, channels = masked.shape
    packed = rows_of_128(masked[...].reshape(width * rows, channels))
    across_ref[: packed.shape[0]] = packed
    ahead = position()[3] == 0
    grown = cot[...].astype(jnp.float32)
    strip = jnp.where(ahead, grown[:, rows - DEPTH :], grown[:, :DEPTH])
    strip = rows_of_128(strip.reshape(width * DEPTH, channels))
    across_ref[packed.shape[0] :] = strip.astype(jnp.bfloat16)


def corner_kernel(near, far, out_ref, edge):
    _, slabs, rows, channels = edge.shape
    _, _, quad, side = position()
    odd = lax.rem(quad, 2)
    f32 = jnp.float32
    edge[odd] = rows_of_192(far[...].astype(f32)).reshape(edge.shape[1:])
    edge[1 - odd] = rows_of_192(near[...].astype(f32)).reshape(edge.shape[1:])
    halo = 2 * DEPTH
    ahead = side == 0
    strip = jnp.where(ahead, edge[:, :2, rows - halo :], edge[:, :2, :halo])
    cots = jnp.where(ahead, edge[:, 2, rows - DEPTH :], edge[:, 2, :DEPTH])
    both = [strip.reshape(4 * halo, channels), cots.reshape(2 * DEPTH, channels)]
    both = rows_of_128(jnp.concatenate(both, axis=0))
    blank = jnp.zeros((out_ref.shape[0] - both.shape[0], 128), f32)
    out_ref[...] = jnp.concatenate([both, blank], axis=0).astype(jnp.bfloat16)


def turn_kernel(weight, out_ref):
    step = 2 * weight.shape[0]
    total = weight.shape[1]
    for start in range(0, total, step):
        stop = min(start + step, total)
        out_ref[start:stop, :] = weight[:, start:stop].T


def bulk_kernel(masked, near, far, across, weight, pre_ref, ext, edge, cols):
    width, rows, channels = masked.shape
    f32 = jnp.float32
    plane, _, quad, side = position()
    use_low = side.astype(f32)
    use_high = (1 - side).astype(f32)
    place = plane * QUAD + quad
    use_left = (place > 0).astype(f32)
    use_right = (place < QUAD * lax.axis_size("depth") - 1).astype(f32)
    halo = 2 * DEPTH
    tall = rows + 2 * halo
    mid = rows + 2 * DEPTH
    span = width + 4
    odd = lax.rem(quad, 2)
    edge[odd] = rows_of_192(far[...].astype(f32)).reshape(edge.shape[1:])
    edge[1 - odd] = rows_of_192(near[...].astype(f32)).reshape(edge.shape[1:])
    ext[0:2, halo : halo + rows, :] = edge[0, 0:2] * use_left
    ext[2 : 2 + width, halo : halo + rows, :] = masked[...].astype(f32)
    ext[2 + width :, halo : halo + rows, :] = edge[1, 0:2] * use_right
    half = width // 2
    count = width * rows * channels // 128
    held = across[:count].astype(f32).reshape(width + half, rows, 128)
    brick = jnp.where(side == 0, held[:, :halo], held[:, rows - halo :])
    rest = jnp.concatenate([brick[width:, :, :64], brick[width:, :, 64:]], axis=0)
    beside = jnp.concatenate([brick[:width], rest], axis=2)
    blank = jnp.zeros((2, halo, channels), f32)
    for use, start in ((use_low, 0), (use_high, halo + rows)):
        at = slice(start, start + halo)
        ext[0:2, at, :] = blank
        ext[2 : 2 + width, at, :] = beside * use
        ext[2 + width :, at, :] = blank
    field = ext[...].reshape(span * tall // DEPTH, DEPTH, channels)
    for c in OFFSETS:
        moved = shift_z(field, c).reshape(span, tall, channels)
        for b in OFFSETS:
            at = ((b + 1) * 3 + c + 1) * channels
            start = DEPTH * (b + 1)
            cols[:, :, at : at + channels] = moved[:, start : start + mid].astype(jnp.bfloat16)
    nine = 9 * channels
    pre = jnp.zeros(((width + 2) * mid, channels), f32)
    for a in range(3):
        pre += jnp.dot(
            cols[a : a + width + 2].reshape((width + 2) * mid, nine),
            weight[a * nine : (a + 1) * nine, :],
            preferred_element_type=f32,
        )
    pre_ref[...] = pre.reshape(pre_ref.shape)


def forward_kernel(bulk, cot, near, far, across, corner, live, weight, pick, *refs):
    act_ref, gp_ref = refs[:2]
    slice_refs = refs[2 : 2 + len(CHIPS)]
    edge, cols, total, slices = refs[2 + len(CHIPS) :]
    width, rows, channels = cot.shape
    f32 = jnp.float32
    plane, me, quad, side = position()
    use_low = side.astype(f32)
    use_high = (1 - side).astype(f32)
    place = plane * QUAD + quad
    use_left = (place > 0).astype(f32)
    use_right = (place < QUAD * lax.axis_size("depth") - 1).astype(f32)
    halo = 2 * DEPTH
    mid = rows + 2 * DEPTH
    count = 4 * halo + 2 * DEPTH
    both = rows_of_192(corner[...].astype(f32)[: count * channels // 128])
    corners = both[: 4 * halo].reshape(2, 2, halo, channels)
    corners = jnp.concatenate([corners[0] * use_left, corners[1] * use_right], axis=0)
    sources = ((0, 1, None, None), (1, None, None, 2), (None, None, 2, 3))
    blank = jnp.zeros((DEPTH, channels), f32)
    six = 6 * channels
    for c in OFFSETS:
        moved = shift_z(corners.reshape(8, DEPTH, channels), c)
        for b, low, high in ((0, (0, 1), (None, 0)), (1, (1, None), (0, 1))):
            at = (b * 3 + c + 1) * channels
            parts = []
            for slab in range(4):
                for below, above in zip(low, high):
                    part = blank if below is None else moved[2 * slab + below] * use_low
                    if above is not None:
                        part = part + moved[2 * slab + above] * use_high
                    parts.append(part)
            for a in range(3):
                rows_a = []
                for source in sources[a]:
                    pair = [blank] * 2 if source is None else parts[2 * source : 2 * source + 2]
                    rows_a += pair
                cols[a, :, at : at + channels] = jnp.concatenate(rows_a, axis=0).astype(
                    jnp.bfloat16
                )
    share = jnp.zeros((4 * halo, channels), f32)
    for a in range(3):
        taps = pl.ds(pl.multiple_of((3 * a + 1 - side) * 3 * channels, 16), six)
        share += jnp.dot(cols[a], weight[taps], preferred_element_type=f32)
    share = share.reshape(4, halo, channels)
    total[...] = bulk[...]
    at = pl.ds(pl.multiple_of((1 - side) * (mid - halo), DEPTH), halo)
    total[0:2, at, :] += share[0:2]
    total[width : width + 2, at, :] += share[2:4]
    pre = total[...].reshape((width + 2) * mid, channels)
    sig = 0.5 * jnp.tanh(0.5 * pre) + 0.5
    act = (pre * sig).reshape(width + 2, mid, channels)[1 : 1 + width, DEPTH : DEPTH + rows]
    act_ref[...] = (act * live[:, :, 0:1]).astype(jnp.bfloat16)
    slope = (sig * (1.0 + pre * (1.0 - sig))).reshape(width + 2, mid, channels)
    ends = both[4 * halo :].reshape(2, 1, DEPTH, channels)
    strip = across[width * rows * channels // 128 :].astype(f32)
    beyond = jnp.concatenate(
        [
            ends[0] * use_left,
            rows_of_192(strip).reshape(width, DEPTH, channels),
            ends[1] * use_right,
        ],
        axis=0,
    )
    odd = lax.rem(quad, 2)
    edge[odd] = rows_of_192(far[...].astype(f32))[2 * rows :]
    edge[1 - odd] = rows_of_192(near[...].astype(f32))[2 * rows :]
    centre = [edge[0:1] * use_left, cot[...].astype(f32), edge[1:2] * use_right]
    centre = jnp.concatenate(centre, axis=0)
    full = jnp.concatenate([beyond * use_low, centre, beyond * use_high], axis=1)
    grad = full * slope
    gp_ref[...] = grad.astype(jnp.bfloat16)
    inner = grad[:, DEPTH : DEPTH + rows].astype(jnp.bfloat16)
    turned = lax.dot_general(
        pick[...],
        inner.reshape((width + 2) * rows, channels),
        (((1,), (1,)), ((), ())),
        preferred_element_type=f32,
    )
    slices[...] = turned.reshape(slices.shape)
    chip = me - lax.rem(quad, 2) * SIDES
    for distance, ref in zip(CHIPS, slice_refs):
        both = [slices[chip ^ distance], slices[(chip ^ distance) + SIDES]]
        ref[...] = jnp.concatenate(both, axis=0).astype(jnp.bfloat16)


def input_kernel(gp, live, turned, act, out_ref, act_ref, cols, weight):
    act_ref[...] = act[...]
    width, rows, channels = out_ref.shape
    f32 = jnp.float32
    tall = rows + 2 * DEPTH
    for tap in range(27):
        weight[tap * channels : (tap + 1) * channels, :] = turned[
            :, tap * channels : (tap + 1) * channels
        ]
    field = gp[...].astype(f32).reshape((width + 2) * tall // DEPTH, DEPTH, channels)
    for c in OFFSETS:
        moved = shift_z(field, -c).reshape(width + 2, tall, channels)
        for b in OFFSETS:
            at = ((b + 1) * 3 + c + 1) * channels
            start = DEPTH * (1 - b)
            cols[:, :, at : at + channels] = moved[:, start : start + rows].astype(jnp.bfloat16)
    nine = 9 * channels
    total = jnp.zeros((width * rows, channels), f32)
    for a in range(3):
        total += jnp.dot(
            cols[2 - a : 2 - a + width].reshape(width * rows, nine),
            weight[a * nine : (a + 1) * nine, :],
            preferred_element_type=f32,
        )
    out_ref[...] = (total.reshape(width, rows, channels) * live[:, :, 0:1]).astype(jnp.bfloat16)


def unpack_pair(bricks, masked):
    per, lane, _ = masked.shape
    half = lane // 2
    side = position()[3]
    for i, brick in enumerate(bricks):
        at_rows = pl.ds(pl.multiple_of((side ^ i) * half, half), half)
        for x in range(per):
            shift = 64 * (x // (per // 2))
            rest = brick[pl.ds((per + x % (per // 2)) * half, half)]
            masked[x, at_rows, :128] = brick[pl.ds(x * half, half)]
            masked[x, at_rows, 128:] = rest[:, shift : shift + 64]


def pair_product(received, masked, cols):
    f32 = jnp.float32
    group, lanes = received[0].shape
    per, lane, channels = masked.shape
    half = lane // 2
    side = position()[3]
    at = lax.broadcasted_iota(jnp.int32, (group, lane), 1)
    y, z = at // DEPTH, at % DEPTH
    tall = lane // DEPTH
    own, other = (ref[...].astype(f32) for ref in received)
    first = jnp.where(side == 0, own, other)
    second = jnp.where(side == 0, other, own)
    for k in range(per + 2):
        one = first[:, k // 2 * lane : (k // 2 + 1) * lane]
        two = second[:, k // 2 * lane : (k // 2 + 1) * lane]
        if k % 2 == 0:
            base = jnp.where(at < half, one, pltpu.roll(two, half, 1))
        else:
            base = jnp.where(at < half, pltpu.roll(one, half, 1), two)
        pieces = []
        for b in OFFSETS:
            for c in OFFSETS:
                step = (DEPTH * b + c) % lane
                moved = base if step == 0 else pltpu.roll(base, step, 1)
                keep = (y - b >= 0) & (y - b < tall) & (z - c >= 0) & (z - c < DEPTH)
                pieces.append(jnp.where(keep, moved, 0.0))
        cols[:, k * lane : (k + 1) * lane] = jnp.concatenate(pieces, axis=0).astype(jnp.bfloat16)
    field = masked[...].reshape(per * lane, channels)
    for a in range(3):
        start = (2 - a) * lane
        got = jnp.dot(
            cols[:, start : start + per * lane], field, preferred_element_type=f32
        ).reshape(9, group, channels)
        yield a, jnp.concatenate([got[tap] for tap in range(9)], axis=1)


def first_pair_kernel(own, other, brick, across, beside, beyond, part_ref, next_ref, cols, masked):
    unpack_pair((beside, beyond), next_ref)
    unpack_pair((brick, across), masked)
    for a, rows in pair_product((own, other), masked, cols):
        width = rows.shape[1]
        part_ref[:, a * width : (a + 1) * width] = rows


def second_pair_kernel(before, other, own, masked, keep_ref, send_ref, part, cols):
    for a, rows in pair_product((own, other), masked, cols):
        width = rows.shape[1]
        at = slice(a * width, (a + 1) * width)
        part[:, at] = before[:, at] + rows
    core = lax.rem(position()[2], 2)
    half = part.shape[0] // 2
    keep_ref[...] = part[pl.ds(pl.multiple_of(core * half, 8), half)]
    send_ref[...] = part[pl.ds(pl.multiple_of((1 - core) * half, 8), half)].astype(jnp.bfloat16)


def fold_kernel(keep, other, own_ref, *refs):
    *send_refs, both, rows = refs
    planes, eight, _ = rows.shape
    count, total = keep.shape
    share = count // planes
    both[:count, :total] = keep[...] + other[...].astype(jnp.float32)
    both[:, total:] = jnp.zeros((both.shape[0], both.shape[1] - total), jnp.float32)
    for to in range(planes):
        rows[to] = fold_rows(both[share * to : share * to + eight, :], total)
    plane = position()[0]
    own_ref[...] = rows[plane]
    for distance, ref in enumerate(send_refs, 1):
        ref[...] = rows[plane ^ distance].astype(jnp.bfloat16)


def sum_kernel(scale, own, one, two, three, out_ref):
    f32 = jnp.float32
    total = own[...] + one[...].astype(f32) + two[...].astype(f32) + three[...].astype(f32)
    out_ref[...] = (total * scale).astype(out_ref.dtype)


def join_kernel(mine, other, out_ref):
    share = out_ref.shape[0] // SIDES
    ahead = position()[3] == 0
    total = out_ref.shape[1]
    here = unfold_rows(mine[...].astype(jnp.float32), total)
    there = unfold_rows(other[...].astype(jnp.float32), total)
    first = jnp.where(ahead, here, there)
    second = jnp.where(ahead, there, here)
    out_ref[0:share] = first[:share]
    out_ref[share:] = second[:share]


def call(body, name, mebibytes, flops, moved, out_shape, scratch=(), in_specs=None):
    spec = pl.BlockSpec(memory_space=pltpu.VMEM)

    def run(*operands):
        return pl.pallas_call(
            body,
            out_shape=out_shape,
            in_specs=in_specs or [spec] * len(operands),
            out_specs=jax.tree.map(lambda _: spec, out_shape),
            scratch_shapes=scratch,
            compiler_params=pltpu.CompilerParams(vmem_limit_bytes=mebibytes << 20),
            cost_estimate=pl.CostEstimate(flops=flops, bytes_accessed=moved, transcendentals=0),
            name=name,
        )(*operands)

    return run


def planes_local(features, weight, voxel_mask, cotangent):
    bf16 = jnp.bfloat16
    f32 = jnp.float32
    array = jax.ShapeDtypeStruct
    width, wide_y, depth, channels = features.shape
    rows = wide_y * depth
    planes = lax.axis_size("depth")
    count = planes * QUAD
    total = 27 * channels
    halo = 2 * DEPTH
    span = (width + 2) * rows
    share = channels // count // SIDES
    group = planes * share

    def swap(piece, axes, distance, size):
        return lax.ppermute(piece, axes, [(i, i ^ distance) for i in range(size)])

    def in_plane(piece, distance):
        return swap(piece, ("quad", "narrow"), distance, MEMBERS)

    brick = array((width, rows, channels), bf16)
    slab = array((3 * rows * channels // 128, 128), bf16)
    slabs = (2, 3, rows, channels)
    pick = call(
        functools.partial(pick_kernel, planes), "pick", 4, 1 << 32, 1 << 16,
        array((MEMBERS * group, channels), bf16),
    )()
    vmem = pl.BlockSpec(memory_space=pltpu.VMEM)
    masked, cot, live, near, far = call(
        prepare_kernel, "prepare", 16, 1 << 20, 1 << 20,
        (brick, brick, array((width, rows, 128), f32), slab, slab),
        (),
        [vmem] * 3 + [pl.BlockSpec(memory_space=pl.ANY)],
    )(
        features.reshape(width, rows, channels),
        cotangent.reshape(width, rows, channels),
        voxel_mask,
        pick,
    )
    near = swap(near, WIDE, 1, count)
    ends = [min(max(((i + 1) ^ 1) - 1, 0), count - 1) for i in range(count)]
    far = lax.ppermute(far, WIDE, list(enumerate(ends)))
    weight_rows = call(
        turn_kernel, "turn", 8, 1 << 20, 4 << 20, array((total, channels), bf16)
    )(weight.T)
    count_128 = width * rows * channels // 128
    strip_128 = width * DEPTH * channels // 128
    across = call(
        across_kernel, "across", 4, 1 << 16, 1 << 19, array((count_128 + strip_128, 128), bf16)
    )(masked, cot)
    across = in_plane(across, CHIPS[1])
    packed = call(
        pack_kernel, "pack", 4, 1 << 16, 1 << 19, array((count_128, 128), bf16), (),
        [vmem, pl.BlockSpec(memory_space=pl.ANY)],
    )(masked, weight_rows)
    near, far, weight_rows, late = lax.optimization_barrier((near, far, weight_rows, packed))
    corner = call(
        corner_kernel, "corner", 4, 1 << 16, 1 << 18,
        array((128, 128), bf16),
        (pltpu.VMEM(slabs, f32),),
    )(near, far)
    corner = in_plane(corner, 1)
    mid = rows + 2 * DEPTH
    bulk = call(
        bulk_kernel, "bulk", 24, 3 << 29, 1 << 20, array((width + 2, mid, channels), f32),
        (
            pltpu.VMEM((width + 4, rows + 2 * halo, channels), f32),
            pltpu.VMEM(slabs, f32),
            pltpu.VMEM((width + 4, mid, 9 * channels), bf16),
        ),
    )(masked, near, far, across, weight_rows)
    bricks = [packed, across, in_plane(packed, CHIPS[2]), in_plane(late, CHIPS[3])]

    act, gp, *slices = call(
        forward_kernel, "forward", 24, 3 << 29, 1 << 20,
        (brick, array((width + 2, mid, channels), bf16))
        + (array((2 * group, span), bf16),) * len(CHIPS),
        (
            pltpu.VMEM((2, rows, channels), f32),
            pltpu.VMEM((3, 4 * halo, 6 * channels), bf16),
            pltpu.VMEM((width + 2, mid, channels), f32),
            pltpu.VMEM((MEMBERS, group, span), f32),
        ),
    )(bulk, cot, near, far, across, corner, live, weight_rows, pick)
    bricks[2], *slices = lax.optimization_barrier((bricks[2], *slices))
    for place in (3, 2, 1):
        slices[place] = in_plane(slices[place], CHIPS[place])

    grad_input, act = call(
        input_kernel, "input_gradient", 20, 2 * 512 * 5184 * 256, 4 << 20, (brick, brick),
        (
            pltpu.VMEM((width + 2, rows, 9 * channels), bf16),
            pltpu.VMEM((total, channels), bf16),
        ),
    )(gp, live, weight.T, act)

    lanes = dense(total)[0]
    cols = pltpu.VMEM((9 * 2 * group, (width + 2) * SIDES * rows), bf16)
    pair = (width, SIDES * rows, channels)
    part, pair_masked = call(
        first_pair_kernel, "first_pair", 16, 1 << 30, 2 << 20,
        (array((2 * group, total), f32), array(pair, bf16)),
        (cols, pltpu.VMEM(pair, bf16)),
    )(*slices[:2], *bricks)
    keep, fold = call(
        second_pair_kernel, "second_pair", 16, 1 << 30, 2 << 20,
        (array((group, total), f32), array((group, total), bf16)),
        (pltpu.VMEM((2 * group, total), f32), cols),
    )(part, *slices[3:1:-1], pair_masked)
    own, *sends = call(
        fold_kernel, "fold", 8, 8 * total * 4, 8 * total * 40,
        (array((8, lanes), f32),) + (array((8, lanes), bf16),) * (planes - 1),
        (
            pltpu.VMEM((group + 8, sum(dense(total))), f32),
            pltpu.VMEM((planes, 8, lanes), f32),
        ),
    )(keep, in_plane(fold, 2))
    got = [swap(sent, "depth", d, planes) for d, sent in list(enumerate(sends, 1))[::-1]]
    grad_input, *got = lax.optimization_barrier((grad_input, *got))
    voxels = count * SIDES * width * rows
    mine = call(
        functools.partial(sum_kernel, float(1.0 / voxels**0.5)),
        "plane_sum", 4, 8 * total * 4, 8 * total * 14, array((8, lanes), bf16),
    )(own, *got)
    grad_weight = call(
        join_kernel, "join", 4, 8 * total, 8 * total * 14, array((channels // count, total), f32)
    )(mine, in_plane(mine, 1))
    shape = features.shape
    return act.reshape(shape), grad_input.reshape(shape), grad_weight


def padded_2(cells, sides, width):
    for axis, dim in sides:
        count = lax.axis_size(axis)
        ends = count - 1
        head = lax.slice_in_dim(cells, 0, width, axis=dim)
        tail = lax.slice_in_dim(cells, cells.shape[dim] - width, cells.shape[dim], axis=dim)
        cells = jnp.concatenate(
            [
                lax.ppermute(tail, axis, [(i, (i + 1) % count) for i in range(ends)]),
                cells,
                lax.ppermute(head, axis, [((i + 1) % count, i) for i in range(ends)]),
            ],
            axis=dim,
        )
    return cells


def gather_taps(padded, width_x, width_y, depth_z, channels, flip):
    pieces = []
    for shift_x in range(3):
        for shift_y in range(3):
            for shift_z in range(3):
                start_x = 2 - shift_x if flip else shift_x
                start_y = 2 - shift_y if flip else shift_y
                start_z = 2 - shift_z if flip else shift_z
                piece = padded[
                    start_x : start_x + width_x,
                    start_y : start_y + width_y,
                    start_z : start_z + depth_z,
                    :,
                ]
                pieces.append(piece.reshape(-1, channels))
    return jnp.concatenate(pieces, axis=1)


def summed_local(features, weight, voxel_mask, cotangent):
    width_x, width_y, depth_z, channels = features.shape
    masked = features * voxel_mask.astype(jnp.bfloat16)[..., None]
    padded = padded_2(masked, (("wide", 0), ("narrow", 1)), 1)
    padded = jnp.pad(padded, ((0, 0), (0, 0), (1, 1), (0, 0)))
    columns = gather_taps(padded, width_x, width_y, depth_z, channels, False)
    pre = jnp.dot(columns, weight, preferred_element_type=jnp.float32)
    live = voxel_mask.reshape(-1, 1).astype(jnp.float32)
    sig = jax.nn.sigmoid(pre)
    activation = (
        (pre * sig * live).astype(jnp.bfloat16).reshape(width_x, width_y, depth_z, channels)
    )
    slope = sig * (1.0 + pre * (1.0 - sig))
    grad_pre = (cotangent.reshape(-1, channels).astype(jnp.float32) * live * slope).astype(
        jnp.bfloat16
    )
    taps = weight.reshape(27, channels, channels)
    grid = grad_pre.reshape(width_x, width_y, depth_z, channels)
    grad_pad = padded_2(grid, (("wide", 0), ("narrow", 1)), 1)
    grad_pad = jnp.pad(grad_pad, ((0, 0), (0, 0), (1, 1), (0, 0)))
    grad_columns = gather_taps(grad_pad, width_x, width_y, depth_z, channels, True)
    flipped = jnp.transpose(taps, (0, 2, 1)).reshape(27 * channels, channels)
    grad_field = jnp.dot(grad_columns, flipped, preferred_element_type=jnp.float32)
    grad_input = (
        (grad_field * live).astype(jnp.bfloat16).reshape(width_x, width_y, depth_z, channels)
    )
    scale = 1.0 / jnp.sqrt(
        jnp.float32(width_x * width_y * depth_z * lax.axis_size("wide") * lax.axis_size("narrow"))
    )
    whole = lax.dot_general(
        grad_pre, columns, (((0,), (0,)), ((), ())), preferred_element_type=jnp.float32
    )
    piece_flat = lax.psum_scatter(
        whole.reshape(-1), ("wide", "narrow"), scatter_dimension=0, tiled=True
    )
    gathered = lax.all_gather(piece_flat, "narrow", axis=0, tiled=True)
    summed = gathered.reshape(channels // lax.axis_size("wide"), 27 * channels)
    grad_weight = summed * scale
    return (activation, grad_input, grad_weight)


def sharded(body, mesh, wide):
    return jax.shard_map(
        body,
        mesh=mesh,
        in_specs=(
            P(wide, "narrow", None, None),
            P(),
            P(wide, "narrow", None),
            P(wide, "narrow", None, None),
        ),
        out_specs=(
            P(wide, "narrow", None, None),
            P(wide, "narrow", None, None),
            P(wide, None),
        ),
        check_vma=False,
    )


def solution(mesh):
    wide, narrow = mesh.shape["wide"], mesh.shape["narrow"]
    if wide != 4 * QUAD or narrow != SIDES:
        return sharded(summed_local, mesh, "wide")
    planes = Mesh(
        mesh.devices.reshape(wide // QUAD, QUAD, narrow), ("depth", "quad", "narrow")
    )
    return sharded(planes_local, planes, WIDE)
```

```python
import functools

import jax
import jax.numpy as jnp
from jax import lax
from jax.experimental import pallas as pl
from jax.experimental.pallas import tpu as pltpu
from jax.sharding import Mesh
from jax.sharding import PartitionSpec as P

WIDE = ("depth", "quad")
QUAD = 4
SIDES = 2
MEMBERS = QUAD * SIDES
CHIPS = (0, 1, 4, 5)
OFFSETS = (-1, 0, 1)
DEPTH = 8


def position():
    quad, side = lax.axis_index("quad"), lax.axis_index("narrow")
    return lax.axis_index("depth"), quad * SIDES + side, quad, side


def shift_z(field, step):
    if step == 0:
        return field
    depth = field.shape[1]
    moved = pltpu.roll(field, (-step) % depth, 1)
    z = lax.broadcasted_iota(jnp.int32, field.shape, 1) + step
    return jnp.where((z >= 0) & (z < depth), moved, 0.0)


def pick_kernel(planes, out_ref):
    index = lax.broadcasted_iota(jnp.int32, out_ref.shape, 0)
    column = lax.broadcasted_iota(jnp.int32, out_ref.shape, 1)
    per = out_ref.shape[1] // (planes * QUAD)
    share = per // SIDES
    group = planes * share
    quad, side = index // (SIDES * group), index // group % SIDES
    plane, row = index // share % planes, index % share
    channel = per * (QUAD * plane + quad) + share * side + row
    out_ref[...] = jnp.where(channel == column, 1.0, 0.0).astype(jnp.bfloat16)


def dense(total):
    tiles = -(-total // 128)
    moved = tiles // 4
    return (tiles - moved) * 128, moved * 128


def fold_rows(block, total):
    kept, moved = dense(total)
    tail = block[:, kept : kept + moved]
    row = lax.broadcasted_iota(jnp.int32, tail.shape, 0)
    pieces = []
    for k in range(3):
        spare = jnp.where(row == 6, pltpu.roll(tail, 6 - k, 0), pltpu.roll(tail, 4 - k, 0))
        pieces.append(jnp.where(row < 6, block[:, k * moved : (k + 1) * moved], spare))
    return jnp.concatenate(pieces + [block[:, 3 * moved : kept]], axis=1)


def unfold_rows(block, total):
    kept, moved = dense(total)
    row = lax.broadcasted_iota(jnp.int32, (8, moved), 0)
    tail = jnp.zeros((8, moved), block.dtype)
    for k in range(3):
        piece = block[:, k * moved : (k + 1) * moved]
        tail = jnp.where(row == k, pltpu.roll(piece, 2 + k, 0), tail)
        tail = jnp.where(row == 3 + k, pltpu.roll(piece, 4 + k, 0), tail)
    return jnp.concatenate([block, tail], axis=1)[:, :total]


def rows_of_128(block):
    half = block.shape[0] // 2
    rest = jnp.concatenate([block[:half, 128:], block[half:, 128:]], axis=1)
    return jnp.concatenate([block[:, :128], rest], axis=0)


def rows_of_192(block):
    count = block.shape[0] * 2 // 3
    rest = jnp.concatenate([block[count:, :64], block[count:, 64:]], axis=0)
    return jnp.concatenate([block[:count], rest], axis=1)


def prepare_kernel(features, cot, mask, first, masked_ref, cot_ref, live_ref, near_ref, far_ref):
    width, rows, channels = features.shape
    f32 = jnp.float32
    flat = mask[...].astype(f32).reshape(width * rows // DEPTH, DEPTH)
    live = jnp.broadcast_to(flat[:, :, None], flat.shape + (channels,)).reshape(features.shape)
    live_ref[...] = live[:, :, :128]
    masked_ref[...] = (features[...].astype(f32) * live).astype(jnp.bfloat16)
    cot_ref[...] = (cot[...].astype(f32) * live).astype(jnp.bfloat16)
    odd = lax.rem(position()[2], 2)
    for ref, upper in ((near_ref, 1 - odd), (far_ref, odd)):
        slabs = [
            masked_ref[pl.ds(upper * (width - 2), 2)],
            cot_ref[pl.ds(upper * (width - 1), 1)],
        ]
        slabs = jnp.concatenate(slabs, axis=0).astype(f32).reshape(3 * rows, channels)
        ref[...] = rows_of_128(slabs).astype(jnp.bfloat16)


def pack_kernel(masked, after, packed_ref):
    count, channels = packed_ref.shape[0] * 128 // masked.shape[2], masked.shape[2]
    block = masked[...].reshape(count, channels)
    packed_ref[...] = rows_of_128(block)


def across_kernel(masked, cot, across_ref):
    width, rows, channels = masked.shape
    packed = rows_of_128(masked[...].reshape(width * rows, channels))
    across_ref[: packed.shape[0]] = packed
    ahead = position()[3] == 0
    grown = cot[...].astype(jnp.float32)
    strip = jnp.where(ahead, grown[:, rows - DEPTH :], grown[:, :DEPTH])
    strip = rows_of_128(strip.reshape(width * DEPTH, channels))
    across_ref[packed.shape[0] :] = strip.astype(jnp.bfloat16)


def corner_kernel(near, far, out_ref, edge):
    _, slabs, rows, channels = edge.shape
    _, _, quad, side = position()
    odd = lax.rem(quad, 2)
    f32 = jnp.float32
    edge[odd] = rows_of_192(far[...].astype(f32)).reshape(edge.shape[1:])
    edge[1 - odd] = rows_of_192(near[...].astype(f32)).reshape(edge.shape[1:])
    halo = 2 * DEPTH
    ahead = side == 0
    strip = jnp.where(ahead, edge[:, :2, rows - halo :], edge[:, :2, :halo])
    cots = jnp.where(ahead, edge[:, 2, rows - DEPTH :], edge[:, 2, :DEPTH])
    both = [strip.reshape(4 * halo, channels), cots.reshape(2 * DEPTH, channels)]
    both = rows_of_128(jnp.concatenate(both, axis=0))
    blank = jnp.zeros((out_ref.shape[0] - both.shape[0], 128), f32)
    out_ref[...] = jnp.concatenate([both, blank], axis=0).astype(jnp.bfloat16)


def turn_kernel(weight, out_ref):
    step = 2 * weight.shape[0]
    total = weight.shape[1]
    for start in range(0, total, step):
        stop = min(start + step, total)
        out_ref[start:stop, :] = weight[:, start:stop].T


def bulk_kernel(masked, near, far, across, weight, pre_ref, ext, edge, cols):
    width, rows, channels = masked.shape
    f32 = jnp.float32
    plane, _, quad, side = position()
    use_low = side.astype(f32)
    use_high = (1 - side).astype(f32)
    place = plane * QUAD + quad
    use_left = (place > 0).astype(f32)
    use_right = (place < QUAD * lax.axis_size("depth") - 1).astype(f32)
    halo = 2 * DEPTH
    tall = rows + 2 * halo
    mid = rows + 2 * DEPTH
    span = width + 4
    odd = lax.rem(quad, 2)
    edge[odd] = rows_of_192(far[...].astype(f32)).reshape(edge.shape[1:])
    edge[1 - odd] = rows_of_192(near[...].astype(f32)).reshape(edge.shape[1:])
    ext[0:2, halo : halo + rows, :] = edge[0, 0:2] * use_left
    ext[2 : 2 + width, halo : halo + rows, :] = masked[...].astype(f32)
    ext[2 + width :, halo : halo + rows, :] = edge[1, 0:2] * use_right
    half = width // 2
    count = width * rows * channels // 128
    held = across[:count].astype(f32).reshape(width + half, rows, 128)
    brick = jnp.where(side == 0, held[:, :halo], held[:, rows - halo :])
    rest = jnp.concatenate([brick[width:, :, :64], brick[width:, :, 64:]], axis=0)
    beside = jnp.concatenate([brick[:width], rest], axis=2)
    blank = jnp.zeros((2, halo, channels), f32)
    for use, start in ((use_low, 0), (use_high, halo + rows)):
        at = slice(start, start + halo)
        ext[0:2, at, :] = blank
        ext[2 : 2 + width, at, :] = beside * use
        ext[2 + width :, at, :] = blank
    field = ext[...].reshape(span * tall // DEPTH, DEPTH, channels)
    for c in OFFSETS:
        moved = shift_z(field, c).reshape(span, tall, channels)
        for b in OFFSETS:
            at = ((b + 1) * 3 + c + 1) * channels
            start = DEPTH * (b + 1)
            cols[:, :, at : at + channels] = moved[:, start : start + mid].astype(jnp.bfloat16)
    nine = 9 * channels
    pre = jnp.zeros(((width + 2) * mid, channels), f32)
    for a in range(3):
        pre += jnp.dot(
            cols[a : a + width + 2].reshape((width + 2) * mid, nine),
            weight[a * nine : (a + 1) * nine, :],
            preferred_element_type=f32,
        )
    pre_ref[...] = pre.reshape(pre_ref.shape)


def forward_kernel(bulk, cot, near, far, across, corner, live, weight, pick, *refs):
    act_ref, gp_ref = refs[:2]
    slice_refs = refs[2 : 2 + len(CHIPS)]
    edge, cols, total, slices = refs[2 + len(CHIPS) :]
    width, rows, channels = cot.shape
    f32 = jnp.float32
    plane, me, quad, side = position()
    use_low = side.astype(f32)
    use_high = (1 - side).astype(f32)
    place = plane * QUAD + quad
    use_left = (place > 0).astype(f32)
    use_right = (place < QUAD * lax.axis_size("depth") - 1).astype(f32)
    halo = 2 * DEPTH
    mid = rows + 2 * DEPTH
    count = 4 * halo + 2 * DEPTH
    both = rows_of_192(corner[...].astype(f32)[: count * channels // 128])
    corners = both[: 4 * halo].reshape(2, 2, halo, channels)
    corners = jnp.concatenate([corners[0] * use_left, corners[1] * use_right], axis=0)
    sources = ((0, 1, None, None), (1, None, None, 2), (None, None, 2, 3))
    blank = jnp.zeros((DEPTH, channels), f32)
    six = 6 * channels
    for c in OFFSETS:
        moved = shift_z(corners.reshape(8, DEPTH, channels), c)
        for b, low, high in ((0, (0, 1), (None, 0)), (1, (1, None), (0, 1))):
            at = (b * 3 + c + 1) * channels
            parts = []
            for slab in range(4):
                for below, above in zip(low, high):
                    part = blank if below is None else moved[2 * slab + below] * use_low
                    if above is not None:
                        part = part + moved[2 * slab + above] * use_high
                    parts.append(part)
            for a in range(3):
                rows_a = []
                for source in sources[a]:
                    pair = [blank] * 2 if source is None else parts[2 * source : 2 * source + 2]
                    rows_a += pair
                cols[a, :, at : at + channels] = jnp.concatenate(rows_a, axis=0).astype(
                    jnp.bfloat16
                )
    share = jnp.zeros((4 * halo, channels), f32)
    for a in range(3):
        taps = pl.ds(pl.multiple_of((3 * a + 1 - side) * 3 * channels, 16), six)
        share += jnp.dot(cols[a], weight[taps], preferred_element_type=f32)
    share = share.reshape(4, halo, channels)
    total[...] = bulk[...]
    at = pl.ds(pl.multiple_of((1 - side) * (mid - halo), DEPTH), halo)
    total[0:2, at, :] += share[0:2]
    total[width : width + 2, at, :] += share[2:4]
    pre = total[...].reshape((width + 2) * mid, channels)
    sig = 0.5 * jnp.tanh(0.5 * pre) + 0.5
    act = (pre * sig).reshape(width + 2, mid, channels)[1 : 1 + width, DEPTH : DEPTH + rows]
    act_ref[...] = (act * live[:, :, 0:1]).astype(jnp.bfloat16)
    slope = (sig * (1.0 + pre * (1.0 - sig))).reshape(width + 2, mid, channels)
    ends = both[4 * halo :].reshape(2, 1, DEPTH, channels)
    strip = across[width * rows * channels // 128 :].astype(f32)
    beyond = jnp.concatenate(
        [
            ends[0] * use_left,
            rows_of_192(strip).reshape(width, DEPTH, channels),
            ends[1] * use_right,
        ],
        axis=0,
    )
    odd = lax.rem(quad, 2)
    edge[odd] = rows_of_192(far[...].astype(f32))[2 * rows :]
    edge[1 - odd] = rows_of_192(near[...].astype(f32))[2 * rows :]
    centre = [edge[0:1] * use_left, cot[...].astype(f32), edge[1:2] * use_right]
    centre = jnp.concatenate(centre, axis=0)
    full = jnp.concatenate([beyond * use_low, centre, beyond * use_high], axis=1)
    grad = full * slope
    gp_ref[...] = grad.astype(jnp.bfloat16)
    inner = grad[:, DEPTH : DEPTH + rows].astype(jnp.bfloat16)
    turned = lax.dot_general(
        pick[...],
        inner.reshape((width + 2) * rows, channels),
        (((1,), (1,)), ((), ())),
        preferred_element_type=f32,
    )
    slices[...] = turned.reshape(slices.shape)
    chip = me - lax.rem(quad, 2) * SIDES
    for distance, ref in zip(CHIPS, slice_refs):
        both = [slices[chip ^ distance], slices[(chip ^ distance) + SIDES]]
        ref[...] = jnp.concatenate(both, axis=0).astype(jnp.bfloat16)


def input_kernel(gp, live, turned, act, out_ref, act_ref, cols, weight):
    act_ref[...] = act[...]
    width, rows, channels = out_ref.shape
    f32 = jnp.float32
    tall = rows + 2 * DEPTH
    for tap in range(27):
        weight[tap * channels : (tap + 1) * channels, :] = turned[
            :, tap * channels : (tap + 1) * channels
        ]
    field = gp[...].astype(f32).reshape((width + 2) * tall // DEPTH, DEPTH, channels)
    for c in OFFSETS:
        moved = shift_z(field, -c).reshape(width + 2, tall, channels)
        for b in OFFSETS:
            at = ((b + 1) * 3 + c + 1) * channels
            start = DEPTH * (1 - b)
            cols[:, :, at : at + channels] = moved[:, start : start + rows].astype(jnp.bfloat16)
    nine = 9 * channels
    total = jnp.zeros((width * rows, channels), f32)
    for a in range(3):
        total += jnp.dot(
            cols[2 - a : 2 - a + width].reshape(width * rows, nine),
            weight[a * nine : (a + 1) * nine, :],
            preferred_element_type=f32,
        )
    out_ref[...] = (total.reshape(width, rows, channels) * live[:, :, 0:1]).astype(jnp.bfloat16)


def unpack_pair(bricks, masked):
    per, lane, _ = masked.shape
    half = lane // 2
    side = position()[3]
    for i, brick in enumerate(bricks):
        at_rows = pl.ds(pl.multiple_of((side ^ i) * half, half), half)
        for x in range(per):
            shift = 64 * (x // (per // 2))
            rest = brick[pl.ds((per + x % (per // 2)) * half, half)]
            masked[x, at_rows, :128] = brick[pl.ds(x * half, half)]
            masked[x, at_rows, 128:] = rest[:, shift : shift + 64]


def pair_product(received, masked, cols):
    f32 = jnp.float32
    group, lanes = received[0].shape
    per, lane, channels = masked.shape
    half = lane // 2
    side = position()[3]
    at = lax.broadcasted_iota(jnp.int32, (group, lane), 1)
    y, z = at // DEPTH, at % DEPTH
    tall = lane // DEPTH
    own, other = (ref[...].astype(f32) for ref in received)
    first = jnp.where(side == 0, own, other)
    second = jnp.where(side == 0, other, own)
    for k in range(per + 2):
        one = first[:, k // 2 * lane : (k // 2 + 1) * lane]
        two = second[:, k // 2 * lane : (k // 2 + 1) * lane]
        if k % 2 == 0:
            base = jnp.where(at < half, one, pltpu.roll(two, half, 1))
        else:
            base = jnp.where(at < half, pltpu.roll(one, half, 1), two)
        pieces = []
        for b in OFFSETS:
            for c in OFFSETS:
                step = (DEPTH * b + c) % lane
                moved = base if step == 0 else pltpu.roll(base, step, 1)
                keep = (y - b >= 0) & (y - b < tall) & (z - c >= 0) & (z - c < DEPTH)
                pieces.append(jnp.where(keep, moved, 0.0))
        cols[:, k * lane : (k + 1) * lane] = jnp.concatenate(pieces, axis=0).astype(jnp.bfloat16)
    field = masked[...].reshape(per * lane, channels)
    for a in range(3):
        start = (2 - a) * lane
        got = jnp.dot(
            cols[:, start : start + per * lane], field, preferred_element_type=f32
        ).reshape(9, group, channels)
        yield a, jnp.concatenate([got[tap] for tap in range(9)], axis=1)


def first_pair_kernel(own, other, brick, across, beside, beyond, part_ref, next_ref, cols, masked):
    unpack_pair((beside, beyond), next_ref)
    unpack_pair((brick, across), masked)
    for a, rows in pair_product((own, other), masked, cols):
        width = rows.shape[1]
        part_ref[:, a * width : (a + 1) * width] = rows


def second_pair_kernel(before, other, own, masked, keep_ref, send_ref, part, cols):
    for a, rows in pair_product((own, other), masked, cols):
        width = rows.shape[1]
        at = slice(a * width, (a + 1) * width)
        part[:, at] = before[:, at] + rows
    core = lax.rem(position()[2], 2)
    half = part.shape[0] // 2
    keep_ref[...] = part[pl.ds(pl.multiple_of(core * half, 8), half)]
    send_ref[...] = part[pl.ds(pl.multiple_of((1 - core) * half, 8), half)].astype(jnp.bfloat16)


def fold_kernel(keep, other, own_ref, *refs):
    *send_refs, both, rows = refs
    planes, eight, _ = rows.shape
    count, total = keep.shape
    share = count // planes
    both[:count, :total] = keep[...] + other[...].astype(jnp.float32)
    both[:, total:] = jnp.zeros((both.shape[0], both.shape[1] - total), jnp.float32)
    for to in range(planes):
        rows[to] = fold_rows(both[share * to : share * to + eight, :], total)
    plane = position()[0]
    own_ref[...] = rows[plane]
    for distance, ref in enumerate(send_refs, 1):
        ref[...] = rows[plane ^ distance].astype(jnp.bfloat16)


def sum_kernel(scale, own, one, two, three, out_ref):
    f32 = jnp.float32
    total = own[...] + one[...].astype(f32) + two[...].astype(f32) + three[...].astype(f32)
    out_ref[...] = (total * scale).astype(out_ref.dtype)


def join_kernel(mine, other, out_ref):
    share = out_ref.shape[0] // SIDES
    ahead = position()[3] == 0
    total = out_ref.shape[1]
    here = unfold_rows(mine[...].astype(jnp.float32), total)
    there = unfold_rows(other[...].astype(jnp.float32), total)
    first = jnp.where(ahead, here, there)
    second = jnp.where(ahead, there, here)
    out_ref[0:share] = first[:share]
    out_ref[share:] = second[:share]


def call(body, name, mebibytes, flops, moved, out_shape, scratch=(), in_specs=None):
    spec = pl.BlockSpec(memory_space=pltpu.VMEM)

    def run(*operands):
        return pl.pallas_call(
            body,
            out_shape=out_shape,
            in_specs=in_specs or [spec] * len(operands),
            out_specs=jax.tree.map(lambda _: spec, out_shape),
            scratch_shapes=scratch,
            compiler_params=pltpu.CompilerParams(vmem_limit_bytes=mebibytes << 20),
            cost_estimate=pl.CostEstimate(flops=flops, bytes_accessed=moved, transcendentals=0),
            name=name,
        )(*operands)

    return run


def planes_local(features, weight, voxel_mask, cotangent):
    bf16 = jnp.bfloat16
    f32 = jnp.float32
    array = jax.ShapeDtypeStruct
    width, wide_y, depth, channels = features.shape
    rows = wide_y * depth
    planes = lax.axis_size("depth")
    count = planes * QUAD
    total = 27 * channels
    halo = 2 * DEPTH
    span = (width + 2) * rows
    share = channels // count // SIDES
    group = planes * share

    def swap(piece, axes, distance, size):
        return lax.ppermute(piece, axes, [(i, i ^ distance) for i in range(size)])

    def in_plane(piece, distance):
        return swap(piece, ("quad", "narrow"), distance, MEMBERS)

    brick = array((width, rows, channels), bf16)
    slab = array((3 * rows * channels // 128, 128), bf16)
    slabs = (2, 3, rows, channels)
    pick = call(
        functools.partial(pick_kernel, planes), "pick", 4, 1 << 32, 1 << 16,
        array((MEMBERS * group, channels), bf16),
    )()
    vmem = pl.BlockSpec(memory_space=pltpu.VMEM)
    masked, cot, live, near, far = call(
        prepare_kernel, "prepare", 16, 1 << 20, 1 << 20,
        (brick, brick, array((width, rows, 128), f32), slab, slab),
        (),
        [vmem] * 3 + [pl.BlockSpec(memory_space=pl.ANY)],
    )(
        features.reshape(width, rows, channels),
        cotangent.reshape(width, rows, channels),
        voxel_mask,
        pick,
    )
    near = swap(near, WIDE, 1, count)
    ends = [min(max(((i + 1) ^ 1) - 1, 0), count - 1) for i in range(count)]
    far = lax.ppermute(far, WIDE, list(enumerate(ends)))
    weight_rows = call(
        turn_kernel, "turn", 8, 1 << 20, 4 << 20, array((total, channels), bf16)
    )(weight.T)
    count_128 = width * rows * channels // 128
    strip_128 = width * DEPTH * channels // 128
    across = call(
        across_kernel, "across", 4, 1 << 16, 1 << 19, array((count_128 + strip_128, 128), bf16)
    )(masked, cot)
    across = in_plane(across, CHIPS[1])
    packed = call(
        pack_kernel, "pack", 4, 1 << 16, 1 << 19, array((count_128, 128), bf16), (),
        [vmem, pl.BlockSpec(memory_space=pl.ANY)],
    )(masked, weight_rows)
    near, far, weight_rows, late = lax.optimization_barrier((near, far, weight_rows, packed))
    corner = call(
        corner_kernel, "corner", 4, 1 << 16, 1 << 18,
        array((128, 128), bf16),
        (pltpu.VMEM(slabs, f32),),
    )(near, far)
    corner = in_plane(corner, 1)
    mid = rows + 2 * DEPTH
    bulk = call(
        bulk_kernel, "bulk", 24, 3 << 29, 1 << 20, array((width + 2, mid, channels), f32),
        (
            pltpu.VMEM((width + 4, rows + 2 * halo, channels), f32),
            pltpu.VMEM(slabs, f32),
            pltpu.VMEM((width + 4, mid, 9 * channels), bf16),
        ),
    )(masked, near, far, across, weight_rows)
    bricks = [packed, across, in_plane(packed, CHIPS[2]), in_plane(late, CHIPS[3])]

    act, gp, *slices = call(
        forward_kernel, "forward", 24, 3 << 29, 1 << 20,
        (brick, array((width + 2, mid, channels), bf16))
        + (array((2 * group, span), bf16),) * len(CHIPS),
        (
            pltpu.VMEM((2, rows, channels), f32),
            pltpu.VMEM((3, 4 * halo, 6 * channels), bf16),
            pltpu.VMEM((width + 2, mid, channels), f32),
            pltpu.VMEM((MEMBERS, group, span), f32),
        ),
    )(bulk, cot, near, far, across, corner, live, weight_rows, pick)
    bricks[2], *slices = lax.optimization_barrier((bricks[2], *slices))
    for place in (3, 2, 1):
        slices[place] = in_plane(slices[place], CHIPS[place])

    grad_input, act = call(
        input_kernel, "input_gradient", 20, 2 * 512 * 5184 * 256, 4 << 20, (brick, brick),
        (
            pltpu.VMEM((width + 2, rows, 9 * channels), bf16),
            pltpu.VMEM((total, channels), bf16),
        ),
    )(gp, live, weight.T, act)

    lanes = dense(total)[0]
    cols = pltpu.VMEM((9 * 2 * group, (width + 2) * SIDES * rows), bf16)
    pair = (width, SIDES * rows, channels)
    part, pair_masked = call(
        first_pair_kernel, "first_pair", 16, 1 << 30, 2 << 20,
        (array((2 * group, total), f32), array(pair, bf16)),
        (cols, pltpu.VMEM(pair, bf16)),
    )(*slices[:2], *bricks)
    keep, fold = call(
        second_pair_kernel, "second_pair", 16, 1 << 30, 2 << 20,
        (array((group, total), f32), array((group, total), bf16)),
        (pltpu.VMEM((2 * group, total), f32), cols),
    )(part, *slices[3:1:-1], pair_masked)
    own, *sends = call(
        fold_kernel, "fold", 8, 8 * total * 4, 8 * total * 40,
        (array((8, lanes), f32),) + (array((8, lanes), bf16),) * (planes - 1),
        (
            pltpu.VMEM((group + 8, sum(dense(total))), f32),
            pltpu.VMEM((planes, 8, lanes), f32),
        ),
    )(keep, in_plane(fold, 2))
    got = [swap(sends[d - 1], "depth", d, planes) for d in (2, 3, 1)]
    grad_input, *got = lax.optimization_barrier((grad_input, *got))
    voxels = count * SIDES * width * rows
    mine = call(
        functools.partial(sum_kernel, float(1.0 / voxels**0.5)),
        "plane_sum", 4, 8 * total * 4, 8 * total * 14, array((8, lanes), bf16),
    )(own, *got)
    grad_weight = call(
        join_kernel, "join", 4, 8 * total, 8 * total * 14, array((channels // count, total), f32)
    )(mine, in_plane(mine, 1))
    shape = features.shape
    return act.reshape(shape), grad_input.reshape(shape), grad_weight


def padded_2(cells, sides, width):
    for axis, dim in sides:
        count = lax.axis_size(axis)
        ends = count - 1
        head = lax.slice_in_dim(cells, 0, width, axis=dim)
        tail = lax.slice_in_dim(cells, cells.shape[dim] - width, cells.shape[dim], axis=dim)
        cells = jnp.concatenate(
            [
                lax.ppermute(tail, axis, [(i, (i + 1) % count) for i in range(ends)]),
                cells,
                lax.ppermute(head, axis, [((i + 1) % count, i) for i in range(ends)]),
            ],
            axis=dim,
        )
    return cells


def gather_taps(padded, width_x, width_y, depth_z, channels, flip):
    pieces = []
    for shift_x in range(3):
        for shift_y in range(3):
            for shift_z in range(3):
                start_x = 2 - shift_x if flip else shift_x
                start_y = 2 - shift_y if flip else shift_y
                start_z = 2 - shift_z if flip else shift_z
                piece = padded[
                    start_x : start_x + width_x,
                    start_y : start_y + width_y,
                    start_z : start_z + depth_z,
                    :,
                ]
                pieces.append(piece.reshape(-1, channels))
    return jnp.concatenate(pieces, axis=1)


def summed_local(features, weight, voxel_mask, cotangent):
    width_x, width_y, depth_z, channels = features.shape
    masked = features * voxel_mask.astype(jnp.bfloat16)[..., None]
    padded = padded_2(masked, (("wide", 0), ("narrow", 1)), 1)
    padded = jnp.pad(padded, ((0, 0), (0, 0), (1, 1), (0, 0)))
    columns = gather_taps(padded, width_x, width_y, depth_z, channels, False)
    pre = jnp.dot(columns, weight, preferred_element_type=jnp.float32)
    live = voxel_mask.reshape(-1, 1).astype(jnp.float32)
    sig = jax.nn.sigmoid(pre)
    activation = (
        (pre * sig * live).astype(jnp.bfloat16).reshape(width_x, width_y, depth_z, channels)
    )
    slope = sig * (1.0 + pre * (1.0 - sig))
    grad_pre = (cotangent.reshape(-1, channels).astype(jnp.float32) * live * slope).astype(
        jnp.bfloat16
    )
    taps = weight.reshape(27, channels, channels)
    grid = grad_pre.reshape(width_x, width_y, depth_z, channels)
    grad_pad = padded_2(grid, (("wide", 0), ("narrow", 1)), 1)
    grad_pad = jnp.pad(grad_pad, ((0, 0), (0, 0), (1, 1), (0, 0)))
    grad_columns = gather_taps(grad_pad, width_x, width_y, depth_z, channels, True)
    flipped = jnp.transpose(taps, (0, 2, 1)).reshape(27 * channels, channels)
    grad_field = jnp.dot(grad_columns, flipped, preferred_element_type=jnp.float32)
    grad_input = (
        (grad_field * live).astype(jnp.bfloat16).reshape(width_x, width_y, depth_z, channels)
    )
    scale = 1.0 / jnp.sqrt(
        jnp.float32(width_x * width_y * depth_z * lax.axis_size("wide") * lax.axis_size("narrow"))
    )
    whole = lax.dot_general(
        grad_pre, columns, (((0,), (0,)), ((), ())), preferred_element_type=jnp.float32
    )
    piece_flat = lax.psum_scatter(
        whole.reshape(-1), ("wide", "narrow"), scatter_dimension=0, tiled=True
    )
    gathered = lax.all_gather(piece_flat, "narrow", axis=0, tiled=True)
    summed = gathered.reshape(channels // lax.axis_size("wide"), 27 * channels)
    grad_weight = summed * scale
    return (activation, grad_input, grad_weight)


def sharded(body, mesh, wide):
    return jax.shard_map(
        body,
        mesh=mesh,
        in_specs=(
            P(wide, "narrow", None, None),
            P(),
            P(wide, "narrow", None),
            P(wide, "narrow", None, None),
        ),
        out_specs=(
            P(wide, "narrow", None, None),
            P(wide, "narrow", None, None),
            P(wide, None),
        ),
        check_vma=False,
    )


def solution(mesh):
    wide, narrow = mesh.shape["wide"], mesh.shape["narrow"]
    if wide != 4 * QUAD or narrow != SIDES:
        return sharded(summed_local, mesh, "wide")
    planes = Mesh(
        mesh.devices.reshape(wide // QUAD, QUAD, narrow), ("depth", "quad", "narrow")
    )
    return sharded(planes_local, planes, WIDE)
```

```python
import functools

import jax
import jax.numpy as jnp
from jax import lax
from jax.experimental import pallas as pl
from jax.experimental.pallas import tpu as pltpu
from jax.sharding import Mesh
from jax.sharding import PartitionSpec as P

WIDE = ("depth", "quad")
QUAD = 4
SIDES = 2
MEMBERS = QUAD * SIDES
CHIPS = (0, 1, 4, 5)
OFFSETS = (-1, 0, 1)
DEPTH = 8


def position():
    quad, side = lax.axis_index("quad"), lax.axis_index("narrow")
    return lax.axis_index("depth"), quad * SIDES + side, quad, side


def shift_z(field, step):
    if step == 0:
        return field
    depth = field.shape[1]
    moved = pltpu.roll(field, (-step) % depth, 1)
    z = lax.broadcasted_iota(jnp.int32, field.shape, 1) + step
    return jnp.where((z >= 0) & (z < depth), moved, 0.0)


def pick_kernel(planes, out_ref):
    index = lax.broadcasted_iota(jnp.int32, out_ref.shape, 0)
    column = lax.broadcasted_iota(jnp.int32, out_ref.shape, 1)
    per = out_ref.shape[1] // (planes * QUAD)
    share = per // SIDES
    group = planes * share
    quad, side = index // (SIDES * group), index // group % SIDES
    plane, row = index // share % planes, index % share
    channel = per * (QUAD * plane + quad) + share * side + row
    out_ref[...] = jnp.where(channel == column, 1.0, 0.0).astype(jnp.bfloat16)


def dense(total):
    tiles = -(-total // 128)
    moved = tiles // 4
    return (tiles - moved) * 128, moved * 128


def fold_rows(block, total):
    kept, moved = dense(total)
    tail = block[:, kept : kept + moved]
    row = lax.broadcasted_iota(jnp.int32, tail.shape, 0)
    pieces = []
    for k in range(3):
        spare = jnp.where(row == 6, pltpu.roll(tail, 6 - k, 0), pltpu.roll(tail, 4 - k, 0))
        pieces.append(jnp.where(row < 6, block[:, k * moved : (k + 1) * moved], spare))
    return jnp.concatenate(pieces + [block[:, 3 * moved : kept]], axis=1)


def unfold_rows(block, total):
    kept, moved = dense(total)
    row = lax.broadcasted_iota(jnp.int32, (8, moved), 0)
    tail = jnp.zeros((8, moved), block.dtype)
    for k in range(3):
        piece = block[:, k * moved : (k + 1) * moved]
        tail = jnp.where(row == k, pltpu.roll(piece, 2 + k, 0), tail)
        tail = jnp.where(row == 3 + k, pltpu.roll(piece, 4 + k, 0), tail)
    return jnp.concatenate([block, tail], axis=1)[:, :total]


def rows_of_128(block):
    half = block.shape[0] // 2
    rest = jnp.concatenate([block[:half, 128:], block[half:, 128:]], axis=1)
    return jnp.concatenate([block[:, :128], rest], axis=0)


def rows_of_192(block):
    count = block.shape[0] * 2 // 3
    rest = jnp.concatenate([block[count:, :64], block[count:, 64:]], axis=0)
    return jnp.concatenate([block[:count], rest], axis=1)


def prepare_kernel(features, cot, mask, first, masked_ref, cot_ref, live_ref, near_ref, far_ref):
    width, rows, channels = features.shape
    f32 = jnp.float32
    flat = mask[...].astype(f32).reshape(width * rows // DEPTH, DEPTH)
    live = jnp.broadcast_to(flat[:, :, None], flat.shape + (channels,)).reshape(features.shape)
    live_ref[...] = live[:, :, :128]
    masked_ref[...] = (features[...].astype(f32) * live).astype(jnp.bfloat16)
    cot_ref[...] = (cot[...].astype(f32) * live).astype(jnp.bfloat16)
    odd = lax.rem(position()[2], 2)
    for ref, upper in ((near_ref, 1 - odd), (far_ref, odd)):
        slabs = [
            masked_ref[pl.ds(upper * (width - 2), 2)],
            cot_ref[pl.ds(upper * (width - 1), 1)],
        ]
        slabs = jnp.concatenate(slabs, axis=0).astype(f32).reshape(3 * rows, channels)
        ref[...] = rows_of_128(slabs).astype(jnp.bfloat16)


def pack_kernel(masked, packed_ref):
    count, channels = packed_ref.shape[0] * 128 // masked.shape[2], masked.shape[2]
    block = masked[...].reshape(count, channels)
    packed_ref[...] = rows_of_128(block)


def across_kernel(masked, cot, across_ref):
    width, rows, channels = masked.shape
    packed = rows_of_128(masked[...].reshape(width * rows, channels))
    across_ref[: packed.shape[0]] = packed
    ahead = position()[3] == 0
    grown = cot[...].astype(jnp.float32)
    strip = jnp.where(ahead, grown[:, rows - DEPTH :], grown[:, :DEPTH])
    strip = rows_of_128(strip.reshape(width * DEPTH, channels))
    across_ref[packed.shape[0] :] = strip.astype(jnp.bfloat16)


def corner_kernel(near, far, out_ref, edge):
    _, slabs, rows, channels = edge.shape
    _, _, quad, side = position()
    odd = lax.rem(quad, 2)
    f32 = jnp.float32
    edge[odd] = rows_of_192(far[...].astype(f32)).reshape(edge.shape[1:])
    edge[1 - odd] = rows_of_192(near[...].astype(f32)).reshape(edge.shape[1:])
    halo = 2 * DEPTH
    ahead = side == 0
    strip = jnp.where(ahead, edge[:, :2, rows - halo :], edge[:, :2, :halo])
    cots = jnp.where(ahead, edge[:, 2, rows - DEPTH :], edge[:, 2, :DEPTH])
    both = [strip.reshape(4 * halo, channels), cots.reshape(2 * DEPTH, channels)]
    both = rows_of_128(jnp.concatenate(both, axis=0))
    blank = jnp.zeros((out_ref.shape[0] - both.shape[0], 128), f32)
    out_ref[...] = jnp.concatenate([both, blank], axis=0).astype(jnp.bfloat16)


def turn_kernel(weight, out_ref):
    step = 2 * weight.shape[0]
    total = weight.shape[1]
    for start in range(0, total, step):
        stop = min(start + step, total)
        out_ref[start:stop, :] = weight[:, start:stop].T


def bulk_kernel(masked, near, far, across, weight, pre_ref, ext, edge, cols):
    width, rows, channels = masked.shape
    f32 = jnp.float32
    plane, _, quad, side = position()
    use_low = side.astype(f32)
    use_high = (1 - side).astype(f32)
    place = plane * QUAD + quad
    use_left = (place > 0).astype(f32)
    use_right = (place < QUAD * lax.axis_size("depth") - 1).astype(f32)
    halo = 2 * DEPTH
    tall = rows + 2 * halo
    mid = rows + 2 * DEPTH
    span = width + 4
    odd = lax.rem(quad, 2)
    edge[odd] = rows_of_192(far[...].astype(f32)).reshape(edge.shape[1:])
    edge[1 - odd] = rows_of_192(near[...].astype(f32)).reshape(edge.shape[1:])
    ext[0:2, halo : halo + rows, :] = edge[0, 0:2] * use_left
    ext[2 : 2 + width, halo : halo + rows, :] = masked[...].astype(f32)
    ext[2 + width :, halo : halo + rows, :] = edge[1, 0:2] * use_right
    half = width // 2
    count = width * rows * channels // 128
    held = across[:count].astype(f32).reshape(width + half, rows, 128)
    brick = jnp.where(side == 0, held[:, :halo], held[:, rows - halo :])
    rest = jnp.concatenate([brick[width:, :, :64], brick[width:, :, 64:]], axis=0)
    beside = jnp.concatenate([brick[:width], rest], axis=2)
    blank = jnp.zeros((2, halo, channels), f32)
    for use, start in ((use_low, 0), (use_high, halo + rows)):
        at = slice(start, start + halo)
        ext[0:2, at, :] = blank
        ext[2 : 2 + width, at, :] = beside * use
        ext[2 + width :, at, :] = blank
    field = ext[...].reshape(span * tall // DEPTH, DEPTH, channels)
    for c in OFFSETS:
        moved = shift_z(field, c).reshape(span, tall, channels)
        for b in OFFSETS:
            at = ((b + 1) * 3 + c + 1) * channels
            start = DEPTH * (b + 1)
            cols[:, :, at : at + channels] = moved[:, start : start + mid].astype(jnp.bfloat16)
    nine = 9 * channels
    pre = jnp.zeros(((width + 2) * mid, channels), f32)
    for a in range(3):
        pre += jnp.dot(
            cols[a : a + width + 2].reshape((width + 2) * mid, nine),
            weight[a * nine : (a + 1) * nine, :],
            preferred_element_type=f32,
        )
    pre_ref[...] = pre.reshape(pre_ref.shape)


def forward_kernel(bulk, cot, near, far, across, corner, live, weight, pick, *refs):
    act_ref, gp_ref = refs[:2]
    slice_refs = refs[2 : 2 + len(CHIPS)]
    edge, cols, total, slices = refs[2 + len(CHIPS) :]
    width, rows, channels = cot.shape
    f32 = jnp.float32
    plane, me, quad, side = position()
    use_low = side.astype(f32)
    use_high = (1 - side).astype(f32)
    place = plane * QUAD + quad
    use_left = (place > 0).astype(f32)
    use_right = (place < QUAD * lax.axis_size("depth") - 1).astype(f32)
    halo = 2 * DEPTH
    mid = rows + 2 * DEPTH
    count = 4 * halo + 2 * DEPTH
    both = rows_of_192(corner[...].astype(f32)[: count * channels // 128])
    corners = both[: 4 * halo].reshape(2, 2, halo, channels)
    corners = jnp.concatenate([corners[0] * use_left, corners[1] * use_right], axis=0)
    sources = ((0, 1, None, None), (1, None, None, 2), (None, None, 2, 3))
    blank = jnp.zeros((DEPTH, channels), f32)
    six = 6 * channels
    for c in OFFSETS:
        moved = shift_z(corners.reshape(8, DEPTH, channels), c)
        for b, low, high in ((0, (0, 1), (None, 0)), (1, (1, None), (0, 1))):
            at = (b * 3 + c + 1) * channels
            parts = []
            for slab in range(4):
                for below, above in zip(low, high):
                    part = blank if below is None else moved[2 * slab + below] * use_low
                    if above is not None:
                        part = part + moved[2 * slab + above] * use_high
                    parts.append(part)
            for a in range(3):
                rows_a = []
                for source in sources[a]:
                    pair = [blank] * 2 if source is None else parts[2 * source : 2 * source + 2]
                    rows_a += pair
                cols[a, :, at : at + channels] = jnp.concatenate(rows_a, axis=0).astype(
                    jnp.bfloat16
                )
    share = jnp.zeros((4 * halo, channels), f32)
    for a in range(3):
        taps = pl.ds(pl.multiple_of((3 * a + 1 - side) * 3 * channels, 16), six)
        share += jnp.dot(cols[a], weight[taps], preferred_element_type=f32)
    share = share.reshape(4, halo, channels)
    total[...] = bulk[...]
    at = pl.ds(pl.multiple_of((1 - side) * (mid - halo), DEPTH), halo)
    total[0:2, at, :] += share[0:2]
    total[width : width + 2, at, :] += share[2:4]
    pre = total[...].reshape((width + 2) * mid, channels)
    sig = 0.5 * jnp.tanh(0.5 * pre) + 0.5
    act = (pre * sig).reshape(width + 2, mid, channels)[1 : 1 + width, DEPTH : DEPTH + rows]
    act_ref[...] = (act * live[:, :, 0:1]).astype(jnp.bfloat16)
    slope = (sig * (1.0 + pre * (1.0 - sig))).reshape(width + 2, mid, channels)
    ends = both[4 * halo :].reshape(2, 1, DEPTH, channels)
    strip = across[width * rows * channels // 128 :].astype(f32)
    beyond = jnp.concatenate(
        [
            ends[0] * use_left,
            rows_of_192(strip).reshape(width, DEPTH, channels),
            ends[1] * use_right,
        ],
        axis=0,
    )
    odd = lax.rem(quad, 2)
    edge[odd] = rows_of_192(far[...].astype(f32))[2 * rows :]
    edge[1 - odd] = rows_of_192(near[...].astype(f32))[2 * rows :]
    centre = [edge[0:1] * use_left, cot[...].astype(f32), edge[1:2] * use_right]
    centre = jnp.concatenate(centre, axis=0)
    full = jnp.concatenate([beyond * use_low, centre, beyond * use_high], axis=1)
    grad = full * slope
    gp_ref[...] = grad.astype(jnp.bfloat16)
    inner = grad[:, DEPTH : DEPTH + rows].astype(jnp.bfloat16)
    turned = lax.dot_general(
        pick[...],
        inner.reshape((width + 2) * rows, channels),
        (((1,), (1,)), ((), ())),
        preferred_element_type=f32,
    )
    slices[...] = turned.reshape(slices.shape)
    chip = me - lax.rem(quad, 2) * SIDES
    for distance, ref in zip(CHIPS, slice_refs):
        both = [slices[chip ^ distance], slices[(chip ^ distance) + SIDES]]
        ref[...] = jnp.concatenate(both, axis=0).astype(jnp.bfloat16)


def input_kernel(gp, live, turned, act, out_ref, act_ref, cols, weight):
    act_ref[...] = act[...]
    width, rows, channels = out_ref.shape
    f32 = jnp.float32
    tall = rows + 2 * DEPTH
    for tap in range(27):
        weight[tap * channels : (tap + 1) * channels, :] = turned[
            :, tap * channels : (tap + 1) * channels
        ]
    field = gp[...].astype(f32).reshape((width + 2) * tall // DEPTH, DEPTH, channels)
    for c in OFFSETS:
        moved = shift_z(field, -c).reshape(width + 2, tall, channels)
        for b in OFFSETS:
            at = ((b + 1) * 3 + c + 1) * channels
            start = DEPTH * (1 - b)
            cols[:, :, at : at + channels] = moved[:, start : start + rows].astype(jnp.bfloat16)
    nine = 9 * channels
    total = jnp.zeros((width * rows, channels), f32)
    for a in range(3):
        total += jnp.dot(
            cols[2 - a : 2 - a + width].reshape(width * rows, nine),
            weight[a * nine : (a + 1) * nine, :],
            preferred_element_type=f32,
        )
    out_ref[...] = (total.reshape(width, rows, channels) * live[:, :, 0:1]).astype(jnp.bfloat16)


def unpack_pair(bricks, masked):
    per, lane, _ = masked.shape
    half = lane // 2
    side = position()[3]
    for i, brick in enumerate(bricks):
        at_rows = pl.ds(pl.multiple_of((side ^ i) * half, half), half)
        for x in range(per):
            shift = 64 * (x // (per // 2))
            rest = brick[pl.ds((per + x % (per // 2)) * half, half)]
            masked[x, at_rows, :128] = brick[pl.ds(x * half, half)]
            masked[x, at_rows, 128:] = rest[:, shift : shift + 64]


def pair_product(received, masked, cols):
    f32 = jnp.float32
    group, lanes = received[0].shape
    per, lane, channels = masked.shape
    half = lane // 2
    side = position()[3]
    at = lax.broadcasted_iota(jnp.int32, (group, lane), 1)
    y, z = at // DEPTH, at % DEPTH
    tall = lane // DEPTH
    own, other = (ref[...].astype(f32) for ref in received)
    first = jnp.where(side == 0, own, other)
    second = jnp.where(side == 0, other, own)
    for k in range(per + 2):
        one = first[:, k // 2 * lane : (k // 2 + 1) * lane]
        two = second[:, k // 2 * lane : (k // 2 + 1) * lane]
        if k % 2 == 0:
            base = jnp.where(at < half, one, pltpu.roll(two, half, 1))
        else:
            base = jnp.where(at < half, pltpu.roll(one, half, 1), two)
        pieces = []
        for b in OFFSETS:
            for c in OFFSETS:
                step = (DEPTH * b + c) % lane
                moved = base if step == 0 else pltpu.roll(base, step, 1)
                keep = (y - b >= 0) & (y - b < tall) & (z - c >= 0) & (z - c < DEPTH)
                pieces.append(jnp.where(keep, moved, 0.0))
        cols[:, k * lane : (k + 1) * lane] = jnp.concatenate(pieces, axis=0).astype(jnp.bfloat16)
    field = masked[...].reshape(per * lane, channels)
    for a in range(3):
        start = (2 - a) * lane
        got = jnp.dot(
            cols[:, start : start + per * lane], field, preferred_element_type=f32
        ).reshape(9, group, channels)
        yield a, jnp.concatenate([got[tap] for tap in range(9)], axis=1)


def first_pair_kernel(own, other, brick, across, beside, beyond, part_ref, next_ref, cols, masked):
    unpack_pair((beside, beyond), next_ref)
    unpack_pair((brick, across), masked)
    for a, rows in pair_product((own, other), masked, cols):
        width = rows.shape[1]
        part_ref[:, a * width : (a + 1) * width] = rows


def second_pair_kernel(before, other, own, masked, keep_ref, send_ref, part, cols):
    for a, rows in pair_product((own, other), masked, cols):
        width = rows.shape[1]
        at = slice(a * width, (a + 1) * width)
        part[:, at] = before[:, at] + rows
    core = lax.rem(position()[2], 2)
    half = part.shape[0] // 2
    keep_ref[...] = part[pl.ds(pl.multiple_of(core * half, 8), half)]
    send_ref[...] = part[pl.ds(pl.multiple_of((1 - core) * half, 8), half)].astype(jnp.bfloat16)


def fold_kernel(keep, other, own_ref, *refs):
    *send_refs, both, rows = refs
    planes, eight, _ = rows.shape
    count, total = keep.shape
    share = count // planes
    both[:count, :total] = keep[...] + other[...].astype(jnp.float32)
    both[:, total:] = jnp.zeros((both.shape[0], both.shape[1] - total), jnp.float32)
    for to in range(planes):
        rows[to] = fold_rows(both[share * to : share * to + eight, :], total)
    plane = position()[0]
    own_ref[...] = rows[plane]
    for distance, ref in enumerate(send_refs, 1):
        ref[...] = rows[plane ^ distance].astype(jnp.bfloat16)


def sum_kernel(scale, own, one, two, three, out_ref):
    f32 = jnp.float32
    total = own[...] + one[...].astype(f32) + two[...].astype(f32) + three[...].astype(f32)
    out_ref[...] = (total * scale).astype(out_ref.dtype)


def join_kernel(mine, other, out_ref):
    share = out_ref.shape[0] // SIDES
    ahead = position()[3] == 0
    total = out_ref.shape[1]
    here = unfold_rows(mine[...].astype(jnp.float32), total)
    there = unfold_rows(other[...].astype(jnp.float32), total)
    first = jnp.where(ahead, here, there)
    second = jnp.where(ahead, there, here)
    out_ref[0:share] = first[:share]
    out_ref[share:] = second[:share]


def call(body, name, mebibytes, flops, moved, out_shape, scratch=(), in_specs=None):
    spec = pl.BlockSpec(memory_space=pltpu.VMEM)

    def run(*operands):
        return pl.pallas_call(
            body,
            out_shape=out_shape,
            in_specs=in_specs or [spec] * len(operands),
            out_specs=jax.tree.map(lambda _: spec, out_shape),
            scratch_shapes=scratch,
            compiler_params=pltpu.CompilerParams(vmem_limit_bytes=mebibytes << 20),
            cost_estimate=pl.CostEstimate(flops=flops, bytes_accessed=moved, transcendentals=0),
            name=name,
        )(*operands)

    return run


def planes_local(features, weight, voxel_mask, cotangent):
    bf16 = jnp.bfloat16
    f32 = jnp.float32
    array = jax.ShapeDtypeStruct
    width, wide_y, depth, channels = features.shape
    rows = wide_y * depth
    planes = lax.axis_size("depth")
    count = planes * QUAD
    total = 27 * channels
    halo = 2 * DEPTH
    span = (width + 2) * rows
    share = channels // count // SIDES
    group = planes * share

    def swap(piece, axes, distance, size):
        return lax.ppermute(piece, axes, [(i, i ^ distance) for i in range(size)])

    def in_plane(piece, distance):
        return swap(piece, ("quad", "narrow"), distance, MEMBERS)

    brick = array((width, rows, channels), bf16)
    slab = array((3 * rows * channels // 128, 128), bf16)
    slabs = (2, 3, rows, channels)
    pick = call(
        functools.partial(pick_kernel, planes), "pick", 4, 1 << 32, 1 << 16,
        array((MEMBERS * group, channels), bf16),
    )()
    vmem = pl.BlockSpec(memory_space=pltpu.VMEM)
    masked, cot, live, near, far = call(
        prepare_kernel, "prepare", 16, 1 << 20, 1 << 20,
        (brick, brick, array((width, rows, 128), f32), slab, slab),
        (),
        [vmem] * 3 + [pl.BlockSpec(memory_space=pl.ANY)],
    )(
        features.reshape(width, rows, channels),
        cotangent.reshape(width, rows, channels),
        voxel_mask,
        pick,
    )
    near = swap(near, WIDE, 1, count)
    ends = [min(max(((i + 1) ^ 1) - 1, 0), count - 1) for i in range(count)]
    far = lax.ppermute(far, WIDE, list(enumerate(ends)))
    weight_rows = call(
        turn_kernel, "turn", 8, 1 << 20, 4 << 20, array((total, channels), bf16)
    )(weight.T)
    count_128 = width * rows * channels // 128
    strip_128 = width * DEPTH * channels // 128
    across = call(
        across_kernel, "across", 4, 1 << 16, 1 << 19, array((count_128 + strip_128, 128), bf16)
    )(masked, cot)
    across = in_plane(across, CHIPS[1])
    packed = call(
        pack_kernel, "pack", 4, 1 << 16, 1 << 19, array((count_128, 128), bf16)
    )(masked)
    beside = in_plane(packed, CHIPS[2])
    near, far, weight_rows, late, beside = lax.optimization_barrier(
        (near, far, weight_rows, packed, beside)
    )
    corner = call(
        corner_kernel, "corner", 4, 1 << 16, 1 << 18,
        array((128, 128), bf16),
        (pltpu.VMEM(slabs, f32),),
    )(near, far)
    corner = in_plane(corner, 1)
    mid = rows + 2 * DEPTH
    bulk = call(
        bulk_kernel, "bulk", 24, 3 << 29, 1 << 20, array((width + 2, mid, channels), f32),
        (
            pltpu.VMEM((width + 4, rows + 2 * halo, channels), f32),
            pltpu.VMEM(slabs, f32),
            pltpu.VMEM((width + 4, mid, 9 * channels), bf16),
        ),
    )(masked, near, far, across, weight_rows)
    bricks = [packed, across, beside, in_plane(late, CHIPS[3])]

    act, gp, *slices = call(
        forward_kernel, "forward", 24, 3 << 29, 1 << 20,
        (brick, array((width + 2, mid, channels), bf16))
        + (array((2 * group, span), bf16),) * len(CHIPS),
        (
            pltpu.VMEM((2, rows, channels), f32),
            pltpu.VMEM((3, 4 * halo, 6 * channels), bf16),
            pltpu.VMEM((width + 2, mid, channels), f32),
            pltpu.VMEM((MEMBERS, group, span), f32),
        ),
    )(bulk, cot, near, far, across, corner, live, weight_rows, pick)
    for place in (3, 2, 1):
        slices[place] = in_plane(slices[place], CHIPS[place])

    grad_input, act = call(
        input_kernel, "input_gradient", 20, 2 * 512 * 5184 * 256, 4 << 20, (brick, brick),
        (
            pltpu.VMEM((width + 2, rows, 9 * channels), bf16),
            pltpu.VMEM((total, channels), bf16),
        ),
    )(gp, live, weight.T, act)

    lanes = dense(total)[0]
    cols = pltpu.VMEM((9 * 2 * group, (width + 2) * SIDES * rows), bf16)
    pair = (width, SIDES * rows, channels)
    part, pair_masked = call(
        first_pair_kernel, "first_pair", 16, 1 << 30, 2 << 20,
        (array((2 * group, total), f32), array(pair, bf16)),
        (cols, pltpu.VMEM(pair, bf16)),
    )(*slices[:2], *bricks)
    keep, fold = call(
        second_pair_kernel, "second_pair", 16, 1 << 30, 2 << 20,
        (array((group, total), f32), array((group, total), bf16)),
        (pltpu.VMEM((2 * group, total), f32), cols),
    )(part, *slices[3:1:-1], pair_masked)
    own, *sends = call(
        fold_kernel, "fold", 8, 8 * total * 4, 8 * total * 40,
        (array((8, lanes), f32),) + (array((8, lanes), bf16),) * (planes - 1),
        (
            pltpu.VMEM((group + 8, sum(dense(total))), f32),
            pltpu.VMEM((planes, 8, lanes), f32),
        ),
    )(keep, in_plane(fold, 2))
    got = [swap(sends[d - 1], "depth", d, planes) for d in (2, 3, 1)]
    grad_input, *got = lax.optimization_barrier((grad_input, *got))
    voxels = count * SIDES * width * rows
    mine = call(
        functools.partial(sum_kernel, float(1.0 / voxels**0.5)),
        "plane_sum", 4, 8 * total * 4, 8 * total * 14, array((8, lanes), bf16),
    )(own, *got)
    grad_weight = call(
        join_kernel, "join", 4, 8 * total, 8 * total * 14, array((channels // count, total), f32)
    )(mine, in_plane(mine, 1))
    shape = features.shape
    return act.reshape(shape), grad_input.reshape(shape), grad_weight


def padded_2(cells, sides, width):
    for axis, dim in sides:
        count = lax.axis_size(axis)
        ends = count - 1
        head = lax.slice_in_dim(cells, 0, width, axis=dim)
        tail = lax.slice_in_dim(cells, cells.shape[dim] - width, cells.shape[dim], axis=dim)
        cells = jnp.concatenate(
            [
                lax.ppermute(tail, axis, [(i, (i + 1) % count) for i in range(ends)]),
                cells,
                lax.ppermute(head, axis, [((i + 1) % count, i) for i in range(ends)]),
            ],
            axis=dim,
        )
    return cells


def gather_taps(padded, width_x, width_y, depth_z, channels, flip):
    pieces = []
    for shift_x in range(3):
        for shift_y in range(3):
            for shift_z in range(3):
                start_x = 2 - shift_x if flip else shift_x
                start_y = 2 - shift_y if flip else shift_y
                start_z = 2 - shift_z if flip else shift_z
                piece = padded[
                    start_x : start_x + width_x,
                    start_y : start_y + width_y,
                    start_z : start_z + depth_z,
                    :,
                ]
                pieces.append(piece.reshape(-1, channels))
    return jnp.concatenate(pieces, axis=1)


def summed_local(features, weight, voxel_mask, cotangent):
    width_x, width_y, depth_z, channels = features.shape
    masked = features * voxel_mask.astype(jnp.bfloat16)[..., None]
    padded = padded_2(masked, (("wide", 0), ("narrow", 1)), 1)
    padded = jnp.pad(padded, ((0, 0), (0, 0), (1, 1), (0, 0)))
    columns = gather_taps(padded, width_x, width_y, depth_z, channels, False)
    pre = jnp.dot(columns, weight, preferred_element_type=jnp.float32)
    live = voxel_mask.reshape(-1, 1).astype(jnp.float32)
    sig = jax.nn.sigmoid(pre)
    activation = (
        (pre * sig * live).astype(jnp.bfloat16).reshape(width_x, width_y, depth_z, channels)
    )
    slope = sig * (1.0 + pre * (1.0 - sig))
    grad_pre = (cotangent.reshape(-1, channels).astype(jnp.float32) * live * slope).astype(
        jnp.bfloat16
    )
    taps = weight.reshape(27, channels, channels)
    grid = grad_pre.reshape(width_x, width_y, depth_z, channels)
    grad_pad = padded_2(grid, (("wide", 0), ("narrow", 1)), 1)
    grad_pad = jnp.pad(grad_pad, ((0, 0), (0, 0), (1, 1), (0, 0)))
    grad_columns = gather_taps(grad_pad, width_x, width_y, depth_z, channels, True)
    flipped = jnp.transpose(taps, (0, 2, 1)).reshape(27 * channels, channels)
    grad_field = jnp.dot(grad_columns, flipped, preferred_element_type=jnp.float32)
    grad_input = (
        (grad_field * live).astype(jnp.bfloat16).reshape(width_x, width_y, depth_z, channels)
    )
    scale = 1.0 / jnp.sqrt(
        jnp.float32(width_x * width_y * depth_z * lax.axis_size("wide") * lax.axis_size("narrow"))
    )
    whole = lax.dot_general(
        grad_pre, columns, (((0,), (0,)), ((), ())), preferred_element_type=jnp.float32
    )
    piece_flat = lax.psum_scatter(
        whole.reshape(-1), ("wide", "narrow"), scatter_dimension=0, tiled=True
    )
    gathered = lax.all_gather(piece_flat, "narrow", axis=0, tiled=True)
    summed = gathered.reshape(channels // lax.axis_size("wide"), 27 * channels)
    grad_weight = summed * scale
    return (activation, grad_input, grad_weight)


def sharded(body, mesh, wide):
    return jax.shard_map(
        body,
        mesh=mesh,
        in_specs=(
            P(wide, "narrow", None, None),
            P(),
            P(wide, "narrow", None),
            P(wide, "narrow", None, None),
        ),
        out_specs=(
            P(wide, "narrow", None, None),
            P(wide, "narrow", None, None),
            P(wide, None),
        ),
        check_vma=False,
    )


def solution(mesh):
    wide, narrow = mesh.shape["wide"], mesh.shape["narrow"]
    if wide != 4 * QUAD or narrow != SIDES:
        return sharded(summed_local, mesh, "wide")
    planes = Mesh(
        mesh.devices.reshape(wide // QUAD, QUAD, narrow), ("depth", "quad", "narrow")
    )
    return sharded(planes_local, planes, WIDE)
```

```python
import functools

import jax
import jax.numpy as jnp
from jax import lax
from jax.experimental import pallas as pl
from jax.experimental.pallas import tpu as pltpu
from jax.sharding import Mesh
from jax.sharding import PartitionSpec as P

WIDE = ("depth", "quad")
QUAD = 4
SIDES = 2
MEMBERS = QUAD * SIDES
CHIPS = (0, 1, 4, 5)
OFFSETS = (-1, 0, 1)
DEPTH = 8


def position():
    quad, side = lax.axis_index("quad"), lax.axis_index("narrow")
    return lax.axis_index("depth"), quad * SIDES + side, quad, side


def shift_z(field, step):
    if step == 0:
        return field
    depth = field.shape[1]
    moved = pltpu.roll(field, (-step) % depth, 1)
    z = lax.broadcasted_iota(jnp.int32, field.shape, 1) + step
    return jnp.where((z >= 0) & (z < depth), moved, 0.0)


def pick_kernel(planes, out_ref):
    index = lax.broadcasted_iota(jnp.int32, out_ref.shape, 0)
    column = lax.broadcasted_iota(jnp.int32, out_ref.shape, 1)
    per = out_ref.shape[1] // (planes * QUAD)
    share = per // SIDES
    group = planes * share
    quad, side = index // (SIDES * group), index // group % SIDES
    plane, row = index // share % planes, index % share
    channel = per * (QUAD * plane + quad) + share * side + row
    out_ref[...] = jnp.where(channel == column, 1.0, 0.0).astype(jnp.bfloat16)


def dense(total):
    tiles = -(-total // 128)
    moved = tiles // 4
    return (tiles - moved) * 128, moved * 128


def fold_rows(block, total):
    kept, moved = dense(total)
    tail = block[:, kept : kept + moved]
    row = lax.broadcasted_iota(jnp.int32, tail.shape, 0)
    pieces = []
    for k in range(3):
        spare = jnp.where(row == 6, pltpu.roll(tail, 6 - k, 0), pltpu.roll(tail, 4 - k, 0))
        pieces.append(jnp.where(row < 6, block[:, k * moved : (k + 1) * moved], spare))
    return jnp.concatenate(pieces + [block[:, 3 * moved : kept]], axis=1)


def unfold_rows(block, total):
    kept, moved = dense(total)
    row = lax.broadcasted_iota(jnp.int32, (8, moved), 0)
    tail = jnp.zeros((8, moved), block.dtype)
    for k in range(3):
        piece = block[:, k * moved : (k + 1) * moved]
        tail = jnp.where(row == k, pltpu.roll(piece, 2 + k, 0), tail)
        tail = jnp.where(row == 3 + k, pltpu.roll(piece, 4 + k, 0), tail)
    return jnp.concatenate([block, tail], axis=1)[:, :total]


def rows_of_128(block):
    half = block.shape[0] // 2
    rest = jnp.concatenate([block[:half, 128:], block[half:, 128:]], axis=1)
    return jnp.concatenate([block[:, :128], rest], axis=0)


def rows_of_192(block):
    count = block.shape[0] * 2 // 3
    rest = jnp.concatenate([block[count:, :64], block[count:, 64:]], axis=0)
    return jnp.concatenate([block[:count], rest], axis=1)


def prepare_kernel(features, cot, mask, first, masked_ref, cot_ref, live_ref, near_ref, far_ref):
    width, rows, channels = features.shape
    f32 = jnp.float32
    flat = mask[...].astype(f32).reshape(width * rows // DEPTH, DEPTH)
    live = jnp.broadcast_to(flat[:, :, None], flat.shape + (channels,)).reshape(features.shape)
    live_ref[...] = live[:, :, :128]
    masked_ref[...] = (features[...].astype(f32) * live).astype(jnp.bfloat16)
    cot_ref[...] = (cot[...].astype(f32) * live).astype(jnp.bfloat16)
    odd = lax.rem(position()[2], 2)
    for ref, upper in ((near_ref, 1 - odd), (far_ref, odd)):
        slabs = [
            masked_ref[pl.ds(upper * (width - 2), 2)],
            cot_ref[pl.ds(upper * (width - 1), 1)],
        ]
        slabs = jnp.concatenate(slabs, axis=0).astype(f32).reshape(3 * rows, channels)
        ref[...] = rows_of_128(slabs).astype(jnp.bfloat16)


def pack_kernel(masked, after, packed_ref):
    count, channels = packed_ref.shape[0] * 128 // masked.shape[2], masked.shape[2]
    block = masked[...].reshape(count, channels)
    packed_ref[...] = rows_of_128(block)


def across_kernel(masked, cot, across_ref):
    width, rows, channels = masked.shape
    packed = rows_of_128(masked[...].reshape(width * rows, channels))
    across_ref[: packed.shape[0]] = packed
    ahead = position()[3] == 0
    grown = cot[...].astype(jnp.float32)
    strip = jnp.where(ahead, grown[:, rows - DEPTH :], grown[:, :DEPTH])
    strip = rows_of_128(strip.reshape(width * DEPTH, channels))
    across_ref[packed.shape[0] :] = strip.astype(jnp.bfloat16)


def corner_kernel(near, far, out_ref, edge):
    _, slabs, rows, channels = edge.shape
    _, _, quad, side = position()
    odd = lax.rem(quad, 2)
    f32 = jnp.float32
    edge[odd] = rows_of_192(far[...].astype(f32)).reshape(edge.shape[1:])
    edge[1 - odd] = rows_of_192(near[...].astype(f32)).reshape(edge.shape[1:])
    halo = 2 * DEPTH
    ahead = side == 0
    strip = jnp.where(ahead, edge[:, :2, rows - halo :], edge[:, :2, :halo])
    cots = jnp.where(ahead, edge[:, 2, rows - DEPTH :], edge[:, 2, :DEPTH])
    both = [strip.reshape(4 * halo, channels), cots.reshape(2 * DEPTH, channels)]
    both = rows_of_128(jnp.concatenate(both, axis=0))
    blank = jnp.zeros((out_ref.shape[0] - both.shape[0], 128), f32)
    out_ref[...] = jnp.concatenate([both, blank], axis=0).astype(jnp.bfloat16)


def turn_kernel(weight, out_ref):
    step = 2 * weight.shape[0]
    total = weight.shape[1]
    for start in range(0, total, step):
        stop = min(start + step, total)
        out_ref[start:stop, :] = weight[:, start:stop].T


def bulk_kernel(masked, near, far, across, weight, pre_ref, ext, edge, cols):
    width, rows, channels = masked.shape
    f32 = jnp.float32
    plane, _, quad, side = position()
    use_low = side.astype(f32)
    use_high = (1 - side).astype(f32)
    place = plane * QUAD + quad
    use_left = (place > 0).astype(f32)
    use_right = (place < QUAD * lax.axis_size("depth") - 1).astype(f32)
    halo = 2 * DEPTH
    tall = rows + 2 * halo
    mid = rows + 2 * DEPTH
    span = width + 4
    odd = lax.rem(quad, 2)
    edge[odd] = rows_of_192(far[...].astype(f32)).reshape(edge.shape[1:])
    edge[1 - odd] = rows_of_192(near[...].astype(f32)).reshape(edge.shape[1:])
    ext[0:2, halo : halo + rows, :] = edge[0, 0:2] * use_left
    ext[2 : 2 + width, halo : halo + rows, :] = masked[...].astype(f32)
    ext[2 + width :, halo : halo + rows, :] = edge[1, 0:2] * use_right
    half = width // 2
    count = width * rows * channels // 128
    held = across[:count].astype(f32).reshape(width + half, rows, 128)
    brick = jnp.where(side == 0, held[:, :halo], held[:, rows - halo :])
    rest = jnp.concatenate([brick[width:, :, :64], brick[width:, :, 64:]], axis=0)
    beside = jnp.concatenate([brick[:width], rest], axis=2)
    blank = jnp.zeros((2, halo, channels), f32)
    for use, start in ((use_low, 0), (use_high, halo + rows)):
        at = slice(start, start + halo)
        ext[0:2, at, :] = blank
        ext[2 : 2 + width, at, :] = beside * use
        ext[2 + width :, at, :] = blank
    field = ext[...].reshape(span * tall // DEPTH, DEPTH, channels)
    for c in OFFSETS:
        moved = shift_z(field, c).reshape(span, tall, channels)
        for b in OFFSETS:
            at = ((b + 1) * 3 + c + 1) * channels
            start = DEPTH * (b + 1)
            cols[:, :, at : at + channels] = moved[:, start : start + mid].astype(jnp.bfloat16)
    nine = 9 * channels
    pre = jnp.zeros(((width + 2) * mid, channels), f32)
    for a in range(3):
        pre += jnp.dot(
            cols[a : a + width + 2].reshape((width + 2) * mid, nine),
            weight[a * nine : (a + 1) * nine, :],
            preferred_element_type=f32,
        )
    pre_ref[...] = pre.reshape(pre_ref.shape)


def forward_kernel(bulk, cot, near, far, across, corner, live, weight, pick, *refs):
    act_ref, gp_ref = refs[:2]
    slice_refs = refs[2 : 2 + len(CHIPS)]
    edge, cols, total, slices = refs[2 + len(CHIPS) :]
    width, rows, channels = cot.shape
    f32 = jnp.float32
    plane, me, quad, side = position()
    use_low = side.astype(f32)
    use_high = (1 - side).astype(f32)
    place = plane * QUAD + quad
    use_left = (place > 0).astype(f32)
    use_right = (place < QUAD * lax.axis_size("depth") - 1).astype(f32)
    halo = 2 * DEPTH
    mid = rows + 2 * DEPTH
    count = 4 * halo + 2 * DEPTH
    both = rows_of_192(corner[...].astype(f32)[: count * channels // 128])
    corners = both[: 4 * halo].reshape(2, 2, halo, channels)
    corners = jnp.concatenate([corners[0] * use_left, corners[1] * use_right], axis=0)
    sources = ((0, 1, None, None), (1, None, None, 2), (None, None, 2, 3))
    blank = jnp.zeros((DEPTH, channels), f32)
    six = 6 * channels
    for c in OFFSETS:
        moved = shift_z(corners.reshape(8, DEPTH, channels), c)
        for b, low, high in ((0, (0, 1), (None, 0)), (1, (1, None), (0, 1))):
            at = (b * 3 + c + 1) * channels
            parts = []
            for slab in range(4):
                for below, above in zip(low, high):
                    part = blank if below is None else moved[2 * slab + below] * use_low
                    if above is not None:
                        part = part + moved[2 * slab + above] * use_high
                    parts.append(part)
            for a in range(3):
                rows_a = []
                for source in sources[a]:
                    pair = [blank] * 2 if source is None else parts[2 * source : 2 * source + 2]
                    rows_a += pair
                cols[a, :, at : at + channels] = jnp.concatenate(rows_a, axis=0).astype(
                    jnp.bfloat16
                )
    share = jnp.zeros((4 * halo, channels), f32)
    for a in range(3):
        taps = pl.ds(pl.multiple_of((3 * a + 1 - side) * 3 * channels, 16), six)
        share += jnp.dot(cols[a], weight[taps], preferred_element_type=f32)
    share = share.reshape(4, halo, channels)
    total[...] = bulk[...]
    at = pl.ds(pl.multiple_of((1 - side) * (mid - halo), DEPTH), halo)
    total[0:2, at, :] += share[0:2]
    total[width : width + 2, at, :] += share[2:4]
    pre = total[...].reshape((width + 2) * mid, channels)
    sig = 0.5 * jnp.tanh(0.5 * pre) + 0.5
    act = (pre * sig).reshape(width + 2, mid, channels)[1 : 1 + width, DEPTH : DEPTH + rows]
    act_ref[...] = (act * live[:, :, 0:1]).astype(jnp.bfloat16)
    slope = (sig * (1.0 + pre * (1.0 - sig))).reshape(width + 2, mid, channels)
    ends = both[4 * halo :].reshape(2, 1, DEPTH, channels)
    strip = across[width * rows * channels // 128 :].astype(f32)
    beyond = jnp.concatenate(
        [
            ends[0] * use_left,
            rows_of_192(strip).reshape(width, DEPTH, channels),
            ends[1] * use_right,
        ],
        axis=0,
    )
    odd = lax.rem(quad, 2)
    edge[odd] = rows_of_192(far[...].astype(f32))[2 * rows :]
    edge[1 - odd] = rows_of_192(near[...].astype(f32))[2 * rows :]
    centre = [edge[0:1] * use_left, cot[...].astype(f32), edge[1:2] * use_right]
    centre = jnp.concatenate(centre, axis=0)
    full = jnp.concatenate([beyond * use_low, centre, beyond * use_high], axis=1)
    grad = full * slope
    gp_ref[...] = grad.astype(jnp.bfloat16)
    inner = grad[:, DEPTH : DEPTH + rows].astype(jnp.bfloat16)
    turned = lax.dot_general(
        pick[...],
        inner.reshape((width + 2) * rows, channels),
        (((1,), (1,)), ((), ())),
        preferred_element_type=f32,
    )
    slices[...] = turned.reshape(slices.shape)
    chip = me - lax.rem(quad, 2) * SIDES
    for distance, ref in zip(CHIPS, slice_refs):
        both = [slices[chip ^ distance], slices[(chip ^ distance) + SIDES]]
        ref[...] = jnp.concatenate(both, axis=0).astype(jnp.bfloat16)


def input_kernel(gp, live, turned, act, out_ref, act_ref, cols, weight):
    act_ref[...] = act[...]
    width, rows, channels = out_ref.shape
    f32 = jnp.float32
    tall = rows + 2 * DEPTH
    for tap in range(27):
        weight[tap * channels : (tap + 1) * channels, :] = turned[
            :, tap * channels : (tap + 1) * channels
        ]
    field = gp[...].astype(f32).reshape((width + 2) * tall // DEPTH, DEPTH, channels)
    for c in OFFSETS:
        moved = shift_z(field, -c).reshape(width + 2, tall, channels)
        for b in OFFSETS:
            at = ((b + 1) * 3 + c + 1) * channels
            start = DEPTH * (1 - b)
            cols[:, :, at : at + channels] = moved[:, start : start + rows].astype(jnp.bfloat16)
    nine = 9 * channels
    total = jnp.zeros((width * rows, channels), f32)
    for a in range(3):
        total += jnp.dot(
            cols[2 - a : 2 - a + width].reshape(width * rows, nine),
            weight[a * nine : (a + 1) * nine, :],
            preferred_element_type=f32,
        )
    out_ref[...] = (total.reshape(width, rows, channels) * live[:, :, 0:1]).astype(jnp.bfloat16)


def unpack_pair(bricks, masked):
    per, lane, _ = masked.shape
    half = lane // 2
    side = position()[3]
    for i, brick in enumerate(bricks):
        at_rows = pl.ds(pl.multiple_of((side ^ i) * half, half), half)
        for x in range(per):
            shift = 64 * (x // (per // 2))
            rest = brick[pl.ds((per + x % (per // 2)) * half, half)]
            masked[x, at_rows, :128] = brick[pl.ds(x * half, half)]
            masked[x, at_rows, 128:] = rest[:, shift : shift + 64]


def pair_product(received, masked, cols):
    f32 = jnp.float32
    group = received[0].shape[0]
    per, lane, channels = masked.shape
    half = lane // 2
    side = position()[3]
    at = lax.broadcasted_iota(jnp.int32, (group, lane), 1)
    y, z = at // DEPTH, at % DEPTH
    tall = lane // DEPTH
    own, other = received
    first = jnp.where(side == 0, own, other)
    second = jnp.where(side == 0, other, own)
    for k in range(per + 2):
        one = first[:, k // 2 * lane : (k // 2 + 1) * lane]
        two = second[:, k // 2 * lane : (k // 2 + 1) * lane]
        if k % 2 == 0:
            base = jnp.where(at < half, one, pltpu.roll(two, half, 1))
        else:
            base = jnp.where(at < half, pltpu.roll(one, half, 1), two)
        pieces = []
        for b in OFFSETS:
            for c in OFFSETS:
                step = (DEPTH * b + c) % lane
                moved = base if step == 0 else pltpu.roll(base, step, 1)
                keep = (y - b >= 0) & (y - b < tall) & (z - c >= 0) & (z - c < DEPTH)
                pieces.append(jnp.where(keep, moved, 0.0))
        cols[:, k * lane : (k + 1) * lane] = jnp.concatenate(pieces, axis=0).astype(jnp.bfloat16)
    field = masked[...].reshape(per * lane, channels)
    for a in range(3):
        start = (2 - a) * lane
        got = jnp.dot(
            cols[:, start : start + per * lane], field, preferred_element_type=f32
        ).reshape(9, group, channels)
        yield a, jnp.concatenate([got[tap] for tap in range(9)], axis=1)


def first_pair_kernel(own, other, brick, across, beside, beyond, part_ref, next_ref, cols, masked):
    unpack_pair((beside, beyond), next_ref)
    unpack_pair((brick, across), masked)
    received = own[...].astype(jnp.float32), other[...].astype(jnp.float32)
    for a, rows in pair_product(received, masked, cols):
        width = rows.shape[1]
        part_ref[:, a * width : (a + 1) * width] = rows


def second_pair_kernel(own_rows, before, other, own, masked, out_ref, cols):
    core = lax.rem(position()[2], 2)
    half = before.shape[0] // 2
    upper = core if own_rows else 1 - core
    received = [ref[...].astype(jnp.float32) for ref in (own, other)]
    received = [jnp.where(upper == 1, block[half:], block[:half]) for block in received]
    held = pl.ds(pl.multiple_of(upper * half, 8), half)
    for a, rows in pair_product(received, masked, cols):
        width = rows.shape[1]
        at = slice(a * width, (a + 1) * width)
        out_ref[:, at] = (before[held, at] + rows).astype(out_ref.dtype)


def fold_kernel(keep, other, own_ref, *refs):
    *send_refs, both, rows = refs
    planes, eight, _ = rows.shape
    count, total = keep.shape
    share = count // planes
    both[:count, :total] = keep[...] + other[...].astype(jnp.float32)
    both[:, total:] = jnp.zeros((both.shape[0], both.shape[1] - total), jnp.float32)
    for to in range(planes):
        rows[to] = fold_rows(both[share * to : share * to + eight, :], total)
    plane = position()[0]
    own_ref[...] = rows[plane]
    for distance, ref in enumerate(send_refs, 1):
        ref[...] = rows[plane ^ distance].astype(jnp.bfloat16)


def sum_kernel(scale, own, one, two, three, out_ref):
    f32 = jnp.float32
    total = own[...] + one[...].astype(f32) + two[...].astype(f32) + three[...].astype(f32)
    out_ref[...] = (total * scale).astype(out_ref.dtype)


def join_kernel(mine, other, out_ref):
    share = out_ref.shape[0] // SIDES
    ahead = position()[3] == 0
    total = out_ref.shape[1]
    here = unfold_rows(mine[...].astype(jnp.float32), total)
    there = unfold_rows(other[...].astype(jnp.float32), total)
    first = jnp.where(ahead, here, there)
    second = jnp.where(ahead, there, here)
    out_ref[0:share] = first[:share]
    out_ref[share:] = second[:share]


def call(body, name, mebibytes, flops, moved, out_shape, scratch=(), in_specs=None):
    spec = pl.BlockSpec(memory_space=pltpu.VMEM)

    def run(*operands):
        return pl.pallas_call(
            body,
            out_shape=out_shape,
            in_specs=in_specs or [spec] * len(operands),
            out_specs=jax.tree.map(lambda _: spec, out_shape),
            scratch_shapes=scratch,
            compiler_params=pltpu.CompilerParams(vmem_limit_bytes=mebibytes << 20),
            cost_estimate=pl.CostEstimate(flops=flops, bytes_accessed=moved, transcendentals=0),
            name=name,
        )(*operands)

    return run


def planes_local(features, weight, voxel_mask, cotangent):
    bf16 = jnp.bfloat16
    f32 = jnp.float32
    array = jax.ShapeDtypeStruct
    width, wide_y, depth, channels = features.shape
    rows = wide_y * depth
    planes = lax.axis_size("depth")
    count = planes * QUAD
    total = 27 * channels
    halo = 2 * DEPTH
    span = (width + 2) * rows
    share = channels // count // SIDES
    group = planes * share

    def swap(piece, axes, distance, size):
        return lax.ppermute(piece, axes, [(i, i ^ distance) for i in range(size)])

    def in_plane(piece, distance):
        return swap(piece, ("quad", "narrow"), distance, MEMBERS)

    brick = array((width, rows, channels), bf16)
    slab = array((3 * rows * channels // 128, 128), bf16)
    slabs = (2, 3, rows, channels)
    pick = call(
        functools.partial(pick_kernel, planes), "pick", 4, 1 << 32, 1 << 16,
        array((MEMBERS * group, channels), bf16),
    )()
    vmem = pl.BlockSpec(memory_space=pltpu.VMEM)
    masked, cot, live, near, far = call(
        prepare_kernel, "prepare", 16, 1 << 20, 1 << 20,
        (brick, brick, array((width, rows, 128), f32), slab, slab),
        (),
        [vmem] * 3 + [pl.BlockSpec(memory_space=pl.ANY)],
    )(
        features.reshape(width, rows, channels),
        cotangent.reshape(width, rows, channels),
        voxel_mask,
        pick,
    )
    near = swap(near, WIDE, 1, count)
    ends = [min(max(((i + 1) ^ 1) - 1, 0), count - 1) for i in range(count)]
    far = lax.ppermute(far, WIDE, list(enumerate(ends)))
    weight_rows = call(
        turn_kernel, "turn", 8, 1 << 20, 4 << 20, array((total, channels), bf16)
    )(weight.T)
    count_128 = width * rows * channels // 128
    strip_128 = width * DEPTH * channels // 128
    across = call(
        across_kernel, "across", 4, 1 << 16, 1 << 19, array((count_128 + strip_128, 128), bf16)
    )(masked, cot)
    across = in_plane(across, CHIPS[1])
    packed = call(
        pack_kernel, "pack", 4, 1 << 16, 1 << 19, array((count_128, 128), bf16), (),
        [vmem, pl.BlockSpec(memory_space=pl.ANY)],
    )(masked, weight_rows)
    near, far, weight_rows, late = lax.optimization_barrier((near, far, weight_rows, packed))
    corner = call(
        corner_kernel, "corner", 4, 1 << 16, 1 << 18,
        array((128, 128), bf16),
        (pltpu.VMEM(slabs, f32),),
    )(near, far)
    corner = in_plane(corner, 1)
    mid = rows + 2 * DEPTH
    bulk = call(
        bulk_kernel, "bulk", 24, 3 << 29, 1 << 20, array((width + 2, mid, channels), f32),
        (
            pltpu.VMEM((width + 4, rows + 2 * halo, channels), f32),
            pltpu.VMEM(slabs, f32),
            pltpu.VMEM((width + 4, mid, 9 * channels), bf16),
        ),
    )(masked, near, far, across, weight_rows)
    bricks = [packed, across, in_plane(packed, CHIPS[2]), in_plane(late, CHIPS[3])]

    act, gp, *slices = call(
        forward_kernel, "forward", 24, 3 << 29, 1 << 20,
        (brick, array((width + 2, mid, channels), bf16))
        + (array((2 * group, span), bf16),) * len(CHIPS),
        (
            pltpu.VMEM((2, rows, channels), f32),
            pltpu.VMEM((3, 4 * halo, 6 * channels), bf16),
            pltpu.VMEM((width + 2, mid, channels), f32),
            pltpu.VMEM((MEMBERS, group, span), f32),
        ),
    )(bulk, cot, near, far, across, corner, live, weight_rows, pick)
    bricks[2], *slices = lax.optimization_barrier((bricks[2], *slices))
    for place in (3, 2, 1):
        slices[place] = in_plane(slices[place], CHIPS[place])

    grad_input, act = call(
        input_kernel, "input_gradient", 20, 2 * 512 * 5184 * 256, 4 << 20, (brick, brick),
        (
            pltpu.VMEM((width + 2, rows, 9 * channels), bf16),
            pltpu.VMEM((total, channels), bf16),
        ),
    )(gp, live, weight.T, act)

    lanes = dense(total)[0]
    cols = pltpu.VMEM((9 * 2 * group, (width + 2) * SIDES * rows), bf16)
    pair = (width, SIDES * rows, channels)
    part, pair_masked = call(
        first_pair_kernel, "first_pair", 16, 1 << 30, 2 << 20,
        (array((2 * group, total), f32), array(pair, bf16)),
        (cols, pltpu.VMEM(pair, bf16)),
    )(*slices[:2], *bricks)
    half_cols = pltpu.VMEM((9 * group, (width + 2) * SIDES * rows), bf16)
    second = part, *slices[3:1:-1], pair_masked
    fold = call(
        functools.partial(second_pair_kernel, False), "second_pair_other", 16, 1 << 29, 1 << 20,
        array((group, total), bf16), (half_cols,),
    )(*second)
    keep = call(
        functools.partial(second_pair_kernel, True), "second_pair_own", 16, 1 << 29, 1 << 20,
        array((group, total), f32), (half_cols,),
    )(*second)
    own, *sends = call(
        fold_kernel, "fold", 8, 8 * total * 4, 8 * total * 40,
        (array((8, lanes), f32),) + (array((8, lanes), bf16),) * (planes - 1),
        (
            pltpu.VMEM((group + 8, sum(dense(total))), f32),
            pltpu.VMEM((planes, 8, lanes), f32),
        ),
    )(keep, in_plane(fold, 2))
    got = [swap(sends[d - 1], "depth", d, planes) for d in (2, 3, 1)]
    grad_input, *got = lax.optimization_barrier((grad_input, *got))
    voxels = count * SIDES * width * rows
    mine = call(
        functools.partial(sum_kernel, float(1.0 / voxels**0.5)),
        "plane_sum", 4, 8 * total * 4, 8 * total * 14, array((8, lanes), bf16),
    )(own, *got)
    grad_weight = call(
        join_kernel, "join", 4, 8 * total, 8 * total * 14, array((channels // count, total), f32)
    )(mine, in_plane(mine, 1))
    shape = features.shape
    return act.reshape(shape), grad_input.reshape(shape), grad_weight


def padded_2(cells, sides, width):
    for axis, dim in sides:
        count = lax.axis_size(axis)
        ends = count - 1
        head = lax.slice_in_dim(cells, 0, width, axis=dim)
        tail = lax.slice_in_dim(cells, cells.shape[dim] - width, cells.shape[dim], axis=dim)
        cells = jnp.concatenate(
            [
                lax.ppermute(tail, axis, [(i, (i + 1) % count) for i in range(ends)]),
                cells,
                lax.ppermute(head, axis, [((i + 1) % count, i) for i in range(ends)]),
            ],
            axis=dim,
        )
    return cells


def gather_taps(padded, width_x, width_y, depth_z, channels, flip):
    pieces = []
    for shift_x in range(3):
        for shift_y in range(3):
            for shift_z in range(3):
                start_x = 2 - shift_x if flip else shift_x
                start_y = 2 - shift_y if flip else shift_y
                start_z = 2 - shift_z if flip else shift_z
                piece = padded[
                    start_x : start_x + width_x,
                    start_y : start_y + width_y,
                    start_z : start_z + depth_z,
                    :,
                ]
                pieces.append(piece.reshape(-1, channels))
    return jnp.concatenate(pieces, axis=1)


def summed_local(features, weight, voxel_mask, cotangent):
    width_x, width_y, depth_z, channels = features.shape
    masked = features * voxel_mask.astype(jnp.bfloat16)[..., None]
    padded = padded_2(masked, (("wide", 0), ("narrow", 1)), 1)
    padded = jnp.pad(padded, ((0, 0), (0, 0), (1, 1), (0, 0)))
    columns = gather_taps(padded, width_x, width_y, depth_z, channels, False)
    pre = jnp.dot(columns, weight, preferred_element_type=jnp.float32)
    live = voxel_mask.reshape(-1, 1).astype(jnp.float32)
    sig = jax.nn.sigmoid(pre)
    activation = (
        (pre * sig * live).astype(jnp.bfloat16).reshape(width_x, width_y, depth_z, channels)
    )
    slope = sig * (1.0 + pre * (1.0 - sig))
    grad_pre = (cotangent.reshape(-1, channels).astype(jnp.float32) * live * slope).astype(
        jnp.bfloat16
    )
    taps = weight.reshape(27, channels, channels)
    grid = grad_pre.reshape(width_x, width_y, depth_z, channels)
    grad_pad = padded_2(grid, (("wide", 0), ("narrow", 1)), 1)
    grad_pad = jnp.pad(grad_pad, ((0, 0), (0, 0), (1, 1), (0, 0)))
    grad_columns = gather_taps(grad_pad, width_x, width_y, depth_z, channels, True)
    flipped = jnp.transpose(taps, (0, 2, 1)).reshape(27 * channels, channels)
    grad_field = jnp.dot(grad_columns, flipped, preferred_element_type=jnp.float32)
    grad_input = (
        (grad_field * live).astype(jnp.bfloat16).reshape(width_x, width_y, depth_z, channels)
    )
    scale = 1.0 / jnp.sqrt(
        jnp.float32(width_x * width_y * depth_z * lax.axis_size("wide") * lax.axis_size("narrow"))
    )
    whole = lax.dot_general(
        grad_pre, columns, (((0,), (0,)), ((), ())), preferred_element_type=jnp.float32
    )
    piece_flat = lax.psum_scatter(
        whole.reshape(-1), ("wide", "narrow"), scatter_dimension=0, tiled=True
    )
    gathered = lax.all_gather(piece_flat, "narrow", axis=0, tiled=True)
    summed = gathered.reshape(channels // lax.axis_size("wide"), 27 * channels)
    grad_weight = summed * scale
    return (activation, grad_input, grad_weight)


def sharded(body, mesh, wide):
    return jax.shard_map(
        body,
        mesh=mesh,
        in_specs=(
            P(wide, "narrow", None, None),
            P(),
            P(wide, "narrow", None),
            P(wide, "narrow", None, None),
        ),
        out_specs=(
            P(wide, "narrow", None, None),
            P(wide, "narrow", None, None),
            P(wide, None),
        ),
        check_vma=False,
    )


def solution(mesh):
    wide, narrow = mesh.shape["wide"], mesh.shape["narrow"]
    if wide != 4 * QUAD or narrow != SIDES:
        return sharded(summed_local, mesh, "wide")
    planes = Mesh(
        mesh.devices.reshape(wide // QUAD, QUAD, narrow), ("depth", "quad", "narrow")
    )
    return sharded(planes_local, planes, WIDE)
```

```python
import functools

import jax
import jax.numpy as jnp
from jax import lax
from jax.experimental import pallas as pl
from jax.experimental.pallas import tpu as pltpu
from jax.sharding import Mesh
from jax.sharding import PartitionSpec as P

WIDE = ("depth", "quad")
QUAD = 4
SIDES = 2
MEMBERS = QUAD * SIDES
CHIPS = (0, 1, 4, 5)
OFFSETS = (-1, 0, 1)
DEPTH = 8


def position():
    quad, side = lax.axis_index("quad"), lax.axis_index("narrow")
    return lax.axis_index("depth"), quad * SIDES + side, quad, side


def shift_z(field, step):
    if step == 0:
        return field
    depth = field.shape[1]
    moved = pltpu.roll(field, (-step) % depth, 1)
    z = lax.broadcasted_iota(jnp.int32, field.shape, 1) + step
    return jnp.where((z >= 0) & (z < depth), moved, 0.0)


def pick_kernel(planes, out_ref):
    index = lax.broadcasted_iota(jnp.int32, out_ref.shape, 0)
    column = lax.broadcasted_iota(jnp.int32, out_ref.shape, 1)
    per = out_ref.shape[1] // (planes * QUAD)
    share = per // SIDES
    group = planes * share
    quad, side = index // (SIDES * group), index // group % SIDES
    plane, row = index // share % planes, index % share
    channel = per * (QUAD * plane + quad) + share * side + row
    out_ref[...] = jnp.where(channel == column, 1.0, 0.0).astype(jnp.bfloat16)


def dense(total):
    tiles = -(-total // 128)
    moved = tiles // 4
    return (tiles - moved) * 128, moved * 128


def fold_rows(block, total):
    kept, moved = dense(total)
    tail = block[:, kept : kept + moved]
    row = lax.broadcasted_iota(jnp.int32, tail.shape, 0)
    pieces = []
    for k in range(3):
        spare = jnp.where(row == 6, pltpu.roll(tail, 6 - k, 0), pltpu.roll(tail, 4 - k, 0))
        pieces.append(jnp.where(row < 6, block[:, k * moved : (k + 1) * moved], spare))
    return jnp.concatenate(pieces + [block[:, 3 * moved : kept]], axis=1)


def unfold_rows(block, total):
    kept, moved = dense(total)
    row = lax.broadcasted_iota(jnp.int32, (8, moved), 0)
    tail = jnp.zeros((8, moved), block.dtype)
    for k in range(3):
        piece = block[:, k * moved : (k + 1) * moved]
        tail = jnp.where(row == k, pltpu.roll(piece, 2 + k, 0), tail)
        tail = jnp.where(row == 3 + k, pltpu.roll(piece, 4 + k, 0), tail)
    return jnp.concatenate([block, tail], axis=1)[:, :total]


def rows_of_128(block):
    half = block.shape[0] // 2
    rest = jnp.concatenate([block[:half, 128:], block[half:, 128:]], axis=1)
    return jnp.concatenate([block[:, :128], rest], axis=0)


def rows_of_192(block):
    count = block.shape[0] * 2 // 3
    rest = jnp.concatenate([block[count:, :64], block[count:, 64:]], axis=0)
    return jnp.concatenate([block[:count], rest], axis=1)


def prepare_kernel(features, cot, mask, first, masked_ref, cot_ref, live_ref, near_ref, far_ref):
    width, rows, channels = features.shape
    f32 = jnp.float32
    flat = mask[...].astype(f32).reshape(width * rows // DEPTH, DEPTH)
    live = jnp.broadcast_to(flat[:, :, None], flat.shape + (channels,)).reshape(features.shape)
    live_ref[...] = live[:, :, :128]
    masked_ref[...] = (features[...].astype(f32) * live).astype(jnp.bfloat16)
    cot_ref[...] = (cot[...].astype(f32) * live).astype(jnp.bfloat16)
    odd = lax.rem(position()[2], 2)
    for ref, upper in ((near_ref, 1 - odd), (far_ref, odd)):
        slabs = [
            masked_ref[pl.ds(upper * (width - 2), 2)],
            cot_ref[pl.ds(upper * (width - 1), 1)],
        ]
        slabs = jnp.concatenate(slabs, axis=0).astype(f32).reshape(3 * rows, channels)
        ref[...] = rows_of_128(slabs).astype(jnp.bfloat16)


def pack_kernel(masked, after, packed_ref):
    count, channels = packed_ref.shape[0] * 128 // masked.shape[2], masked.shape[2]
    block = masked[...].reshape(count, channels)
    packed_ref[...] = rows_of_128(block)


def across_kernel(masked, cot, across_ref):
    width, rows, channels = masked.shape
    packed = rows_of_128(masked[...].reshape(width * rows, channels))
    across_ref[: packed.shape[0]] = packed
    ahead = position()[3] == 0
    grown = cot[...].astype(jnp.float32)
    strip = jnp.where(ahead, grown[:, rows - DEPTH :], grown[:, :DEPTH])
    strip = rows_of_128(strip.reshape(width * DEPTH, channels))
    across_ref[packed.shape[0] :] = strip.astype(jnp.bfloat16)


def corner_kernel(near, far, out_ref, edge):
    _, slabs, rows, channels = edge.shape
    _, _, quad, side = position()
    odd = lax.rem(quad, 2)
    f32 = jnp.float32
    edge[odd] = rows_of_192(far[...].astype(f32)).reshape(edge.shape[1:])
    edge[1 - odd] = rows_of_192(near[...].astype(f32)).reshape(edge.shape[1:])
    halo = 2 * DEPTH
    ahead = side == 0
    strip = jnp.where(ahead, edge[:, :2, rows - halo :], edge[:, :2, :halo])
    cots = jnp.where(ahead, edge[:, 2, rows - DEPTH :], edge[:, 2, :DEPTH])
    both = [strip.reshape(4 * halo, channels), cots.reshape(2 * DEPTH, channels)]
    both = rows_of_128(jnp.concatenate(both, axis=0))
    blank = jnp.zeros((out_ref.shape[0] - both.shape[0], 128), f32)
    out_ref[...] = jnp.concatenate([both, blank], axis=0).astype(jnp.bfloat16)


def turn_kernel(weight, out_ref):
    step = 2 * weight.shape[0]
    total = weight.shape[1]
    for start in range(0, total, step):
        stop = min(start + step, total)
        out_ref[start:stop, :] = weight[:, start:stop].T


def bulk_kernel(masked, near, far, across, weight, pre_ref, ext, edge, cols):
    width, rows, channels = masked.shape
    f32 = jnp.float32
    plane, _, quad, side = position()
    use_low = side.astype(f32)
    use_high = (1 - side).astype(f32)
    place = plane * QUAD + quad
    use_left = (place > 0).astype(f32)
    use_right = (place < QUAD * lax.axis_size("depth") - 1).astype(f32)
    halo = 2 * DEPTH
    tall = rows + 2 * halo
    mid = rows + 2 * DEPTH
    span = width + 4
    odd = lax.rem(quad, 2)
    edge[odd] = rows_of_192(far[...].astype(f32)).reshape(edge.shape[1:])
    edge[1 - odd] = rows_of_192(near[...].astype(f32)).reshape(edge.shape[1:])
    ext[0:2, halo : halo + rows, :] = edge[0, 0:2] * use_left
    ext[2 : 2 + width, halo : halo + rows, :] = masked[...].astype(f32)
    ext[2 + width :, halo : halo + rows, :] = edge[1, 0:2] * use_right
    half = width // 2
    count = width * rows * channels // 128
    held = across[:count].astype(f32).reshape(width + half, rows, 128)
    brick = jnp.where(side == 0, held[:, :halo], held[:, rows - halo :])
    rest = jnp.concatenate([brick[width:, :, :64], brick[width:, :, 64:]], axis=0)
    beside = jnp.concatenate([brick[:width], rest], axis=2)
    blank = jnp.zeros((2, halo, channels), f32)
    for use, start in ((use_low, 0), (use_high, halo + rows)):
        at = slice(start, start + halo)
        ext[0:2, at, :] = blank
        ext[2 : 2 + width, at, :] = beside * use
        ext[2 + width :, at, :] = blank
    field = ext[...].reshape(span * tall // DEPTH, DEPTH, channels)
    for c in OFFSETS:
        moved = shift_z(field, c).reshape(span, tall, channels)
        for b in OFFSETS:
            at = ((b + 1) * 3 + c + 1) * channels
            start = DEPTH * (b + 1)
            cols[:, :, at : at + channels] = moved[:, start : start + mid].astype(jnp.bfloat16)
    nine = 9 * channels
    pre = jnp.zeros(((width + 2) * mid, channels), f32)
    for a in range(3):
        pre += jnp.dot(
            cols[a : a + width + 2].reshape((width + 2) * mid, nine),
            weight[a * nine : (a + 1) * nine, :],
            preferred_element_type=f32,
        )
    pre_ref[...] = pre.reshape(pre_ref.shape)


def forward_kernel(bulk, cot, near, far, across, corner, live, weight, pick, *refs):
    act_ref, gp_ref = refs[:2]
    slice_refs = refs[2 : 2 + len(CHIPS)]
    edge, cols, total, slices = refs[2 + len(CHIPS) :]
    width, rows, channels = cot.shape
    f32 = jnp.float32
    plane, me, quad, side = position()
    use_low = side.astype(f32)
    use_high = (1 - side).astype(f32)
    place = plane * QUAD + quad
    use_left = (place > 0).astype(f32)
    use_right = (place < QUAD * lax.axis_size("depth") - 1).astype(f32)
    halo = 2 * DEPTH
    mid = rows + 2 * DEPTH
    count = 4 * halo + 2 * DEPTH
    both = rows_of_192(corner[...].astype(f32)[: count * channels // 128])
    corners = both[: 4 * halo].reshape(2, 2, halo, channels)
    corners = jnp.concatenate([corners[0] * use_left, corners[1] * use_right], axis=0)
    sources = ((0, 1, None, None), (1, None, None, 2), (None, None, 2, 3))
    blank = jnp.zeros((DEPTH, channels), f32)
    six = 6 * channels
    for c in OFFSETS:
        moved = shift_z(corners.reshape(8, DEPTH, channels), c)
        for b, low, high in ((0, (0, 1), (None, 0)), (1, (1, None), (0, 1))):
            at = (b * 3 + c + 1) * channels
            parts = []
            for slab in range(4):
                for below, above in zip(low, high):
                    part = blank if below is None else moved[2 * slab + below] * use_low
                    if above is not None:
                        part = part + moved[2 * slab + above] * use_high
                    parts.append(part)
            for a in range(3):
                rows_a = []
                for source in sources[a]:
                    pair = [blank] * 2 if source is None else parts[2 * source : 2 * source + 2]
                    rows_a += pair
                cols[a, :, at : at + channels] = jnp.concatenate(rows_a, axis=0).astype(
                    jnp.bfloat16
                )
    share = jnp.zeros((4 * halo, channels), f32)
    for a in range(3):
        taps = pl.ds(pl.multiple_of((3 * a + 1 - side) * 3 * channels, 16), six)
        share += jnp.dot(cols[a], weight[taps], preferred_element_type=f32)
    share = share.reshape(4, halo, channels)
    total[...] = bulk[...]
    at = pl.ds(pl.multiple_of((1 - side) * (mid - halo), DEPTH), halo)
    total[0:2, at, :] += share[0:2]
    total[width : width + 2, at, :] += share[2:4]
    pre = total[...].reshape((width + 2) * mid, channels)
    sig = 0.5 * jnp.tanh(0.5 * pre) + 0.5
    act = (pre * sig).reshape(width + 2, mid, channels)[1 : 1 + width, DEPTH : DEPTH + rows]
    act_ref[...] = (act * live[:, :, 0:1]).astype(jnp.bfloat16)
    slope = (sig * (1.0 + pre * (1.0 - sig))).reshape(width + 2, mid, channels)
    ends = both[4 * halo :].reshape(2, 1, DEPTH, channels)
    strip = across[width * rows * channels // 128 :].astype(f32)
    beyond = jnp.concatenate(
        [
            ends[0] * use_left,
            rows_of_192(strip).reshape(width, DEPTH, channels),
            ends[1] * use_right,
        ],
        axis=0,
    )
    odd = lax.rem(quad, 2)
    edge[odd] = rows_of_192(far[...].astype(f32))[2 * rows :]
    edge[1 - odd] = rows_of_192(near[...].astype(f32))[2 * rows :]
    centre = [edge[0:1] * use_left, cot[...].astype(f32), edge[1:2] * use_right]
    centre = jnp.concatenate(centre, axis=0)
    full = jnp.concatenate([beyond * use_low, centre, beyond * use_high], axis=1)
    grad = full * slope
    gp_ref[...] = grad.astype(jnp.bfloat16)
    inner = grad[:, DEPTH : DEPTH + rows].astype(jnp.bfloat16)
    turned = lax.dot_general(
        pick[...],
        inner.reshape((width + 2) * rows, channels),
        (((1,), (1,)), ((), ())),
        preferred_element_type=f32,
    )
    slices[...] = turned.reshape(slices.shape)
    chip = me - lax.rem(quad, 2) * SIDES
    for distance, ref in zip(CHIPS, slice_refs):
        both = [slices[chip ^ distance], slices[(chip ^ distance) + SIDES]]
        ref[...] = jnp.concatenate(both, axis=0).astype(jnp.bfloat16)


def input_kernel(gp, live, turned, act, out_ref, act_ref, cols, weight):
    act_ref[...] = act[...]
    width, rows, channels = out_ref.shape
    f32 = jnp.float32
    tall = rows + 2 * DEPTH
    for tap in range(27):
        weight[tap * channels : (tap + 1) * channels, :] = turned[
            :, tap * channels : (tap + 1) * channels
        ]
    field = gp[...].astype(f32).reshape((width + 2) * tall // DEPTH, DEPTH, channels)
    for c in OFFSETS:
        moved = shift_z(field, -c).reshape(width + 2, tall, channels)
        for b in OFFSETS:
            at = ((b + 1) * 3 + c + 1) * channels
            start = DEPTH * (1 - b)
            cols[:, :, at : at + channels] = moved[:, start : start + rows].astype(jnp.bfloat16)
    nine = 9 * channels
    total = jnp.zeros((width * rows, channels), f32)
    for a in range(3):
        total += jnp.dot(
            cols[2 - a : 2 - a + width].reshape(width * rows, nine),
            weight[a * nine : (a + 1) * nine, :],
            preferred_element_type=f32,
        )
    out_ref[...] = (total.reshape(width, rows, channels) * live[:, :, 0:1]).astype(jnp.bfloat16)


def unpack_pair(bricks, masked):
    per, lane, _ = masked.shape
    half = lane // 2
    side = position()[3]
    for i, brick in enumerate(bricks):
        at_rows = pl.ds(pl.multiple_of((side ^ i) * half, half), half)
        for x in range(per):
            shift = 64 * (x // (per // 2))
            rest = brick[pl.ds((per + x % (per // 2)) * half, half)]
            masked[x, at_rows, :128] = brick[pl.ds(x * half, half)]
            masked[x, at_rows, 128:] = rest[:, shift : shift + 64]


def pair_product(received, masked, cols):
    f32 = jnp.float32
    group = received[0].shape[0]
    per, lane, channels = masked.shape
    half = lane // 2
    side = position()[3]
    at = lax.broadcasted_iota(jnp.int32, (group, lane), 1)
    y, z = at // DEPTH, at % DEPTH
    tall = lane // DEPTH
    own, other = received
    first = jnp.where(side == 0, own, other)
    second = jnp.where(side == 0, other, own)
    for k in range(per + 2):
        one = first[:, k // 2 * lane : (k // 2 + 1) * lane]
        two = second[:, k // 2 * lane : (k // 2 + 1) * lane]
        if k % 2 == 0:
            base = jnp.where(at < half, one, pltpu.roll(two, half, 1))
        else:
            base = jnp.where(at < half, pltpu.roll(one, half, 1), two)
        pieces = []
        for b in OFFSETS:
            for c in OFFSETS:
                step = (DEPTH * b + c) % lane
                moved = base if step == 0 else pltpu.roll(base, step, 1)
                keep = (y - b >= 0) & (y - b < tall) & (z - c >= 0) & (z - c < DEPTH)
                pieces.append(jnp.where(keep, moved, 0.0))
        cols[:, k * lane : (k + 1) * lane] = jnp.concatenate(pieces, axis=0).astype(jnp.bfloat16)
    field = masked[...].reshape(per * lane, channels)
    for a in range(3):
        start = (2 - a) * lane
        got = jnp.dot(
            cols[:, start : start + per * lane], field, preferred_element_type=f32
        ).reshape(9, group, channels)
        yield a, jnp.concatenate([got[tap] for tap in range(9)], axis=1)


def unpack_kernel(brick, across, beside, beyond, here_ref, next_ref):
    unpack_pair((brick, across), here_ref)
    unpack_pair((beside, beyond), next_ref)


def first_pair_kernel(own, other, masked, part_ref, cols):
    received = own[...].astype(jnp.float32), other[...].astype(jnp.float32)
    for a, rows in pair_product(received, masked, cols):
        width = rows.shape[1]
        part_ref[:, a * width : (a + 1) * width] = rows


def second_pair_kernel(own_rows, before, other, own, masked, out_ref, cols):
    core = lax.rem(position()[2], 2)
    half = before.shape[0] // 2
    upper = core if own_rows else 1 - core
    received = [ref[...].astype(jnp.float32) for ref in (own, other)]
    received = [jnp.where(upper == 1, block[half:], block[:half]) for block in received]
    held = pl.ds(pl.multiple_of(upper * half, 8), half)
    for a, rows in pair_product(received, masked, cols):
        width = rows.shape[1]
        at = slice(a * width, (a + 1) * width)
        out_ref[:, at] = (before[held, at] + rows).astype(out_ref.dtype)


def fold_kernel(keep, other, own_ref, *refs):
    *send_refs, both, rows = refs
    planes, eight, _ = rows.shape
    count, total = keep.shape
    share = count // planes
    both[:count, :total] = keep[...] + other[...].astype(jnp.float32)
    both[:, total:] = jnp.zeros((both.shape[0], both.shape[1] - total), jnp.float32)
    for to in range(planes):
        rows[to] = fold_rows(both[share * to : share * to + eight, :], total)
    plane = position()[0]
    own_ref[...] = rows[plane]
    for distance, ref in enumerate(send_refs, 1):
        ref[...] = rows[plane ^ distance].astype(jnp.bfloat16)


def sum_kernel(scale, own, one, two, three, out_ref):
    f32 = jnp.float32
    total = own[...] + one[...].astype(f32) + two[...].astype(f32) + three[...].astype(f32)
    out_ref[...] = (total * scale).astype(out_ref.dtype)


def join_kernel(mine, other, out_ref):
    share = out_ref.shape[0] // SIDES
    ahead = position()[3] == 0
    total = out_ref.shape[1]
    here = unfold_rows(mine[...].astype(jnp.float32), total)
    there = unfold_rows(other[...].astype(jnp.float32), total)
    first = jnp.where(ahead, here, there)
    second = jnp.where(ahead, there, here)
    out_ref[0:share] = first[:share]
    out_ref[share:] = second[:share]


def call(body, name, mebibytes, flops, moved, out_shape, scratch=(), in_specs=None):
    spec = pl.BlockSpec(memory_space=pltpu.VMEM)

    def run(*operands):
        return pl.pallas_call(
            body,
            out_shape=out_shape,
            in_specs=in_specs or [spec] * len(operands),
            out_specs=jax.tree.map(lambda _: spec, out_shape),
            scratch_shapes=scratch,
            compiler_params=pltpu.CompilerParams(vmem_limit_bytes=mebibytes << 20),
            cost_estimate=pl.CostEstimate(flops=flops, bytes_accessed=moved, transcendentals=0),
            name=name,
        )(*operands)

    return run


def planes_local(features, weight, voxel_mask, cotangent):
    bf16 = jnp.bfloat16
    f32 = jnp.float32
    array = jax.ShapeDtypeStruct
    width, wide_y, depth, channels = features.shape
    rows = wide_y * depth
    planes = lax.axis_size("depth")
    count = planes * QUAD
    total = 27 * channels
    halo = 2 * DEPTH
    span = (width + 2) * rows
    share = channels // count // SIDES
    group = planes * share

    def swap(piece, axes, distance, size):
        return lax.ppermute(piece, axes, [(i, i ^ distance) for i in range(size)])

    def in_plane(piece, distance):
        return swap(piece, ("quad", "narrow"), distance, MEMBERS)

    brick = array((width, rows, channels), bf16)
    slab = array((3 * rows * channels // 128, 128), bf16)
    slabs = (2, 3, rows, channels)
    pick = call(
        functools.partial(pick_kernel, planes), "pick", 4, 1 << 32, 1 << 16,
        array((MEMBERS * group, channels), bf16),
    )()
    vmem = pl.BlockSpec(memory_space=pltpu.VMEM)
    masked, cot, live, near, far = call(
        prepare_kernel, "prepare", 16, 1 << 20, 1 << 20,
        (brick, brick, array((width, rows, 128), f32), slab, slab),
        (),
        [vmem] * 3 + [pl.BlockSpec(memory_space=pl.ANY)],
    )(
        features.reshape(width, rows, channels),
        cotangent.reshape(width, rows, channels),
        voxel_mask,
        pick,
    )
    near = swap(near, WIDE, 1, count)
    ends = [min(max(((i + 1) ^ 1) - 1, 0), count - 1) for i in range(count)]
    far = lax.ppermute(far, WIDE, list(enumerate(ends)))
    weight_rows = call(
        turn_kernel, "turn", 8, 1 << 20, 4 << 20, array((total, channels), bf16)
    )(weight.T)
    count_128 = width * rows * channels // 128
    strip_128 = width * DEPTH * channels // 128
    across = call(
        across_kernel, "across", 4, 1 << 16, 1 << 19, array((count_128 + strip_128, 128), bf16)
    )(masked, cot)
    across = in_plane(across, CHIPS[1])
    packed = call(
        pack_kernel, "pack", 4, 1 << 16, 1 << 19, array((count_128, 128), bf16), (),
        [vmem, pl.BlockSpec(memory_space=pl.ANY)],
    )(masked, weight_rows)
    near, far, weight_rows, late = lax.optimization_barrier((near, far, weight_rows, packed))
    corner = call(
        corner_kernel, "corner", 4, 1 << 16, 1 << 18,
        array((128, 128), bf16),
        (pltpu.VMEM(slabs, f32),),
    )(near, far)
    corner = in_plane(corner, 1)
    mid = rows + 2 * DEPTH
    bulk = call(
        bulk_kernel, "bulk", 24, 3 << 29, 1 << 20, array((width + 2, mid, channels), f32),
        (
            pltpu.VMEM((width + 4, rows + 2 * halo, channels), f32),
            pltpu.VMEM(slabs, f32),
            pltpu.VMEM((width + 4, mid, 9 * channels), bf16),
        ),
    )(masked, near, far, across, weight_rows)
    bricks = [packed, across, in_plane(packed, CHIPS[2]), in_plane(late, CHIPS[3])]

    act, gp, *slices = call(
        forward_kernel, "forward", 24, 3 << 29, 1 << 20,
        (brick, array((width + 2, mid, channels), bf16))
        + (array((2 * group, span), bf16),) * len(CHIPS),
        (
            pltpu.VMEM((2, rows, channels), f32),
            pltpu.VMEM((3, 4 * halo, 6 * channels), bf16),
            pltpu.VMEM((width + 2, mid, channels), f32),
            pltpu.VMEM((MEMBERS, group, span), f32),
        ),
    )(bulk, cot, near, far, across, corner, live, weight_rows, pick)
    bricks[2], *slices = lax.optimization_barrier((bricks[2], *slices))
    for place in (3, 2, 1):
        slices[place] = in_plane(slices[place], CHIPS[place])

    grad_input, act = call(
        input_kernel, "input_gradient", 20, 2 * 512 * 5184 * 256, 4 << 20, (brick, brick),
        (
            pltpu.VMEM((width + 2, rows, 9 * channels), bf16),
            pltpu.VMEM((total, channels), bf16),
        ),
    )(gp, live, weight.T, act)

    lanes = dense(total)[0]
    cols = pltpu.VMEM((9 * 2 * group, (width + 2) * SIDES * rows), bf16)
    pair = (width, SIDES * rows, channels)
    here_masked, next_masked = call(
        unpack_kernel, "unpack", 4, 1 << 20, 1 << 20, (array(pair, bf16),) * 2
    )(*bricks)
    part = call(
        first_pair_kernel, "first_pair", 16, 1 << 30, 2 << 20,
        array((2 * group, total), f32), (cols,),
    )(*slices[:2], here_masked)
    half_cols = pltpu.VMEM((9 * group, (width + 2) * SIDES * rows), bf16)
    second = part, *slices[3:1:-1], next_masked
    fold = call(
        functools.partial(second_pair_kernel, False), "second_pair_other", 16, 1 << 29, 1 << 20,
        array((group, total), bf16), (half_cols,),
    )(*second)
    keep = call(
        functools.partial(second_pair_kernel, True), "second_pair_own", 16, 1 << 29, 1 << 20,
        array((group, total), f32), (half_cols,),
    )(*second)
    own, *sends = call(
        fold_kernel, "fold", 8, 8 * total * 4, 8 * total * 40,
        (array((8, lanes), f32),) + (array((8, lanes), bf16),) * (planes - 1),
        (
            pltpu.VMEM((group + 8, sum(dense(total))), f32),
            pltpu.VMEM((planes, 8, lanes), f32),
        ),
    )(keep, in_plane(fold, 2))
    got = [swap(sends[d - 1], "depth", d, planes) for d in (2, 3, 1)]
    grad_input, *got = lax.optimization_barrier((grad_input, *got))
    voxels = count * SIDES * width * rows
    mine = call(
        functools.partial(sum_kernel, float(1.0 / voxels**0.5)),
        "plane_sum", 4, 8 * total * 4, 8 * total * 14, array((8, lanes), bf16),
    )(own, *got)
    grad_weight = call(
        join_kernel, "join", 4, 8 * total, 8 * total * 14, array((channels // count, total), f32)
    )(mine, in_plane(mine, 1))
    shape = features.shape
    return act.reshape(shape), grad_input.reshape(shape), grad_weight


def padded_2(cells, sides, width):
    for axis, dim in sides:
        count = lax.axis_size(axis)
        ends = count - 1
        head = lax.slice_in_dim(cells, 0, width, axis=dim)
        tail = lax.slice_in_dim(cells, cells.shape[dim] - width, cells.shape[dim], axis=dim)
        cells = jnp.concatenate(
            [
                lax.ppermute(tail, axis, [(i, (i + 1) % count) for i in range(ends)]),
                cells,
                lax.ppermute(head, axis, [((i + 1) % count, i) for i in range(ends)]),
            ],
            axis=dim,
        )
    return cells


def gather_taps(padded, width_x, width_y, depth_z, channels, flip):
    pieces = []
    for shift_x in range(3):
        for shift_y in range(3):
            for shift_z in range(3):
                start_x = 2 - shift_x if flip else shift_x
                start_y = 2 - shift_y if flip else shift_y
                start_z = 2 - shift_z if flip else shift_z
                piece = padded[
                    start_x : start_x + width_x,
                    start_y : start_y + width_y,
                    start_z : start_z + depth_z,
                    :,
                ]
                pieces.append(piece.reshape(-1, channels))
    return jnp.concatenate(pieces, axis=1)


def summed_local(features, weight, voxel_mask, cotangent):
    width_x, width_y, depth_z, channels = features.shape
    masked = features * voxel_mask.astype(jnp.bfloat16)[..., None]
    padded = padded_2(masked, (("wide", 0), ("narrow", 1)), 1)
    padded = jnp.pad(padded, ((0, 0), (0, 0), (1, 1), (0, 0)))
    columns = gather_taps(padded, width_x, width_y, depth_z, channels, False)
    pre = jnp.dot(columns, weight, preferred_element_type=jnp.float32)
    live = voxel_mask.reshape(-1, 1).astype(jnp.float32)
    sig = jax.nn.sigmoid(pre)
    activation = (
        (pre * sig * live).astype(jnp.bfloat16).reshape(width_x, width_y, depth_z, channels)
    )
    slope = sig * (1.0 + pre * (1.0 - sig))
    grad_pre = (cotangent.reshape(-1, channels).astype(jnp.float32) * live * slope).astype(
        jnp.bfloat16
    )
    taps = weight.reshape(27, channels, channels)
    grid = grad_pre.reshape(width_x, width_y, depth_z, channels)
    grad_pad = padded_2(grid, (("wide", 0), ("narrow", 1)), 1)
    grad_pad = jnp.pad(grad_pad, ((0, 0), (0, 0), (1, 1), (0, 0)))
    grad_columns = gather_taps(grad_pad, width_x, width_y, depth_z, channels, True)
    flipped = jnp.transpose(taps, (0, 2, 1)).reshape(27 * channels, channels)
    grad_field = jnp.dot(grad_columns, flipped, preferred_element_type=jnp.float32)
    grad_input = (
        (grad_field * live).astype(jnp.bfloat16).reshape(width_x, width_y, depth_z, channels)
    )
    scale = 1.0 / jnp.sqrt(
        jnp.float32(width_x * width_y * depth_z * lax.axis_size("wide") * lax.axis_size("narrow"))
    )
    whole = lax.dot_general(
        grad_pre, columns, (((0,), (0,)), ((), ())), preferred_element_type=jnp.float32
    )
    piece_flat = lax.psum_scatter(
        whole.reshape(-1), ("wide", "narrow"), scatter_dimension=0, tiled=True
    )
    gathered = lax.all_gather(piece_flat, "narrow", axis=0, tiled=True)
    summed = gathered.reshape(channels // lax.axis_size("wide"), 27 * channels)
    grad_weight = summed * scale
    return (activation, grad_input, grad_weight)


def sharded(body, mesh, wide):
    return jax.shard_map(
        body,
        mesh=mesh,
        in_specs=(
            P(wide, "narrow", None, None),
            P(),
            P(wide, "narrow", None),
            P(wide, "narrow", None, None),
        ),
        out_specs=(
            P(wide, "narrow", None, None),
            P(wide, "narrow", None, None),
            P(wide, None),
        ),
        check_vma=False,
    )


def solution(mesh):
    wide, narrow = mesh.shape["wide"], mesh.shape["narrow"]
    if wide != 4 * QUAD or narrow != SIDES:
        return sharded(summed_local, mesh, "wide")
    planes = Mesh(
        mesh.devices.reshape(wide // QUAD, QUAD, narrow), ("depth", "quad", "narrow")
    )
    return sharded(planes_local, planes, WIDE)
```

```python
import functools

import jax
import jax.numpy as jnp
from jax import lax
from jax.experimental import pallas as pl
from jax.experimental.pallas import tpu as pltpu
from jax.sharding import Mesh
from jax.sharding import PartitionSpec as P

WIDE = ("depth", "quad")
QUAD = 4
SIDES = 2
MEMBERS = QUAD * SIDES
CHIPS = (0, 1, 4, 5)
OFFSETS = (-1, 0, 1)
DEPTH = 8


def position():
    quad, side = lax.axis_index("quad"), lax.axis_index("narrow")
    return lax.axis_index("depth"), quad * SIDES + side, quad, side


def shift_z(field, step):
    if step == 0:
        return field
    depth = field.shape[1]
    moved = pltpu.roll(field, (-step) % depth, 1)
    z = lax.broadcasted_iota(jnp.int32, field.shape, 1) + step
    return jnp.where((z >= 0) & (z < depth), moved, 0.0)


def pick_kernel(planes, out_ref):
    index = lax.broadcasted_iota(jnp.int32, out_ref.shape, 0)
    column = lax.broadcasted_iota(jnp.int32, out_ref.shape, 1)
    per = out_ref.shape[1] // (planes * QUAD)
    share = per // SIDES
    group = planes * share
    quad, side = index // (SIDES * group), index // group % SIDES
    plane, row = index // share % planes, index % share
    channel = per * (QUAD * plane + quad) + share * side + row
    out_ref[...] = jnp.where(channel == column, 1.0, 0.0).astype(jnp.bfloat16)


def dense(total):
    tiles = -(-total // 128)
    moved = tiles // 4
    return (tiles - moved) * 128, moved * 128


def fold_rows(block, total):
    kept, moved = dense(total)
    tail = block[:, kept : kept + moved]
    row = lax.broadcasted_iota(jnp.int32, tail.shape, 0)
    pieces = []
    for k in range(3):
        spare = jnp.where(row == 6, pltpu.roll(tail, 6 - k, 0), pltpu.roll(tail, 4 - k, 0))
        pieces.append(jnp.where(row < 6, block[:, k * moved : (k + 1) * moved], spare))
    return jnp.concatenate(pieces + [block[:, 3 * moved : kept]], axis=1)


def unfold_rows(block, total):
    kept, moved = dense(total)
    row = lax.broadcasted_iota(jnp.int32, (8, moved), 0)
    tail = jnp.zeros((8, moved), block.dtype)
    for k in range(3):
        piece = block[:, k * moved : (k + 1) * moved]
        tail = jnp.where(row == k, pltpu.roll(piece, 2 + k, 0), tail)
        tail = jnp.where(row == 3 + k, pltpu.roll(piece, 4 + k, 0), tail)
    return jnp.concatenate([block, tail], axis=1)[:, :total]


def rows_of_128(block):
    half = block.shape[0] // 2
    rest = jnp.concatenate([block[:half, 128:], block[half:, 128:]], axis=1)
    return jnp.concatenate([block[:, :128], rest], axis=0)


def rows_of_192(block):
    count = block.shape[0] * 2 // 3
    rest = jnp.concatenate([block[count:, :64], block[count:, 64:]], axis=0)
    return jnp.concatenate([block[:count], rest], axis=1)


def prepare_kernel(features, cot, mask, first, masked_ref, cot_ref, live_ref, near_ref, far_ref):
    width, rows, channels = features.shape
    f32 = jnp.float32
    flat = mask[...].astype(f32).reshape(width * rows // DEPTH, DEPTH)
    live = jnp.broadcast_to(flat[:, :, None], flat.shape + (channels,)).reshape(features.shape)
    live_ref[...] = live[:, :, :128]
    masked_ref[...] = (features[...].astype(f32) * live).astype(jnp.bfloat16)
    cot_ref[...] = (cot[...].astype(f32) * live).astype(jnp.bfloat16)
    odd = lax.rem(position()[2], 2)
    for ref, upper in ((near_ref, 1 - odd), (far_ref, odd)):
        slabs = [
            masked_ref[pl.ds(upper * (width - 2), 2)],
            cot_ref[pl.ds(upper * (width - 1), 1)],
        ]
        slabs = jnp.concatenate(slabs, axis=0).astype(f32).reshape(3 * rows, channels)
        ref[...] = rows_of_128(slabs).astype(jnp.bfloat16)


def pack_kernel(masked, after, packed_ref):
    count, channels = packed_ref.shape[0] * 128 // masked.shape[2], masked.shape[2]
    block = masked[...].reshape(count, channels)
    packed_ref[...] = rows_of_128(block)


def across_kernel(masked, cot, across_ref):
    width, rows, channels = masked.shape
    packed = rows_of_128(masked[...].reshape(width * rows, channels))
    across_ref[: packed.shape[0]] = packed
    ahead = position()[3] == 0
    grown = cot[...].astype(jnp.float32)
    strip = jnp.where(ahead, grown[:, rows - DEPTH :], grown[:, :DEPTH])
    strip = rows_of_128(strip.reshape(width * DEPTH, channels))
    across_ref[packed.shape[0] :] = strip.astype(jnp.bfloat16)


def corner_kernel(near, far, out_ref, edge):
    _, slabs, rows, channels = edge.shape
    _, _, quad, side = position()
    odd = lax.rem(quad, 2)
    f32 = jnp.float32
    edge[odd] = rows_of_192(far[...].astype(f32)).reshape(edge.shape[1:])
    edge[1 - odd] = rows_of_192(near[...].astype(f32)).reshape(edge.shape[1:])
    halo = 2 * DEPTH
    ahead = side == 0
    strip = jnp.where(ahead, edge[:, :2, rows - halo :], edge[:, :2, :halo])
    cots = jnp.where(ahead, edge[:, 2, rows - DEPTH :], edge[:, 2, :DEPTH])
    both = [strip.reshape(4 * halo, channels), cots.reshape(2 * DEPTH, channels)]
    both = rows_of_128(jnp.concatenate(both, axis=0))
    blank = jnp.zeros((out_ref.shape[0] - both.shape[0], 128), f32)
    out_ref[...] = jnp.concatenate([both, blank], axis=0).astype(jnp.bfloat16)


def turn_kernel(weight, out_ref):
    step = 2 * weight.shape[0]
    total = weight.shape[1]
    for start in range(0, total, step):
        stop = min(start + step, total)
        out_ref[start:stop, :] = weight[:, start:stop].T


def bulk_kernel(masked, near, far, across, weight, pre_ref, ext, edge, cols):
    width, rows, channels = masked.shape
    f32 = jnp.float32
    plane, _, quad, side = position()
    use_low = side.astype(f32)
    use_high = (1 - side).astype(f32)
    place = plane * QUAD + quad
    use_left = (place > 0).astype(f32)
    use_right = (place < QUAD * lax.axis_size("depth") - 1).astype(f32)
    halo = 2 * DEPTH
    tall = rows + 2 * halo
    mid = rows + 2 * DEPTH
    span = width + 4
    odd = lax.rem(quad, 2)
    edge[odd] = rows_of_192(far[...].astype(f32)).reshape(edge.shape[1:])
    edge[1 - odd] = rows_of_192(near[...].astype(f32)).reshape(edge.shape[1:])
    ext[0:2, halo : halo + rows, :] = edge[0, 0:2] * use_left
    ext[2 : 2 + width, halo : halo + rows, :] = masked[...].astype(f32)
    ext[2 + width :, halo : halo + rows, :] = edge[1, 0:2] * use_right
    half = width // 2
    count = width * rows * channels // 128
    held = across[:count].astype(f32).reshape(width + half, rows, 128)
    brick = jnp.where(side == 0, held[:, :halo], held[:, rows - halo :])
    rest = jnp.concatenate([brick[width:, :, :64], brick[width:, :, 64:]], axis=0)
    beside = jnp.concatenate([brick[:width], rest], axis=2)
    blank = jnp.zeros((2, halo, channels), f32)
    for use, start in ((use_low, 0), (use_high, halo + rows)):
        at = slice(start, start + halo)
        ext[0:2, at, :] = blank
        ext[2 : 2 + width, at, :] = beside * use
        ext[2 + width :, at, :] = blank
    field = ext[...].reshape(span * tall // DEPTH, DEPTH, channels)
    for c in OFFSETS:
        moved = shift_z(field, c).reshape(span, tall, channels)
        for b in OFFSETS:
            at = ((b + 1) * 3 + c + 1) * channels
            start = DEPTH * (b + 1)
            cols[:, :, at : at + channels] = moved[:, start : start + mid].astype(jnp.bfloat16)
    nine = 9 * channels
    pre = jnp.zeros(((width + 2) * mid, channels), f32)
    for a in range(3):
        pre += jnp.dot(
            cols[a : a + width + 2].reshape((width + 2) * mid, nine),
            weight[a * nine : (a + 1) * nine, :],
            preferred_element_type=f32,
        )
    pre_ref[...] = pre.reshape(pre_ref.shape)


def forward_kernel(bulk, cot, near, far, across, corner, live, weight, pick, *refs):
    act_ref, gp_ref = refs[:2]
    slice_refs = refs[2 : 2 + len(CHIPS)]
    edge, cols, total, slices = refs[2 + len(CHIPS) :]
    width, rows, channels = cot.shape
    f32 = jnp.float32
    plane, me, quad, side = position()
    use_low = side.astype(f32)
    use_high = (1 - side).astype(f32)
    place = plane * QUAD + quad
    use_left = (place > 0).astype(f32)
    use_right = (place < QUAD * lax.axis_size("depth") - 1).astype(f32)
    halo = 2 * DEPTH
    mid = rows + 2 * DEPTH
    count = 4 * halo + 2 * DEPTH
    both = rows_of_192(corner[...].astype(f32)[: count * channels // 128])
    corners = both[: 4 * halo].reshape(2, 2, halo, channels)
    corners = jnp.concatenate([corners[0] * use_left, corners[1] * use_right], axis=0)
    sources = ((0, 1, None, None), (1, None, None, 2), (None, None, 2, 3))
    blank = jnp.zeros((DEPTH, channels), f32)
    six = 6 * channels
    for c in OFFSETS:
        moved = shift_z(corners.reshape(8, DEPTH, channels), c)
        for b, low, high in ((0, (0, 1), (None, 0)), (1, (1, None), (0, 1))):
            at = (b * 3 + c + 1) * channels
            parts = []
            for slab in range(4):
                for below, above in zip(low, high):
                    part = blank if below is None else moved[2 * slab + below] * use_low
                    if above is not None:
                        part = part + moved[2 * slab + above] * use_high
                    parts.append(part)
            for a in range(3):
                rows_a = []
                for source in sources[a]:
                    pair = [blank] * 2 if source is None else parts[2 * source : 2 * source + 2]
                    rows_a += pair
                cols[a, :, at : at + channels] = jnp.concatenate(rows_a, axis=0).astype(
                    jnp.bfloat16
                )
    share = jnp.zeros((4 * halo, channels), f32)
    for a in range(3):
        taps = pl.ds(pl.multiple_of((3 * a + 1 - side) * 3 * channels, 16), six)
        share += jnp.dot(cols[a], weight[taps], preferred_element_type=f32)
    share = share.reshape(4, halo, channels)
    total[...] = bulk[...]
    at = pl.ds(pl.multiple_of((1 - side) * (mid - halo), DEPTH), halo)
    total[0:2, at, :] += share[0:2]
    total[width : width + 2, at, :] += share[2:4]
    pre = total[...].reshape((width + 2) * mid, channels)
    sig = 0.5 * jnp.tanh(0.5 * pre) + 0.5
    act = (pre * sig).reshape(width + 2, mid, channels)[1 : 1 + width, DEPTH : DEPTH + rows]
    act_ref[...] = (act * live[:, :, 0:1]).astype(jnp.bfloat16)
    slope = (sig * (1.0 + pre * (1.0 - sig))).reshape(width + 2, mid, channels)
    ends = both[4 * halo :].reshape(2, 1, DEPTH, channels)
    strip = across[width * rows * channels // 128 :].astype(f32)
    beyond = jnp.concatenate(
        [
            ends[0] * use_left,
            rows_of_192(strip).reshape(width, DEPTH, channels),
            ends[1] * use_right,
        ],
        axis=0,
    )
    odd = lax.rem(quad, 2)
    edge[odd] = rows_of_192(far[...].astype(f32))[2 * rows :]
    edge[1 - odd] = rows_of_192(near[...].astype(f32))[2 * rows :]
    centre = [edge[0:1] * use_left, cot[...].astype(f32), edge[1:2] * use_right]
    centre = jnp.concatenate(centre, axis=0)
    full = jnp.concatenate([beyond * use_low, centre, beyond * use_high], axis=1)
    grad = full * slope
    gp_ref[...] = grad.astype(jnp.bfloat16)
    inner = grad[:, DEPTH : DEPTH + rows].astype(jnp.bfloat16)
    turned = lax.dot_general(
        pick[...],
        inner.reshape((width + 2) * rows, channels),
        (((1,), (1,)), ((), ())),
        preferred_element_type=f32,
    )
    slices[...] = turned.reshape(slices.shape)
    chip = me - lax.rem(quad, 2) * SIDES
    for distance, ref in zip(CHIPS, slice_refs):
        both = [slices[chip ^ distance], slices[(chip ^ distance) + SIDES]]
        ref[...] = jnp.concatenate(both, axis=0).astype(jnp.bfloat16)


def input_kernel(gp, live, turned, act, out_ref, act_ref, cols, weight):
    act_ref[...] = act[...]
    width, rows, channels = out_ref.shape
    f32 = jnp.float32
    tall = rows + 2 * DEPTH
    for tap in range(27):
        weight[tap * channels : (tap + 1) * channels, :] = turned[
            :, tap * channels : (tap + 1) * channels
        ]
    field = gp[...].astype(f32).reshape((width + 2) * tall // DEPTH, DEPTH, channels)
    for c in OFFSETS:
        moved = shift_z(field, -c).reshape(width + 2, tall, channels)
        for b in OFFSETS:
            at = ((b + 1) * 3 + c + 1) * channels
            start = DEPTH * (1 - b)
            cols[:, :, at : at + channels] = moved[:, start : start + rows].astype(jnp.bfloat16)
    nine = 9 * channels
    total = jnp.zeros((width * rows, channels), f32)
    for a in range(3):
        total += jnp.dot(
            cols[2 - a : 2 - a + width].reshape(width * rows, nine),
            weight[a * nine : (a + 1) * nine, :],
            preferred_element_type=f32,
        )
    out_ref[...] = (total.reshape(width, rows, channels) * live[:, :, 0:1]).astype(jnp.bfloat16)


def unpack_pair(bricks, masked):
    per, lane, _ = masked.shape
    half = lane // 2
    side = position()[3]
    for i, brick in enumerate(bricks):
        at_rows = pl.ds(pl.multiple_of((side ^ i) * half, half), half)
        for x in range(per):
            shift = 64 * (x // (per // 2))
            rest = brick[pl.ds((per + x % (per // 2)) * half, half)]
            masked[x, at_rows, :128] = brick[pl.ds(x * half, half)]
            masked[x, at_rows, 128:] = rest[:, shift : shift + 64]


def pair_product(received, masked, cols):
    f32 = jnp.float32
    group = received[0].shape[0]
    per, lane, channels = masked.shape
    half = lane // 2
    side = position()[3]
    at = lax.broadcasted_iota(jnp.int32, (group, lane), 1)
    y, z = at // DEPTH, at % DEPTH
    tall = lane // DEPTH
    own, other = received
    first = jnp.where(side == 0, own, other)
    second = jnp.where(side == 0, other, own)
    for k in range(per + 2):
        one = first[:, k // 2 * lane : (k // 2 + 1) * lane]
        two = second[:, k // 2 * lane : (k // 2 + 1) * lane]
        if k % 2 == 0:
            base = jnp.where(at < half, one, pltpu.roll(two, half, 1))
        else:
            base = jnp.where(at < half, pltpu.roll(one, half, 1), two)
        pieces = []
        for b in OFFSETS:
            for c in OFFSETS:
                step = (DEPTH * b + c) % lane
                moved = base if step == 0 else pltpu.roll(base, step, 1)
                keep = (y - b >= 0) & (y - b < tall) & (z - c >= 0) & (z - c < DEPTH)
                pieces.append(jnp.where(keep, moved, 0.0))
        cols[:, k * lane : (k + 1) * lane] = jnp.concatenate(pieces, axis=0).astype(jnp.bfloat16)
    field = masked[...].reshape(per * lane, channels)
    for a in range(3):
        start = (2 - a) * lane
        got = jnp.dot(
            cols[:, start : start + per * lane], field, preferred_element_type=f32
        ).reshape(9, group, channels)
        yield a, jnp.concatenate([got[tap] for tap in range(9)], axis=1)


def unpack_kernel(brick, across, beside, beyond, here_ref, next_ref):
    unpack_pair((brick, across), here_ref)
    unpack_pair((beside, beyond), next_ref)


def first_pair_kernel(own, other, masked, part_ref, cols):
    received = own[...].astype(jnp.float32), other[...].astype(jnp.float32)
    for a, rows in pair_product(received, masked, cols):
        width = rows.shape[1]
        part_ref[:, a * width : (a + 1) * width] = rows


def second_pair_kernel(own_rows, before, other, own, masked, out_ref, cols):
    core = lax.rem(position()[2], 2)
    half = before.shape[0] // 2
    upper = core if own_rows else 1 - core
    received = [ref[...].astype(jnp.float32) for ref in (own, other)]
    received = [jnp.where(upper == 1, block[half:], block[:half]) for block in received]
    held = pl.ds(pl.multiple_of(upper * half, 8), half)
    for a, rows in pair_product(received, masked, cols):
        width = rows.shape[1]
        at = slice(a * width, (a + 1) * width)
        out_ref[:, at] = (before[held, at] + rows).astype(out_ref.dtype)


def fold_kernel(keep, other, own_ref, *refs):
    *send_refs, both, rows = refs
    planes, eight, _ = rows.shape
    count, total = keep.shape
    share = count // planes
    both[:count, :total] = keep[...] + other[...].astype(jnp.float32)
    both[:, total:] = jnp.zeros((both.shape[0], both.shape[1] - total), jnp.float32)
    for to in range(planes):
        rows[to] = fold_rows(both[share * to : share * to + eight, :], total)
    plane = position()[0]
    own_ref[...] = rows[plane]
    for distance, ref in enumerate(send_refs, 1):
        ref[...] = rows[plane ^ distance].astype(jnp.bfloat16)


def sum_kernel(scale, own, one, two, three, out_ref):
    f32 = jnp.float32
    total = own[...] + one[...].astype(f32) + two[...].astype(f32) + three[...].astype(f32)
    out_ref[...] = (total * scale).astype(out_ref.dtype)


def unfold_kernel(mine, out_ref):
    out_ref[...] = unfold_rows(mine[...].astype(jnp.float32), out_ref.shape[1])


def join_kernel(here, other, out_ref):
    share = out_ref.shape[0] // SIDES
    there = unfold_rows(other[...].astype(jnp.float32), out_ref.shape[1])
    ahead = position()[3] == 0
    out_ref[0:share] = jnp.where(ahead, here[...], there)[:share]
    out_ref[share:] = jnp.where(ahead, there, here[...])[:share]


def call(body, name, mebibytes, flops, moved, out_shape, scratch=(), in_specs=None):
    spec = pl.BlockSpec(memory_space=pltpu.VMEM)

    def run(*operands):
        return pl.pallas_call(
            body,
            out_shape=out_shape,
            in_specs=in_specs or [spec] * len(operands),
            out_specs=jax.tree.map(lambda _: spec, out_shape),
            scratch_shapes=scratch,
            compiler_params=pltpu.CompilerParams(vmem_limit_bytes=mebibytes << 20),
            cost_estimate=pl.CostEstimate(flops=flops, bytes_accessed=moved, transcendentals=0),
            name=name,
        )(*operands)

    return run


def planes_local(features, weight, voxel_mask, cotangent):
    bf16 = jnp.bfloat16
    f32 = jnp.float32
    array = jax.ShapeDtypeStruct
    width, wide_y, depth, channels = features.shape
    rows = wide_y * depth
    planes = lax.axis_size("depth")
    count = planes * QUAD
    total = 27 * channels
    halo = 2 * DEPTH
    span = (width + 2) * rows
    share = channels // count // SIDES
    group = planes * share

    def swap(piece, axes, distance, size):
        return lax.ppermute(piece, axes, [(i, i ^ distance) for i in range(size)])

    def in_plane(piece, distance):
        return swap(piece, ("quad", "narrow"), distance, MEMBERS)

    brick = array((width, rows, channels), bf16)
    slab = array((3 * rows * channels // 128, 128), bf16)
    slabs = (2, 3, rows, channels)
    pick = call(
        functools.partial(pick_kernel, planes), "pick", 4, 1 << 32, 1 << 16,
        array((MEMBERS * group, channels), bf16),
    )()
    vmem = pl.BlockSpec(memory_space=pltpu.VMEM)
    masked, cot, live, near, far = call(
        prepare_kernel, "prepare", 16, 1 << 20, 1 << 20,
        (brick, brick, array((width, rows, 128), f32), slab, slab),
        (),
        [vmem] * 3 + [pl.BlockSpec(memory_space=pl.ANY)],
    )(
        features.reshape(width, rows, channels),
        cotangent.reshape(width, rows, channels),
        voxel_mask,
        pick,
    )
    near = swap(near, WIDE, 1, count)
    ends = [min(max(((i + 1) ^ 1) - 1, 0), count - 1) for i in range(count)]
    far = lax.ppermute(far, WIDE, list(enumerate(ends)))
    weight_rows = call(
        turn_kernel, "turn", 8, 1 << 20, 4 << 20, array((total, channels), bf16)
    )(weight.T)
    count_128 = width * rows * channels // 128
    strip_128 = width * DEPTH * channels // 128
    across = call(
        across_kernel, "across", 4, 1 << 16, 1 << 19, array((count_128 + strip_128, 128), bf16)
    )(masked, cot)
    across = in_plane(across, CHIPS[1])
    packed = call(
        pack_kernel, "pack", 4, 1 << 16, 1 << 19, array((count_128, 128), bf16), (),
        [vmem, pl.BlockSpec(memory_space=pl.ANY)],
    )(masked, weight_rows)
    near, far, weight_rows, late = lax.optimization_barrier((near, far, weight_rows, packed))
    corner = call(
        corner_kernel, "corner", 4, 1 << 16, 1 << 18,
        array((128, 128), bf16),
        (pltpu.VMEM(slabs, f32),),
    )(near, far)
    corner = in_plane(corner, 1)
    mid = rows + 2 * DEPTH
    bulk = call(
        bulk_kernel, "bulk", 24, 3 << 29, 1 << 20, array((width + 2, mid, channels), f32),
        (
            pltpu.VMEM((width + 4, rows + 2 * halo, channels), f32),
            pltpu.VMEM(slabs, f32),
            pltpu.VMEM((width + 4, mid, 9 * channels), bf16),
        ),
    )(masked, near, far, across, weight_rows)
    bricks = [packed, across, in_plane(packed, CHIPS[2]), in_plane(late, CHIPS[3])]

    act, gp, *slices = call(
        forward_kernel, "forward", 24, 3 << 29, 1 << 20,
        (brick, array((width + 2, mid, channels), bf16))
        + (array((2 * group, span), bf16),) * len(CHIPS),
        (
            pltpu.VMEM((2, rows, channels), f32),
            pltpu.VMEM((3, 4 * halo, 6 * channels), bf16),
            pltpu.VMEM((width + 2, mid, channels), f32),
            pltpu.VMEM((MEMBERS, group, span), f32),
        ),
    )(bulk, cot, near, far, across, corner, live, weight_rows, pick)
    bricks[2], *slices = lax.optimization_barrier((bricks[2], *slices))
    for place in (3, 2, 1):
        slices[place] = in_plane(slices[place], CHIPS[place])

    grad_input, act = call(
        input_kernel, "input_gradient", 20, 2 * 512 * 5184 * 256, 4 << 20, (brick, brick),
        (
            pltpu.VMEM((width + 2, rows, 9 * channels), bf16),
            pltpu.VMEM((total, channels), bf16),
        ),
    )(gp, live, weight.T, act)

    lanes = dense(total)[0]
    cols = pltpu.VMEM((9 * 2 * group, (width + 2) * SIDES * rows), bf16)
    pair = (width, SIDES * rows, channels)
    here_masked, next_masked = call(
        unpack_kernel, "unpack", 4, 1 << 20, 1 << 20, (array(pair, bf16),) * 2
    )(*bricks)
    part = call(
        first_pair_kernel, "first_pair", 16, 1 << 30, 2 << 20,
        array((2 * group, total), f32), (cols,),
    )(*slices[:2], here_masked)
    half_cols = pltpu.VMEM((9 * group, (width + 2) * SIDES * rows), bf16)
    second = part, *slices[3:1:-1], next_masked
    fold = call(
        functools.partial(second_pair_kernel, False), "second_pair_other", 16, 1 << 29, 1 << 20,
        array((group, total), bf16), (half_cols,),
    )(*second)
    keep = call(
        functools.partial(second_pair_kernel, True), "second_pair_own", 16, 1 << 29, 1 << 20,
        array((group, total), f32), (half_cols,),
    )(*second)
    own, *sends = call(
        fold_kernel, "fold", 8, 8 * total * 4, 8 * total * 40,
        (array((8, lanes), f32),) + (array((8, lanes), bf16),) * (planes - 1),
        (
            pltpu.VMEM((group + 8, sum(dense(total))), f32),
            pltpu.VMEM((planes, 8, lanes), f32),
        ),
    )(keep, in_plane(fold, 2))
    got = [swap(sends[d - 1], "depth", d, planes) for d in (2, 3, 1)]
    grad_input, *got = lax.optimization_barrier((grad_input, *got))
    voxels = count * SIDES * width * rows
    mine = call(
        functools.partial(sum_kernel, float(1.0 / voxels**0.5)),
        "plane_sum", 4, 8 * total * 4, 8 * total * 14, array((8, lanes), bf16),
    )(own, *got)
    here = call(
        unfold_kernel, "unfold", 4, 8 * total, 8 * total * 6, array((8, total), f32)
    )(mine)
    grad_weight = call(
        join_kernel, "join", 4, 8 * total, 8 * total * 14, array((channels // count, total), f32)
    )(here, in_plane(mine, 1))
    shape = features.shape
    return act.reshape(shape), grad_input.reshape(shape), grad_weight


def padded_2(cells, sides, width):
    for axis, dim in sides:
        count = lax.axis_size(axis)
        ends = count - 1
        head = lax.slice_in_dim(cells, 0, width, axis=dim)
        tail = lax.slice_in_dim(cells, cells.shape[dim] - width, cells.shape[dim], axis=dim)
        cells = jnp.concatenate(
            [
                lax.ppermute(tail, axis, [(i, (i + 1) % count) for i in range(ends)]),
                cells,
                lax.ppermute(head, axis, [((i + 1) % count, i) for i in range(ends)]),
            ],
            axis=dim,
        )
    return cells


def gather_taps(padded, width_x, width_y, depth_z, channels, flip):
    pieces = []
    for shift_x in range(3):
        for shift_y in range(3):
            for shift_z in range(3):
                start_x = 2 - shift_x if flip else shift_x
                start_y = 2 - shift_y if flip else shift_y
                start_z = 2 - shift_z if flip else shift_z
                piece = padded[
                    start_x : start_x + width_x,
                    start_y : start_y + width_y,
                    start_z : start_z + depth_z,
                    :,
                ]
                pieces.append(piece.reshape(-1, channels))
    return jnp.concatenate(pieces, axis=1)


def summed_local(features, weight, voxel_mask, cotangent):
    width_x, width_y, depth_z, channels = features.shape
    masked = features * voxel_mask.astype(jnp.bfloat16)[..., None]
    padded = padded_2(masked, (("wide", 0), ("narrow", 1)), 1)
    padded = jnp.pad(padded, ((0, 0), (0, 0), (1, 1), (0, 0)))
    columns = gather_taps(padded, width_x, width_y, depth_z, channels, False)
    pre = jnp.dot(columns, weight, preferred_element_type=jnp.float32)
    live = voxel_mask.reshape(-1, 1).astype(jnp.float32)
    sig = jax.nn.sigmoid(pre)
    activation = (
        (pre * sig * live).astype(jnp.bfloat16).reshape(width_x, width_y, depth_z, channels)
    )
    slope = sig * (1.0 + pre * (1.0 - sig))
    grad_pre = (cotangent.reshape(-1, channels).astype(jnp.float32) * live * slope).astype(
        jnp.bfloat16
    )
    taps = weight.reshape(27, channels, channels)
    grid = grad_pre.reshape(width_x, width_y, depth_z, channels)
    grad_pad = padded_2(grid, (("wide", 0), ("narrow", 1)), 1)
    grad_pad = jnp.pad(grad_pad, ((0, 0), (0, 0), (1, 1), (0, 0)))
    grad_columns = gather_taps(grad_pad, width_x, width_y, depth_z, channels, True)
    flipped = jnp.transpose(taps, (0, 2, 1)).reshape(27 * channels, channels)
    grad_field = jnp.dot(grad_columns, flipped, preferred_element_type=jnp.float32)
    grad_input = (
        (grad_field * live).astype(jnp.bfloat16).reshape(width_x, width_y, depth_z, channels)
    )
    scale = 1.0 / jnp.sqrt(
        jnp.float32(width_x * width_y * depth_z * lax.axis_size("wide") * lax.axis_size("narrow"))
    )
    whole = lax.dot_general(
        grad_pre, columns, (((0,), (0,)), ((), ())), preferred_element_type=jnp.float32
    )
    piece_flat = lax.psum_scatter(
        whole.reshape(-1), ("wide", "narrow"), scatter_dimension=0, tiled=True
    )
    gathered = lax.all_gather(piece_flat, "narrow", axis=0, tiled=True)
    summed = gathered.reshape(channels // lax.axis_size("wide"), 27 * channels)
    grad_weight = summed * scale
    return (activation, grad_input, grad_weight)


def sharded(body, mesh, wide):
    return jax.shard_map(
        body,
        mesh=mesh,
        in_specs=(
            P(wide, "narrow", None, None),
            P(),
            P(wide, "narrow", None),
            P(wide, "narrow", None, None),
        ),
        out_specs=(
            P(wide, "narrow", None, None),
            P(wide, "narrow", None, None),
            P(wide, None),
        ),
        check_vma=False,
    )


def solution(mesh):
    wide, narrow = mesh.shape["wide"], mesh.shape["narrow"]
    if wide != 4 * QUAD or narrow != SIDES:
        return sharded(summed_local, mesh, "wide")
    planes = Mesh(
        mesh.devices.reshape(wide // QUAD, QUAD, narrow), ("depth", "quad", "narrow")
    )
    return sharded(planes_local, planes, WIDE)
```

```python
import functools

import jax
import jax.numpy as jnp
from jax import lax
from jax.experimental import pallas as pl
from jax.experimental.pallas import tpu as pltpu
from jax.sharding import Mesh
from jax.sharding import PartitionSpec as P

WIDE = ("depth", "quad")
QUAD = 4
SIDES = 2
MEMBERS = QUAD * SIDES
CHIPS = (0, 1, 4, 5)
OFFSETS = (-1, 0, 1)
DEPTH = 8


def position():
    quad, side = lax.axis_index("quad"), lax.axis_index("narrow")
    return lax.axis_index("depth"), quad * SIDES + side, quad, side


def shift_z(field, step):
    if step == 0:
        return field
    depth = field.shape[1]
    moved = pltpu.roll(field, (-step) % depth, 1)
    z = lax.broadcasted_iota(jnp.int32, field.shape, 1) + step
    return jnp.where((z >= 0) & (z < depth), moved, 0.0)


def pick_kernel(planes, out_ref):
    index = lax.broadcasted_iota(jnp.int32, out_ref.shape, 0)
    column = lax.broadcasted_iota(jnp.int32, out_ref.shape, 1)
    per = out_ref.shape[1] // (planes * QUAD)
    share = per // SIDES
    group = planes * share
    quad, side = index // (SIDES * group), index // group % SIDES
    plane, row = index // share % planes, index % share
    channel = per * (QUAD * plane + quad) + share * side + row
    out_ref[...] = jnp.where(channel == column, 1.0, 0.0).astype(jnp.bfloat16)


def dense(total):
    tiles = -(-total // 128)
    moved = tiles // 4
    return (tiles - moved) * 128, moved * 128


def fold_rows(block, total):
    kept, moved = dense(total)
    tail = block[:, kept : kept + moved]
    row = lax.broadcasted_iota(jnp.int32, tail.shape, 0)
    pieces = []
    for k in range(3):
        spare = jnp.where(row == 6, pltpu.roll(tail, 6 - k, 0), pltpu.roll(tail, 4 - k, 0))
        pieces.append(jnp.where(row < 6, block[:, k * moved : (k + 1) * moved], spare))
    return jnp.concatenate(pieces + [block[:, 3 * moved : kept]], axis=1)


def unfold_rows(block, total):
    kept, moved = dense(total)
    row = lax.broadcasted_iota(jnp.int32, (8, moved), 0)
    tail = jnp.zeros((8, moved), block.dtype)
    for k in range(3):
        piece = block[:, k * moved : (k + 1) * moved]
        tail = jnp.where(row == k, pltpu.roll(piece, 2 + k, 0), tail)
        tail = jnp.where(row == 3 + k, pltpu.roll(piece, 4 + k, 0), tail)
    return jnp.concatenate([block, tail], axis=1)[:, :total]


def rows_of_128(block):
    half = block.shape[0] // 2
    rest = jnp.concatenate([block[:half, 128:], block[half:, 128:]], axis=1)
    return jnp.concatenate([block[:, :128], rest], axis=0)


def rows_of_192(block):
    count = block.shape[0] * 2 // 3
    rest = jnp.concatenate([block[count:, :64], block[count:, 64:]], axis=0)
    return jnp.concatenate([block[:count], rest], axis=1)


def prepare_kernel(features, cot, mask, first, masked_ref, cot_ref, live_ref, near_ref, far_ref):
    width, rows, channels = features.shape
    f32 = jnp.float32
    flat = mask[...].astype(f32).reshape(width * rows // DEPTH, DEPTH)
    live = jnp.broadcast_to(flat[:, :, None], flat.shape + (channels,)).reshape(features.shape)
    live_ref[...] = live[:, :, :128]
    masked_ref[...] = (features[...].astype(f32) * live).astype(jnp.bfloat16)
    cot_ref[...] = (cot[...].astype(f32) * live).astype(jnp.bfloat16)
    odd = lax.rem(position()[2], 2)
    for ref, upper in ((near_ref, 1 - odd), (far_ref, odd)):
        slabs = [
            masked_ref[pl.ds(upper * (width - 2), 2)],
            cot_ref[pl.ds(upper * (width - 1), 1)],
        ]
        slabs = jnp.concatenate(slabs, axis=0).astype(f32).reshape(3 * rows, channels)
        ref[...] = rows_of_128(slabs).astype(jnp.bfloat16)


def pack_kernel(masked, after, packed_ref):
    count, channels = packed_ref.shape[0] * 128 // masked.shape[2], masked.shape[2]
    block = masked[...].reshape(count, channels)
    packed_ref[...] = rows_of_128(block)


def across_kernel(masked, cot, across_ref):
    width, rows, channels = masked.shape
    packed = rows_of_128(masked[...].reshape(width * rows, channels))
    across_ref[: packed.shape[0]] = packed
    ahead = position()[3] == 0
    grown = cot[...].astype(jnp.float32)
    strip = jnp.where(ahead, grown[:, rows - DEPTH :], grown[:, :DEPTH])
    strip = rows_of_128(strip.reshape(width * DEPTH, channels))
    across_ref[packed.shape[0] :] = strip.astype(jnp.bfloat16)


def corner_kernel(near, far, out_ref, edge):
    _, slabs, rows, channels = edge.shape
    _, _, quad, side = position()
    odd = lax.rem(quad, 2)
    f32 = jnp.float32
    edge[odd] = rows_of_192(far[...].astype(f32)).reshape(edge.shape[1:])
    edge[1 - odd] = rows_of_192(near[...].astype(f32)).reshape(edge.shape[1:])
    halo = 2 * DEPTH
    ahead = side == 0
    strip = jnp.where(ahead, edge[:, :2, rows - halo :], edge[:, :2, :halo])
    cots = jnp.where(ahead, edge[:, 2, rows - DEPTH :], edge[:, 2, :DEPTH])
    both = [strip.reshape(4 * halo, channels), cots.reshape(2 * DEPTH, channels)]
    both = rows_of_128(jnp.concatenate(both, axis=0))
    blank = jnp.zeros((out_ref.shape[0] - both.shape[0], 128), f32)
    out_ref[...] = jnp.concatenate([both, blank], axis=0).astype(jnp.bfloat16)


def turn_kernel(weight, out_ref):
    step = 2 * weight.shape[0]
    total = weight.shape[1]
    for start in range(0, total, step):
        stop = min(start + step, total)
        out_ref[start:stop, :] = weight[:, start:stop].T


def bulk_kernel(masked, near, far, across, weight, pre_ref, ext, edge, cols):
    width, rows, channels = masked.shape
    f32 = jnp.float32
    plane, _, quad, side = position()
    use_low = side.astype(f32)
    use_high = (1 - side).astype(f32)
    place = plane * QUAD + quad
    use_left = (place > 0).astype(f32)
    use_right = (place < QUAD * lax.axis_size("depth") - 1).astype(f32)
    halo = 2 * DEPTH
    tall = rows + 2 * halo
    mid = rows + 2 * DEPTH
    span = width + 4
    odd = lax.rem(quad, 2)
    edge[odd] = rows_of_192(far[...].astype(f32)).reshape(edge.shape[1:])
    edge[1 - odd] = rows_of_192(near[...].astype(f32)).reshape(edge.shape[1:])
    ext[0:2, halo : halo + rows, :] = edge[0, 0:2] * use_left
    ext[2 : 2 + width, halo : halo + rows, :] = masked[...].astype(f32)
    ext[2 + width :, halo : halo + rows, :] = edge[1, 0:2] * use_right
    half = width // 2
    count = width * rows * channels // 128
    held = across[:count].astype(f32).reshape(width + half, rows, 128)
    brick = jnp.where(side == 0, held[:, :halo], held[:, rows - halo :])
    rest = jnp.concatenate([brick[width:, :, :64], brick[width:, :, 64:]], axis=0)
    beside = jnp.concatenate([brick[:width], rest], axis=2)
    blank = jnp.zeros((2, halo, channels), f32)
    for use, start in ((use_low, 0), (use_high, halo + rows)):
        at = slice(start, start + halo)
        ext[0:2, at, :] = blank
        ext[2 : 2 + width, at, :] = beside * use
        ext[2 + width :, at, :] = blank
    field = ext[...].reshape(span * tall // DEPTH, DEPTH, channels)
    for c in OFFSETS:
        moved = shift_z(field, c).reshape(span, tall, channels)
        for b in OFFSETS:
            at = ((b + 1) * 3 + c + 1) * channels
            start = DEPTH * (b + 1)
            cols[:, :, at : at + channels] = moved[:, start : start + mid].astype(jnp.bfloat16)
    nine = 9 * channels
    pre = jnp.zeros(((width + 2) * mid, channels), f32)
    for a in range(3):
        pre += jnp.dot(
            cols[a : a + width + 2].reshape((width + 2) * mid, nine),
            weight[a * nine : (a + 1) * nine, :],
            preferred_element_type=f32,
        )
    pre_ref[...] = pre.reshape(pre_ref.shape)


def forward_kernel(bulk, cot, near, far, across, corner, live, weight, pick, *refs):
    act_ref, gp_ref = refs[:2]
    slice_refs = refs[2 : 2 + len(CHIPS)]
    edge, cols, total, slices = refs[2 + len(CHIPS) :]
    width, rows, channels = cot.shape
    f32 = jnp.float32
    plane, me, quad, side = position()
    use_low = side.astype(f32)
    use_high = (1 - side).astype(f32)
    place = plane * QUAD + quad
    use_left = (place > 0).astype(f32)
    use_right = (place < QUAD * lax.axis_size("depth") - 1).astype(f32)
    halo = 2 * DEPTH
    mid = rows + 2 * DEPTH
    count = 4 * halo + 2 * DEPTH
    both = rows_of_192(corner[...].astype(f32)[: count * channels // 128])
    corners = both[: 4 * halo].reshape(2, 2, halo, channels)
    corners = jnp.concatenate([corners[0] * use_left, corners[1] * use_right], axis=0)
    sources = ((0, 1, None, None), (1, None, None, 2), (None, None, 2, 3))
    blank = jnp.zeros((DEPTH, channels), f32)
    six = 6 * channels
    for c in OFFSETS:
        moved = shift_z(corners.reshape(8, DEPTH, channels), c)
        for b, low, high in ((0, (0, 1), (None, 0)), (1, (1, None), (0, 1))):
            at = (b * 3 + c + 1) * channels
            parts = []
            for slab in range(4):
                for below, above in zip(low, high):
                    part = blank if below is None else moved[2 * slab + below] * use_low
                    if above is not None:
                        part = part + moved[2 * slab + above] * use_high
                    parts.append(part)
            for a in range(3):
                rows_a = []
                for source in sources[a]:
                    pair = [blank] * 2 if source is None else parts[2 * source : 2 * source + 2]
                    rows_a += pair
                cols[a, :, at : at + channels] = jnp.concatenate(rows_a, axis=0).astype(
                    jnp.bfloat16
                )
    share = jnp.zeros((4 * halo, channels), f32)
    for a in range(3):
        taps = pl.ds(pl.multiple_of((3 * a + 1 - side) * 3 * channels, 16), six)
        share += jnp.dot(cols[a], weight[taps], preferred_element_type=f32)
    share = share.reshape(4, halo, channels)
    total[...] = bulk[...]
    at = pl.ds(pl.multiple_of((1 - side) * (mid - halo), DEPTH), halo)
    total[0:2, at, :] += share[0:2]
    total[width : width + 2, at, :] += share[2:4]
    pre = total[...].reshape((width + 2) * mid, channels)
    sig = 0.5 * jnp.tanh(0.5 * pre) + 0.5
    act = (pre * sig).reshape(width + 2, mid, channels)[1 : 1 + width, DEPTH : DEPTH + rows]
    act_ref[...] = (act * live[:, :, 0:1]).astype(jnp.bfloat16)
    slope = (sig * (1.0 + pre * (1.0 - sig))).reshape(width + 2, mid, channels)
    ends = both[4 * halo :].reshape(2, 1, DEPTH, channels)
    strip = across[width * rows * channels // 128 :].astype(f32)
    beyond = jnp.concatenate(
        [
            ends[0] * use_left,
            rows_of_192(strip).reshape(width, DEPTH, channels),
            ends[1] * use_right,
        ],
        axis=0,
    )
    odd = lax.rem(quad, 2)
    edge[odd] = rows_of_192(far[...].astype(f32))[2 * rows :]
    edge[1 - odd] = rows_of_192(near[...].astype(f32))[2 * rows :]
    centre = [edge[0:1] * use_left, cot[...].astype(f32), edge[1:2] * use_right]
    centre = jnp.concatenate(centre, axis=0)
    full = jnp.concatenate([beyond * use_low, centre, beyond * use_high], axis=1)
    grad = full * slope
    gp_ref[...] = grad.astype(jnp.bfloat16)
    inner = grad[:, DEPTH : DEPTH + rows].astype(jnp.bfloat16)
    turned = lax.dot_general(
        pick[...],
        inner.reshape((width + 2) * rows, channels),
        (((1,), (1,)), ((), ())),
        preferred_element_type=f32,
    )
    slices[...] = turned.reshape(slices.shape)
    chip = me - lax.rem(quad, 2) * SIDES
    for distance, ref in zip(CHIPS, slice_refs):
        both = [slices[chip ^ distance], slices[(chip ^ distance) + SIDES]]
        ref[...] = jnp.concatenate(both, axis=0).astype(jnp.bfloat16)


def input_kernel(gp, live, turned, act, out_ref, act_ref, cols, weight):
    act_ref[...] = act[...]
    width, rows, channels = out_ref.shape
    f32 = jnp.float32
    tall = rows + 2 * DEPTH
    for tap in range(27):
        weight[tap * channels : (tap + 1) * channels, :] = turned[
            :, tap * channels : (tap + 1) * channels
        ]
    field = gp[...].astype(f32).reshape((width + 2) * tall // DEPTH, DEPTH, channels)
    for c in OFFSETS:
        moved = shift_z(field, -c).reshape(width + 2, tall, channels)
        for b in OFFSETS:
            at = ((b + 1) * 3 + c + 1) * channels
            start = DEPTH * (1 - b)
            cols[:, :, at : at + channels] = moved[:, start : start + rows].astype(jnp.bfloat16)
    nine = 9 * channels
    total = jnp.zeros((width * rows, channels), f32)
    for a in range(3):
        total += jnp.dot(
            cols[2 - a : 2 - a + width].reshape(width * rows, nine),
            weight[a * nine : (a + 1) * nine, :],
            preferred_element_type=f32,
        )
    out_ref[...] = (total.reshape(width, rows, channels) * live[:, :, 0:1]).astype(jnp.bfloat16)


def unpack_pair(bricks, masked):
    per, lane, _ = masked.shape
    half = lane // 2
    side = position()[3]
    for i, brick in enumerate(bricks):
        at_rows = pl.ds(pl.multiple_of((side ^ i) * half, half), half)
        for x in range(per):
            shift = 64 * (x // (per // 2))
            rest = brick[pl.ds((per + x % (per // 2)) * half, half)]
            masked[x, at_rows, :128] = brick[pl.ds(x * half, half)]
            masked[x, at_rows, 128:] = rest[:, shift : shift + 64]


def pair_product(received, masked, cols):
    f32 = jnp.float32
    group = received[0].shape[0]
    per, lane, channels = masked.shape
    half = lane // 2
    side = position()[3]
    at = lax.broadcasted_iota(jnp.int32, (group, lane), 1)
    y, z = at // DEPTH, at % DEPTH
    tall = lane // DEPTH
    own, other = received
    first = jnp.where(side == 0, own, other)
    second = jnp.where(side == 0, other, own)
    for k in range(per + 2):
        one = first[:, k // 2 * lane : (k // 2 + 1) * lane]
        two = second[:, k // 2 * lane : (k // 2 + 1) * lane]
        if k % 2 == 0:
            base = jnp.where(at < half, one, pltpu.roll(two, half, 1))
        else:
            base = jnp.where(at < half, pltpu.roll(one, half, 1), two)
        pieces = []
        for b in OFFSETS:
            for c in OFFSETS:
                step = (DEPTH * b + c) % lane
                moved = base if step == 0 else pltpu.roll(base, step, 1)
                keep = (y - b >= 0) & (y - b < tall) & (z - c >= 0) & (z - c < DEPTH)
                pieces.append(jnp.where(keep, moved, 0.0))
        cols[:, k * lane : (k + 1) * lane] = jnp.concatenate(pieces, axis=0).astype(jnp.bfloat16)
    field = masked[...].reshape(per * lane, channels)
    for a in range(3):
        start = (2 - a) * lane
        got = jnp.dot(
            cols[:, start : start + per * lane], field, preferred_element_type=f32
        ).reshape(9, group, channels)
        yield a, jnp.concatenate([got[tap] for tap in range(9)], axis=1)


def unpack_kernel(brick, across, beside, beyond, here_ref, next_ref):
    unpack_pair((brick, across), here_ref)
    unpack_pair((beside, beyond), next_ref)


def first_pair_kernel(own, other, masked, part_ref, cols):
    received = own[...].astype(jnp.float32), other[...].astype(jnp.float32)
    for a, rows in pair_product(received, masked, cols):
        width = rows.shape[1]
        part_ref[:, a * width : (a + 1) * width] = rows


def second_pair_kernel(own_rows, before, other, own, masked, out_ref, cols):
    core = lax.rem(position()[2], 2)
    half = before.shape[0] // 2
    upper = core if own_rows else 1 - core
    received = [ref[...].astype(jnp.float32) for ref in (own, other)]
    received = [jnp.where(upper == 1, block[half:], block[:half]) for block in received]
    held = pl.ds(pl.multiple_of(upper * half, 8), half)
    for a, rows in pair_product(received, masked, cols):
        width = rows.shape[1]
        at = slice(a * width, (a + 1) * width)
        out_ref[:, at] = (before[held, at] + rows).astype(out_ref.dtype)


def fold_kernel(keep, other, own_ref, *refs):
    *send_refs, both, rows = refs
    planes, eight, _ = rows.shape
    count, total = keep.shape
    share = count // planes
    both[:count, :total] = keep[...] + other[...].astype(jnp.float32)
    both[:, total:] = jnp.zeros((both.shape[0], both.shape[1] - total), jnp.float32)
    for to in range(planes):
        rows[to] = fold_rows(both[share * to : share * to + eight, :], total)
    plane = position()[0]
    own_ref[...] = rows[plane]
    for distance, ref in enumerate(send_refs, 1):
        ref[...] = rows[plane ^ distance].astype(jnp.bfloat16)


def sum_kernel(scale, own, one, two, three, out_ref):
    f32 = jnp.float32
    total = own[...] + one[...].astype(f32) + two[...].astype(f32) + three[...].astype(f32)
    out_ref[...] = (total * scale).astype(out_ref.dtype)


def join_kernel(mine, other, out_ref):
    share = out_ref.shape[0] // SIDES
    ahead = position()[3] == 0
    total = out_ref.shape[1]
    here = unfold_rows(mine[...].astype(jnp.float32), total)
    there = unfold_rows(other[...].astype(jnp.float32), total)
    first = jnp.where(ahead, here, there)
    second = jnp.where(ahead, there, here)
    out_ref[0:share] = first[:share]
    out_ref[share:] = second[:share]


def call(body, name, mebibytes, flops, moved, out_shape, scratch=(), in_specs=None):
    spec = pl.BlockSpec(memory_space=pltpu.VMEM)

    def run(*operands):
        return pl.pallas_call(
            body,
            out_shape=out_shape,
            in_specs=in_specs or [spec] * len(operands),
            out_specs=jax.tree.map(lambda _: spec, out_shape),
            scratch_shapes=scratch,
            compiler_params=pltpu.CompilerParams(vmem_limit_bytes=mebibytes << 20),
            cost_estimate=pl.CostEstimate(flops=flops, bytes_accessed=moved, transcendentals=0),
            name=name,
        )(*operands)

    return run


def planes_local(features, weight, voxel_mask, cotangent):
    bf16 = jnp.bfloat16
    f32 = jnp.float32
    array = jax.ShapeDtypeStruct
    width, wide_y, depth, channels = features.shape
    rows = wide_y * depth
    planes = lax.axis_size("depth")
    count = planes * QUAD
    total = 27 * channels
    halo = 2 * DEPTH
    span = (width + 2) * rows
    share = channels // count // SIDES
    group = planes * share

    def swap(piece, axes, distance, size):
        return lax.ppermute(piece, axes, [(i, i ^ distance) for i in range(size)])

    def in_plane(piece, distance):
        return swap(piece, ("quad", "narrow"), distance, MEMBERS)

    brick = array((width, rows, channels), bf16)
    slab = array((3 * rows * channels // 128, 128), bf16)
    slabs = (2, 3, rows, channels)
    pick = call(
        functools.partial(pick_kernel, planes), "pick", 4, 1 << 32, 1 << 16,
        array((MEMBERS * group, channels), bf16),
    )()
    vmem = pl.BlockSpec(memory_space=pltpu.VMEM)
    masked, cot, live, near, far = call(
        prepare_kernel, "prepare", 16, 1 << 20, 1 << 20,
        (brick, brick, array((width, rows, 128), f32), slab, slab),
        (),
        [vmem] * 3 + [pl.BlockSpec(memory_space=pl.ANY)],
    )(
        features.reshape(width, rows, channels),
        cotangent.reshape(width, rows, channels),
        voxel_mask,
        pick,
    )
    near = swap(near, WIDE, 1, count)
    ends = [min(max(((i + 1) ^ 1) - 1, 0), count - 1) for i in range(count)]
    far = lax.ppermute(far, WIDE, list(enumerate(ends)))
    weight_rows = call(
        turn_kernel, "turn", 8, 1 << 20, 4 << 20, array((total, channels), bf16)
    )(weight.T)
    count_128 = width * rows * channels // 128
    strip_128 = width * DEPTH * channels // 128
    across = call(
        across_kernel, "across", 4, 1 << 16, 1 << 19, array((count_128 + strip_128, 128), bf16)
    )(masked, cot)
    across = in_plane(across, CHIPS[1])
    packed = call(
        pack_kernel, "pack", 4, 1 << 16, 1 << 19, array((count_128, 128), bf16), (),
        [vmem, pl.BlockSpec(memory_space=pl.ANY)],
    )(masked, near)
    near, far, weight_rows, late = lax.optimization_barrier((near, far, weight_rows, packed))
    corner = call(
        corner_kernel, "corner", 4, 1 << 16, 1 << 18,
        array((128, 128), bf16),
        (pltpu.VMEM(slabs, f32),),
    )(near, far)
    corner = in_plane(corner, 1)
    mid = rows + 2 * DEPTH
    bulk = call(
        bulk_kernel, "bulk", 24, 3 << 29, 1 << 20, array((width + 2, mid, channels), f32),
        (
            pltpu.VMEM((width + 4, rows + 2 * halo, channels), f32),
            pltpu.VMEM(slabs, f32),
            pltpu.VMEM((width + 4, mid, 9 * channels), bf16),
        ),
    )(masked, near, far, across, weight_rows)
    bricks = [packed, across, in_plane(packed, CHIPS[2]), in_plane(late, CHIPS[3])]

    act, gp, *slices = call(
        forward_kernel, "forward", 24, 3 << 29, 1 << 20,
        (brick, array((width + 2, mid, channels), bf16))
        + (array((2 * group, span), bf16),) * len(CHIPS),
        (
            pltpu.VMEM((2, rows, channels), f32),
            pltpu.VMEM((3, 4 * halo, 6 * channels), bf16),
            pltpu.VMEM((width + 2, mid, channels), f32),
            pltpu.VMEM((MEMBERS, group, span), f32),
        ),
    )(bulk, cot, near, far, across, corner, live, weight_rows, pick)
    bricks[2], *slices = lax.optimization_barrier((bricks[2], *slices))
    for place in (3, 2, 1):
        slices[place] = in_plane(slices[place], CHIPS[place])

    grad_input, act = call(
        input_kernel, "input_gradient", 20, 2 * 512 * 5184 * 256, 4 << 20, (brick, brick),
        (
            pltpu.VMEM((width + 2, rows, 9 * channels), bf16),
            pltpu.VMEM((total, channels), bf16),
        ),
    )(gp, live, weight.T, act)

    lanes = dense(total)[0]
    cols = pltpu.VMEM((9 * 2 * group, (width + 2) * SIDES * rows), bf16)
    pair = (width, SIDES * rows, channels)
    here_masked, next_masked = call(
        unpack_kernel, "unpack", 4, 1 << 20, 1 << 20, (array(pair, bf16),) * 2
    )(*bricks)
    part = call(
        first_pair_kernel, "first_pair", 16, 1 << 30, 2 << 20,
        array((2 * group, total), f32), (cols,),
    )(*slices[:2], here_masked)
    half_cols = pltpu.VMEM((9 * group, (width + 2) * SIDES * rows), bf16)
    second = part, *slices[3:1:-1], next_masked
    fold = call(
        functools.partial(second_pair_kernel, False), "second_pair_other", 16, 1 << 29, 1 << 20,
        array((group, total), bf16), (half_cols,),
    )(*second)
    keep = call(
        functools.partial(second_pair_kernel, True), "second_pair_own", 16, 1 << 29, 1 << 20,
        array((group, total), f32), (half_cols,),
    )(*second)
    own, *sends = call(
        fold_kernel, "fold", 8, 8 * total * 4, 8 * total * 40,
        (array((8, lanes), f32),) + (array((8, lanes), bf16),) * (planes - 1),
        (
            pltpu.VMEM((group + 8, sum(dense(total))), f32),
            pltpu.VMEM((planes, 8, lanes), f32),
        ),
    )(keep, in_plane(fold, 2))
    got = [swap(sends[d - 1], "depth", d, planes) for d in (2, 3, 1)]
    grad_input, *got = lax.optimization_barrier((grad_input, *got))
    voxels = count * SIDES * width * rows
    mine = call(
        functools.partial(sum_kernel, float(1.0 / voxels**0.5)),
        "plane_sum", 4, 8 * total * 4, 8 * total * 14, array((8, lanes), bf16),
    )(own, *got)
    grad_weight = call(
        join_kernel, "join", 4, 8 * total, 8 * total * 14, array((channels // count, total), f32)
    )(mine, in_plane(mine, 1))
    shape = features.shape
    return act.reshape(shape), grad_input.reshape(shape), grad_weight


def padded_2(cells, sides, width):
    for axis, dim in sides:
        count = lax.axis_size(axis)
        ends = count - 1
        head = lax.slice_in_dim(cells, 0, width, axis=dim)
        tail = lax.slice_in_dim(cells, cells.shape[dim] - width, cells.shape[dim], axis=dim)
        cells = jnp.concatenate(
            [
                lax.ppermute(tail, axis, [(i, (i + 1) % count) for i in range(ends)]),
                cells,
                lax.ppermute(head, axis, [((i + 1) % count, i) for i in range(ends)]),
            ],
            axis=dim,
        )
    return cells


def gather_taps(padded, width_x, width_y, depth_z, channels, flip):
    pieces = []
    for shift_x in range(3):
        for shift_y in range(3):
            for shift_z in range(3):
                start_x = 2 - shift_x if flip else shift_x
                start_y = 2 - shift_y if flip else shift_y
                start_z = 2 - shift_z if flip else shift_z
                piece = padded[
                    start_x : start_x + width_x,
                    start_y : start_y + width_y,
                    start_z : start_z + depth_z,
                    :,
                ]
                pieces.append(piece.reshape(-1, channels))
    return jnp.concatenate(pieces, axis=1)


def summed_local(features, weight, voxel_mask, cotangent):
    width_x, width_y, depth_z, channels = features.shape
    masked = features * voxel_mask.astype(jnp.bfloat16)[..., None]
    padded = padded_2(masked, (("wide", 0), ("narrow", 1)), 1)
    padded = jnp.pad(padded, ((0, 0), (0, 0), (1, 1), (0, 0)))
    columns = gather_taps(padded, width_x, width_y, depth_z, channels, False)
    pre = jnp.dot(columns, weight, preferred_element_type=jnp.float32)
    live = voxel_mask.reshape(-1, 1).astype(jnp.float32)
    sig = jax.nn.sigmoid(pre)
    activation = (
        (pre * sig * live).astype(jnp.bfloat16).reshape(width_x, width_y, depth_z, channels)
    )
    slope = sig * (1.0 + pre * (1.0 - sig))
    grad_pre = (cotangent.reshape(-1, channels).astype(jnp.float32) * live * slope).astype(
        jnp.bfloat16
    )
    taps = weight.reshape(27, channels, channels)
    grid = grad_pre.reshape(width_x, width_y, depth_z, channels)
    grad_pad = padded_2(grid, (("wide", 0), ("narrow", 1)), 1)
    grad_pad = jnp.pad(grad_pad, ((0, 0), (0, 0), (1, 1), (0, 0)))
    grad_columns = gather_taps(grad_pad, width_x, width_y, depth_z, channels, True)
    flipped = jnp.transpose(taps, (0, 2, 1)).reshape(27 * channels, channels)
    grad_field = jnp.dot(grad_columns, flipped, preferred_element_type=jnp.float32)
    grad_input = (
        (grad_field * live).astype(jnp.bfloat16).reshape(width_x, width_y, depth_z, channels)
    )
    scale = 1.0 / jnp.sqrt(
        jnp.float32(width_x * width_y * depth_z * lax.axis_size("wide") * lax.axis_size("narrow"))
    )
    whole = lax.dot_general(
        grad_pre, columns, (((0,), (0,)), ((), ())), preferred_element_type=jnp.float32
    )
    piece_flat = lax.psum_scatter(
        whole.reshape(-1), ("wide", "narrow"), scatter_dimension=0, tiled=True
    )
    gathered = lax.all_gather(piece_flat, "narrow", axis=0, tiled=True)
    summed = gathered.reshape(channels // lax.axis_size("wide"), 27 * channels)
    grad_weight = summed * scale
    return (activation, grad_input, grad_weight)


def sharded(body, mesh, wide):
    return jax.shard_map(
        body,
        mesh=mesh,
        in_specs=(
            P(wide, "narrow", None, None),
            P(),
            P(wide, "narrow", None),
            P(wide, "narrow", None, None),
        ),
        out_specs=(
            P(wide, "narrow", None, None),
            P(wide, "narrow", None, None),
            P(wide, None),
        ),
        check_vma=False,
    )


def solution(mesh):
    wide, narrow = mesh.shape["wide"], mesh.shape["narrow"]
    if wide != 4 * QUAD or narrow != SIDES:
        return sharded(summed_local, mesh, "wide")
    planes = Mesh(
        mesh.devices.reshape(wide // QUAD, QUAD, narrow), ("depth", "quad", "narrow")
    )
    return sharded(planes_local, planes, WIDE)
```
